32 devices in a mesh: dp: 8 (over z, y), mp: 4 (over x, core).
Axes of the slice: x: 2, y: 2, z: 4, core: 2. Of those that a mesh axis runs over, the one named last changes fastest.
Arguments:
- image_in: bfloat16 [512, 64, 2048], P(('dp', 'mp')), may hold values from -64 to 64
- cotangent: bfloat16 [512, 64, 2048], P(('dp', 'mp')), may hold values from -9 to 9
- heights: int32 [2, 8], replicated, may hold values from 1 to 63, as said below
- widths: int32 [2, 8], replicated, may hold values from 16 to 64, as said below
- weight_in_a: bfloat16 [2048, 512], P('dp', 'mp'), may hold values from -0.125 to 0.125
- weight_offset: bfloat16 [4608, 18], replicated, may hold values from -0.25 to 0.25
- bias_offset: float32 [18], replicated, may hold values from -3 to 3
- weight_mid_a: bfloat16 [4608, 512], P('dp', 'mp'), may hold values from -0.09375 to 0.09375
- weight_out_a: bfloat16 [512, 2048], P('dp', 'mp'), may hold values from -0.25 to 0.25
- weight_in_b: bfloat16 [2048, 512], P('dp', 'mp'), may hold values from -0.125 to 0.125
- weight_mid_b: bfloat16 [4608, 512], P('dp', 'mp'), may hold values from -0.09375 to 0.09375
- weight_out_b: bfloat16 [512, 2048], P('dp', 'mp'), may hold values from -0.25 to 0.25
- mid_gain: float32 [2, 2, 512], replicated, may hold values from 0.25 to 1.75
- mid_bias: float32 [2, 2, 512], replicated, may hold values from -3 to 3
- out_gain: float32 [2, 2048], replicated, may hold values from 0.25 to 1.75
- out_bias: float32 [2, 2048], replicated, may hold values from -3 to 3
Outputs:
- image_out: bfloat16 [512, 64, 2048], P(('dp', 'mp'))
- image_grad: float32 [512, 64, 2048], P(('dp', 'mp'))
- grad_in_a: float32 [2048, 512], P('dp', 'mp')
- grad_offset: float32 [4608, 18], replicated
- grad_offset_bias: float32 [18], replicated
- grad_mid_a: float32 [4608, 512], P('dp', 'mp')
- grad_out_a: float32 [512, 2048], P('dp', 'mp')
- grad_in_b: float32 [2048, 512], P('dp', 'mp')
- grad_mid_b: float32 [4608, 512], P('dp', 'mp')
- grad_out_b: float32 [512, 2048], P('dp', 'mp')
- grad_mid_gain: float32 [2, 2, 512], replicated
- grad_mid_bias: float32 [2, 2, 512], replicated
- grad_out_gain: float32 [2, 2048], replicated
- grad_out_bias: float32 [2, 2048], replicated
The draws below stay inside these ranges and needn't reach their ends.
Inputs may be any that keep to these rules, and one draw needn't show every extreme that they name: Group 0's heights sum to 264 and group 1's to 248; the last image of group 0 and the first image of group 1 have exactly 63 rows. Group 0 widths lie from 32 to 64, group 1 widths from 16 to 40; in each group one image has the largest width of its range.
All inputs are finite; a program needn't handle non-finite values.
Results may differ from the reference program's by a relative error of at most 0.023.
Values may be sent and summed in bfloat16 or wider, within the bound.
A program may use at most 384 MiB of HBM per device.

```python
import jax
import jax.numpy as jnp
from jax import lax

C_IN = 2048
C_MID = 512
TAPS = 9
OFFSETS = 18
WIDE = 64
MOST_H = 63
ROWS = 512
ROWS_GRP = 264
IMG_GRP = 8


def rising_scales(key, count, spread):
    position = jnp.arange(count, dtype=jnp.float32) / count
    rough = jax.random.uniform(key, (count,), jnp.float32)
    return 3.0 ** (position - 0.5) * 10.0 ** (spread * (rough - 0.5))


def draw_image_in(key, part):
    key = jax.random.fold_in(key, 11)
    sub_keys = jax.random.split(key, 4)
    row_scale = rising_scales(sub_keys[0], ROWS, 1.0)
    chan_scale = 10.0 ** (0.5 * (jax.random.uniform(sub_keys[1], (C_IN,), jnp.float32) - 0.5))
    base_draw = jnp.clip(jax.random.normal(sub_keys[3], (ROWS, WIDE, C_IN), jnp.float32), -5.0, 5.0)
    return (base_draw * row_scale[:, None, None] * chan_scale).astype(jnp.bfloat16)


def draw_cotangent(key, part):
    key = jax.random.fold_in(key, 12)
    sub_keys = jax.random.split(key, 3)
    row_scale = rising_scales(sub_keys[0], ROWS, 0.0)
    base_draw = jnp.clip(jax.random.normal(sub_keys[2], (ROWS, WIDE, C_IN), jnp.float32), -5.0, 5.0)
    return (base_draw * row_scale[:, None, None]).astype(jnp.bfloat16)


def group_heights(key, total_rows, tall_last):
    slots_each = MOST_H - 1
    slot_count = (IMG_GRP - 1) * slots_each
    extra_rows = total_rows - MOST_H - (IMG_GRP - 1)
    order = jax.random.permutation(key, slot_count)
    chosen = (order < extra_rows).astype(jnp.int32)
    owner = jnp.arange(slot_count, dtype=jnp.int32) // slots_each
    images = jnp.arange(IMG_GRP - 1, dtype=jnp.int32)
    counts = jnp.sum(jnp.where(owner[None, :] == images[:, None], chosen[None, :], 0), axis=1).astype(jnp.int32)
    others = 1 + counts
    tallest = jnp.full((1,), MOST_H, jnp.int32)
    if tall_last:
        return jnp.concatenate([others, tallest])
    return jnp.concatenate([tallest, others])


def draw_heights(key, part):
    key = jax.random.fold_in(key, 14)
    sub_keys = jax.random.split(key, 2)
    first_group = group_heights(sub_keys[0], ROWS_GRP, True)
    second_group = group_heights(sub_keys[1], ROWS - ROWS_GRP, False)
    return jnp.stack([first_group, second_group]).astype(jnp.int32)


def draw_widths(key, part):
    key = jax.random.fold_in(key, 13)
    sub_keys = jax.random.split(key, 4)
    wide_group = jax.random.randint(sub_keys[0], (IMG_GRP,), WIDE // 2, WIDE + 1)
    narrow_group = jax.random.randint(sub_keys[1], (IMG_GRP,), WIDE // 4, 5 * WIDE // 8 + 1)
    wide_pick = jax.random.randint(sub_keys[2], (), 0, IMG_GRP)
    narrow_pick = jax.random.randint(sub_keys[3], (), 0, IMG_GRP)
    slots = jnp.arange(IMG_GRP)
    wide_group = jnp.where(slots == wide_pick, WIDE, wide_group)
    narrow_group = jnp.where(slots == narrow_pick, 5 * WIDE // 8, narrow_group)
    return jnp.stack([wide_group, narrow_group]).astype(jnp.int32)


def levels(rng, shape, cuts, least, largest):
    level, own = 1.0, jax.random.fold_in(rng, 6)
    for dim, shards_of in cuts:
        draws = jnp.exp(jax.random.uniform(jax.random.fold_in(own, dim), (shards_of,), jnp.float32, least / len(cuts), largest / len(cuts)))
        level = level * jnp.repeat(draws, shape[dim] // shards_of).reshape([-1 if axis == dim else 1 for axis in range(len(shape))])
    return level


def gaussian(key, dims, deviation, limit, cuts=(), kind=jnp.bfloat16):
    loudness = levels(key, dims, cuts, -0.22, 0.18) if cuts else 1.0
    drawn = jax.random.normal(key, dims, jnp.float32) * deviation * loudness
    return jnp.minimum(jnp.maximum(drawn, -limit), limit).astype(kind)


def setup_inputs(seed: int = 0) -> dict:
    arg_keys = jax.random.split(jax.random.key(seed), 17)
    return {
        "image_in": draw_image_in(jax.random.fold_in(arg_keys[16], 71), 0),
        "cotangent": draw_cotangent(jax.random.fold_in(arg_keys[16], 71), 0),
        "heights": draw_heights(jax.random.fold_in(arg_keys[16], 71), 0),
        "widths": draw_widths(jax.random.fold_in(arg_keys[16], 71), 0),
        "weight_in_a": gaussian(arg_keys[4], (C_IN, C_MID), C_IN ** -0.5, 0.125, ((0, 8), (1, 4))),
        "weight_offset": gaussian(arg_keys[5], (TAPS * C_MID, OFFSETS), C_MID ** -0.5, 0.25),
        "bias_offset": gaussian(arg_keys[6], (OFFSETS,), 0.5, 3.0, (), jnp.float32),
        "weight_mid_a": gaussian(arg_keys[7], (TAPS * C_MID, C_MID), (TAPS * C_MID) ** -0.5, 0.09375, ((0, 8), (1, 4))),
        "weight_out_a": gaussian(arg_keys[8], (C_MID, C_IN), C_MID ** -0.5, 0.25, ((0, 8), (1, 4))),
        "weight_in_b": gaussian(arg_keys[9], (C_IN, C_MID), C_IN ** -0.5, 0.125, ((0, 8), (1, 4))),
        "weight_mid_b": gaussian(arg_keys[10], (TAPS * C_MID, C_MID), (TAPS * C_MID) ** -0.5, 0.09375, ((0, 8), (1, 4))),
        "weight_out_b": gaussian(arg_keys[11], (C_MID, C_IN), C_MID ** -0.5, 0.25, ((0, 8), (1, 4))),
        "mid_gain": jnp.clip(1.0 + 0.15 * jax.random.normal(arg_keys[12], (2, 2, C_MID), jnp.float32), 0.25, 1.75),
        "mid_bias": gaussian(arg_keys[13], (2, 2, C_MID), 0.5, 3.0, (), jnp.float32),
        "out_gain": jnp.clip(1.0 + 0.15 * jax.random.normal(arg_keys[14], (2, C_IN), jnp.float32), 0.25, 1.75),
        "out_bias": gaussian(arg_keys[15], (2, C_IN), 0.5, 3.0, (), jnp.float32),
    }


norm_eps = 1e-05
halo_rows = 3

@jax.custom_vjp
def low(v):
    return lax.optimization_barrier(v.astype(jnp.bfloat16)).astype(jnp.float32)

@jax.custom_vjp
def low_back(v):
    return v

def low_keep(v):
    return (low(v), None)

def low_pass(kept, grad):
    return (grad,)

def back_keep(v):
    return (v, None)

def back_low(kept, grad):
    return (low(grad),)
low.defvjp(low_keep, low_pass)
low_back.defvjp(back_keep, back_low)

def gelu_tanh(values):
    return jax.nn.gelu(values, approximate=True)

def row_info(row_index, heights, widths, group_rows, total_rows):
    image_count = heights.shape[1]
    inside = (row_index >= 0) & (row_index < total_rows)
    group_of = jnp.clip(row_index // group_rows, 0, 1).astype(jnp.int32)
    local_row = (row_index - group_of * group_rows).astype(jnp.int32)
    image_ends = jnp.cumsum(heights, axis=1).astype(jnp.int32)
    is_first = (group_of == 0)[:, None]
    ends_by_row = jnp.where(is_first, image_ends[0][None, :], image_ends[1][None, :])
    image_num = lax.optimization_barrier(jnp.sum((local_row[:, None] >= ends_by_row).astype(jnp.int32), axis=1)).astype(jnp.int32)
    identity = jnp.where(inside, group_of * image_count + image_num, -1).astype(jnp.int32)
    width_table = jnp.where(is_first, widths[0][None, :], widths[1][None, :])
    picked = jnp.arange(image_count, dtype=jnp.int32)[None, :] == image_num[:, None]
    width_row = lax.optimization_barrier(jnp.sum(jnp.where(picked, width_table, 0), axis=1)).astype(jnp.int32)
    return (identity, jnp.where(inside, width_row, 0).astype(jnp.int32))

def tap_masks(identity, height):
    centre = identity[halo_rows:halo_rows + height]
    return [(identity[halo_rows + row_shift:halo_rows + row_shift + height] == centre).astype(jnp.float32)[:, None, None] for row_shift in range(-2, 4)]

def window(padded, row_shift, col_shift, height, breadth):
    return padded[halo_rows + row_shift:halo_rows + row_shift + height, halo_rows + col_shift:halo_rows + col_shift + breadth]

def tap_columns(field_ext, row_masks):
    height = field_ext.shape[0] - 2 * halo_rows
    breadth = field_ext.shape[1]
    padded = jnp.pad(field_ext, ((0, 0), (halo_rows, halo_rows), (0, 0)))
    pieces = []
    for tap_row in range(3):
        for tap_col in range(3):
            row_shift = 2 * tap_row - 2
            col_shift = 2 * tap_col - 2
            pieces.append(row_masks[row_shift + 2] * window(padded, row_shift, col_shift, height, breadth))
    return jnp.concatenate(pieces, axis=-1)

def sample_columns(field_ext, offsets, row_masks):
    height = field_ext.shape[0] - 2 * halo_rows
    breadth = field_ext.shape[1]
    padded = jnp.pad(field_ext, ((0, 0), (halo_rows, halo_rows), (0, 0)))
    pieces = []
    for tap_row in range(3):
        for tap_col in range(3):
            tap_index = 3 * tap_row + tap_col
            row_shift = 2 * tap_row - 2
            col_shift = 2 * tap_col - 2
            row_weight = offsets[:, :, 2 * tap_index][:, :, None]
            col_weight = offsets[:, :, 2 * tap_index + 1][:, :, None]
            upper_pair = (1.0 - col_weight) * window(padded, row_shift, col_shift, height, breadth) + col_weight * window(padded, row_shift, col_shift + 1, height, breadth)
            lower_pair = (1.0 - col_weight) * window(padded, row_shift + 1, col_shift, height, breadth) + col_weight * window(padded, row_shift + 1, col_shift + 1, height, breadth)
            pieces.append((1.0 - row_weight) * row_masks[row_shift + 2] * upper_pair + row_weight * row_masks[row_shift + 3] * lower_pair)
    return jnp.concatenate(pieces, axis=-1)

def batch_norm(values, gain_vec, bias_vec, valid_map, pixels):
    average = lax.optimization_barrier(jnp.sum(values * valid_map, axis=(0, 1))) / pixels
    centred = values - average
    spread = lax.optimization_barrier(jnp.sum(centred * centred * valid_map, axis=(0, 1))) / pixels
    return centred * lax.rsqrt(spread + norm_eps) * gain_vec + bias_vec

def product(left_side, right_side):
    return jnp.einsum('hwc,cd->hwd', left_side, right_side, precision=lax.Precision.HIGHEST)

def bottleneck(inputs, in_weight, mid_weight, out_weight, block_gain, block_bias, tail_gain, tail_bias, offset_params, geometry):
    valid_map, row_masks, pixels = geometry
    first_out = low_back(product(inputs, in_weight))
    hidden = low(valid_map * gelu_tanh(batch_norm(first_out, block_gain[0], block_bias[0], valid_map, pixels)))
    ext_float = jnp.pad(hidden, ((halo_rows, halo_rows), (0, 0), (0, 0)))
    columns = jax.checkpoint(tap_columns)(ext_float, row_masks)
    if offset_params is None:
        sampled = columns
    else:
        raw_offset = low_back(product(columns, offset_params[0]) + offset_params[1])
        sampled = low(jax.checkpoint(sample_columns)(ext_float, 0.5 + 0.45 * jnp.tanh(raw_offset), row_masks))
    second_out = low_back(product(sampled, mid_weight))
    hidden_two = low(valid_map * gelu_tanh(batch_norm(second_out, block_gain[1], block_bias[1], valid_map, pixels)))
    third_out = low_back(product(hidden_two, out_weight))
    return low(valid_map * gelu_tanh(inputs + batch_norm(third_out, tail_gain, tail_bias, valid_map, pixels)))

def reference(image_in, cotangent, heights, widths, weight_in_a, weight_offset, bias_offset, weight_mid_a, weight_out_a, weight_in_b, weight_mid_b, weight_out_b, mid_gain, mid_bias, out_gain, out_bias):
    row_index = jnp.arange(-halo_rows, ROWS + halo_rows, dtype=jnp.int32)
    identity, width_row = row_info(row_index, heights, widths, ROWS_GRP, ROWS)
    row_masks = tap_masks(identity, ROWS)
    col_index = jnp.arange(WIDE, dtype=jnp.int32)
    valid_map = (col_index[None, :] < width_row[halo_rows:halo_rows + ROWS, None]).astype(jnp.float32)[:, :, None]
    pixels = jnp.sum(heights * widths).astype(jnp.float32)
    geometry = (valid_map, row_masks, pixels)

    def forward(image, in_first, offset_weight, offset_bias, mid_first, out_first, in_second, mid_second, out_second, gains_mid, biases_mid, gains_out, biases_out):
        middle = bottleneck(image, in_first, mid_first, out_first, gains_mid[0], biases_mid[0], gains_out[0], biases_out[0], (offset_weight, offset_bias), geometry)
        return bottleneck(middle, in_second, mid_second, out_second, gains_mid[1], biases_mid[1], gains_out[1], biases_out[1], None, geometry)
    result, pullback = jax.vjp(forward, image_in.astype(jnp.float32), weight_in_a.astype(jnp.float32), weight_offset.astype(jnp.float32), bias_offset.astype(jnp.float32), weight_mid_a.astype(jnp.float32), weight_out_a.astype(jnp.float32), weight_in_b.astype(jnp.float32), weight_mid_b.astype(jnp.float32), weight_out_b.astype(jnp.float32), mid_gain.astype(jnp.float32), mid_bias.astype(jnp.float32), out_gain.astype(jnp.float32), out_bias.astype(jnp.float32))
    image_grad, grad_in_a, grad_offset, grad_offset_bias, grad_mid_a, grad_out_a, grad_in_b, grad_mid_b, grad_out_b, grad_mid_gain, grad_mid_bias, grad_out_gain, grad_out_bias = pullback(cotangent.astype(jnp.float32))
    return (result.astype(jnp.bfloat16), image_grad, grad_in_a, grad_offset, grad_offset_bias, grad_mid_a, grad_out_a, grad_in_b, grad_mid_b, grad_out_b, grad_mid_gain, grad_mid_bias, grad_out_gain, grad_out_bias)
```

```python
from functools import partial

import jax
import jax.numpy as jnp
from jax import lax
from jax.experimental import pallas as pl
from jax.experimental.pallas import tpu as pltpu
from jax.sharding import PartitionSpec as P

norm_eps = 1e-05
halo_rows = 3
MESH = pl.DeviceIdType.MESH
f32 = jnp.float32
bf16 = jnp.bfloat16


class Place:
    def __init__(self, dp_size, mp_size):
        self.dp_size, self.mp_size = dp_size, mp_size
        self.count = dp_size * mp_size
        self.high = dp_size // 2

    def read(self):
        self.dp = lax.axis_index("dp")
        self.mp = lax.axis_index("mp")
        self.me = self.dp * self.mp_size + self.mp
        self.z = self.dp // 2
        self.y = lax.rem(self.dp, 2)
        self.x = self.mp // 2
        self.core = lax.rem(self.mp, 2)
        return self

    def at(self, linear):
        return (linear // self.mp_size, lax.rem(linear, self.mp_size))

    def core_peer(self):
        return (self.dp, self.mp + 1 - 2 * self.core)

    def x_peer(self):
        return (self.dp, self.mp + 2 - 4 * self.x)

    def y_peer(self):
        return (self.dp + 1 - 2 * self.y, self.mp)

    def z_peer(self, step):
        return (lax.rem(self.z + step, self.high) * 2 + self.y, self.mp)


def greet(peers):
    barrier = pltpu.get_barrier_semaphore()
    for peer in peers:
        pl.semaphore_signal(barrier, inc=1, device_id=peer, device_id_type=MESH)
    pl.semaphore_wait(barrier, len(peers))


def remote(src, dst, send, recv, peer):
    return pltpu.make_async_remote_copy(
        src_ref=src,
        dst_ref=dst,
        send_sem=send,
        recv_sem=recv,
        device_id=peer,
        device_id_type=MESH,
    )


def gather_kernel(sizes, *refs):
    shards, fulls = refs[:6], refs[6:12]
    local_sem, send_sem, recv_sem = refs[12:]
    place = Place(*sizes).read()
    high, z, y, x, core = place.high, place.z, place.y, place.x, place.core
    half = high // 2
    greet(
        [place.z_peer(k) for k in range(1, high)]
        + [place.x_peer(), place.y_peer(), place.core_peer()]
    )

    def cols(array, x_at, core_at):
        width = shards[array].shape[1]
        return pl.ds(pl.multiple_of((2 * x_at + core_at) * width, 128), width)

    def stage_copies(array, stage):
        full = fulls[array]
        mine = cols(array, x, core)
        lower, upper = pl.ds(0, half), pl.ds(half, high - half)
        if stage == 0:
            return [
                remote(
                    shards[array],
                    full.at[z, y, :, mine],
                    send_sem.at[array, k - 1],
                    recv_sem.at[array, k - 1],
                    place.z_peer(k),
                )
                for k in range(1, high)
            ]
        if stage == 1:
            pairs = [
                (full.at[lower, y, :, mine], place.x_peer()),
                (full.at[upper, y, :, mine], place.y_peer()),
            ]
        elif stage == 2:
            pairs = [
                (full.at[lower, y, :, cols(array, 0, core)], place.y_peer()),
                (full.at[lower, y, :, cols(array, 1, core)], place.y_peer()),
                (full.at[upper, :, :, mine], place.x_peer()),
            ]
        else:
            pairs = [
                (full.at[:, :, :, cols(array, 0, core)], place.core_peer()),
                (full.at[:, :, :, cols(array, 1, core)], place.core_peer()),
            ]
        base = high - 1 + [0, 0, 2, 5][stage]
        return [
            remote(ref, ref, send_sem.at[array, base + i], recv_sem.at[array, base + i], peer)
            for i, (ref, peer) in enumerate(pairs)
        ]

    running = {}
    for step in range(6 + 4):
        for array in range(6):
            stage = step - array
            if not 0 <= stage <= 4:
                continue
            if stage == 0:
                own = pltpu.make_async_copy(
                    shards[array], fulls[array].at[z, y, :, cols(array, x, core)], local_sem.at[array]
                )
                own.start()
                running[array] = [own]
            else:
                for copy in running[array]:
                    copy.wait()
                running[array] = []
            if stage < 4:
                copies = stage_copies(array, stage)
                for copy in copies:
                    copy.start()
                running[array] = running[array] + copies


def gather_weights(shards, sizes):
    high = sizes[0] // 2
    full_shapes = [
        jax.ShapeDtypeStruct((high, 2, s.shape[0], s.shape[1] * sizes[1]), s.dtype) for s in shards
    ]
    anywhere = pl.BlockSpec(memory_space=pl.ANY)
    copies = high - 1 + 7
    fulls = pl.pallas_call(
        partial(gather_kernel, sizes),
        out_shape=full_shapes,
        in_specs=[anywhere] * 6,
        out_specs=[anywhere] * 6,
        scratch_shapes=[
            pltpu.SemaphoreType.DMA((6,)),
            pltpu.SemaphoreType.DMA((6, copies)),
            pltpu.SemaphoreType.DMA((6, copies)),
        ],
        compiler_params=pltpu.CompilerParams(collective_id=0, has_side_effects=True),
        name="gather_weights",
    )(*shards)
    return [w.reshape(-1, w.shape[-1]) for w in fulls]


def scatter_kernel(sizes, *refs):
    fulls, outs = refs[:6], refs[6:12]
    keep, from_core, from_one, from_two, from_high = [refs[12 + 6 * i : 18 + 6 * i] for i in range(5)]
    local_sem, send_sem, recv_sem = refs[42:]
    place = Place(*sizes).read()
    high, z, y, x, core = place.high, place.z, place.y, place.x, place.core
    half = high // 2
    greet(
        [place.z_peer(k) for k in range(1, high)]
        + [place.x_peer(), place.y_peer(), place.core_peer()]
    )

    def cols(array, x_at, core_at):
        width = outs[array].shape[1]
        return pl.ds(pl.multiple_of((2 * x_at + core_at) * width, 128), width)

    def copies_of(array, stage):
        send, recv = send_sem.at[array], recv_sem.at[array]
        kept = keep[array]
        if stage == 0:
            items = [
                (fulls[array].at[:, :, :, cols(array, i, 1 - core)], from_core[array].at[i], place.core_peer())
                for i in (0, 1)
            ]
        elif stage == 1:
            first = from_one[array].at[0]
            second = from_one[array].at[1]
            items = []
            for i in (0, 1):
                items.append((kept.at[i, pl.ds(0, half), 1 - y], first.at[i], place.y_peer()))
            for i in (0, 1):
                items.append((kept.at[1 - x, pl.ds(half, half), i], second.at[i], place.x_peer()))
        elif stage == 2:
            items = [
                (kept.at[1 - x, pl.ds(0, half), y], from_two[array].at[0], place.x_peer()),
                (kept.at[x, pl.ds(half, half), 1 - y], from_two[array].at[1], place.y_peer()),
            ]
        else:
            items = [
                (
                    kept.at[x, lax.rem(z + k, high), y],
                    from_high[array].at[k - 1],
                    place.z_peer(k),
                )
                for k in range(1, high)
            ]
        base = [0, 2, 6, 8][stage]
        return [
            remote(src, dst, send.at[base + i], recv.at[base + i], peer)
            for i, (src, dst, peer) in enumerate(items)
        ]

    def add_into(target, extra):
        target[...] = (target[...].astype(f32) + extra[...].astype(f32)).astype(bf16)

    def finish(array, stage):
        kept = keep[array]
        if stage == 0:
            for i in (0, 1):

                def add(b, _, i=i):
                    for c in (0, 1):
                        add_into(kept.at[i, b, c], from_core[array].at[i, b, c])
                    return 0

                lax.fori_loop(0, high, add, 0)
        elif stage == 1:

            def add(b, _):
                for i in (0, 1):
                    add_into(kept.at[i, b, y], from_one[array].at[0, i, b])
                    add_into(kept.at[x, half + b, i], from_one[array].at[1, i, b])
                return 0

            lax.fori_loop(0, half, add, 0)
        elif stage == 2:

            def add(b, _):
                add_into(kept.at[x, b, y], from_two[array].at[0, b])
                add_into(kept.at[x, half + b, y], from_two[array].at[1, b])
                return 0

            lax.fori_loop(0, half, add, 0)
        else:
            total = kept[x, z, y].astype(f32)
            for k in range(1, high):
                total = total + from_high[array][k - 1].astype(f32)
            outs[array][...] = total

    running = {}
    for step in range(6 + 4):
        for array in range(6):
            stage = step - array
            if not 0 <= stage <= 4:
                continue
            if stage == 0:
                running[array] = [
                    pltpu.make_async_copy(
                        fulls[array].at[:, :, :, cols(array, i, core)],
                        keep[array].at[i],
                        local_sem.at[array, i],
                    )
                    for i in (0, 1)
                ]
                for copy in running[array]:
                    copy.start()
            else:
                for copy in running[array]:
                    copy.wait()
                finish(array, stage - 1)
                running[array] = []
            if stage < 4:
                copies = copies_of(array, stage)
                for copy in copies:
                    copy.start()
                running[array] = running[array] + copies


def scatter_grads(grads, sizes):
    high, mp_size = sizes[0] // 2, sizes[1]
    half = high // 2
    blocked, outs = [], []
    scratch = [[] for _ in range(5)]
    for grad in grads:
        rows, width = grad.shape[0] // sizes[0], grad.shape[1] // mp_size
        blocked.append(grad.astype(bf16).reshape(high, 2, rows, grad.shape[1]))
        outs.append(jax.ShapeDtypeStruct((rows, width), f32))
        tile = (rows, width)
        scratch[0].append(pltpu.VMEM((2, high, 2) + tile, bf16))
        scratch[1].append(pltpu.VMEM((2, high, 2) + tile, bf16))
        scratch[2].append(pltpu.VMEM((2, 2, half) + tile, bf16))
        scratch[3].append(pltpu.VMEM((2, half) + tile, bf16))
        scratch[4].append(pltpu.VMEM((high - 1,) + tile, bf16))
    copies = 8 + high - 1
    return pl.pallas_call(
        partial(scatter_kernel, sizes),
        out_shape=outs,
        in_specs=[pl.BlockSpec(memory_space=pl.ANY)] * 6,
        out_specs=[pl.BlockSpec(memory_space=pltpu.VMEM)] * 6,
        scratch_shapes=sum(scratch, [])
        + [
            pltpu.SemaphoreType.DMA((6, 2)),
            pltpu.SemaphoreType.DMA((6, copies)),
            pltpu.SemaphoreType.DMA((6, copies)),
        ],
        compiler_params=pltpu.CompilerParams(
            collective_id=1, has_side_effects=True, vmem_limit_bytes=58 * 1024 * 1024
        ),
        name="scatter_grads",
    )(*blocked)


def merge(parts, moments_mode):
    if not moments_mode:
        return jnp.sum(parts, axis=0)
    pixels, sums, squares = parts[:, 0:1], parts[:, 1:2], parts[:, 2:3]
    all_pixels, all_sums = jnp.sum(pixels, axis=0), jnp.sum(sums, axis=0)
    apart = sums / pixels - (all_sums / all_pixels)[None]
    all_squares = jnp.sum(squares + pixels * apart * apart, axis=0)
    return jnp.concatenate([all_pixels, all_sums, all_squares], axis=0)


def sync_kernel(sizes, groups, moments_mode, x_ref, o_ref, *scratch):
    place = Place(*sizes).read()
    me = place.me
    barrier = pltpu.get_barrier_semaphore()
    links = []
    stride = 1
    for size in groups:
        digit = lax.rem(me // stride, size)
        links.append((stride, size, digit))
        stride = stride * size

    def peer(link, step):
        stride, size, digit = link
        return place.at(me + (lax.rem(digit + step, size) - digit) * stride)

    for link in links:

        def greet_one(k, _, link=link):
            pl.semaphore_signal(barrier, inc=1, device_id=peer(link, k), device_id_type=MESH)
            return 0

        lax.fori_loop(1, link[1], greet_one, 0)
    pl.semaphore_wait(barrier, sum(size - 1 for size in groups))
    value = x_ref[...]
    for i, link in enumerate(links):
        stride, size, digit = link
        src, slots, send, recv = scratch[4 * i : 4 * i + 4]
        src[...] = value

        def push(k, _, link=link, src=src, slots=slots, send=send, recv=recv, digit=digit):
            remote(src, slots.at[digit], send, recv, peer(link, k)).start()
            return 0

        lax.fori_loop(1, size, push, 0)
        pltpu.make_async_copy(src, slots.at[digit], recv).start()
        pltpu.make_async_copy(slots, slots, recv).wait()
        rest = slots.at[pl.ds(0, size - 1)]
        pltpu.make_async_copy(rest, rest, send).wait()
        value = merge(slots[...], moments_mode)
    o_ref[...] = value


def sync(values, sizes, moments_mode=False):
    wide = values.shape[1] > 1024
    groups = (sizes[1], sizes[0]) if wide else (sizes[0] * sizes[1],)
    ids = {(3, 512, True): 2, (3, 2048, True): 3, (2, 512, False): 4, (2, 2048, False): 5}
    scratch = []
    for size in groups:
        scratch += [
            pltpu.VMEM(values.shape, f32),
            pltpu.VMEM((size,) + values.shape, f32),
            pltpu.SemaphoreType.DMA,
            pltpu.SemaphoreType.DMA,
        ]
    return pl.pallas_call(
        partial(sync_kernel, sizes, groups, moments_mode),
        out_shape=jax.ShapeDtypeStruct(values.shape, f32),
        in_specs=[pl.BlockSpec(memory_space=pltpu.VMEM)],
        out_specs=pl.BlockSpec(memory_space=pltpu.VMEM),
        scratch_shapes=scratch,
        compiler_params=pltpu.CompilerParams(
            collective_id=ids[values.shape + (moments_mode,)], has_side_effects=True
        ),
        name="sync",
    )(values)


def spread_kernel(sizes, x_ref, o_ref, got, total, send, recv):
    place = Place(*sizes).read()
    me, count = place.me, place.count
    barrier = pltpu.get_barrier_semaphore()

    def peer(step):
        return lax.rem(me + step, count)

    def greet_one(k, _):
        pl.semaphore_signal(barrier, inc=1, device_id=place.at(peer(k)), device_id_type=MESH)
        return 0

    lax.fori_loop(1, count, greet_one, 0)
    pl.semaphore_wait(barrier, count - 1)

    def push(k, _):
        to = peer(k)
        remote(x_ref.at[to], got.at[me], send.at[0], recv.at[0], place.at(to)).start()
        return 0

    lax.fori_loop(1, count, push, 0)
    pltpu.make_async_copy(x_ref.at[me], got.at[me], recv.at[0]).start()
    pltpu.make_async_copy(got, got, recv.at[0]).wait()
    rest = got.at[pl.ds(0, count - 1)]
    pltpu.make_async_copy(rest, rest, send.at[0]).wait()
    total[...] = jnp.sum(got[...], axis=0)

    def push_total(k, _):
        remote(total, o_ref.at[me], send.at[1], recv.at[1], place.at(peer(k))).start()
        return 0

    lax.fori_loop(1, count, push_total, 0)
    pltpu.make_async_copy(total, o_ref.at[me], recv.at[1]).start()
    pltpu.make_async_copy(o_ref, o_ref, recv.at[1]).wait()
    rest = o_ref.at[pl.ds(0, count - 1)]
    pltpu.make_async_copy(rest, rest, send.at[1]).wait()


def sum_everywhere(table, sizes):
    count = sizes[0] * sizes[1]
    rows, width = table.shape
    each = 8 * (-(-rows // (8 * count)))
    padded = jnp.pad(table, ((0, each * count - rows), (0, 0))).reshape(count, each, width)
    whole = pl.pallas_call(
        partial(spread_kernel, sizes),
        out_shape=jax.ShapeDtypeStruct(padded.shape, f32),
        in_specs=[pl.BlockSpec(memory_space=pltpu.VMEM)],
        out_specs=pl.BlockSpec(memory_space=pltpu.VMEM),
        scratch_shapes=[
            pltpu.VMEM(padded.shape, f32),
            pltpu.VMEM(padded.shape[1:], f32),
            pltpu.SemaphoreType.DMA((2,)),
            pltpu.SemaphoreType.DMA((2,)),
        ],
        compiler_params=pltpu.CompilerParams(collective_id=6, has_side_effects=True),
        name="sum_everywhere",
    )(padded)
    return whole.reshape(count * each, width)[:rows]


def from_behind(value, axis, steps):
    count = lax.axis_size(axis)
    leading, last = (max(0, -steps), min(count, count - steps))
    return lax.ppermute(value, axis, [(source, source + steps) for source in range(leading, last)])


def extended_2(cells, sides, width):
    for axis, dim in sides:
        count = lax.axis_size(axis)
        ends = count - 1
        head = lax.slice_in_dim(cells, 0, width, axis=dim)
        tail = lax.slice_in_dim(cells, cells.shape[dim] - width, cells.shape[dim], axis=dim)
        cells = jnp.concatenate(
            [
                lax.ppermute(tail, axis, [(i, (i + 1) % count) for i in range(ends)]),
                cells,
                lax.ppermute(head, axis, [((i + 1) % count, i) for i in range(ends)]),
            ],
            axis=dim,
        )
    return cells


def gelu_tanh(values):
    return jax.nn.gelu(values, approximate=True)


def row_info(row_index, heights, widths, group_rows, total_rows):
    image_count = heights.shape[1]
    inside = (row_index >= 0) & (row_index < total_rows)
    group_of = jnp.clip(row_index // group_rows, 0, 1)
    local_row = row_index - group_of * group_rows
    image_ends = jnp.cumsum(heights, axis=1)
    is_first = (group_of == 0)[:, None]
    ends_by_row = jnp.where(is_first, image_ends[0][None, :], image_ends[1][None, :])
    image_num = jnp.sum((local_row[:, None] >= ends_by_row).astype(jnp.int32), axis=1)
    identity = jnp.where(inside, group_of * image_count + image_num, -1)
    width_table = jnp.where(is_first, widths[0][None, :], widths[1][None, :])
    picked = jnp.arange(image_count, dtype=jnp.int32)[None, :] == image_num[:, None]
    width_row = jnp.sum(jnp.where(picked, width_table, 0), axis=1)
    return (identity, jnp.where(inside, width_row, 0))


def tap_masks(identity, height):
    centre = identity[halo_rows : halo_rows + height]
    return [
        (identity[halo_rows + row_shift : halo_rows + row_shift + height] == centre).astype(
            jnp.float32
        )[:, None, None]
        for row_shift in range(-2, 4)
    ]


def window(padded, row_shift, col_shift, height, breadth):
    return padded[
        halo_rows + row_shift : halo_rows + row_shift + height,
        halo_rows + col_shift : halo_rows + col_shift + breadth,
    ]


def tap_columns(field_ext, row_masks):
    height = field_ext.shape[0] - 2 * halo_rows
    breadth = field_ext.shape[1]
    padded = jnp.pad(field_ext, ((0, 0), (halo_rows, halo_rows), (0, 0)))
    pieces = []
    for tap_row in range(3):
        for tap_col in range(3):
            row_shift = 2 * tap_row - 2
            col_shift = 2 * tap_col - 2
            pieces.append(
                row_masks[row_shift + 2] * window(padded, row_shift, col_shift, height, breadth)
            )
    return jnp.concatenate(pieces, axis=-1)


def sample_columns(field_ext, offsets, row_masks):
    height = field_ext.shape[0] - 2 * halo_rows
    breadth = field_ext.shape[1]
    padded = jnp.pad(field_ext, ((0, 0), (halo_rows, halo_rows), (0, 0)))
    pieces = []
    for tap_row in range(3):
        for tap_col in range(3):
            tap_index = 3 * tap_row + tap_col
            row_shift = 2 * tap_row - 2
            col_shift = 2 * tap_col - 2
            row_weight = offsets[:, :, 2 * tap_index][:, :, None]
            col_weight = offsets[:, :, 2 * tap_index + 1][:, :, None]
            upper_pair = (1.0 - col_weight) * window(
                padded, row_shift, col_shift, height, breadth
            ) + col_weight * window(padded, row_shift, col_shift + 1, height, breadth)
            lower_pair = (1.0 - col_weight) * window(
                padded, row_shift + 1, col_shift, height, breadth
            ) + col_weight * window(padded, row_shift + 1, col_shift + 1, height, breadth)
            pieces.append(
                (1.0 - row_weight) * row_masks[row_shift + 2] * upper_pair
                + row_weight * row_masks[row_shift + 3] * lower_pair
            )
    return jnp.concatenate(pieces, axis=-1)


def inner_rows(left_side, right_side):
    return lax.dot_general(
        left_side, right_side, (((0,), (0,)), ((), ())), preferred_element_type=jnp.float32
    )


def times_transposed(left_side, right_side):
    return lax.dot_general(
        left_side, right_side, (((1,), (1,)), ((), ())), preferred_element_type=jnp.float32
    )


def flat_dot(values, matrix):
    height, breadth = (values.shape[0], values.shape[1])
    return jnp.dot(
        values.reshape(height * breadth, -1), matrix, preferred_element_type=jnp.float32
    ).reshape(height, breadth, -1)


def gelu_back(values, valid_map, upstream):

    def gated(inner_values):
        return valid_map * gelu_tanh(inner_values)

    ignored, pullback = jax.vjp(gated, values)
    return pullback(upstream)[0]


def moments(values, valid_map, local_pixels, sizes):
    count = jnp.full((values.shape[-1],), local_pixels)
    total = jnp.sum(values * valid_map, axis=(0, 1))
    centred = values - total / local_pixels
    squares = jnp.sum(centred * centred * valid_map, axis=(0, 1))
    merged = sync(jnp.stack([count, total, squares]), sizes, True)
    pixels = merged[0]
    return (merged[1] / pixels, lax.rsqrt(merged[2] / pixels + norm_eps))


def norm_back(grad_act, normed, inverse, gain_vec, valid_map, pixels, sizes):
    weighted = grad_act * valid_map
    bias_part = jnp.sum(weighted, axis=(0, 1))
    gain_part = jnp.sum(weighted * normed, axis=(0, 1))
    bias_grad, gain_grad = sync(jnp.stack([bias_part, gain_part]), sizes)
    grad_in = (
        valid_map
        * (gain_vec * inverse)
        * (grad_act - bias_grad / pixels - normed * gain_grad / pixels)
    )
    return (grad_in.astype(jnp.bfloat16), gain_grad, bias_grad)


def fold_rims(grad_ext, height):
    middle = grad_ext[halo_rows : halo_rows + height]
    for direction in (1, -1):
        if direction == 1:
            rim_piece = grad_ext[halo_rows + height :]
        else:
            rim_piece = grad_ext[:halo_rows]
        arrived = from_behind(rim_piece.astype(jnp.bfloat16), ("dp", "mp"), direction).astype(
            rim_piece.dtype
        )
        if direction == 1:
            middle = middle + jnp.pad(arrived, ((0, height - halo_rows), (0, 0), (0, 0)))
        else:
            middle = middle + jnp.pad(arrived, ((height - halo_rows, 0), (0, 0), (0, 0)))
    return middle


def block_forward(
    inputs, weights, block_gain, block_bias, tail_gain, tail_bias, offset_params, geometry
):
    in_weight, mid_weight, out_weight = weights
    valid_map, row_masks, pixels, local_pixels, sizes = geometry
    first_out = flat_dot(inputs, in_weight)
    first_avg, first_inv = moments(first_out, valid_map, local_pixels, sizes)
    first_hat = (first_out - first_avg) * first_inv
    first_act = first_hat * block_gain[0] + block_bias[0]
    hidden = (valid_map * gelu_tanh(first_act)).astype(jnp.bfloat16)
    extended = extended_2(hidden, ((("dp", "mp"), 0),), halo_rows)
    ext_float = extended.astype(jnp.float32)
    columns = tap_columns(ext_float, row_masks).astype(jnp.bfloat16)
    if offset_params is None:
        raw_offset = None
        sampled = columns
    else:
        raw_offset = flat_dot(columns, offset_params[0]) + offset_params[1]
        offsets = 0.5 + 0.45 * jnp.tanh(raw_offset)
        sampled = sample_columns(ext_float, offsets, row_masks).astype(jnp.bfloat16)
    second_out = flat_dot(sampled, mid_weight)
    second_avg, second_inv = moments(second_out, valid_map, local_pixels, sizes)
    second_hat = (second_out - second_avg) * second_inv
    second_act = second_hat * block_gain[1] + block_bias[1]
    hidden_two = (valid_map * gelu_tanh(second_act)).astype(jnp.bfloat16)
    third_out = flat_dot(hidden_two, out_weight)
    third_avg, third_inv = moments(third_out, valid_map, local_pixels, sizes)
    third_hat = (third_out - third_avg) * third_inv
    total_pre = inputs.astype(jnp.float32) + (third_hat * tail_gain + tail_bias)
    result = (valid_map * gelu_tanh(total_pre)).astype(jnp.bfloat16)
    kept_state = (
        first_hat,
        first_inv,
        first_act,
        ext_float,
        columns,
        raw_offset,
        second_hat,
        second_inv,
        second_act,
        hidden_two,
        third_hat,
        third_inv,
        total_pre,
    )
    return (result, kept_state)


def block_backward(
    grad_out, inputs, weights, block_gain, tail_gain, offset_params, geometry, kept_state
):
    in_weight, mid_weight, out_weight = weights
    valid_map, row_masks, pixels, local_pixels, sizes = geometry
    (
        first_hat,
        first_inv,
        first_act,
        ext_float,
        columns,
        raw_offset,
        second_hat,
        second_inv,
        second_act,
        hidden_two,
        third_hat,
        third_inv,
        total_pre,
    ) = kept_state
    height, breadth = (inputs.shape[0], inputs.shape[1])
    pixel_rows = height * breadth
    grad_pre = gelu_back(total_pre, valid_map, grad_out)
    grad_third, tail_gain_grad, tail_bias_grad = norm_back(
        grad_pre, third_hat, third_inv, tail_gain, valid_map, pixels, sizes
    )
    flat_third = grad_third.reshape(pixel_rows, -1)
    grad_out_weight = inner_rows(hidden_two.reshape(pixel_rows, -1), flat_third)
    grad_hidden_two = times_transposed(flat_third, out_weight).reshape(height, breadth, -1)
    grad_second_act = gelu_back(second_act, valid_map, grad_hidden_two)
    grad_second, mid_gain_grad, mid_bias_grad = norm_back(
        grad_second_act, second_hat, second_inv, block_gain[1], valid_map, pixels, sizes
    )
    flat_second = grad_second.reshape(pixel_rows, -1)
    column_pull = jax.vjp(partial(tap_columns, row_masks=row_masks), ext_float)[1]
    if offset_params is None:
        grad_mid_weight = inner_rows(columns.reshape(pixel_rows, -1), flat_second)
        grad_columns = times_transposed(flat_second, mid_weight).reshape(height, breadth, -1)
        grad_ext = column_pull(grad_columns)[0]
        offset_terms = None
    else:
        tanh_raw = jnp.tanh(raw_offset)

        def sampler(field_ext, offsets):
            return sample_columns(field_ext, offsets, row_masks)

        sampled, sample_pull = jax.vjp(sampler, ext_float, 0.5 + 0.45 * tanh_raw)
        flat_sampled = sampled.astype(jnp.bfloat16).reshape(pixel_rows, -1)
        grad_mid_weight = inner_rows(flat_sampled, flat_second)
        grad_sampled = times_transposed(flat_second, mid_weight).reshape(height, breadth, -1)
        grad_ext, grad_offsets = sample_pull(grad_sampled)
        grad_raw = (grad_offsets * (0.45 * (1.0 - tanh_raw * tanh_raw))).astype(jnp.bfloat16)
        flat_raw = grad_raw.reshape(pixel_rows, -1)
        offset_terms = (
            inner_rows(flat_raw, columns.reshape(pixel_rows, -1)),
            jnp.sum(flat_raw.astype(jnp.float32), axis=0),
        )
        grad_columns = times_transposed(flat_raw, offset_params[0]).reshape(height, breadth, -1)
        grad_ext = grad_ext + column_pull(grad_columns)[0]
    grad_hidden = fold_rims(grad_ext, height)
    grad_first_act = gelu_back(first_act, valid_map, grad_hidden)
    grad_first, first_gain_grad, first_bias_grad = norm_back(
        grad_first_act, first_hat, first_inv, block_gain[0], valid_map, pixels, sizes
    )
    offset_sums = offset_terms
    flat_first = grad_first.reshape(pixel_rows, -1)
    grad_in_weight = inner_rows(inputs.reshape(pixel_rows, -1), flat_first)
    grad_inputs = grad_pre + times_transposed(flat_first, in_weight).reshape(height, breadth, -1)
    gain_grads = jnp.stack([first_gain_grad, mid_gain_grad])
    bias_grads = jnp.stack([first_bias_grad, mid_bias_grad])
    return (
        grad_inputs,
        (grad_in_weight, grad_mid_weight, grad_out_weight),
        gain_grads,
        bias_grads,
        tail_gain_grad,
        tail_bias_grad,
        offset_sums,
    )


def per_device(
    image_in,
    cotangent,
    heights,
    widths,
    weight_in_a,
    weight_offset,
    bias_offset,
    weight_mid_a,
    weight_out_a,
    weight_in_b,
    weight_mid_b,
    weight_out_b,
    mid_gain,
    mid_bias,
    out_gain,
    out_bias,
):
    height, breadth = (image_in.shape[0], image_in.shape[1])
    total_rows = height * lax.axis_size(("dp", "mp"))
    first_row = lax.axis_index(("dp", "mp")) * height
    row_index = first_row - halo_rows + jnp.arange(height + 2 * halo_rows, dtype=jnp.int32)
    identity, width_row = row_info(
        row_index, heights, widths, total_rows // 2 + height // 2, total_rows
    )
    row_masks = tap_masks(identity, height)
    col_index = jnp.arange(breadth, dtype=jnp.int32)
    valid_map = (col_index[None, :] < width_row[halo_rows : halo_rows + height, None]).astype(
        jnp.float32
    )[:, :, None]
    pixels = jnp.sum(heights * widths).astype(jnp.float32)
    sizes = (lax.axis_size("dp"), lax.axis_size("mp"))
    geometry = (valid_map, row_masks, pixels, jnp.sum(valid_map), sizes)
    gathered = gather_weights(
        (weight_in_a, weight_mid_a, weight_out_a, weight_in_b, weight_mid_b, weight_out_b), sizes
    )
    offset_params = (weight_offset, bias_offset)
    middle_out, state_one = block_forward(
        image_in,
        gathered[0:3],
        mid_gain[0],
        mid_bias[0],
        out_gain[0],
        out_bias[0],
        offset_params,
        geometry,
    )
    image_out, state_two = block_forward(
        middle_out,
        gathered[3:6],
        mid_gain[1],
        mid_bias[1],
        out_gain[1],
        out_bias[1],
        None,
        geometry,
    )
    grad_middle, grads_two, gains_two, biases_two, tail_gain_two, tail_bias_two, unused = (
        block_backward(
            cotangent.astype(jnp.float32),
            middle_out,
            gathered[3:6],
            mid_gain[1],
            out_gain[1],
            None,
            geometry,
            state_two,
        )
    )
    image_grad, grads_one, gains_one, biases_one, tail_gain_one, tail_bias_one, offset_sums = (
        block_backward(
            grad_middle,
            image_in,
            gathered[0:3],
            mid_gain[0],
            out_gain[0],
            offset_params,
            geometry,
            state_one,
        )
    )
    shards = scatter_grads(grads_one + grads_two, sizes)
    offset_table = jnp.concatenate(
        [offset_sums[0].reshape(-1, 512), jnp.pad(offset_sums[1], (0, 512 - 18))[None]]
    )
    offset_table = sum_everywhere(offset_table, sizes)
    offset_weight_grad = offset_table[:-1].reshape(18, -1).T
    offset_bias_grad = offset_table[-1, :18]
    return (
        image_out,
        image_grad,
        shards[0],
        offset_weight_grad,
        offset_bias_grad,
        shards[1],
        shards[2],
        shards[3],
        shards[4],
        shards[5],
        jnp.stack([gains_one, gains_two]),
        jnp.stack([biases_one, biases_two]),
        jnp.stack([tail_gain_one, tail_gain_two]),
        jnp.stack([tail_bias_one, tail_bias_two]),
    )


def solution(mesh):
    in_specs = (
        P(("dp", "mp"), None, None),
        P(("dp", "mp"), None, None),
        P(),
        P(),
        P("dp", "mp"),
        P(),
        P(),
        P("dp", "mp"),
        P("dp", "mp"),
        P("dp", "mp"),
        P("dp", "mp"),
        P("dp", "mp"),
        P(),
        P(),
        P(),
        P(),
    )
    out_specs = (
        P(("dp", "mp"), None, None),
        P(("dp", "mp"), None, None),
        P("dp", "mp"),
        P(),
        P(),
        P("dp", "mp"),
        P("dp", "mp"),
        P("dp", "mp"),
        P("dp", "mp"),
        P("dp", "mp"),
        P(),
        P(),
        P(),
        P(),
    )
    return jax.shard_map(
        per_device, mesh=mesh, in_specs=in_specs, out_specs=out_specs, check_vma=False
    )
```

```python
from functools import partial
from types import SimpleNamespace

import jax
import jax.numpy as jnp
from jax import lax
from jax.experimental import pallas as pl
from jax.experimental.pallas import tpu as pltpu
from jax.sharding import PartitionSpec as P

norm_eps = 1e-05
halo_rows = 3
breadth = 64
chunk = 256
strip = 16
lane_block = 512
offsets_count = 18
gelu_a = 0.7978845608028654
gelu_b = gelu_a * 0.044715
MESH = pl.DeviceIdType.MESH
f32 = jnp.float32
bf16 = jnp.bfloat16
shape = jax.ShapeDtypeStruct
dma = pltpu.SemaphoreType.DMA
vmem = pl.BlockSpec(memory_space=pltpu.VMEM)
smem = pl.BlockSpec(memory_space=pltpu.SMEM)
anywhere = pl.BlockSpec(memory_space=pl.ANY)


class Place:
    def __init__(self, dp_size, mp_size):
        self.dp_size, self.mp_size = dp_size, mp_size
        self.count = dp_size * mp_size
        self.high = dp_size // 2
        self.dp = lax.axis_index("dp")
        self.mp = lax.axis_index("mp")
        self.me = self.dp * mp_size + self.mp
        self.z = self.dp // 2
        self.y = lax.rem(self.dp, 2)
        self.x = self.mp // 2
        self.core = lax.rem(self.mp, 2)

    def at(self, linear):
        return (linear // self.mp_size, lax.rem(linear, self.mp_size))

    def next(self, step):
        return self.at(lax.rem(self.me + self.count + step, self.count))

    def core_peer(self):
        return (self.dp, self.mp + 1 - 2 * self.core)

    def x_peer(self):
        return (self.dp, self.mp + 2 - 4 * self.x)

    def y_peer(self):
        return (self.dp + 1 - 2 * self.y, self.mp)

    def z_peer(self, step):
        return (lax.rem(self.z + step, self.high) * 2 + self.y, self.mp)

    def greet_all(self):
        barrier = pltpu.get_barrier_semaphore()

        def greet_one(k):
            pl.semaphore_signal(barrier, inc=1, device_id=self.next(k + 1), device_id_type=MESH)

        loop(self.count - 1, greet_one)
        pl.semaphore_wait(barrier, self.count - 1)


def remote(src, dst, send, recv, peer):
    return pltpu.make_async_remote_copy(
        src_ref=src,
        dst_ref=dst,
        send_sem=send,
        recv_sem=recv,
        device_id=peer,
        device_id_type=MESH,
    )


def slab(index, size):
    return pl.ds(pl.multiple_of(index * size, size), size)


def loop(count, body):
    def step(i, carry):
        body(i)
        return carry

    lax.fori_loop(0, count, step, 0)


def launch(kernel, ins, specs, outs, out_specs, scratch, collective_id, vmem_mib):
    flat_in, tree_in = jax.tree.flatten(ins)
    flat_out, tree_out = jax.tree.flatten(outs)
    is_leaf = lambda s: not isinstance(s, (dict, list))
    flat_scratch, tree_scratch = jax.tree.flatten(scratch, is_leaf=is_leaf)
    spec_in = [s for n in sorted(ins) for s in [specs.get(n, vmem)] * len(jax.tree.leaves(ins[n]))]
    spec_out = [
        s for n in sorted(outs) for s in [out_specs.get(n, anywhere)] * len(jax.tree.leaves(outs[n]))
    ]

    def body(*refs):
        a, b = len(flat_in), len(flat_in) + len(flat_out)
        everything = dict(jax.tree.unflatten(tree_in, refs[:a]))
        everything.update(jax.tree.unflatten(tree_out, refs[a:b]))
        everything.update(jax.tree.unflatten(tree_scratch, refs[b:]))
        kernel(SimpleNamespace(**everything))

    results = pl.pallas_call(
        body,
        out_shape=flat_out,
        in_specs=spec_in,
        out_specs=spec_out,
        scratch_shapes=flat_scratch,
        compiler_params=pltpu.CompilerParams(
            collective_id=collective_id,
            has_side_effects=True,
            vmem_limit_bytes=vmem_mib * 1024 * 1024,
        ),
        name=kernel.func.__name__,
    )(*flat_in)
    return SimpleNamespace(**jax.tree.unflatten(tree_out, results))


def gelu_of(v):
    return 0.5 * v * (1.0 + jnp.tanh(v * (gelu_a + gelu_b * v * v)))


def gelu_slope(v):
    square = v * v
    t = jnp.tanh(v * (gelu_a + gelu_b * square))
    return 0.5 * (1.0 + t) + 0.5 * v * (1.0 - t * t) * (gelu_a + 3.0 * gelu_b * square)


def wide_valid(valid, rows, width):
    mask = valid[rows, :]
    return jnp.concatenate([mask] * (width // 128), axis=1)


def fold8(x):
    return jnp.sum(x.reshape(x.shape[0] // 8, 8, x.shape[1]), axis=0)


def strip_sums(pixel_count, width, terms, out, row_at):
    for block in range(width // lane_block):
        lanes = pl.ds(block * lane_block, lane_block)

        def step(i, carry, lanes=lanes):
            parts = terms(slab(i, strip), lanes)
            return tuple(c + fold8(p) for c, p in zip(carry, parts))

        zeros = tuple(jnp.zeros((8, lane_block), f32) for _ in row_at)
        sums = lax.fori_loop(0, pixel_count // strip, step, zeros)
        for row, total in zip(row_at, sums):
            out[row : row + 1, lanes] = jnp.sum(total, axis=0, keepdims=True)


def merge(parts, moments_mode):
    if not moments_mode:
        return jnp.sum(parts, axis=0)
    pixels, sums, squares = parts[:, 0:1], parts[:, 1:2], parts[:, 2:3]
    all_pixels, all_sums = jnp.sum(pixels, axis=0), jnp.sum(sums, axis=0)
    apart = sums / pixels - (all_sums / all_pixels)[None]
    all_squares = jnp.sum(squares + pixels * apart * apart, axis=0)
    return jnp.concatenate([all_pixels, all_sums, all_squares], axis=0)


def sync_groups(width, sizes):
    count = sizes[0] * sizes[1]
    if count > 64:
        return (16, count // 16)
    return sizes[::-1] if width > 1024 else (count,)


def sync_scratch(plan, sizes):
    out = []
    for rows, width in plan:
        for size in sync_groups(width, sizes):
            out += [pltpu.VMEM((rows, width), f32), pltpu.VMEM((size, rows, width), f32), dma, dma]
    return out


class Syncs:
    def __init__(self, place, buffers):
        self.place, self.buffers = place, buffers
        self.at = 0

    def take(self, width):
        stages = []
        stride = 1
        for size in sync_groups(width, (self.place.dp_size, self.place.mp_size)):
            digit = lax.rem(self.place.me // stride, size)
            stages.append((stride, size, digit, self.buffers[self.at : self.at + 4]))
            self.at += 4
            stride *= size
        return stages

    def start(self, stage, value=None):
        stride, size, digit, (src, slots, send, recv) = stage
        me = self.place.me
        if value is not None:
            src[...] = value

        def push(k):
            peer = me + (lax.rem(digit + k + 1, size) - digit) * stride
            remote(src, slots.at[digit], send, recv, self.place.at(peer)).start()

        loop(size - 1, push)
        pltpu.make_async_copy(src, slots.at[digit], recv).start()

    def finish(self, stage, moments_mode):
        stride, size, digit, (src, slots, send, recv) = stage
        pltpu.make_async_copy(slots, slots, recv).wait()
        rest = slots.at[pl.ds(0, size - 1)]
        pltpu.make_async_copy(rest, rest, send).wait()
        return merge(slots[...], moments_mode)

    def rest(self, stages, moments_mode):
        value = self.finish(stages[0], moments_mode)
        for stage in stages[1:]:
            self.start(stage, value)
            value = self.finish(stage, moments_mode)
        return value


def shifted(x, shift):
    if shift == 0:
        return x
    pixels = x.shape[0]
    column = lax.broadcasted_iota(jnp.int32, x.shape, 0) % breadth + shift
    inside = (column >= 0) & (column < breadth)
    return jnp.where(inside, pltpu.roll(x, (-shift) % pixels, 0), 0.0)


def row_scales(masks, first_row, which, width):
    row_of = lax.broadcasted_iota(jnp.int32, (chunk, width), 0) // breadth
    scale = jnp.zeros((chunk, width), f32)
    for k in range(chunk // breadth):
        scale = jnp.where(row_of == k, masks[first_row + k, which], scale)
    return scale


def masked_rows(part, masks, first_row, which):
    scaled = []
    for k in range(part.shape[0] // breadth):
        piece = part[breadth * k : breadth * (k + 1)].astype(f32)
        scaled.append((piece * masks[first_row + k, which]).astype(bf16))
    return jnp.concatenate(scaled, axis=0)


def tap_terms(off, masks, row, tap_row, tap_col):
    lane = lax.broadcasted_iota(jnp.int32, (breadth, 2 * breadth), 1)
    sub = lax.broadcasted_iota(jnp.int32, (breadth, 2 * breadth), 0)
    upper = lane >= breadth
    apart = jnp.where(upper, lane - breadth, lane) - sub
    tap, shift = 3 * tap_row + tap_col, 2 * tap_col - 2
    oy, ox = off[:, 2 * tap : 2 * tap + 1], off[:, 2 * tap + 1 : 2 * tap + 2]
    low, high = masks[row, 2 * tap_row], masks[row, 2 * tap_row + 1]
    down = jnp.where(upper, oy * high, (1.0 - oy) * low)
    across = jnp.where(apart == shift, 1.0 - ox, jnp.where(apart == shift + 1, ox, 0.0))
    down_slope = jnp.where(upper, high, -low)
    across_slope = jnp.where(apart == shift, -1.0, jnp.where(apart == shift + 1, 1.0, 0.0))
    return down, across, down_slope, across_slope


def nt_dot(a, b):
    return lax.dot_general(a, b, (((1,), (1,)), ((), ())), preferred_element_type=f32)


def tn_dot(a, b):
    return lax.dot_general(a, b, (((0,), (0,)), ((), ())), preferred_element_type=f32)


def nn_dot(a, b):
    return jnp.dot(a, b, preferred_element_type=f32)


class Outbox:
    def __init__(self, sems):
        self.sems, self.running = sems, {}

    def put(self, at, src, dst):
        copy = pltpu.make_async_copy(src, dst, self.sems.at[at])
        copy.start()
        self.running[at] = copy

    def settle(self, *which):
        for at in which or list(self.running):
            self.running.pop(at).wait()


def load_weight(full, dst, sem):
    if len(full.shape) == 2:
        copy = pltpu.make_async_copy(full, dst, sem)
        copy.start()
        return copy
    block = full.shape[2]
    for z in range(full.shape[0]):
        for y in range(2):
            rows = pl.ds((2 * z + y) * block, block)
            pltpu.make_async_copy(full.at[z, y], dst.at[rows], sem).start()
    return pltpu.make_async_copy(dst, dst, sem)


class Gather:
    def __init__(self, place, r):
        self.place, self.fulls, self.sems = place, r.fulls, (r.gather_local, r.gather_send, r.gather_recv)
        self.shards = r.shards
        self.stage = [0] * 6
        self.running = [[] for _ in range(6)]

    def cols(self, array, x_at, core_at):
        width = self.shards[array].shape[1]
        return pl.ds(pl.multiple_of((2 * x_at + core_at) * width, 128), width)

    def copies(self, array, stage):
        place, full = self.place, self.fulls[array]
        high, z, y, x, core = place.high, place.z, place.y, place.x, place.core
        half = high // 2
        mine = self.cols(array, x, core)
        lower, upper = pl.ds(0, half), pl.ds(half, high - half)
        local, send, recv = self.sems
        if stage == 0:
            target = full.at[z, y, :, mine]
            own = pltpu.make_async_copy(self.shards[array], target, local.at[array])
            return [own] + [
                remote(
                    self.shards[array],
                    target,
                    send.at[array, k - 1],
                    recv.at[array, k - 1],
                    place.z_peer(k),
                )
                for k in range(1, high)
            ]
        if stage == 1:
            pairs = [
                (full.at[lower, y, :, mine], place.x_peer()),
                (full.at[upper, y, :, mine], place.y_peer()),
            ]
        elif stage == 2:
            pairs = [
                (full.at[lower, y, :, self.cols(array, 0, core)], place.y_peer()),
                (full.at[lower, y, :, self.cols(array, 1, core)], place.y_peer()),
                (full.at[upper, :, :, mine], place.x_peer()),
            ]
        else:
            pairs = [
                (full.at[:, :, :, self.cols(array, 0, core)], place.core_peer()),
                (full.at[:, :, :, self.cols(array, 1, core)], place.core_peer()),
            ]
        base = high - 1 + [0, 0, 2, 5][stage]
        return [
            remote(ref, ref, send.at[array, base + i], recv.at[array, base + i], peer)
            for i, (ref, peer) in enumerate(pairs)
        ]

    def advance(self, *arrays):
        for array in arrays if self.shards else ():
            for copy in self.running[array]:
                copy.wait()
            self.running[array] = []
            if self.stage[array] < 4:
                self.running[array] = self.copies(array, self.stage[array])
                for copy in self.running[array]:
                    copy.start()
            self.stage[array] += 1


def forward_pass(sizes, r):
    place = Place(*sizes)
    syncs = Syncs(place, r.syncs)
    gather = Gather(place, r)
    out = Outbox(r.out_sem)
    valid, masks, counts = r.valid, r.masks, r.counts
    first, third, ext, hidden = r.first, r.third, r.ext, r.hidden
    pixels, width, wide = first.shape[0], first.shape[1], third.shape[1]
    halo = halo_rows * breadth
    chunks = pixels // chunk

    def load(array, dst, sem):
        return load_weight(r.fulls[array], dst, r.load_sem.at[sem])

    def moments(ref, rstd, mean, during=()):
        block_width = ref.shape[1]
        stages = syncs.take(block_width)
        src = stages[0][3][0]

        def sums(at, lanes):
            return (ref[at, lanes] * wide_valid(valid, at, lane_block),)

        strip_sums(pixels, block_width, sums, src, [1])
        src[0:1, :] = jnp.full((1, block_width), counts[0], f32)

        def squares(at, lanes):
            centred = ref[at, lanes] - src[1:2, lanes] * counts[1]
            return (centred * centred * wide_valid(valid, at, lane_block),)

        strip_sums(pixels, block_width, squares, src, [2])
        syncs.start(stages[0])
        for call in during:
            call()
        merged = syncs.rest(stages, True)
        mean[...] = merged[1:2] / merged[0:1]
        rstd[...] = lax.rsqrt(merged[2:3] / merged[0:1] + norm_eps)

    def activate(norm, hat, target, target_row):
        mean, rstd = r.mean_narrow, r.rstd_narrow.at[norm : norm + 1, :]
        gain, bias = r.mid_gain.at[norm : norm + 1, :], r.mid_bias.at[norm : norm + 1, :]

        def body(i):
            at = slab(i, strip)
            normed = (first[at, :] - mean[...]) * rstd[...]
            hat[at, :] = normed.astype(bf16)
            act = gelu_of(normed * gain[...] + bias[...]) * wide_valid(valid, at, width)
            rows = pl.ds(pl.multiple_of(target_row + i * strip, strip), strip)
            target[rows, :] = act.astype(bf16)

        loop(pixels // strip, body)

    def narrow_moments(norm, during=()):
        moments(first, r.rstd_narrow.at[norm : norm + 1, :], r.mean_narrow, during)

    def project(lhs, weight, target):
        def body(i):
            at = slab(i, chunk)
            target[at, :] = nn_dot(lhs[at, :], weight[...])

        loop(chunks, body)

    def halo_copies(block):
        field = ext.at[block]
        send, recv = r.halo_send.at[block], r.halo_recv.at[block]
        return [
            remote(
                field.at[pl.ds(pixels, halo)],
                field.at[pl.ds(0, halo)],
                send.at[0],
                recv.at[0],
                place.next(1),
            ),
            remote(
                field.at[pl.ds(halo, halo)],
                field.at[pl.ds(pixels + halo, halo)],
                send.at[1],
                recv.at[1],
                place.next(-1),
            ),
        ]

    def mid_deformable(i, slot):
        field = ext.at[0]
        base = halo + i * chunk
        first_row = i * (chunk // breadth)
        total = jnp.zeros((chunk, 128), f32)
        for tap_row in range(3):
            start = pl.multiple_of(base + (2 * tap_row - 2) * breadth, breadth)
            part = nn_dot(field[pl.ds(start, chunk), :], r.offset_weight[tap_row])
            total = total + part * row_scales(masks, first_row, 2 * tap_row, 128)
        left = shifted(total, -2)
        middle = pltpu.roll(total, 128 - 32, 1)
        right = pltpu.roll(shifted(total, 2), 128 - 64, 1)
        lane = lax.broadcasted_iota(jnp.int32, total.shape, 1)
        raw = jnp.where(lane < 32, left + middle + right, 0.0) + r.offset_bias[...]
        tanh_raw = jnp.tanh(raw)
        r.tanh_raw[slab(i, chunk), :] = tanh_raw
        r.off[...] = 0.5 + 0.45 * tanh_raw

        def one_row(k):
            off = r.off[slab(k, breadth), :]
            for tap_row in range(3):
                weights = []
                for tap_col in range(3):
                    down, across, _, _ = tap_terms(off, masks, first_row + k, tap_row, tap_col)
                    weights.append((down * across).astype(bf16))
                start = pl.multiple_of(base + (k + 2 * tap_row - 2) * breadth, breadth)
                got = nn_dot(jnp.concatenate(weights, axis=0), field[pl.ds(start, 2 * breadth), :])
                for tap_col in range(3):
                    lanes = pl.ds((3 * tap_row + tap_col) * width, width)
                    piece = got[breadth * tap_col : breadth * (tap_col + 1)]
                    r.samp[slot, slab(k, breadth), lanes] = piece.astype(bf16)

        loop(chunk // breadth, one_row)
        first[slab(i, chunk), :] = nn_dot(r.samp[slot], r.w_mid[...])

    def mid_plain(i):
        field = ext.at[1]
        lhs = []
        for tap_row in range(3):
            start = pl.multiple_of(halo + i * chunk + (2 * tap_row - 2) * breadth, breadth)
            part = field[pl.ds(start, chunk), :]
            if tap_row != 1:
                part = masked_rows(part, masks, i * (chunk // breadth), 2 * tap_row)
            lhs.append(part)
        total = None
        for tap_col in range(3):
            partial_sum = None
            for tap_row in range(3):
                weight = r.w_mid[pl.ds((3 * tap_row + tap_col) * width, width), :]
                part = nn_dot(lhs[tap_row], weight)
                partial_sum = part if partial_sum is None else partial_sum + part
            partial_sum = shifted(partial_sum, 2 * tap_col - 2)
            total = partial_sum if total is None else total + partial_sum
        first[slab(i, chunk), :] = total

    def finish_block(block, inputs, result):
        gain, bias = r.out_gain.at[block : block + 1, :], r.out_bias.at[block : block + 1, :]
        mean, rstd = r.mean_wide, r.rstd_wide.at[block : block + 1, :]

        def body(i):
            at = slab(i, strip)
            mask = wide_valid(valid, at, lane_block)
            for j in range(wide // lane_block):
                lanes = pl.ds(j * lane_block, lane_block)
                normed = (third[at, lanes] - mean[:, lanes]) * rstd[:, lanes]
                r.hat3[at, lanes] = normed.astype(bf16)
                pre = inputs[at, lanes].astype(f32) + (normed * gain[:, lanes] + bias[:, lanes])
                result[at, lanes] = (mask * gelu_of(pre)).astype(bf16)

        loop(pixels // strip, body)

    def wide_moments(block, during=()):
        moments(third, r.rstd_wide.at[block : block + 1, :], r.mean_wide, during)

    def samp_copy(i):
        slot = i % 2
        return pltpu.make_async_copy(
            r.samp.at[slot], r.samp_out.at[slab(i, chunk)], r.samp_sem.at[slot]
        )

    place.greet_all()
    gather.advance(0)
    gather.advance(0, 1)
    gather.advance(0)
    gather.advance(0, 1, 2)
    gather.advance(0)
    load(0, r.w_in, 0).wait()
    project(r.image, r.w_in, first)
    gather.advance(1)
    narrow_moments(0, [lambda: gather.advance(2)])
    gather.advance(3)
    activate(0, r.hat_a, ext.at[0], halo)
    out.put(0, r.hat_a, r.hat1_out[0])
    edges = halo_copies(0)
    for copy in edges:
        copy.start()
    gather.advance(1, 2, 3)
    for copy in edges:
        copy.wait()
    out.put(1, ext.at[0], r.field_out[0])
    gather.advance(1)
    gather.advance(4)
    load(1, r.w_mid, 1).wait()
    for i in range(chunks):
        if i >= 2:
            samp_copy(i - 2).wait()
        mid_deformable(i, i % 2)
        samp_copy(i).start()
        gather.advance(*{0: (2, 3), 1: (2, 3), 2: (3, 4, 5)}.get(i, ()))
    loaded = load(2, r.w_out, 2)
    loaded_in = load(3, r.w_in, 0)
    narrow_moments(1, [lambda: gather.advance(4, 5)])
    activate(1, r.hat_b, hidden, 0)
    out.put(2, r.hat_b, r.hat2_out[0])
    out.put(3, hidden, r.hidden_out[0])
    loaded.wait()
    project(hidden, r.w_out, third)
    wide_moments(0, [lambda: gather.advance(4, 5)])
    finish_block(0, r.image, r.middle)
    out.put(4, r.middle, r.middle_out)
    out.put(5, r.hat3, r.hat3_out[0])
    loaded_in.wait()
    gather.advance(4, 5)
    project(r.middle, r.w_in, first)
    gather.advance(4)
    loaded = load(4, r.w_mid, 1)
    narrow_moments(2, [lambda: gather.advance(5)])
    out.settle(0)
    activate(2, r.hat_a, ext.at[1], halo)
    out.put(0, r.hat_a, r.hat1_out[1])
    edges = halo_copies(1)
    for copy in edges:
        copy.start()
    loaded_out = load(5, r.w_out, 2)
    loaded.wait()
    for copy in edges:
        copy.wait()
    out.put(6, ext.at[1], r.field_out[1])
    loop(chunks, mid_plain)
    narrow_moments(3)
    out.settle(2, 3)
    activate(3, r.hat_b, hidden, 0)
    out.put(2, r.hat_b, r.hat2_out[1])
    out.put(3, hidden, r.hidden_out[1])
    loaded_out.wait()
    project(hidden, r.w_out, third)
    wide_moments(1)
    out.settle(5)
    finish_block(1, r.middle, r.result)
    out.put(7, r.result, r.image_out)
    out.put(5, r.hat3, r.hat3_out[1])
    for i in range(max(0, chunks - 2), chunks):
        samp_copy(i).wait()
    out.settle()


def forward(image, shards, geometry, offset_weight, offset_bias, mid_norms, out_norms, sizes):
    valid, masks, counts = geometry
    pixels, wide = image.shape
    width = shards[0].shape[1] * sizes[1]
    taps = 9 * width
    high = sizes[0] // 2
    ext_pixels = pixels + 2 * halo_rows * breadth
    in_kernel = all(s.shape[0] % 16 == 0 for s in shards)
    fulls = []
    if not in_kernel:
        fulls = [lax.all_gather(s, "mp", axis=1, tiled=True) for s in shards]
        fulls = [lax.all_gather(s, "dp", axis=0, tiled=True) for s in fulls]
    ins = dict(
        image=image,
        valid=valid,
        masks=masks,
        counts=counts,
        offset_weight=offset_weight,
        offset_bias=offset_bias,
        mid_gain=mid_norms[0],
        mid_bias=mid_norms[1],
        out_gain=out_norms[0],
        out_bias=out_norms[1],
        shards=list(shards) if in_kernel else [],
    )
    narrow, broad = shape((pixels, width), bf16), shape((pixels, wide), bf16)
    outs = dict(
        hat1_out=[narrow] * 2,
        hat2_out=[narrow] * 2,
        hidden_out=[narrow] * 2,
        field_out=[shape((ext_pixels, width), bf16)] * 2,
        hat3_out=[broad] * 2,
        middle_out=broad,
        image_out=broad,
        samp_out=shape((pixels, taps), bf16),
        tanh_raw=shape((pixels, 128), f32),
        rstd_narrow=shape((4, width), f32),
        rstd_wide=shape((2, wide), f32),
    )
    if in_kernel:
        outs.update(
            fulls=[shape((high, 2, s.shape[0], s.shape[1] * sizes[1]), bf16) for s in shards]
        )
    else:
        ins.update(fulls=fulls)
    plan = [(3, width), (3, width), (3, wide)] * 2
    scratch = dict(
        first=pltpu.VMEM((pixels, width), f32),
        third=pltpu.VMEM((pixels, wide), f32),
        ext=pltpu.VMEM((2, ext_pixels, width), bf16),
        hidden=pltpu.VMEM((pixels, width), bf16),
        hat_a=pltpu.VMEM((pixels, width), bf16),
        hat_b=pltpu.VMEM((pixels, width), bf16),
        hat3=pltpu.VMEM((pixels, wide), bf16),
        middle=pltpu.VMEM((pixels, wide), bf16),
        result=pltpu.VMEM((pixels, wide), bf16),
        samp=pltpu.VMEM((2, chunk, taps), bf16),
        off=pltpu.VMEM((chunk, 128), f32),
        w_in=pltpu.VMEM((wide, width), bf16),
        w_mid=pltpu.VMEM((taps, width), bf16),
        w_out=pltpu.VMEM((width, wide), bf16),
        mean_narrow=pltpu.VMEM((1, width), f32),
        mean_wide=pltpu.VMEM((1, wide), f32),
        gather_local=dma((6,)),
        gather_send=dma((6, high - 1 + 7)),
        gather_recv=dma((6, high - 1 + 7)),
        halo_send=dma((2, 2)),
        halo_recv=dma((2, 2)),
        out_sem=dma((8,)),
        samp_sem=dma((2,)),
        load_sem=dma((3,)),
        syncs=sync_scratch(plan, sizes),
    )
    kept = launch(
        partial(forward_pass, sizes),
        ins,
        dict(shards=anywhere, fulls=anywhere, masks=smem, counts=smem),
        outs,
        dict(tanh_raw=vmem, rstd_narrow=vmem, rstd_wide=vmem),
        scratch,
        0,
        62,
    )
    if not in_kernel:
        kept.fulls = fulls
    return kept


class Scatter:
    def __init__(self, place, r, kind, use, result):
        self.place, self.use, self.result = place, use, result
        self.keep, self.from_core = r.keep[kind], r.from_core[kind]
        self.low, self.upper = r.from_low[kind], r.from_upper[kind]
        self.two, self.from_high = r.from_two[kind], r.from_high[kind]
        self.send, self.recv, self.free = r.scatter_send[kind], r.scatter_recv[kind], r.scatter_free[kind]
        self.staging, self.staging_sem = r.staging, r.staging_sem
        self.rows, self.width = self.keep.shape[1], self.keep.shape[2]
        self.block = self.rows // place.dp_size
        self.tiles = self.rows // lane_block
        self.stage = 0
        self.running = []

    def cols(self, x_at, core_at):
        return pl.ds(pl.multiple_of((2 * x_at + core_at) * self.width, 128), self.width)

    def at(self, high, y):
        return pl.ds(pl.multiple_of((2 * high + y) * self.block, self.block), self.block)

    def to_core(self, t, i, src):
        rows = pl.ds(pl.multiple_of(t * lane_block, lane_block), lane_block)
        return remote(
            src,
            self.from_core.at[i, rows],
            self.send.at[2 * t + i],
            self.recv.at[2 * t + i],
            self.place.core_peer(),
        )

    def tile_copies(self, t):
        slot = lax.rem(t, 2)
        rows = pl.ds(pl.multiple_of(t * lane_block, lane_block), lane_block)
        core = self.place.core
        away = [self.to_core(t, i, self.staging.at[slot, :, self.cols(i, 1 - core)]) for i in (0, 1)]
        home = [
            pltpu.make_async_copy(
                self.staging.at[slot, :, self.cols(i, core)],
                self.keep.at[i, rows],
                self.staging_sem.at[slot, i],
            )
            for i in (0, 1)
        ]
        return away, home

    def settle_tile(self, t):
        away, home = self.tile_copies(t)
        for copy in away:
            copy.wait_send()
        for copy in home:
            copy.wait()

    def begin(self):
        if self.use == 1:
            pl.semaphore_wait(self.free.at[0], 1)

    def fill(self, first, last, compute):
        def body(i):
            t = first + i

            @pl.when(i >= 2)
            def _():
                self.settle_tile(t - 2)

            compute(t, self.staging.at[lax.rem(t, 2)])
            away, home = self.tile_copies(t)
            for copy in away + home:
                copy.start()

        loop(last - first, body)
        for t in range(max(first, last - 2), last):
            self.settle_tile(t)

    def fill_by_columns(self, compute):
        core = self.place.core

        def away(i):
            self.staging[i] = compute(self.cols(i, 1 - core)).astype(bf16)
            self.to_core(0, i, self.staging.at[i]).start()

        def home(i):
            self.keep[i] = compute(self.cols(i, core)).astype(bf16)

        loop(2, away)
        loop(2, home)
        for i in (0, 1):
            self.to_core(0, i, self.staging.at[i]).wait_send()

    def copies(self, stage):
        place = self.place
        x, y, z, half = place.x, place.y, place.z, place.high // 2
        items = []
        if stage == 1:
            for i in (0, 1):
                for b in range(half):
                    items.append((self.keep.at[i, self.at(b, 1 - y)], self.low.at[i, b], place.y_peer()))
            upper = pl.ds(self.rows // 2, self.rows // 2)
            items.append((self.keep.at[1 - x, upper], self.upper, place.x_peer()))
        elif stage == 2:
            for b in range(half):
                items.append((self.keep.at[1 - x, self.at(b, y)], self.two.at[0, b], place.x_peer()))
                items.append(
                    (self.keep.at[x, self.at(half + b, 1 - y)], self.two.at[1, b], place.y_peer())
                )
        else:
            for k in range(1, place.high):
                there = self.at(lax.rem(z + k, place.high), y)
                items.append((self.keep.at[x, there], self.from_high.at[k - 1], place.z_peer(k)))
        base = 2 * self.tiles + [0, 0, 2 * half + 1, 4 * half + 1][stage]
        return [
            remote(src, dst, self.send.at[base + i], self.recv.at[base + i], peer)
            for i, (src, dst, peer) in enumerate(items)
        ]

    def add(self, target, extra):
        target[...] = (target[...].astype(f32) + extra[...].astype(f32)).astype(bf16)

    def finish(self, stage):
        place = self.place
        x, y, z, half = place.x, place.y, place.z, place.high // 2
        if stage == 0:
            piece = 64
            for i in (0, 1):

                def body(k, i=i):
                    rows = slab(k, piece)
                    self.add(self.keep.at[i, rows], self.from_core.at[i, rows])

                loop(self.rows // piece, body)
            peers = [place.core_peer()]
        elif stage == 1:
            for b in range(half):
                for i in (0, 1):
                    self.add(self.keep.at[i, self.at(b, y)], self.low.at[i, b])
            piece = 64

            def body(k):
                rows = pl.ds(pl.multiple_of(self.rows // 2 + k * piece, piece), piece)
                self.add(self.keep.at[x, rows], self.upper.at[slab(k, piece)])

            loop(self.rows // 2 // piece, body)
            peers = [place.x_peer(), place.y_peer()]
        elif stage == 2:
            for b in range(half):
                self.add(self.keep.at[x, self.at(b, y)], self.two.at[0, b])
                self.add(self.keep.at[x, self.at(half + b, y)], self.two.at[1, b])
            peers = [place.x_peer(), place.y_peer()]
        else:
            total = self.keep[x, self.at(z, y)].astype(f32)
            for k in range(1, place.high):
                total = total + self.from_high[k - 1].astype(f32)
            self.result[...] = total
            peers = [place.z_peer(k) for k in range(1, place.high)]
        if self.use == 0:
            for peer in peers:
                pl.semaphore_signal(self.free.at[stage], inc=1, device_id=peer, device_id_type=MESH)

    def advance(self):
        if self.stage > 3:
            return
        if self.stage == 0:
            for t in range(self.tiles):
                for i in (0, 1):
                    self.to_core(t, i, self.staging.at[0, :, self.cols(i, 0)] if self.tiles > 1 else self.staging.at[i]).wait_recv()
        for copy in self.running:
            copy.wait()
        self.finish(self.stage)
        self.stage += 1
        if self.stage <= 3:
            if self.use == 1:
                waits = [0, 2, 2, self.place.high - 1][self.stage]
                pl.semaphore_wait(self.free.at[self.stage], waits)
            self.running = self.copies(self.stage)
            for copy in self.running:
                copy.start()

    def drain(self):
        while self.stage <= 3:
            self.advance()


class Whole:
    def __init__(self, r, result):
        self.staging, self.staging_sem, self.result = r.staging, r.staging_sem, result

    def begin(self):
        pass

    def fill(self, first, last, compute):
        def body(i):
            t = first + i
            compute(t, self.staging.at[0])
            rows = pl.ds(pl.multiple_of(t * lane_block, lane_block), lane_block)
            pltpu.sync_copy(self.staging.at[0], self.result.at[rows])

        loop(last - first, body)

    def fill_by_columns(self, compute):
        def body(i):
            lanes = pl.ds(pl.multiple_of(i * lane_block, lane_block), lane_block)
            self.staging[0] = compute(lanes).astype(bf16)
            pltpu.sync_copy(self.staging.at[0], self.result.at[:, lanes])

        loop(self.result.shape[1] // lane_block, body)

    def advance(self):
        pass

    drain = advance


def backward_pass(sizes, in_kernel, r):
    place = Place(*sizes)
    syncs = Syncs(place, r.syncs)
    box = Outbox(r.load_sem)
    valid, masks, counts = r.valid, r.masks, r.counts
    grad, small, inputs, hat3, wide_act = r.grad, r.small, r.inputs, r.hat3, r.wide_act
    pixels, wide, width = grad.shape[0], grad.shape[1], small.shape[1]
    halo = halo_rows * breadth
    chunks, chunk_rows = pixels // chunk, chunk // breadth
    per_pixel = counts[2]
    own = pl.ds(halo, pixels)
    kinds = [0, 1, 2]

    def scatter(kind, use):
        result = r.grads[3 * use + kind]
        if in_kernel:
            return Scatter(place, r, kind, use, result)
        return Whole(r, result)

    def weight(array, dst, sem):
        box.running[sem] = load_weight(r.fulls[array], dst, r.load_sem.at[sem])

    def open_sync(terms, block_width, rows=2, last_row=None):
        stages = syncs.take(block_width)
        src = stages[0][3][0]
        strip_sums(pixels, block_width, terms, src, [0, 1])
        if last_row is not None:
            src[2:3, :] = jnp.zeros((1, block_width), f32)
            src[2:3, 0:128] = last_row
        syncs.start(stages[0])
        return stages

    def pre_back(block, upstream, image):
        gain, bias = r.out_gain.at[block : block + 1, :], r.out_bias.at[block : block + 1, :]

        def terms(at, lanes):
            hat = hat3[at, lanes].astype(f32)
            pre = image[at, lanes].astype(f32) + (hat * gain[:, lanes] + bias[:, lanes])
            slope = gelu_slope(pre) * wide_valid(valid, at, lane_block)
            d = upstream[at, lanes].astype(f32) * slope
            grad[at, lanes] = d
            return d, d * hat

        return open_sync(terms, wide)

    def last_norm_back(block):
        sums, rstd = r.wide_sums.at[block], r.rstd_wide.at[block : block + 1, :]
        gain = r.out_gain.at[block : block + 1, :]

        def body(i):
            at = slab(i, strip)
            mask = wide_valid(valid, at, lane_block)
            for j in range(wide // lane_block):
                lanes = pl.ds(j * lane_block, lane_block)
                hat = hat3[at, lanes].astype(f32)
                inner = grad[at, lanes] - sums[0:1, lanes] * per_pixel
                inner = inner - hat * (sums[1:2, lanes] * per_pixel)
                scaled = mask * (gain[:, lanes] * rstd[:, lanes]) * inner
                wide_act[at, lanes] = scaled.astype(bf16)

        loop(pixels // strip, body)

    def act_back(norm, hat):
        gain, bias = r.mid_gain.at[norm : norm + 1, :], r.mid_bias.at[norm : norm + 1, :]

        def terms(at, lanes):
            normed = hat[at, lanes].astype(f32)
            slope = gelu_slope(normed * gain[:, lanes] + bias[:, lanes])
            rows = pl.ds(pl.multiple_of(halo + at.start, strip), strip)
            d = small[rows, lanes] * slope * wide_valid(valid, at, lane_block)
            small[rows, lanes] = d
            return d, d * normed

        return terms

    def inner_norm_back(norm, hat, target, target_row):
        sums, rstd = r.narrow_sums.at[norm], r.rstd_narrow.at[norm : norm + 1, :]
        gain = r.mid_gain.at[norm : norm + 1, :]

        def body(i):
            at = slab(i, strip)
            rows = pl.ds(pl.multiple_of(halo + i * strip, strip), strip)
            inner = small[rows, :] - sums[0:1, :] * per_pixel
            inner = inner - hat[at, :].astype(f32) * (sums[1:2, :] * per_pixel)
            scaled = wide_valid(valid, at, width) * (gain[...] * rstd[...]) * inner
            target[pl.ds(pl.multiple_of(target_row + i * strip, strip), strip), :] = scaled.astype(bf16)

        loop(pixels // strip, body)

    def out_back(block):
        def body(i):
            rows = pl.ds(pl.multiple_of(halo + i * chunk, breadth), chunk)
            small[rows, :] = nt_dot(wide_act[slab(i, chunk), :], r.w_out[...])

        loop(chunks, body)
        return open_sync(act_back(2 * block + 1, r.hat2), width)

    def out_grad(target):
        target.begin()
        target.fill_by_columns(lambda lanes: tn_dot(r.hidden[...], wide_act[:, lanes]))

    def in_grad(target):
        target.begin()

        def compute(t, ref):
            lanes = pl.ds(pl.multiple_of(t * lane_block, lane_block), lane_block)
            ref[...] = tn_dot(inputs[:, lanes], r.da[...]).astype(bf16)

        target.fill(0, wide // lane_block, compute)

    def in_back(i):
        at = slab(i, chunk)
        grad[at, :] = grad[at, :] + nt_dot(r.da[at, :], r.w_in[...])

    def neighbours(before_src, before_dst, after_src, after_dst, which):
        send, recv = r.edge_send.at[which], r.edge_recv.at[which]
        return [
            remote(after_src, after_dst, send.at[0], recv.at[0], place.next(1)),
            remote(before_src, before_dst, send.at[1], recv.at[1], place.next(-1)),
        ]

    place.greet_all()
    box.put(0, r.middle, inputs)
    box.put(1, r.hat3_in[1], hat3)
    box.put(2, r.cotangent, wide_act)
    weight(5, r.w_out, 3)
    box.put(4, r.hat2_in[1], r.hat2)
    box.put(5, r.hidden_in[1], r.hidden)
    box.put(6, r.field_in[1].at[own], r.field.at[own])
    weight(4, r.w_mid, 7)
    weight(3, r.w_in, 8)

    out_b, mid_b, in_b = [scatter(kind, 0) for kind in kinds]
    box.settle(0, 1, 2)
    stages = pre_back(1, wide_act, inputs)
    r.wide_sums[1] = syncs.rest(stages, False)
    last_norm_back(1)
    box.put(1, r.hat3_in[0], hat3)
    box.settle(3, 4)
    stages = out_back(1)
    box.settle(5)
    out_grad(out_b)
    box.put(2, r.image, wide_act)
    weight(2, r.w_out, 3)
    r.narrow_sums[3] = syncs.rest(stages, False)
    box.put(5, r.hat1_in[1], r.hidden)

    pool, side = r.pool, 2 * breadth
    span = pixels + 2 * side
    centre = 2 * span
    inner_norm_back(3, r.hat2, pool, centre + side)
    box.put(4, r.hat2_in[0], r.hat2)
    edges = neighbours(
        pool.at[pl.ds(centre + side, side)],
        pool.at[pl.ds(centre + side + pixels, side)],
        pool.at[pl.ds(centre + pixels, side)],
        pool.at[pl.ds(centre, side)],
        0,
    )
    for copy in edges:
        copy.start()

    def shift_row(row):
        at = pl.ds(pl.multiple_of(centre + row * breadth, breadth), breadth)
        value = pool[at, :].astype(f32)
        for slot, amount in ((0, 2), (1, -2)):
            rows = pl.ds(pl.multiple_of(slot * span + row * breadth, breadth), breadth)
            pool[rows, :] = shifted(value, amount).astype(bf16)

    loop(pixels // breadth, lambda row: shift_row(row + 2))
    out_b.advance()
    for copy in edges:
        copy.wait()
    loop(2, shift_row)
    loop(2, lambda row: shift_row(row + 2 + pixels // breadth))
    slot_of = (0, 2, 1)
    box.settle(6, 7)

    def mid_back_plain(i):
        first_row = i * chunk_rows
        total = None
        for tap_row in range(3):
            for tap_col in range(3):
                start = slot_of[tap_col] * span + (4 - 2 * tap_row) * breadth + i * chunk
                part = pool[pl.ds(pl.multiple_of(start, breadth), chunk), :]
                if tap_row != 1:
                    part = masked_rows(part, masks, first_row, 4 - 2 * tap_row)
                tap = pl.ds((3 * tap_row + tap_col) * width, width)
                term = nt_dot(part, r.w_mid[tap, :])
                total = term if total is None else total + term
        rows = pl.ds(pl.multiple_of(halo + i * chunk, breadth), chunk)
        small[rows, :] = total

    loop(chunks, mid_back_plain)
    weight(1, r.w_mid, 7)
    out_b.advance()
    box.settle(5)
    stages = open_sync(act_back(2, r.hidden), width)
    mid_b.begin()
    shifted_rows = 3 * span

    def mid_grad_plain(t, ref):
        tap_row, tap_col = t // 3, lax.rem(t, 3)
        slot = jnp.where(tap_col == 0, 0, jnp.where(tap_col == 1, 2, 1))

        def copy_row(row):
            start = slot * span + (4 - 2 * tap_row + row) * breadth
            part = pool[pl.ds(pl.multiple_of(start, breadth), breadth), :]
            rows = pl.ds(pl.multiple_of(shifted_rows + row * breadth, breadth), breadth)
            pool[rows, :] = masked_rows(part, masks, row, 4 - 2 * tap_row)

        loop(pixels // breadth, copy_row)
        ref[...] = tn_dot(r.field[own, :], pool[pl.ds(shifted_rows, pixels), :]).astype(bf16)

    mid_b.fill(0, 9, mid_grad_plain)
    out_b.advance()
    r.narrow_sums[2] = syncs.rest(stages, False)
    inner_norm_back(2, r.hidden, r.da, 0)
    box.put(5, r.hidden_in[0], r.hidden)
    box.put(6, r.field_in[0], r.field)
    box.settle(8)
    loop(chunks, in_back)
    out_b.advance()
    mid_b.advance()
    weight(0, r.w_in, 8)

    out_a, mid_a, in_a = [scatter(kind, 1) for kind in kinds]
    box.settle(1, 2)
    stages = pre_back(0, grad, wide_act)
    in_grad(in_b)
    mid_b.advance()
    r.wide_sums[0] = syncs.rest(stages, False)
    box.put(0, r.image, inputs)
    last_norm_back(0)
    mid_b.advance()
    box.settle(3, 4)
    stages = out_back(0)
    box.settle(5)
    out_b.drain()
    out_grad(out_a)
    in_b.advance()
    mid_b.advance()
    r.narrow_sums[1] = syncs.rest(stages, False)
    inner_norm_back(1, r.hat2, r.da, 0)
    box.put(5, r.hat1_in[0], r.hidden)
    box.settle(6, 7)

    def clear(i):
        small[slab(i, breadth), :] = jnp.zeros((breadth, width), f32)

    loop((pixels + 2 * halo) // breadth, clear)
    table = r.table
    table[...] = jnp.zeros_like(table)
    r.draw_sum[...] = jnp.zeros_like(r.draw_sum)

    def mid_back_deformable(i):
        first_row = i * chunk_rows
        part = r.da[slab(i, chunk), :]
        for tap_row in range(3):
            for tap_col in range(3):
                tap = pl.ds((3 * tap_row + tap_col) * width, width)
                dsamp = nt_dot(part, r.w_mid[tap, :]).astype(bf16)
                for k in range(chunk_rows):
                    start = ((tap_row * chunk_rows + k) * 3 + tap_col) * breadth
                    pool[pl.ds(start, breadth), :] = dsamp[breadth * k : breadth * (k + 1)]
        th = r.tanh_raw[slab(i, chunk), :]
        r.off[...] = 0.5 + 0.45 * th
        lane = lax.broadcasted_iota(jnp.int32, (breadth, 128), 1)

        def one_row(k):
            off = r.off[slab(k, breadth), :]
            doff = jnp.zeros((breadth, 128), f32)
            for tap_row in range(3):
                start = (tap_row * chunk_rows + k) * 3 * breadth
                dsamp = pool[pl.ds(pl.multiple_of(start, breadth), 3 * breadth), :]
                start = halo + i * chunk + (k + 2 * tap_row - 2) * breadth
                rows = pl.ds(pl.multiple_of(start, breadth), 2 * breadth)
                dots = nt_dot(dsamp, r.field[rows, :])
                weights = []
                for tap_col in range(3):
                    terms = tap_terms(off, masks, first_row + k, tap_row, tap_col)
                    down, across, down_slope, across_slope = terms
                    weights.append((down * across).astype(bf16))
                    part = dots[breadth * tap_col : breadth * (tap_col + 1)]
                    doy = jnp.sum(part * (across * down_slope), axis=1, keepdims=True)
                    dox = jnp.sum(part * (across_slope * down), axis=1, keepdims=True)
                    tap = 3 * tap_row + tap_col
                    doff = jnp.where(lane == 2 * tap, doy, jnp.where(lane == 2 * tap + 1, dox, doff))
                small[rows, :] = small[rows, :] + tn_dot(jnp.concatenate(weights, axis=0), dsamp)
            th_row = r.tanh_raw[pl.ds(pl.multiple_of(i * chunk + k * breadth, breadth), breadth), :]
            draw = (0.45 * (1.0 - th_row * th_row) * doff).astype(bf16).astype(f32)
            r.off[slab(k, breadth), :] = draw
            r.draw_sum[...] = r.draw_sum[...] + fold8(draw)

        loop(chunk_rows, one_row)
        draw = r.off[...]
        spread = shifted(draw, 2) + pltpu.roll(draw, 32, 1) + pltpu.roll(shifted(draw, -2), 64, 1)
        for tap_row in range(3):
            part = (spread * row_scales(masks, first_row, 2 * tap_row, 128)).astype(bf16)
            start = halo + i * chunk + (2 * tap_row - 2) * breadth
            rows = pl.ds(pl.multiple_of(start, breadth), chunk)
            small[rows, :] = small[rows, :] + nt_dot(part, r.offset_weight[tap_row])
            to = pl.ds(tap_row * width, width)
            table[to, :] = table[to, :] + tn_dot(r.field[rows, :], part)

    def deform_part(first, last):
        loop(last - first, lambda i: mid_back_deformable(first + i))

    deform_part(0, chunks // 2)
    in_b.advance()
    mid_b.drain()
    out_a.advance()
    deform_part(chunks // 2, chunks)

    r.rims[0] = small[pl.ds(0, halo), :].astype(bf16)
    r.rims[1] = small[pl.ds(halo + pixels, halo), :].astype(bf16)
    edges = neighbours(r.rims.at[0], r.got_rims.at[0], r.rims.at[1], r.got_rims.at[1], 1)
    for copy in edges:
        copy.start()

    each = table.shape[0] // place.count

    def slice_of(device):
        return pl.ds(pl.multiple_of(device * each, each), each)

    def push(k):
        to = lax.rem(place.me + k + 1, place.count)
        remote(
            table.at[slice_of(to)], r.table_got.at[place.me], r.table_sem.at[0], r.table_sem.at[1], place.at(to)
        ).start()

    loop(place.count - 1, push)
    pltpu.make_async_copy(
        table.at[slice_of(place.me)], r.table_got.at[place.me], r.table_sem.at[1]
    ).start()

    mid_a.begin()
    slots = 9 * chunk

    def samp_load(t):
        slot = pl.ds(pl.multiple_of(slots + lax.rem(t, 2) * pixels, breadth), pixels)
        lanes = pl.ds(pl.multiple_of(t * width, 128), width)
        return pltpu.make_async_copy(r.samp_in.at[:, lanes], pool.at[slot], r.samp_sem.at[lax.rem(t, 2)])

    def mid_grad_deformable(t, ref):
        @pl.when(t < 8)
        def _():
            samp_load(t + 1).start()

        samp_load(t).wait()
        slot = pl.ds(pl.multiple_of(slots + lax.rem(t, 2) * pixels, breadth), pixels)
        ref[...] = tn_dot(pool[slot, :], r.da[...]).astype(bf16)

    samp_load(0).start()
    mid_a.fill(0, 4, mid_grad_deformable)
    in_b.advance()
    out_a.advance()
    for copy in edges:
        copy.wait()
    first_rows, last_rows = pl.ds(halo, halo), pl.ds(pixels, halo)
    small[first_rows, :] = small[first_rows, :] + r.got_rims[1].astype(f32)
    small[last_rows, :] = small[last_rows, :] + r.got_rims[0].astype(f32)
    box.settle(5)
    draw_sum = jnp.sum(r.draw_sum[...], axis=0, keepdims=True)
    stages = open_sync(act_back(0, r.hidden), width, 3, draw_sum)
    mid_a.fill(4, 9, mid_grad_deformable)
    in_b.advance()
    out_a.advance()

    got = r.table_got
    pltpu.make_async_copy(got, got, r.table_sem.at[1]).wait()
    rest = got.at[pl.ds(0, place.count - 1)]
    pltpu.make_async_copy(rest, rest, r.table_sem.at[0]).wait()
    r.table_total[...] = jnp.sum(got[...], axis=0)

    def push_total(k):
        remote(
            r.table_total,
            r.offset_grad.at[slice_of(place.me)],
            r.table_sem.at[2],
            r.table_sem.at[3],
            place.next(k + 1),
        ).start()

    loop(place.count - 1, push_total)
    pltpu.make_async_copy(
        r.table_total, r.offset_grad.at[slice_of(place.me)], r.table_sem.at[3]
    ).start()

    merged = syncs.rest(stages, False)
    r.narrow_sums[0] = merged[0:2]
    r.bias_sum[...] = merged[2:3, 0:128]
    inner_norm_back(0, r.hidden, r.da, 0)
    in_b.drain()
    mid_a.advance()
    box.settle(0)
    in_grad(in_a)
    out_a.drain()
    box.settle(8)
    for i in range(chunks):
        in_back(i)
        at = slab(i, chunk)
        box.put(9 + i, grad.at[at], r.image_grad.at[at])
        (mid_a if i % 2 else in_a).advance()
    in_a.drain()
    mid_a.drain()
    whole = r.offset_grad
    pltpu.make_async_copy(whole, whole, r.table_sem.at[3]).wait()
    rest = whole.at[pl.ds(0, (place.count - 1) * each)]
    pltpu.make_async_copy(rest, rest, r.table_sem.at[2]).wait()
    box.settle()


def backward(kept, image, cotangent, geometry, offset_weight, mid_norms, out_norms, sizes, in_kernel):
    valid, masks, counts = geometry
    pixels, wide = image.shape
    width = mid_norms[0].shape[1]
    taps = 9 * width
    count, high = sizes[0] * sizes[1], sizes[0] // 2
    half = high // 2
    ext_pixels = pixels + 2 * halo_rows * breadth
    each = 8 * (-(-3 * width // (8 * count)))
    fulls = [(width, wide), (taps, width), (wide, width)]
    owned = [(rows // sizes[0], cols // sizes[1]) for rows, cols in fulls]
    if in_kernel:
        grads = [shape(o, f32) for o in owned] * 2
        scatter = dict(
            keep=[pltpu.VMEM((2, rows, b), bf16) for (rows, _), (_, b) in zip(fulls, owned)],
            from_core=[pltpu.VMEM((2, rows, b), bf16) for (rows, _), (_, b) in zip(fulls, owned)],
            from_low=[pltpu.VMEM((2, half) + o, bf16) for o in owned],
            from_upper=[
                pltpu.VMEM((rows // 2, b), bf16) for (rows, _), (_, b) in zip(fulls, owned)
            ],
            from_two=[pltpu.VMEM((2, half) + o, bf16) for o in owned],
            from_high=[pltpu.VMEM((high - 1,) + o, bf16) for o in owned],
            scatter_free=[pltpu.SemaphoreType.REGULAR((4,))] * 3,
        )
        sems = [dma((2 * (rows // lane_block) + 4 * half + high,)) for rows, _ in fulls]
        scatter.update(scatter_send=sems, scatter_recv=sems)
    else:
        grads = [shape(full, bf16) for full in fulls] * 2
        scatter = dict()
    ins = dict(
        image=image,
        cotangent=cotangent,
        middle=kept.middle_out,
        hat1_in=kept.hat1_out,
        hat2_in=kept.hat2_out,
        hat3_in=kept.hat3_out,
        hidden_in=kept.hidden_out,
        field_in=kept.field_out,
        samp_in=kept.samp_out,
        fulls=kept.fulls,
        tanh_raw=kept.tanh_raw,
        rstd_narrow=kept.rstd_narrow,
        rstd_wide=kept.rstd_wide,
        valid=valid,
        masks=masks,
        counts=counts,
        offset_weight=offset_weight,
        mid_gain=mid_norms[0],
        mid_bias=mid_norms[1],
        out_gain=out_norms[0],
        out_bias=out_norms[1],
    )
    specs = dict(
        image=anywhere,
        cotangent=anywhere,
        middle=anywhere,
        hat1_in=anywhere,
        hat2_in=anywhere,
        hat3_in=anywhere,
        hidden_in=anywhere,
        field_in=anywhere,
        samp_in=anywhere,
        fulls=anywhere,
        masks=smem,
        counts=smem,
    )
    outs = dict(
        image_grad=shape((pixels, wide), f32),
        grads=grads,
        narrow_sums=shape((4, 2, width), f32),
        wide_sums=shape((2, 2, wide), f32),
        offset_grad=shape((count * each, 128), f32),
        bias_sum=shape((1, 128), f32),
    )
    out_specs = dict(narrow_sums=vmem, wide_sums=vmem, offset_grad=vmem, bias_sum=vmem)
    if in_kernel:
        out_specs.update(grads=vmem)
    plan = [(2, wide), (2, width), (2, width), (2, wide), (2, width), (3, width)]
    span = pixels + 4 * breadth
    pool_rows = max(3 * span + pixels, 9 * chunk + 2 * pixels)
    scratch = dict(
        grad=pltpu.VMEM((pixels, wide), f32),
        inputs=pltpu.VMEM((pixels, wide), bf16),
        hat3=pltpu.VMEM((pixels, wide), bf16),
        wide_act=pltpu.VMEM((pixels, wide), bf16),
        w_in=pltpu.VMEM((wide, width), bf16),
        w_mid=pltpu.VMEM((taps, width), bf16),
        w_out=pltpu.VMEM((width, wide), bf16),
        small=pltpu.VMEM((ext_pixels, width), f32),
        hat2=pltpu.VMEM((pixels, width), bf16),
        hidden=pltpu.VMEM((pixels, width), bf16),
        da=pltpu.VMEM((pixels, width), bf16),
        field=pltpu.VMEM((ext_pixels, width), bf16),
        pool=pltpu.VMEM((pool_rows, width), bf16),
        off=pltpu.VMEM((chunk, 128), f32),
        draw_sum=pltpu.VMEM((8, 128), f32),
        table=pltpu.VMEM((count * each, 128), f32),
        table_got=pltpu.VMEM((count, each, 128), f32),
        table_total=pltpu.VMEM((each, 128), f32),
        rims=pltpu.VMEM((2, halo_rows * breadth, width), bf16),
        got_rims=pltpu.VMEM((2, halo_rows * breadth, width), bf16),
        staging=pltpu.VMEM((2, lane_block, lane_block), bf16),
        staging_sem=dma((2, 2)),
        table_sem=dma((4,)),
        edge_send=dma((2, 2)),
        edge_recv=dma((2, 2)),
        samp_sem=dma((2,)),
        load_sem=dma((9 + pixels // chunk,)),
        syncs=sync_scratch(plan, sizes),
        **scatter,
    )
    return launch(
        partial(backward_pass, sizes, in_kernel), ins, specs, outs, out_specs, scratch, 1, 63
    )


def row_info(row_index, heights, widths, group_rows, total_rows):
    image_count = heights.shape[1]
    inside = (row_index >= 0) & (row_index < total_rows)
    group_of = jnp.clip(row_index // group_rows, 0, 1)
    local_row = row_index - group_of * group_rows
    image_ends = jnp.cumsum(heights, axis=1)
    is_first = (group_of == 0)[:, None]
    ends_by_row = jnp.where(is_first, image_ends[0][None, :], image_ends[1][None, :])
    image_num = jnp.sum((local_row[:, None] >= ends_by_row).astype(jnp.int32), axis=1)
    identity = jnp.where(inside, group_of * image_count + image_num, -1)
    width_table = jnp.where(is_first, widths[0][None, :], widths[1][None, :])
    picked = jnp.arange(image_count, dtype=jnp.int32)[None, :] == image_num[:, None]
    width_row = jnp.sum(jnp.where(picked, width_table, 0), axis=1)
    return (identity, jnp.where(inside, width_row, 0))


def per_device(
    image_in,
    cotangent,
    heights,
    widths,
    weight_in_a,
    weight_offset,
    bias_offset,
    weight_mid_a,
    weight_out_a,
    weight_in_b,
    weight_mid_b,
    weight_out_b,
    mid_gain,
    mid_bias,
    out_gain,
    out_bias,
):
    height, wide = image_in.shape[0], image_in.shape[2]
    sizes = (lax.axis_size("dp"), lax.axis_size("mp"))
    total_rows = height * sizes[0] * sizes[1]
    first_row = lax.axis_index(("dp", "mp")) * height
    row_index = first_row - halo_rows + jnp.arange(height + 2 * halo_rows, dtype=jnp.int32)
    identity, width_row = row_info(
        row_index, heights, widths, total_rows // 2 + height // 2, total_rows
    )
    centre = identity[halo_rows : halo_rows + height]
    masks = jnp.stack(
        [(identity[halo_rows + s : halo_rows + s + height] == centre) for s in range(-2, 4)], axis=1
    ).astype(f32)
    col_index = jnp.arange(breadth, dtype=jnp.int32)
    own_width = width_row[halo_rows : halo_rows + height]
    valid = (col_index[None, :] < own_width[:, None]).astype(f32)
    valid = jnp.broadcast_to(valid.reshape(-1, 1), (height * breadth, 128))
    local_pixels = jnp.sum(own_width).astype(f32)
    pixels = jnp.sum(heights * widths).astype(f32)
    counts = jnp.stack([local_pixels, 1.0 / local_pixels, 1.0 / pixels])
    geometry = (valid, masks, counts)
    width = weight_offset.shape[0] // 9
    by_tap = weight_offset.reshape(3, 3, width, offsets_count).transpose(0, 2, 1, 3)
    by_tap = jnp.pad(by_tap, ((0, 0), (0, 0), (0, 1), (0, 32 - offsets_count)))
    offset_weight = by_tap.reshape(3, width, 128)
    offset_bias = jnp.pad(bias_offset, (0, 128 - offsets_count))[None]
    mid_norms = (mid_gain.reshape(4, width), mid_bias.reshape(4, width))
    out_norms = (out_gain, out_bias)
    shards = (weight_in_a, weight_mid_a, weight_out_a, weight_in_b, weight_mid_b, weight_out_b)
    in_kernel = all(s.shape[0] % 16 == 0 for s in shards)
    image = image_in.reshape(height * breadth, wide)
    kept = forward(
        image, shards, geometry, offset_weight, offset_bias, mid_norms, out_norms, sizes
    )
    back = backward(
        kept,
        image,
        cotangent.reshape(height * breadth, wide),
        geometry,
        offset_weight,
        mid_norms,
        out_norms,
        sizes,
        in_kernel,
    )
    grads = back.grads
    if not in_kernel:
        grads = [
            lax.psum_scatter(
                lax.psum_scatter(g.astype(f32), "dp", scatter_dimension=0, tiled=True),
                "mp",
                scatter_dimension=1,
                tiled=True,
            )
            for g in grads
        ]
    offset_grad = back.offset_grad[: 3 * width].reshape(3, width, 4, 32)[:, :, :3, :offsets_count]
    offset_grad = offset_grad.transpose(0, 2, 1, 3).reshape(9 * width, offsets_count)
    narrow = back.narrow_sums.reshape(2, 2, 2, width)
    return (
        kept.image_out.reshape(image_in.shape),
        back.image_grad.reshape(image_in.shape),
        grads[5],
        offset_grad,
        back.bias_sum[0, :offsets_count],
        grads[4],
        grads[3],
        grads[2],
        grads[1],
        grads[0],
        narrow[:, :, 1],
        narrow[:, :, 0],
        back.wide_sums[:, 1],
        back.wide_sums[:, 0],
    )


def solution(mesh):
    rows, split, both = P(("dp", "mp"), None, None), P("dp", "mp"), P()
    in_specs = (rows, rows, both, both, split, both, both, split, split, split, split, split)
    in_specs += (both,) * 4
    out_specs = (rows, rows, split, both, both, split, split, split, split, split) + (both,) * 4
    return jax.shard_map(
        per_device, mesh=mesh, in_specs=in_specs, out_specs=out_specs, check_vma=False
    )
```

```python
from functools import partial
from types import SimpleNamespace

import jax
import jax.numpy as jnp
from jax import lax
from jax.experimental import pallas as pl
from jax.experimental.pallas import tpu as pltpu
from jax.sharding import PartitionSpec as P

norm_eps = 1e-05
halo_rows = 3
breadth = 64
chunk = 256
strip = 32
lane_block = 512
offsets_count = 18
gelu_a = 0.7978845608028654
gelu_b = gelu_a * 0.044715
MESH = pl.DeviceIdType.MESH
f32 = jnp.float32
bf16 = jnp.bfloat16
shape = jax.ShapeDtypeStruct
dma = pltpu.SemaphoreType.DMA
vmem = pl.BlockSpec(memory_space=pltpu.VMEM)
smem = pl.BlockSpec(memory_space=pltpu.SMEM)
anywhere = pl.BlockSpec(memory_space=pl.ANY)


class Place:
    def __init__(self, dp_size, mp_size):
        self.dp_size, self.mp_size = dp_size, mp_size
        self.count = dp_size * mp_size
        self.high = dp_size // 2
        self.dp = lax.axis_index("dp")
        self.mp = lax.axis_index("mp")
        self.me = self.dp * mp_size + self.mp
        self.z = self.dp // 2
        self.y = lax.rem(self.dp, 2)
        self.x = self.mp // 2
        self.core = lax.rem(self.mp, 2)

    def at(self, linear):
        return (linear // self.mp_size, lax.rem(linear, self.mp_size))

    def next(self, step):
        return self.at(lax.rem(self.me + self.count + step, self.count))

    def core_peer(self):
        return (self.dp, self.mp + 1 - 2 * self.core)

    def x_peer(self):
        return (self.dp, self.mp + 2 - 4 * self.x)

    def y_peer(self):
        return (self.dp + 1 - 2 * self.y, self.mp)

    def z_peer(self, step):
        return (lax.rem(self.z + step, self.high) * 2 + self.y, self.mp)

    def greet_all(self):
        barrier = pltpu.get_barrier_semaphore()

        def greet_one(k):
            pl.semaphore_signal(barrier, inc=1, device_id=self.next(k + 1), device_id_type=MESH)

        loop(self.count - 1, greet_one)
        pl.semaphore_wait(barrier, self.count - 1)


def remote(src, dst, send, recv, peer):
    return pltpu.make_async_remote_copy(
        src_ref=src,
        dst_ref=dst,
        send_sem=send,
        recv_sem=recv,
        device_id=peer,
        device_id_type=MESH,
    )


def slab(index, size):
    return pl.ds(pl.multiple_of(index * size, size), size)


def loop(count, body):
    def step(i, carry):
        body(i)
        return carry

    lax.fori_loop(0, count, step, 0)


def launch(kernel, ins, specs, outs, out_specs, scratch, collective_id, vmem_mib):
    flat_in, tree_in = jax.tree.flatten(ins)
    flat_out, tree_out = jax.tree.flatten(outs)
    is_leaf = lambda s: not isinstance(s, (dict, list))
    flat_scratch, tree_scratch = jax.tree.flatten(scratch, is_leaf=is_leaf)
    spec_in = [s for n in sorted(ins) for s in [specs.get(n, vmem)] * len(jax.tree.leaves(ins[n]))]
    spec_out = [
        s for n in sorted(outs) for s in [out_specs.get(n, anywhere)] * len(jax.tree.leaves(outs[n]))
    ]

    def body(*refs):
        a, b = len(flat_in), len(flat_in) + len(flat_out)
        everything = dict(jax.tree.unflatten(tree_in, refs[:a]))
        everything.update(jax.tree.unflatten(tree_out, refs[a:b]))
        everything.update(jax.tree.unflatten(tree_scratch, refs[b:]))
        kernel(SimpleNamespace(**everything))

    results = pl.pallas_call(
        body,
        out_shape=flat_out,
        in_specs=spec_in,
        out_specs=spec_out,
        scratch_shapes=flat_scratch,
        compiler_params=pltpu.CompilerParams(
            collective_id=collective_id,
            has_side_effects=True,
            vmem_limit_bytes=vmem_mib * 1024 * 1024,
        ),
        name=kernel.func.__name__,
    )(*flat_in)
    return SimpleNamespace(**jax.tree.unflatten(tree_out, results))


def gelu_of(v):
    return 0.5 * v * (1.0 + jnp.tanh(v * (gelu_a + gelu_b * v * v)))


def gelu_slope(v):
    square = v * v
    half = 0.5 + 0.5 * jnp.tanh(v * (gelu_a + gelu_b * square))
    return half * (1.0 + (1.0 - half) * (v * (2.0 * gelu_a + 6.0 * gelu_b * square)))


def wide_valid(valid, rows, width):
    mask = valid[rows, :]
    return jnp.concatenate([mask] * (width // 128), axis=1)


def fold8(x):
    return jnp.sum(x.reshape(x.shape[0] // 8, 8, x.shape[1]), axis=0)


def strip_sums(pixel_count, width, terms, out, row_at):
    for block in range(width // lane_block):
        lanes = pl.ds(block * lane_block, lane_block)

        def step(i, carry, lanes=lanes):
            parts = terms(slab(i, strip), lanes)
            return tuple(c + fold8(p) for c, p in zip(carry, parts))

        zeros = tuple(jnp.zeros((8, lane_block), f32) for _ in row_at)
        sums = lax.fori_loop(0, pixel_count // strip, step, zeros)
        for row, total in zip(row_at, sums):
            out[row : row + 1, lanes] = jnp.sum(total, axis=0, keepdims=True)


def merge(parts, moments_mode):
    if not moments_mode:
        return jnp.sum(parts, axis=0)
    pixels, sums, squares = parts[:, 0:1], parts[:, 1:2], parts[:, 2:3]
    all_pixels, all_sums = jnp.sum(pixels, axis=0), jnp.sum(sums, axis=0)
    apart = sums / pixels - (all_sums / all_pixels)[None]
    all_squares = jnp.sum(squares + pixels * apart * apart, axis=0)
    return jnp.concatenate([all_pixels, all_sums, all_squares], axis=0)


def sync_groups(width, sizes):
    count = sizes[0] * sizes[1]
    if count > 64:
        return (16, count // 16)
    return sizes[::-1] if width > 1024 else (count,)


def sync_scratch(plan, sizes):
    out = []
    for rows, width in plan:
        for size in sync_groups(width, sizes):
            out += [pltpu.VMEM((rows, width), f32), pltpu.VMEM((size, rows, width), f32), dma, dma]
    return out


class Syncs:
    def __init__(self, place, buffers):
        self.place, self.buffers = place, buffers
        self.at = 0

    def take(self, width):
        stages = []
        stride = 1
        for size in sync_groups(width, (self.place.dp_size, self.place.mp_size)):
            digit = lax.rem(self.place.me // stride, size)
            stages.append((stride, size, digit, self.buffers[self.at : self.at + 4]))
            self.at += 4
            stride *= size
        return stages

    def start(self, stage, value=None):
        stride, size, digit, (src, slots, send, recv) = stage
        me = self.place.me
        if value is not None:
            src[...] = value

        def push(k):
            peer = me + (lax.rem(digit + k + 1, size) - digit) * stride
            remote(src, slots.at[digit], send, recv, self.place.at(peer)).start()

        loop(size - 1, push)
        pltpu.make_async_copy(src, slots.at[digit], recv).start()

    def finish(self, stage, moments_mode):
        stride, size, digit, (src, slots, send, recv) = stage
        pltpu.make_async_copy(slots, slots, recv).wait()
        rest = slots.at[pl.ds(0, size - 1)]
        pltpu.make_async_copy(rest, rest, send).wait()
        return merge(slots[...], moments_mode)

    def rest(self, stages, moments_mode, meanwhile=None):
        value = self.finish(stages[0], moments_mode)
        for stage in stages[1:]:
            self.start(stage, value)
            if meanwhile is not None:
                meanwhile()
            value = self.finish(stage, moments_mode)
        return value


def shifted(x, shift):
    if shift == 0:
        return x
    pixels = x.shape[0]
    column = lax.broadcasted_iota(jnp.int32, x.shape, 0) % breadth + shift
    inside = (column >= 0) & (column < breadth)
    return jnp.where(inside, pltpu.roll(x, (-shift) % pixels, 0), 0.0)


def row_scales(masks, first_row, which, width):
    row_of = lax.broadcasted_iota(jnp.int32, (chunk, width), 0) // breadth
    scale = jnp.zeros((chunk, width), f32)
    for k in range(chunk // breadth):
        scale = jnp.where(row_of == k, masks[first_row + k, which], scale)
    return scale


def masked_rows(part, masks, first_row, which):
    scaled = []
    for k in range(part.shape[0] // breadth):
        piece = part[breadth * k : breadth * (k + 1)].astype(f32)
        scaled.append((piece * masks[first_row + k, which]).astype(bf16))
    return jnp.concatenate(scaled, axis=0)


def tap_terms(off, masks, row, tap_row, tap_col):
    lane = lax.broadcasted_iota(jnp.int32, (breadth, 2 * breadth), 1)
    sub = lax.broadcasted_iota(jnp.int32, (breadth, 2 * breadth), 0)
    upper = lane >= breadth
    apart = jnp.where(upper, lane - breadth, lane) - sub
    tap, shift = 3 * tap_row + tap_col, 2 * tap_col - 2
    oy, ox = off[:, 2 * tap : 2 * tap + 1], off[:, 2 * tap + 1 : 2 * tap + 2]
    low, high = masks[row, 2 * tap_row], masks[row, 2 * tap_row + 1]
    down = jnp.where(upper, oy * high, (1.0 - oy) * low)
    across = jnp.where(apart == shift, 1.0 - ox, jnp.where(apart == shift + 1, ox, 0.0))
    down_slope = jnp.where(upper, high, -low)
    across_slope = jnp.where(apart == shift, -1.0, jnp.where(apart == shift + 1, 1.0, 0.0))
    return down, across, down_slope, across_slope


def nt_dot(a, b):
    return lax.dot_general(a, b, (((1,), (1,)), ((), ())), preferred_element_type=f32)


def tn_dot(a, b):
    return lax.dot_general(a, b, (((0,), (0,)), ((), ())), preferred_element_type=f32)


def nn_dot(a, b):
    return jnp.dot(a, b, preferred_element_type=f32)


class Outbox:
    def __init__(self, sems):
        self.sems, self.running = sems, {}

    def put(self, at, src, dst):
        copy = pltpu.make_async_copy(src, dst, self.sems.at[at])
        copy.start()
        self.running[at] = copy

    def settle(self, *which):
        for at in which or list(self.running):
            self.running.pop(at).wait()


def load_weight(full, dst, sem):
    if len(full.shape) == 2:
        copy = pltpu.make_async_copy(full, dst, sem)
        copy.start()
        return copy
    block = full.shape[2]
    for z in range(full.shape[0]):
        for y in range(2):
            rows = pl.ds((2 * z + y) * block, block)
            pltpu.make_async_copy(full.at[z, y], dst.at[rows], sem).start()
    return pltpu.make_async_copy(dst, dst, sem)


class Gather:
    def __init__(self, place, r):
        self.place, self.fulls, self.sems = place, r.fulls, (r.gather_local, r.gather_send, r.gather_recv)
        self.shards = r.shards
        self.stage = [0] * 6
        self.running = [[] for _ in range(6)]

    def cols(self, array, x_at, core_at):
        width = self.shards[array].shape[1]
        return pl.ds(pl.multiple_of((2 * x_at + core_at) * width, 128), width)

    def copies(self, array, stage):
        place, full = self.place, self.fulls[array]
        high, z, y, x, core = place.high, place.z, place.y, place.x, place.core
        half = high // 2
        mine = self.cols(array, x, core)
        lower, upper = pl.ds(0, half), pl.ds(half, high - half)
        local, send, recv = self.sems
        if stage == 0:
            target = full.at[z, y, :, mine]
            own = pltpu.make_async_copy(self.shards[array], target, local.at[array])
            return [own] + [
                remote(
                    self.shards[array],
                    target,
                    send.at[array, k - 1],
                    recv.at[array, k - 1],
                    place.z_peer(k),
                )
                for k in range(1, high)
            ]
        if stage == 1:
            pairs = [
                (full.at[lower, y, :, mine], place.x_peer()),
                (full.at[upper, y, :, mine], place.y_peer()),
            ]
        elif stage == 2:
            pairs = [
                (full.at[lower, y, :, self.cols(array, 0, core)], place.y_peer()),
                (full.at[lower, y, :, self.cols(array, 1, core)], place.y_peer()),
                (full.at[upper, :, :, mine], place.x_peer()),
            ]
        else:
            pairs = [
                (full.at[:, :, :, self.cols(array, 0, core)], place.core_peer()),
                (full.at[:, :, :, self.cols(array, 1, core)], place.core_peer()),
            ]
        base = high - 1 + [0, 0, 2, 5][stage]
        return [
            remote(ref, ref, send.at[array, base + i], recv.at[array, base + i], peer)
            for i, (ref, peer) in enumerate(pairs)
        ]

    def advance(self, *arrays):
        for array in arrays if self.shards else ():
            for copy in self.running[array]:
                copy.wait()
            self.running[array] = []
            if self.stage[array] < 4:
                self.running[array] = self.copies(array, self.stage[array])
                for copy in self.running[array]:
                    copy.start()
            self.stage[array] += 1


def forward_pass(sizes, r):
    place = Place(*sizes)
    syncs = Syncs(place, r.syncs)
    gather = Gather(place, r)
    out = Outbox(r.out_sem)
    valid, masks, counts = r.valid, r.masks, r.counts
    first, third, ext, hidden = r.first, r.third, r.ext, r.hidden
    pixels, width, wide = first.shape[0], first.shape[1], third.shape[1]
    halo = halo_rows * breadth
    chunks = pixels // chunk

    def load(array, dst, sem):
        return load_weight(r.fulls[array], dst, r.load_sem.at[sem])

    def gather_sums(i, got, first_chunk):
        block_width = got.shape[1]
        sums, centre = r.sums.at[:, :, 0:block_width], r.centre.at[:, 0:block_width]
        mask = wide_valid(valid, slab(i, chunk), block_width)
        if first_chunk:
            centre[...] = jnp.sum(fold8(got * mask), axis=0, keepdims=True) * counts[3]
            sums[...] = jnp.zeros((2, 8, block_width), f32)
        apart = (got - centre[...]) * mask
        sums[0] = sums[0] + fold8(apart)
        sums[1] = sums[1] + fold8(apart * apart)

    def over_chunks(target, compute):
        def body(i, first_chunk=False):
            got = compute(i)
            target[slab(i, chunk), :] = got
            gather_sums(i, got, first_chunk)

        body(0, True)
        loop(chunks - 1, lambda i: body(i + 1))

    def moments(block_width, rstd, mean, meanwhile=None):
        stages = syncs.take(block_width)
        src = stages[0][3][0]
        first_sum = jnp.sum(r.sums[0, :, 0:block_width], axis=0, keepdims=True)
        second_sum = jnp.sum(r.sums[1, :, 0:block_width], axis=0, keepdims=True)
        src[0:1, :] = jnp.full((1, block_width), counts[0], f32)
        src[1:2, :] = first_sum + r.centre[:, 0:block_width] * counts[0]
        src[2:3, :] = second_sum - first_sum * first_sum * counts[1]
        syncs.start(stages[0])
        merged = syncs.rest(stages, True, meanwhile)
        mean[...] = merged[1:2] / merged[0:1]
        rstd[...] = lax.rsqrt(jnp.maximum(merged[2:3], 0.0) / merged[0:1] + norm_eps)

    def activate(norm, hat, target, target_row):
        mean, rstd = r.mean_narrow, r.rstd_narrow.at[norm : norm + 1, :]
        gain, bias = r.mid_gain.at[norm : norm + 1, :], r.mid_bias.at[norm : norm + 1, :]

        def body(i):
            at = slab(i, strip)
            normed = (first[at, :] - mean[...]) * rstd[...]
            hat[at, :] = normed.astype(bf16)
            act = gelu_of(normed * gain[...] + bias[...]) * wide_valid(valid, at, width)
            rows = pl.ds(pl.multiple_of(target_row + i * strip, strip), strip)
            target[rows, :] = act.astype(bf16)

        loop(pixels // strip, body)

    def narrow_moments(norm):
        moments(width, r.rstd_narrow.at[norm : norm + 1, :], r.mean_narrow)

    def project(lhs, weight, target):
        over_chunks(target, lambda i: nn_dot(lhs[slab(i, chunk), :], weight[...]))

    def halo_copies(block):
        field = ext.at[block]
        send, recv = r.halo_send.at[block], r.halo_recv.at[block]
        return [
            remote(
                field.at[pl.ds(pixels, halo)],
                field.at[pl.ds(0, halo)],
                send.at[0],
                recv.at[0],
                place.next(1),
            ),
            remote(
                field.at[pl.ds(halo, halo)],
                field.at[pl.ds(pixels + halo, halo)],
                send.at[1],
                recv.at[1],
                place.next(-1),
            ),
        ]

    def mid_deformable(i, slot):
        field = ext.at[0]
        base = halo + i * chunk
        first_row = i * (chunk // breadth)
        total = jnp.zeros((chunk, 128), f32)
        for tap_row in range(3):
            start = pl.multiple_of(base + (2 * tap_row - 2) * breadth, breadth)
            part = nn_dot(field[pl.ds(start, chunk), :], r.offset_weight[tap_row])
            total = total + part * row_scales(masks, first_row, 2 * tap_row, 128)
        left = shifted(total, -2)
        middle = pltpu.roll(total, 128 - 32, 1)
        right = pltpu.roll(shifted(total, 2), 128 - 64, 1)
        lane = lax.broadcasted_iota(jnp.int32, total.shape, 1)
        raw = jnp.where(lane < 32, left + middle + right, 0.0) + r.offset_bias[...]
        tanh_raw = jnp.tanh(raw)
        r.tanh_raw[slab(i, chunk), :] = tanh_raw
        r.off[...] = 0.5 + 0.45 * tanh_raw

        def one_row(k):
            off = r.off[slab(k, breadth), :]
            for tap_row in range(3):
                weights = []
                for tap_col in range(3):
                    down, across, _, _ = tap_terms(off, masks, first_row + k, tap_row, tap_col)
                    weights.append((down * across).astype(bf16))
                start = pl.multiple_of(base + (k + 2 * tap_row - 2) * breadth, breadth)
                got = nn_dot(jnp.concatenate(weights, axis=0), field[pl.ds(start, 2 * breadth), :])
                for tap_col in range(3):
                    lanes = pl.ds((3 * tap_row + tap_col) * width, width)
                    piece = got[breadth * tap_col : breadth * (tap_col + 1)]
                    r.samp[slot, slab(k, breadth), lanes] = piece.astype(bf16)

        loop(chunk // breadth // 2, lambda k: [one_row(2 * k), one_row(2 * k + 1)])
        got = nn_dot(r.samp[slot], r.w_mid[...])
        first[slab(i, chunk), :] = got
        gather_sums(i, got, i == 0)

    def mid_plain(i):
        field = ext.at[1]
        lhs = []
        for tap_row in range(3):
            start = pl.multiple_of(halo + i * chunk + (2 * tap_row - 2) * breadth, breadth)
            part = field[pl.ds(start, chunk), :]
            if tap_row != 1:
                part = masked_rows(part, masks, i * (chunk // breadth), 2 * tap_row)
            lhs.append(part)
        total = None
        for tap_col in range(3):
            partial_sum = None
            for tap_row in range(3):
                weight = r.w_mid[pl.ds((3 * tap_row + tap_col) * width, width), :]
                part = nn_dot(lhs[tap_row], weight)
                partial_sum = part if partial_sum is None else partial_sum + part
            partial_sum = shifted(partial_sum, 2 * tap_col - 2)
            total = partial_sum if total is None else total + partial_sum
        return total

    def finish_block(block, inputs, result):
        gain, bias = r.out_gain.at[block : block + 1, :], r.out_bias.at[block : block + 1, :]
        mean, rstd = r.mean_wide, r.rstd_wide.at[block : block + 1, :]

        def body(i):
            at = slab(i, strip)
            mask = wide_valid(valid, at, lane_block)
            for j in range(wide // lane_block):
                lanes = pl.ds(j * lane_block, lane_block)
                normed = (third[at, lanes] - mean[:, lanes]) * rstd[:, lanes]
                r.hat3[at, lanes] = normed.astype(bf16)
                pre = inputs[at, lanes].astype(f32) + (normed * gain[:, lanes] + bias[:, lanes])
                result[at, lanes] = (mask * gelu_of(pre)).astype(bf16)

        loop(pixels // strip, body)

    def wide_moments(block, meanwhile=None):
        moments(wide, r.rstd_wide.at[block : block + 1, :], r.mean_wide, meanwhile)

    def samp_copy(i):
        slot = i % 2
        return pltpu.make_async_copy(
            r.samp.at[slot], r.samp_out.at[slab(i, chunk)], r.samp_sem.at[slot]
        )

    place.greet_all()
    gather.advance(0)
    gather.advance(1)
    gather.advance(0)
    gather.advance(0)
    gather.advance(2)
    gather.advance(0)
    gather.advance(1)
    gather.advance(0)
    loaded = load(0, r.w_in, 0)
    gather.advance(1)
    loaded.wait()
    project(r.image, r.w_in, first)
    narrow_moments(0)
    activate(0, r.hat_a, ext.at[0], halo)
    out.put(0, r.hat_a, r.hat1_out[0])
    edges = halo_copies(0)
    for copy in edges:
        copy.start()
    gather.advance(1, 2)
    for copy in edges:
        copy.wait()
    out.put(1, ext.at[0], r.field_out[0])
    gather.advance(1, 3)
    load(1, r.w_mid, 1).wait()
    for i in range(chunks):
        if i >= 2:
            samp_copy(i - 2).wait()
        mid_deformable(i, i % 2)
        samp_copy(i).start()
        gather.advance(*{0: (2,), 1: (3, 4), 2: (2,), 3: (2, 3)}.get(i, ()))
    loaded = load(2, r.w_out, 2)
    narrow_moments(1)
    gather.advance(3, 4)
    activate(1, r.hat_b, hidden, 0)
    out.put(2, r.hat_b, r.hat2_out[0])
    out.put(3, hidden, r.hidden_out[0])
    loaded.wait()
    project(hidden, r.w_out, third)
    gather.advance(3)
    loaded_in = load(3, r.w_in, 0)
    gather.advance(5)
    wide_moments(0, lambda: gather.advance(4))
    finish_block(0, r.image, r.middle)
    out.put(4, r.middle, r.middle_out)
    out.put(5, r.hat3, r.hat3_out[0])
    gather.advance(5)
    loaded_in.wait()
    project(r.middle, r.w_in, first)
    gather.advance(4)
    narrow_moments(2)
    gather.advance(4, 5)
    loaded = load(4, r.w_mid, 1)
    out.settle(0)
    activate(2, r.hat_a, ext.at[1], halo)
    out.put(0, r.hat_a, r.hat1_out[1])
    edges = halo_copies(1)
    for copy in edges:
        copy.start()
    for copy in edges:
        copy.wait()
    out.put(6, ext.at[1], r.field_out[1])
    loaded.wait()
    over_chunks(first, mid_plain)
    gather.advance(5)
    narrow_moments(3)
    gather.advance(5)
    loaded_out = load(5, r.w_out, 2)
    out.settle(2, 3)
    activate(3, r.hat_b, hidden, 0)
    out.put(2, r.hat_b, r.hat2_out[1])
    out.put(3, hidden, r.hidden_out[1])
    loaded_out.wait()
    project(hidden, r.w_out, third)
    wide_moments(1)
    out.settle(5)
    finish_block(1, r.middle, r.result)
    out.put(7, r.result, r.image_out)
    out.put(5, r.hat3, r.hat3_out[1])
    for i in range(max(0, chunks - 2), chunks):
        samp_copy(i).wait()
    out.settle()


def forward(image, shards, geometry, offset_weight, offset_bias, mid_norms, out_norms, sizes):
    valid, masks, counts = geometry
    pixels, wide = image.shape
    width = shards[0].shape[1] * sizes[1]
    taps = 9 * width
    high = sizes[0] // 2
    ext_pixels = pixels + 2 * halo_rows * breadth
    in_kernel = all(s.shape[0] % 16 == 0 for s in shards)
    fulls = []
    if not in_kernel:
        fulls = [lax.all_gather(s, "mp", axis=1, tiled=True) for s in shards]
        fulls = [lax.all_gather(s, "dp", axis=0, tiled=True) for s in fulls]
    ins = dict(
        image=image,
        valid=valid,
        masks=masks,
        counts=counts,
        offset_weight=offset_weight,
        offset_bias=offset_bias,
        mid_gain=mid_norms[0],
        mid_bias=mid_norms[1],
        out_gain=out_norms[0],
        out_bias=out_norms[1],
        shards=list(shards) if in_kernel else [],
    )
    narrow, broad = shape((pixels, width), bf16), shape((pixels, wide), bf16)
    outs = dict(
        hat1_out=[narrow] * 2,
        hat2_out=[narrow] * 2,
        hidden_out=[narrow] * 2,
        field_out=[shape((ext_pixels, width), bf16)] * 2,
        hat3_out=[broad] * 2,
        middle_out=broad,
        image_out=broad,
        samp_out=shape((pixels, taps), bf16),
        tanh_raw=shape((pixels, 128), f32),
        rstd_narrow=shape((4, width), f32),
        rstd_wide=shape((2, wide), f32),
    )
    if in_kernel:
        outs.update(
            fulls=[shape((high, 2, s.shape[0], s.shape[1] * sizes[1]), bf16) for s in shards]
        )
    else:
        ins.update(fulls=fulls)
    plan = [(3, width), (3, width), (3, wide)] * 2
    scratch = dict(
        first=pltpu.VMEM((pixels, width), f32),
        third=pltpu.VMEM((pixels, wide), f32),
        ext=pltpu.VMEM((2, ext_pixels, width), bf16),
        hidden=pltpu.VMEM((pixels, width), bf16),
        hat_a=pltpu.VMEM((pixels, width), bf16),
        hat_b=pltpu.VMEM((pixels, width), bf16),
        hat3=pltpu.VMEM((pixels, wide), bf16),
        middle=pltpu.VMEM((pixels, wide), bf16),
        result=pltpu.VMEM((pixels, wide), bf16),
        samp=pltpu.VMEM((2, chunk, taps), bf16),
        off=pltpu.VMEM((chunk, 128), f32),
        w_in=pltpu.VMEM((wide, width), bf16),
        w_mid=pltpu.VMEM((taps, width), bf16),
        w_out=pltpu.VMEM((width, wide), bf16),
        sums=pltpu.VMEM((2, 8, wide), f32),
        centre=pltpu.VMEM((1, wide), f32),
        mean_narrow=pltpu.VMEM((1, width), f32),
        mean_wide=pltpu.VMEM((1, wide), f32),
        gather_local=dma((6,)),
        gather_send=dma((6, high - 1 + 7)),
        gather_recv=dma((6, high - 1 + 7)),
        halo_send=dma((2, 2)),
        halo_recv=dma((2, 2)),
        out_sem=dma((8,)),
        samp_sem=dma((2,)),
        load_sem=dma((3,)),
        syncs=sync_scratch(plan, sizes),
    )
    kept = launch(
        partial(forward_pass, sizes),
        ins,
        dict(shards=anywhere, fulls=anywhere, masks=smem, counts=smem),
        outs,
        dict(tanh_raw=vmem, rstd_narrow=vmem, rstd_wide=vmem),
        scratch,
        0,
        62,
    )
    if not in_kernel:
        kept.fulls = fulls
    return kept


class Scatter:
    def __init__(self, place, r, kind, use, result):
        self.place, self.use, self.result = place, use, result
        self.keep, self.from_core = r.keep[kind], r.from_core[kind]
        self.low, self.upper = r.from_low[kind], r.from_upper[kind]
        self.two, self.from_high = r.from_two[kind], r.from_high[kind]
        self.send, self.recv, self.free = r.scatter_send[kind], r.scatter_recv[kind], r.scatter_free[kind]
        self.staging, self.staging_sem = r.staging, r.staging_sem
        self.rows, self.width = self.keep.shape[1], self.keep.shape[2]
        self.block = self.rows // place.dp_size
        self.tiles = self.rows // lane_block
        self.stage = 0
        self.running = []

    def cols(self, x_at, core_at):
        return pl.ds(pl.multiple_of((2 * x_at + core_at) * self.width, 128), self.width)

    def at(self, high, y):
        return pl.ds(pl.multiple_of((2 * high + y) * self.block, self.block), self.block)

    def to_core(self, t, i, src):
        rows = pl.ds(pl.multiple_of(t * lane_block, lane_block), lane_block)
        return remote(
            src,
            self.from_core.at[i, rows],
            self.send.at[2 * t + i],
            self.recv.at[2 * t + i],
            self.place.core_peer(),
        )

    def tile_copies(self, t):
        slot = lax.rem(t, 2)
        rows = pl.ds(pl.multiple_of(t * lane_block, lane_block), lane_block)
        core = self.place.core
        away = [self.to_core(t, i, self.staging.at[slot, :, self.cols(i, 1 - core)]) for i in (0, 1)]
        home = [
            pltpu.make_async_copy(
                self.staging.at[slot, :, self.cols(i, core)],
                self.keep.at[i, rows],
                self.staging_sem.at[slot, i],
            )
            for i in (0, 1)
        ]
        return away, home

    def settle_tile(self, t):
        away, home = self.tile_copies(t)
        for copy in away:
            copy.wait_send()
        for copy in home:
            copy.wait()

    def begin(self):
        if self.use == 1:
            pl.semaphore_wait(self.free.at[0], 1)

    def fill(self, first, last, compute):
        def body(i):
            t = first + i

            @pl.when(i >= 2)
            def _():
                self.settle_tile(t - 2)

            compute(t, self.staging.at[lax.rem(t, 2)])
            away, home = self.tile_copies(t)
            for copy in away + home:
                copy.start()

        loop(last - first, body)
        for t in range(max(first, last - 2), last):
            self.settle_tile(t)

    def fill_by_columns(self, compute):
        core = self.place.core

        def away(i):
            self.staging[i] = compute(self.cols(i, 1 - core)).astype(bf16)
            self.to_core(0, i, self.staging.at[i]).start()

        def home(i):
            self.keep[i] = compute(self.cols(i, core)).astype(bf16)

        loop(2, away)
        loop(2, home)
        for i in (0, 1):
            self.to_core(0, i, self.staging.at[i]).wait_send()

    def copies(self, stage):
        place = self.place
        x, y, z, half = place.x, place.y, place.z, place.high // 2
        items = []
        if stage == 1:
            for i in (0, 1):
                for b in range(half):
                    items.append((self.keep.at[i, self.at(b, 1 - y)], self.low.at[i, b], place.y_peer()))
            upper = pl.ds(self.rows // 2, self.rows // 2)
            items.append((self.keep.at[1 - x, upper], self.upper, place.x_peer()))
        elif stage == 2:
            for b in range(half):
                items.append((self.keep.at[1 - x, self.at(b, y)], self.two.at[0, b], place.x_peer()))
                items.append(
                    (self.keep.at[x, self.at(half + b, 1 - y)], self.two.at[1, b], place.y_peer())
                )
        else:
            for k in range(1, place.high):
                there = self.at(lax.rem(z + k, place.high), y)
                items.append((self.keep.at[x, there], self.from_high.at[k - 1], place.z_peer(k)))
        base = 2 * self.tiles + [0, 0, 2 * half + 1, 4 * half + 1][stage]
        return [
            remote(src, dst, self.send.at[base + i], self.recv.at[base + i], peer)
            for i, (src, dst, peer) in enumerate(items)
        ]

    def add(self, target, extra):
        target[...] = target[...] + extra[...]

    def finish(self, stage):
        place = self.place
        x, y, z, half = place.x, place.y, place.z, place.high // 2
        if stage == 0:
            piece = 64
            for i in (0, 1):

                def body(k, i=i):
                    rows = slab(k, piece)
                    self.add(self.keep.at[i, rows], self.from_core.at[i, rows])

                loop(self.rows // piece, body)
            peers = [place.core_peer()]
        elif stage == 1:
            for b in range(half):
                for i in (0, 1):
                    self.add(self.keep.at[i, self.at(b, y)], self.low.at[i, b])
            piece = 64

            def body(k):
                rows = pl.ds(pl.multiple_of(self.rows // 2 + k * piece, piece), piece)
                self.add(self.keep.at[x, rows], self.upper.at[slab(k, piece)])

            loop(self.rows // 2 // piece, body)
            peers = [place.x_peer(), place.y_peer()]
        elif stage == 2:
            for b in range(half):
                self.add(self.keep.at[x, self.at(b, y)], self.two.at[0, b])
                self.add(self.keep.at[x, self.at(half + b, y)], self.two.at[1, b])
            peers = [place.x_peer(), place.y_peer()]
        else:
            total = self.keep[x, self.at(z, y)].astype(f32)
            for k in range(1, place.high):
                total = total + self.from_high[k - 1].astype(f32)
            self.result[...] = total
            peers = [place.z_peer(k) for k in range(1, place.high)]
        if self.use == 0:
            for peer in peers:
                pl.semaphore_signal(self.free.at[stage], inc=1, device_id=peer, device_id_type=MESH)

    def advance(self):
        if self.stage > 3:
            return
        if self.stage == 0:
            for t in range(self.tiles):
                for i in (0, 1):
                    self.to_core(t, i, self.staging.at[0, :, self.cols(i, 0)] if self.tiles > 1 else self.staging.at[i]).wait_recv()
        for copy in self.running:
            copy.wait()
        self.finish(self.stage)
        self.stage += 1
        if self.stage <= 3:
            if self.use == 1:
                waits = [0, 2, 2, self.place.high - 1][self.stage]
                pl.semaphore_wait(self.free.at[self.stage], waits)
            self.running = self.copies(self.stage)
            for copy in self.running:
                copy.start()

    def drain(self):
        while self.stage <= 3:
            self.advance()


class Whole:
    def __init__(self, r, result):
        self.staging, self.staging_sem, self.result = r.staging, r.staging_sem, result

    def begin(self):
        pass

    def fill(self, first, last, compute):
        def body(i):
            t = first + i
            compute(t, self.staging.at[0])
            rows = pl.ds(pl.multiple_of(t * lane_block, lane_block), lane_block)
            pltpu.sync_copy(self.staging.at[0], self.result.at[rows])

        loop(last - first, body)

    def fill_by_columns(self, compute):
        def body(i):
            lanes = pl.ds(pl.multiple_of(i * lane_block, lane_block), lane_block)
            self.staging[0] = compute(lanes).astype(bf16)
            pltpu.sync_copy(self.staging.at[0], self.result.at[:, lanes])

        loop(self.result.shape[1] // lane_block, body)

    def advance(self):
        pass

    drain = advance


class TableSum:
    def __init__(self, place, r):
        self.place, self.r = place, r
        self.each = r.table16.shape[0] // place.count
        self.stage, self.running = 0, []

    def part(self, mp, dp=None):
        quarter = self.each * self.place.dp_size
        if dp is None:
            return pl.ds(pl.multiple_of(mp * quarter, self.each), quarter)
        return pl.ds(pl.multiple_of(mp * quarter + dp * self.each, self.each), self.each)

    def copies(self, stage):
        place, r = self.place, self.r
        dp, mp, table, result = place.dp, place.mp, r.table16, r.offset_grad
        items = []
        over_mp = [lax.rem(mp + k, place.mp_size) for k in range(1, place.mp_size)]
        over_dp = [lax.rem(dp + k, place.dp_size) for k in range(1, place.dp_size)]
        if stage == 0:
            for k, to in enumerate(over_mp):
                items.append((table.at[self.part(to)], r.table_one.at[k], (dp, to)))
        elif stage == 1:
            for k, to in enumerate(over_dp):
                items.append((table.at[self.part(mp, to)], r.table_two.at[k], (to, mp)))
        elif stage == 2:
            mine = self.part(mp, dp)
            items = [(result.at[mine], result.at[mine], (to, mp)) for to in over_dp]
        else:
            mine = self.part(mp)
            items = [(result.at[mine], result.at[mine], (dp, to)) for to in over_mp]
        send, recv = r.table_send.at[stage], r.table_recv.at[stage]
        return [remote(a, b, send.at[i], recv.at[i], to) for i, (a, b, to) in enumerate(items)]

    def advance(self):
        place, r = self.place, self.r
        for copy in self.running:
            copy.wait()
        mine = self.part(place.mp), self.part(place.mp, place.dp)
        if self.stage == 0:
            r.table16[...] = r.table[...].astype(bf16)
        elif self.stage == 1:
            total = r.table16[mine[0], :].astype(f32)
            for k in range(place.mp_size - 1):
                total = total + r.table_one[k].astype(f32)
            r.table16[mine[0], :] = total.astype(bf16)
        elif self.stage == 2:
            total = r.table16[mine[1], :].astype(f32)
            for k in range(place.dp_size - 1):
                total = total + r.table_two[k].astype(f32)
            r.offset_grad[mine[1], :] = total.astype(bf16)
        self.running = self.copies(self.stage) if self.stage < 4 else []
        for copy in self.running:
            copy.start()
        self.stage += 1


def backward_pass(sizes, in_kernel, r):
    place = Place(*sizes)
    syncs = Syncs(place, r.syncs)
    box = Outbox(r.load_sem)
    valid, masks, counts = r.valid, r.masks, r.counts
    grad, small, inputs, hat3, wide_act = r.grad, r.small, r.inputs, r.hat3, r.wide_act
    pixels, wide, width = grad.shape[0], grad.shape[1], small.shape[1]
    halo = halo_rows * breadth
    chunks, chunk_rows = pixels // chunk, chunk // breadth
    per_pixel = counts[2]
    own = pl.ds(halo, pixels)
    kinds = [0, 1, 2]

    def scatter(kind, use):
        result = r.grads[3 * use + kind]
        if in_kernel:
            return Scatter(place, r, kind, use, result)
        return Whole(r, result)

    def weight(array, dst, sem):
        box.running[sem] = load_weight(r.fulls[array], dst, r.load_sem.at[sem])

    def open_sync(terms, block_width, rows=2, last_row=None):
        stages = syncs.take(block_width)
        src = stages[0][3][0]
        strip_sums(pixels, block_width, terms, src, [0, 1])
        if last_row is not None:
            src[2:3, :] = jnp.zeros((1, block_width), f32)
            src[2:3, 0:128] = last_row
        syncs.start(stages[0])
        return stages

    def pre_back(block, upstream, image):
        gain, bias = r.out_gain.at[block : block + 1, :], r.out_bias.at[block : block + 1, :]

        def terms(at, lanes):
            hat = hat3[at, lanes].astype(f32)
            pre = image[at, lanes].astype(f32) + (hat * gain[:, lanes] + bias[:, lanes])
            slope = gelu_slope(pre) * wide_valid(valid, at, lane_block)
            d = upstream[at, lanes].astype(f32) * slope
            grad[at, lanes] = d
            return d, d * hat

        return open_sync(terms, wide)

    def last_norm_back(block):
        sums, rstd = r.wide_sums.at[block], r.rstd_wide.at[block : block + 1, :]
        gain = r.out_gain.at[block : block + 1, :]

        def body(i):
            at = slab(i, strip)
            mask = wide_valid(valid, at, lane_block)
            for j in range(wide // lane_block):
                lanes = pl.ds(j * lane_block, lane_block)
                hat = hat3[at, lanes].astype(f32)
                inner = grad[at, lanes] - sums[0:1, lanes] * per_pixel
                inner = inner - hat * (sums[1:2, lanes] * per_pixel)
                scaled = mask * (gain[:, lanes] * rstd[:, lanes]) * inner
                wide_act[at, lanes] = scaled.astype(bf16)

        loop(pixels // strip, body)

    def act_back(norm, hat):
        gain, bias = r.mid_gain.at[norm : norm + 1, :], r.mid_bias.at[norm : norm + 1, :]

        def terms(at, lanes):
            normed = hat[at, lanes].astype(f32)
            slope = gelu_slope(normed * gain[:, lanes] + bias[:, lanes])
            rows = pl.ds(pl.multiple_of(halo + at.start, strip), strip)
            d = small[rows, lanes] * slope * wide_valid(valid, at, lane_block)
            small[rows, lanes] = d
            return d, d * normed

        return terms

    def inner_norm_back(norm, hat, target, target_row):
        sums, rstd = r.narrow_sums.at[norm], r.rstd_narrow.at[norm : norm + 1, :]
        gain = r.mid_gain.at[norm : norm + 1, :]

        def body(i):
            at = slab(i, strip)
            rows = pl.ds(pl.multiple_of(halo + i * strip, strip), strip)
            inner = small[rows, :] - sums[0:1, :] * per_pixel
            inner = inner - hat[at, :].astype(f32) * (sums[1:2, :] * per_pixel)
            scaled = wide_valid(valid, at, width) * (gain[...] * rstd[...]) * inner
            target[pl.ds(pl.multiple_of(target_row + i * strip, strip), strip), :] = scaled.astype(bf16)

        loop(pixels // strip, body)

    def out_back(block):
        def body(i):
            rows = pl.ds(pl.multiple_of(halo + i * chunk, breadth), chunk)
            small[rows, :] = nt_dot(wide_act[slab(i, chunk), :], r.w_out[...])

        loop(chunks, body)
        return open_sync(act_back(2 * block + 1, r.hat2), width)

    def out_grad(target):
        target.begin()
        target.fill_by_columns(lambda lanes: tn_dot(r.hidden[...], wide_act[:, lanes]))

    def in_grad(target):
        target.begin()

        def compute(t, ref):
            lanes = pl.ds(pl.multiple_of(t * lane_block, lane_block), lane_block)
            ref[...] = tn_dot(inputs[:, lanes], r.da[...]).astype(bf16)

        target.fill(0, wide // lane_block, compute)

    def in_back(i):
        at = slab(i, chunk)
        grad[at, :] = grad[at, :] + nt_dot(r.da[at, :], r.w_in[...])

    def neighbours(before_src, before_dst, after_src, after_dst, which):
        send, recv = r.edge_send.at[which], r.edge_recv.at[which]
        return [
            remote(after_src, after_dst, send.at[0], recv.at[0], place.next(1)),
            remote(before_src, before_dst, send.at[1], recv.at[1], place.next(-1)),
        ]

    place.greet_all()
    box.put(0, r.middle, inputs)
    box.put(1, r.hat3_in[1], hat3)
    box.put(2, r.cotangent, wide_act)
    weight(5, r.w_out, 3)
    box.put(4, r.hat2_in[1], r.hat2)
    box.put(5, r.hidden_in[1], r.hidden)
    box.put(6, r.field_in[1].at[own], r.field.at[own])
    weight(4, r.w_mid, 7)
    weight(3, r.w_in, 8)

    out_b, mid_b, in_b = [scatter(kind, 0) for kind in kinds]
    box.settle(0, 1, 2)
    stages = pre_back(1, wide_act, inputs)
    r.wide_sums[1] = syncs.rest(stages, False)
    last_norm_back(1)
    box.put(1, r.hat3_in[0], hat3)
    box.settle(3, 4)
    stages = out_back(1)
    box.settle(5)
    out_grad(out_b)
    box.put(2, r.image, wide_act)
    weight(2, r.w_out, 3)
    r.narrow_sums[3] = syncs.rest(stages, False)
    box.put(5, r.hat1_in[1], r.hidden)

    pool, side = r.pool, 2 * breadth
    span = pixels + 2 * side
    centre = 2 * span
    inner_norm_back(3, r.hat2, pool, centre + side)
    box.put(4, r.hat2_in[0], r.hat2)
    edges = neighbours(
        pool.at[pl.ds(centre + side, side)],
        pool.at[pl.ds(centre + side + pixels, side)],
        pool.at[pl.ds(centre + pixels, side)],
        pool.at[pl.ds(centre, side)],
        0,
    )
    for copy in edges:
        copy.start()

    def shift_row(row):
        at = pl.ds(pl.multiple_of(centre + row * breadth, breadth), breadth)
        value = pool[at, :].astype(f32)
        for slot, amount in ((0, 2), (1, -2)):
            rows = pl.ds(pl.multiple_of(slot * span + row * breadth, breadth), breadth)
            pool[rows, :] = shifted(value, amount).astype(bf16)

    loop(pixels // breadth, lambda row: shift_row(row + 2))
    out_b.advance()
    for copy in edges:
        copy.wait()
    loop(2, shift_row)
    loop(2, lambda row: shift_row(row + 2 + pixels // breadth))
    slot_of = (0, 2, 1)
    box.settle(6, 7)

    def mid_back_plain(i):
        first_row = i * chunk_rows
        total = None
        for tap_row in range(3):
            for tap_col in range(3):
                start = slot_of[tap_col] * span + (4 - 2 * tap_row) * breadth + i * chunk
                part = pool[pl.ds(pl.multiple_of(start, breadth), chunk), :]
                if tap_row != 1:
                    part = masked_rows(part, masks, first_row, 4 - 2 * tap_row)
                tap = pl.ds((3 * tap_row + tap_col) * width, width)
                term = nt_dot(part, r.w_mid[tap, :])
                total = term if total is None else total + term
        rows = pl.ds(pl.multiple_of(halo + i * chunk, breadth), chunk)
        small[rows, :] = total

    loop(chunks, mid_back_plain)
    weight(1, r.w_mid, 7)
    out_b.advance()
    box.settle(5)
    stages = open_sync(act_back(2, r.hidden), width)
    mid_b.begin()
    shifted_rows = 3 * span

    def mid_grad_plain(t, ref):
        tap_row, tap_col = t // 3, lax.rem(t, 3)
        slot = jnp.where(tap_col == 0, 0, jnp.where(tap_col == 1, 2, 1))

        def copy_row(row):
            start = slot * span + (4 - 2 * tap_row + row) * breadth
            part = pool[pl.ds(pl.multiple_of(start, breadth), breadth), :]
            rows = pl.ds(pl.multiple_of(shifted_rows + row * breadth, breadth), breadth)
            pool[rows, :] = masked_rows(part, masks, row, 4 - 2 * tap_row)

        loop(pixels // breadth, copy_row)
        ref[...] = tn_dot(r.field[own, :], pool[pl.ds(shifted_rows, pixels), :]).astype(bf16)

    mid_b.fill(0, 9, mid_grad_plain)
    out_b.advance()
    r.narrow_sums[2] = syncs.rest(stages, False)
    inner_norm_back(2, r.hidden, r.da, 0)
    box.put(5, r.hidden_in[0], r.hidden)
    box.put(6, r.field_in[0], r.field)
    box.settle(8)
    loop(chunks, in_back)
    mid_b.advance()
    out_b.advance()
    weight(0, r.w_in, 8)

    out_a, mid_a, in_a = [scatter(kind, 1) for kind in kinds]
    box.settle(1, 2)
    stages = pre_back(0, grad, wide_act)
    out_b.drain()
    in_grad(in_b)
    r.wide_sums[0] = syncs.rest(stages, False)
    box.put(0, r.image, inputs)
    mid_b.advance()
    in_b.advance()
    last_norm_back(0)
    box.settle(3, 4)
    stages = out_back(0)
    box.settle(5)
    out_grad(out_a)
    r.narrow_sums[1] = syncs.rest(stages, False)
    inner_norm_back(1, r.hat2, r.da, 0)
    mid_b.advance()
    in_b.advance()
    out_a.advance()
    box.put(5, r.hat1_in[0], r.hidden)
    slots = 9 * chunk

    def samp_load(t):
        slot = pl.ds(pl.multiple_of(slots + lax.rem(t, 2) * pixels, breadth), pixels)
        lanes = pl.ds(pl.multiple_of(t * width, 128), width)
        return pltpu.make_async_copy(r.samp_in.at[:, lanes], pool.at[slot], r.samp_sem.at[lax.rem(t, 2)])

    def mid_grad_deformable(t, ref):
        @pl.when(t < 8)
        def _():
            samp_load(t + 1).start()

        samp_load(t).wait()
        slot = pl.ds(pl.multiple_of(slots + lax.rem(t, 2) * pixels, breadth), pixels)
        ref[...] = tn_dot(pool[slot, :], r.da[...]).astype(bf16)

    box.settle(6, 7)

    def clear(i):
        small[slab(i, breadth), :] = jnp.zeros((breadth, width), f32)

    loop((pixels + 2 * halo) // breadth, clear)
    table = r.table
    table[...] = jnp.zeros_like(table)
    r.draw_sum[...] = jnp.zeros_like(r.draw_sum)

    def mid_back_deformable(i):
        first_row = i * chunk_rows
        part = r.da[slab(i, chunk), :]
        for tap_row in range(3):
            for tap_col in range(3):
                tap = pl.ds((3 * tap_row + tap_col) * width, width)
                dsamp = nt_dot(part, r.w_mid[tap, :]).astype(bf16)
                for k in range(chunk_rows):
                    start = ((tap_row * chunk_rows + k) * 3 + tap_col) * breadth
                    pool[pl.ds(start, breadth), :] = dsamp[breadth * k : breadth * (k + 1)]
        th = r.tanh_raw[slab(i, chunk), :]
        r.off[...] = 0.5 + 0.45 * th
        lane = lax.broadcasted_iota(jnp.int32, (breadth, 128), 1)

        def one_row(k):
            off = r.off[slab(k, breadth), :]
            doff = jnp.zeros((breadth, 128), f32)
            for tap_row in range(3):
                start = (tap_row * chunk_rows + k) * 3 * breadth
                dsamp = pool[pl.ds(pl.multiple_of(start, breadth), 3 * breadth), :]
                start = halo + i * chunk + (k + 2 * tap_row - 2) * breadth
                rows = pl.ds(pl.multiple_of(start, breadth), 2 * breadth)
                dots = nt_dot(dsamp, r.field[rows, :])
                weights = []
                for tap_col in range(3):
                    terms = tap_terms(off, masks, first_row + k, tap_row, tap_col)
                    down, across, down_slope, across_slope = terms
                    weights.append((down * across).astype(bf16))
                    part = dots[breadth * tap_col : breadth * (tap_col + 1)]
                    doy = jnp.sum(part * (across * down_slope), axis=1, keepdims=True)
                    dox = jnp.sum(part * (across_slope * down), axis=1, keepdims=True)
                    tap = 3 * tap_row + tap_col
                    doff = jnp.where(lane == 2 * tap, doy, jnp.where(lane == 2 * tap + 1, dox, doff))
                small[rows, :] = small[rows, :] + tn_dot(jnp.concatenate(weights, axis=0), dsamp)
            th_row = r.tanh_raw[pl.ds(pl.multiple_of(i * chunk + k * breadth, breadth), breadth), :]
            draw = (0.45 * (1.0 - th_row * th_row) * doff).astype(bf16).astype(f32)
            r.off[slab(k, breadth), :] = draw
            r.draw_sum[...] = r.draw_sum[...] + fold8(draw)

        loop(chunk_rows // 2, lambda k: [one_row(2 * k), one_row(2 * k + 1)])
        draw = r.off[...]
        spread = shifted(draw, 2) + pltpu.roll(draw, 32, 1) + pltpu.roll(shifted(draw, -2), 64, 1)
        for tap_row in range(3):
            part = (spread * row_scales(masks, first_row, 2 * tap_row, 128)).astype(bf16)
            start = halo + i * chunk + (2 * tap_row - 2) * breadth
            rows = pl.ds(pl.multiple_of(start, breadth), chunk)
            small[rows, :] = small[rows, :] + nt_dot(part, r.offset_weight[tap_row])
            to = pl.ds(tap_row * width, width)
            table[to, :] = table[to, :] + tn_dot(r.field[rows, :], part)

    mid_back_deformable(0)
    mid_b.drain()
    in_b.advance()
    out_a.advance()
    mid_a.begin()
    samp_load(0).start()
    mid_a.fill(0, 9, mid_grad_deformable)
    in_b.drain()
    out_a.advance()
    mid_back_deformable(chunks - 1)
    mid_a.advance()
    r.rims[0] = small[pl.ds(0, halo), :].astype(bf16)
    r.rims[1] = small[pl.ds(halo + pixels, halo), :].astype(bf16)
    edges = neighbours(r.rims.at[0], r.got_rims.at[0], r.rims.at[1], r.got_rims.at[1], 1)
    for copy in edges:
        copy.start()
    loop(chunks - 2, lambda i: mid_back_deformable(i + 1))
    out_a.drain()

    offset_sum = TableSum(place, r)
    offset_sum.advance()
    for copy in edges:
        copy.wait()
    first_rows, last_rows = pl.ds(halo, halo), pl.ds(pixels, halo)
    small[first_rows, :] = small[first_rows, :] + r.got_rims[1].astype(f32)
    small[last_rows, :] = small[last_rows, :] + r.got_rims[0].astype(f32)
    box.settle(5)
    draw_sum = jnp.sum(r.draw_sum[...], axis=0, keepdims=True)
    stages = open_sync(act_back(0, r.hidden), width, 3, draw_sum)
    mid_a.advance()

    merged = syncs.rest(stages, False)
    r.narrow_sums[0] = merged[0:2]
    r.bias_sum[...] = merged[2:3, 0:128]
    inner_norm_back(0, r.hidden, r.da, 0)
    box.settle(0)
    mid_a.advance()
    offset_sum.advance()
    in_grad(in_a)
    box.settle(8)
    for i in range(chunks):
        in_back(i)
        at = slab(i, chunk)
        box.put(9 + i, grad.at[at], r.image_grad.at[at])
        if i == 0:
            in_a.advance()
    offset_sum.advance()
    mid_a.drain()
    in_a.advance()
    offset_sum.advance()
    in_a.drain()
    offset_sum.advance()
    box.settle()


def backward(kept, image, cotangent, geometry, offset_weight, mid_norms, out_norms, sizes, in_kernel):
    valid, masks, counts = geometry
    pixels, wide = image.shape
    width = mid_norms[0].shape[1]
    taps = 9 * width
    count, high = sizes[0] * sizes[1], sizes[0] // 2
    half = high // 2
    ext_pixels = pixels + 2 * halo_rows * breadth
    each = 16 * (-(-3 * width // (16 * count)))
    fulls = [(width, wide), (taps, width), (wide, width)]
    owned = [(rows // sizes[0], cols // sizes[1]) for rows, cols in fulls]
    if in_kernel:
        grads = [shape(o, f32) for o in owned] * 2
        scatter = dict(
            keep=[pltpu.VMEM((2, rows, b), bf16) for (rows, _), (_, b) in zip(fulls, owned)],
            from_core=[pltpu.VMEM((2, rows, b), bf16) for (rows, _), (_, b) in zip(fulls, owned)],
            from_low=[pltpu.VMEM((2, half) + o, bf16) for o in owned],
            from_upper=[
                pltpu.VMEM((rows // 2, b), bf16) for (rows, _), (_, b) in zip(fulls, owned)
            ],
            from_two=[pltpu.VMEM((2, half) + o, bf16) for o in owned],
            from_high=[pltpu.VMEM((high - 1,) + o, bf16) for o in owned],
            scatter_free=[pltpu.SemaphoreType.REGULAR((4,))] * 3,
        )
        sems = [dma((2 * (rows // lane_block) + 4 * half + high,)) for rows, _ in fulls]
        scatter.update(scatter_send=sems, scatter_recv=sems)
    else:
        grads = [shape(full, bf16) for full in fulls] * 2
        scatter = dict()
    ins = dict(
        image=image,
        cotangent=cotangent,
        middle=kept.middle_out,
        hat1_in=kept.hat1_out,
        hat2_in=kept.hat2_out,
        hat3_in=kept.hat3_out,
        hidden_in=kept.hidden_out,
        field_in=kept.field_out,
        samp_in=kept.samp_out,
        fulls=kept.fulls,
        tanh_raw=kept.tanh_raw,
        rstd_narrow=kept.rstd_narrow,
        rstd_wide=kept.rstd_wide,
        valid=valid,
        masks=masks,
        counts=counts,
        offset_weight=offset_weight,
        mid_gain=mid_norms[0],
        mid_bias=mid_norms[1],
        out_gain=out_norms[0],
        out_bias=out_norms[1],
    )
    specs = dict(
        image=anywhere,
        cotangent=anywhere,
        middle=anywhere,
        hat1_in=anywhere,
        hat2_in=anywhere,
        hat3_in=anywhere,
        hidden_in=anywhere,
        field_in=anywhere,
        samp_in=anywhere,
        fulls=anywhere,
        masks=smem,
        counts=smem,
    )
    outs = dict(
        image_grad=shape((pixels, wide), f32),
        grads=grads,
        narrow_sums=shape((4, 2, width), f32),
        wide_sums=shape((2, 2, wide), f32),
        offset_grad=shape((count * each, 128), bf16),
        bias_sum=shape((1, 128), f32),
    )
    out_specs = dict(narrow_sums=vmem, wide_sums=vmem, offset_grad=vmem, bias_sum=vmem)
    if in_kernel:
        out_specs.update(grads=vmem)
    plan = [(2, wide), (2, width), (2, width), (2, wide), (2, width), (3, width)]
    span = pixels + 4 * breadth
    pool_rows = max(3 * span + pixels, 9 * chunk + 2 * pixels)
    scratch = dict(
        grad=pltpu.VMEM((pixels, wide), f32),
        inputs=pltpu.VMEM((pixels, wide), bf16),
        hat3=pltpu.VMEM((pixels, wide), bf16),
        wide_act=pltpu.VMEM((pixels, wide), bf16),
        w_in=pltpu.VMEM((wide, width), bf16),
        w_mid=pltpu.VMEM((taps, width), bf16),
        w_out=pltpu.VMEM((width, wide), bf16),
        small=pltpu.VMEM((ext_pixels, width), f32),
        hat2=pltpu.VMEM((pixels, width), bf16),
        hidden=pltpu.VMEM((pixels, width), bf16),
        da=pltpu.VMEM((pixels, width), bf16),
        field=pltpu.VMEM((ext_pixels, width), bf16),
        pool=pltpu.VMEM((pool_rows, width), bf16),
        off=pltpu.VMEM((chunk, 128), f32),
        draw_sum=pltpu.VMEM((8, 128), f32),
        table=pltpu.VMEM((count * each, 128), f32),
        table16=pltpu.VMEM((count * each, 128), bf16),
        table_one=pltpu.VMEM((sizes[1] - 1, sizes[0] * each, 128), bf16),
        table_two=pltpu.VMEM((sizes[0] - 1, each, 128), bf16),
        rims=pltpu.VMEM((2, halo_rows * breadth, width), bf16),
        got_rims=pltpu.VMEM((2, halo_rows * breadth, width), bf16),
        staging=pltpu.VMEM((2, lane_block, lane_block), bf16),
        staging_sem=dma((2, 2)),
        table_send=dma((4, max(sizes))),
        table_recv=dma((4, max(sizes))),
        edge_send=dma((2, 2)),
        edge_recv=dma((2, 2)),
        samp_sem=dma((2,)),
        load_sem=dma((9 + pixels // chunk,)),
        syncs=sync_scratch(plan, sizes),
        **scatter,
    )
    return launch(
        partial(backward_pass, sizes, in_kernel), ins, specs, outs, out_specs, scratch, 1, 63
    )


def row_info(row_index, heights, widths, group_rows, total_rows):
    image_count = heights.shape[1]
    inside = (row_index >= 0) & (row_index < total_rows)
    group_of = jnp.clip(row_index // group_rows, 0, 1)
    local_row = row_index - group_of * group_rows
    image_ends = jnp.cumsum(heights, axis=1)
    is_first = (group_of == 0)[:, None]
    ends_by_row = jnp.where(is_first, image_ends[0][None, :], image_ends[1][None, :])
    image_num = jnp.sum((local_row[:, None] >= ends_by_row).astype(jnp.int32), axis=1)
    identity = jnp.where(inside, group_of * image_count + image_num, -1)
    width_table = jnp.where(is_first, widths[0][None, :], widths[1][None, :])
    picked = jnp.arange(image_count, dtype=jnp.int32)[None, :] == image_num[:, None]
    width_row = jnp.sum(jnp.where(picked, width_table, 0), axis=1)
    return (identity, jnp.where(inside, width_row, 0))


def per_device(
    image_in,
    cotangent,
    heights,
    widths,
    weight_in_a,
    weight_offset,
    bias_offset,
    weight_mid_a,
    weight_out_a,
    weight_in_b,
    weight_mid_b,
    weight_out_b,
    mid_gain,
    mid_bias,
    out_gain,
    out_bias,
):
    height, wide = image_in.shape[0], image_in.shape[2]
    sizes = (lax.axis_size("dp"), lax.axis_size("mp"))
    total_rows = height * sizes[0] * sizes[1]
    first_row = lax.axis_index(("dp", "mp")) * height
    row_index = first_row - halo_rows + jnp.arange(height + 2 * halo_rows, dtype=jnp.int32)
    identity, width_row = row_info(
        row_index, heights, widths, total_rows // 2 + height // 2, total_rows
    )
    centre = identity[halo_rows : halo_rows + height]
    masks = jnp.stack(
        [(identity[halo_rows + s : halo_rows + s + height] == centre) for s in range(-2, 4)], axis=1
    ).astype(f32)
    col_index = jnp.arange(breadth, dtype=jnp.int32)
    own_width = width_row[halo_rows : halo_rows + height]
    valid = (col_index[None, :] < own_width[:, None]).astype(f32)
    valid = jnp.broadcast_to(valid.reshape(-1, 1), (height * breadth, 128))
    local_pixels = jnp.sum(own_width).astype(f32)
    pixels = jnp.sum(heights * widths).astype(f32)
    first_pixels = jnp.sum(own_width[: chunk // breadth]).astype(f32)
    counts = jnp.stack([local_pixels, 1.0 / local_pixels, 1.0 / pixels, 1.0 / first_pixels])
    geometry = (valid, masks, counts)
    width = weight_offset.shape[0] // 9
    by_tap = weight_offset.reshape(3, 3, width, offsets_count).transpose(0, 2, 1, 3)
    by_tap = jnp.pad(by_tap, ((0, 0), (0, 0), (0, 1), (0, 32 - offsets_count)))
    offset_weight = by_tap.reshape(3, width, 128)
    offset_bias = jnp.pad(bias_offset, (0, 128 - offsets_count))[None]
    mid_norms = (mid_gain.reshape(4, width), mid_bias.reshape(4, width))
    out_norms = (out_gain, out_bias)
    shards = (weight_in_a, weight_mid_a, weight_out_a, weight_in_b, weight_mid_b, weight_out_b)
    in_kernel = all(s.shape[0] % 16 == 0 for s in shards)
    image = image_in.reshape(height * breadth, wide)
    kept = forward(
        image, shards, geometry, offset_weight, offset_bias, mid_norms, out_norms, sizes
    )
    back = backward(
        kept,
        image,
        cotangent.reshape(height * breadth, wide),
        geometry,
        offset_weight,
        mid_norms,
        out_norms,
        sizes,
        in_kernel,
    )
    grads = back.grads
    if not in_kernel:
        grads = [
            lax.psum_scatter(
                lax.psum_scatter(g.astype(f32), "dp", scatter_dimension=0, tiled=True),
                "mp",
                scatter_dimension=1,
                tiled=True,
            )
            for g in grads
        ]
    offset_grad = back.offset_grad[: 3 * width].astype(f32).reshape(3, width, 4, 32)[:, :, :3, :offsets_count]
    offset_grad = offset_grad.transpose(0, 2, 1, 3).reshape(9 * width, offsets_count)
    narrow = back.narrow_sums.reshape(2, 2, 2, width)
    return (
        kept.image_out.reshape(image_in.shape),
        back.image_grad.reshape(image_in.shape),
        grads[5],
        offset_grad,
        back.bias_sum[0, :offsets_count],
        grads[4],
        grads[3],
        grads[2],
        grads[1],
        grads[0],
        narrow[:, :, 1],
        narrow[:, :, 0],
        back.wide_sums[:, 1],
        back.wide_sums[:, 0],
    )


def solution(mesh):
    rows, split, both = P(("dp", "mp"), None, None), P("dp", "mp"), P()
    in_specs = (rows, rows, both, both, split, both, both, split, split, split, split, split)
    in_specs += (both,) * 4
    out_specs = (rows, rows, split, both, both, split, split, split, split, split) + (both,) * 4
    return jax.shard_map(
        per_device, mesh=mesh, in_specs=in_specs, out_specs=out_specs, check_vma=False
    )
```

```python
from functools import partial
from types import SimpleNamespace

import jax
import jax.numpy as jnp
from jax import lax
from jax.experimental import pallas as pl
from jax.experimental.pallas import tpu as pltpu
from jax.sharding import PartitionSpec as P

norm_eps = 1e-05
halo_rows = 3
breadth = 64
chunk = 256
strip = 32
lane_block = 512
offsets_count = 18
gelu_a = 0.7978845608028654
gelu_b = gelu_a * 0.044715
MESH = pl.DeviceIdType.MESH
f32 = jnp.float32
bf16 = jnp.bfloat16
shape = jax.ShapeDtypeStruct
dma = pltpu.SemaphoreType.DMA
vmem = pl.BlockSpec(memory_space=pltpu.VMEM)
smem = pl.BlockSpec(memory_space=pltpu.SMEM)
anywhere = pl.BlockSpec(memory_space=pl.ANY)


class Place:
    def __init__(self, dp_size, mp_size):
        self.dp_size, self.mp_size = dp_size, mp_size
        self.count = dp_size * mp_size
        self.high = dp_size // 2
        self.dp = lax.axis_index("dp")
        self.mp = lax.axis_index("mp")
        self.me = self.dp * mp_size + self.mp
        self.z = self.dp // 2
        self.y = lax.rem(self.dp, 2)
        self.x = self.mp // 2
        self.core = lax.rem(self.mp, 2)

    def at(self, linear):
        return (linear // self.mp_size, lax.rem(linear, self.mp_size))

    def next(self, step):
        return self.at(lax.rem(self.me + self.count + step, self.count))

    def core_peer(self):
        return (self.dp, self.mp + 1 - 2 * self.core)

    def x_peer(self):
        return (self.dp, self.mp + 2 - 4 * self.x)

    def y_peer(self):
        return (self.dp + 1 - 2 * self.y, self.mp)

    def z_peer(self, step):
        return (lax.rem(self.z + step, self.high) * 2 + self.y, self.mp)

    def greet_all(self):
        barrier = pltpu.get_barrier_semaphore()

        def greet_one(k):
            pl.semaphore_signal(barrier, inc=1, device_id=self.next(k + 1), device_id_type=MESH)

        loop(self.count - 1, greet_one)
        pl.semaphore_wait(barrier, self.count - 1)


def remote(src, dst, send, recv, peer):
    return pltpu.make_async_remote_copy(
        src_ref=src,
        dst_ref=dst,
        send_sem=send,
        recv_sem=recv,
        device_id=peer,
        device_id_type=MESH,
    )


def slab(index, size):
    return pl.ds(pl.multiple_of(index * size, size), size)


def loop(count, body):
    def step(i, carry):
        body(i)
        return carry

    lax.fori_loop(0, count, step, 0)


def launch(kernel, ins, specs, outs, out_specs, scratch, collective_id, vmem_mib):
    flat_in, tree_in = jax.tree.flatten(ins)
    flat_out, tree_out = jax.tree.flatten(outs)
    is_leaf = lambda s: not isinstance(s, (dict, list))
    flat_scratch, tree_scratch = jax.tree.flatten(scratch, is_leaf=is_leaf)
    spec_in = [s for n in sorted(ins) for s in [specs.get(n, vmem)] * len(jax.tree.leaves(ins[n]))]
    spec_out = [
        s for n in sorted(outs) for s in [out_specs.get(n, anywhere)] * len(jax.tree.leaves(outs[n]))
    ]

    def body(*refs):
        a, b = len(flat_in), len(flat_in) + len(flat_out)
        everything = dict(jax.tree.unflatten(tree_in, refs[:a]))
        everything.update(jax.tree.unflatten(tree_out, refs[a:b]))
        everything.update(jax.tree.unflatten(tree_scratch, refs[b:]))
        kernel(SimpleNamespace(**everything))

    results = pl.pallas_call(
        body,
        out_shape=flat_out,
        in_specs=spec_in,
        out_specs=spec_out,
        scratch_shapes=flat_scratch,
        compiler_params=pltpu.CompilerParams(
            collective_id=collective_id,
            has_side_effects=collective_id is not None,
            vmem_limit_bytes=vmem_mib * 1024 * 1024,
        ),
        name=kernel.func.__name__,
    )(*flat_in)
    return SimpleNamespace(**jax.tree.unflatten(tree_out, results))


def gelu_of(v):
    return 0.5 * v * (1.0 + jnp.tanh(v * (gelu_a + gelu_b * v * v)))


def gelu_pair(v):
    square = v * v
    half = 0.5 + 0.5 * jnp.tanh(v * (gelu_a + gelu_b * square))
    return half, half * (1.0 + (1.0 - half) * (v * (2.0 * gelu_a + 6.0 * gelu_b * square)))


def gelu_slope(v):
    return gelu_pair(v)[1]


def mid_row(table, norm):
    return table.at[norm // 2, norm % 2 : norm % 2 + 1, :]


def wide_valid(valid, rows, width):
    mask = valid[rows, :]
    return jnp.concatenate([mask] * (width // 128), axis=1)


def fold8(x):
    return jnp.sum(x.reshape(x.shape[0] // 8, 8, x.shape[1]), axis=0)


def strip_sums(pixel_count, width, terms, out, row_at):
    for block in range(width // lane_block):
        lanes = pl.ds(block * lane_block, lane_block)

        def step(i, carry, lanes=lanes):
            parts = terms(slab(i, strip), lanes)
            return tuple(c + fold8(p) for c, p in zip(carry, parts))

        zeros = tuple(jnp.zeros((8, lane_block), f32) for _ in row_at)
        sums = lax.fori_loop(0, pixel_count // strip, step, zeros)
        for row, total in zip(row_at, sums):
            out[row : row + 1, lanes] = jnp.sum(total, axis=0, keepdims=True)


def merge(parts, moments_mode):
    if not moments_mode:
        return jnp.sum(parts, axis=0)
    width = parts.shape[2] - 128
    pixels = jnp.concatenate([parts[:, 0:1, width:]] * (width // 128), axis=2)
    sums, squares = parts[:, 0:1, 0:width], parts[:, 1:2, 0:width]
    all_pixels, all_sums = jnp.sum(pixels, axis=0), jnp.sum(sums, axis=0)
    apart = sums / pixels - (all_sums / all_pixels)[None]
    all_squares = jnp.sum(squares + pixels * apart * apart, axis=0)
    behind = jnp.sum(parts[:, :, width:], axis=0)
    return jnp.concatenate([jnp.concatenate([all_sums, all_squares], axis=0), behind], axis=1)


def sync_groups(width, sizes):
    count = sizes[0] * sizes[1]
    if count > 64:
        return (16, count // 16)
    return sizes[::-1] if width > 1024 else (count,)


def sync_scratch(plan, sizes):
    out = []
    for rows, width in plan:
        for size in sync_groups(width, sizes):
            out += [pltpu.VMEM((rows, width), f32), pltpu.VMEM((size, rows, width), f32), dma, dma]
    return out


class Syncs:
    def __init__(self, place, buffers):
        self.place, self.buffers = place, buffers
        self.at = 0

    def take(self, width):
        stages = []
        stride = 1
        for size in sync_groups(width, (self.place.dp_size, self.place.mp_size)):
            digit = lax.rem(self.place.me // stride, size)
            stages.append((stride, size, digit, self.buffers[self.at : self.at + 4]))
            self.at += 4
            stride *= size
        return stages

    def start(self, stage, value=None):
        stride, size, digit, (src, slots, send, recv) = stage
        me = self.place.me
        if value is not None:
            src[...] = value

        def push(k):
            peer = me + (lax.rem(digit + k + 1, size) - digit) * stride
            remote(src, slots.at[digit], send, recv, self.place.at(peer)).start()

        loop(size - 1, push)
        pltpu.make_async_copy(src, slots.at[digit], recv).start()

    def finish(self, stage, moments_mode):
        stride, size, digit, (src, slots, send, recv) = stage
        pltpu.make_async_copy(slots, slots, recv).wait()
        rest = slots.at[pl.ds(0, size - 1)]
        pltpu.make_async_copy(rest, rest, send).wait()
        return merge(slots[...], moments_mode)

    def rest(self, stages, moments_mode, meanwhile=None):
        value = self.finish(stages[0], moments_mode)
        for stage in stages[1:]:
            self.start(stage, value)
            if meanwhile is not None:
                meanwhile()
            value = self.finish(stage, moments_mode)
        return value


def shifted(x, shift):
    if shift == 0:
        return x
    pixels = x.shape[0]
    column = lax.broadcasted_iota(jnp.int32, x.shape, 0) % breadth + shift
    inside = (column >= 0) & (column < breadth)
    return jnp.where(inside, pltpu.roll(x, (-shift) % pixels, 0), 0.0)


def row_scales(masks, first_row, which, width):
    row_of = lax.broadcasted_iota(jnp.int32, (chunk, width), 0) // breadth
    scale = jnp.zeros((chunk, width), f32)
    for k in range(chunk // breadth):
        scale = jnp.where(row_of == k, masks[first_row + k, which], scale)
    return scale


def masked_rows(part, masks, first_row, which):
    scaled = []
    for k in range(part.shape[0] // breadth):
        piece = part[breadth * k : breadth * (k + 1)].astype(f32)
        scaled.append((piece * masks[first_row + k, which]).astype(bf16))
    return jnp.concatenate(scaled, axis=0)


def tap_terms(off, masks, row, tap_row, tap_col):
    lane = lax.broadcasted_iota(jnp.int32, (breadth, 2 * breadth), 1)
    sub = lax.broadcasted_iota(jnp.int32, (breadth, 2 * breadth), 0)
    upper = lane >= breadth
    apart = jnp.where(upper, lane - breadth, lane) - sub
    tap, shift = 3 * tap_row + tap_col, 2 * tap_col - 2
    oy, ox = off[:, 2 * tap : 2 * tap + 1], off[:, 2 * tap + 1 : 2 * tap + 2]
    low, high = masks[row, 2 * tap_row], masks[row, 2 * tap_row + 1]
    down = jnp.where(upper, oy * high, (1.0 - oy) * low)
    across = jnp.where(apart == shift, 1.0 - ox, jnp.where(apart == shift + 1, ox, 0.0))
    down_slope = jnp.where(upper, high, -low)
    across_slope = jnp.where(apart == shift, -1.0, jnp.where(apart == shift + 1, 1.0, 0.0))
    return down, across, down_slope, across_slope


def nt_dot(a, b):
    return lax.dot_general(a, b, (((1,), (1,)), ((), ())), preferred_element_type=f32)


def tn_dot(a, b):
    return lax.dot_general(a, b, (((0,), (0,)), ((), ())), preferred_element_type=f32)


def nn_dot(a, b):
    return jnp.dot(a, b, preferred_element_type=f32)


class Outbox:
    def __init__(self, sems):
        self.sems, self.running = sems, {}

    def put(self, at, src, dst):
        copy = pltpu.make_async_copy(src, dst, self.sems.at[at])
        copy.start()
        self.running[at] = copy

    def settle(self, *which):
        for at in which or list(self.running):
            self.running.pop(at).wait()


def load_weight(full, dst, sem):
    if len(full.shape) == 2:
        copy = pltpu.make_async_copy(full, dst, sem)
        copy.start()
        return copy
    block = full.shape[2]
    for z in range(full.shape[0]):
        for y in range(2):
            rows = pl.ds((2 * z + y) * block, block)
            pltpu.make_async_copy(full.at[z, y], dst.at[rows], sem).start()
    return pltpu.make_async_copy(dst, dst, sem)


class Gather:
    def __init__(self, place, r):
        self.place, self.fulls, self.sems = place, r.fulls, (r.gather_local, r.gather_send, r.gather_recv)
        self.shards = r.shards
        self.stage = [0] * 6
        self.running = [[] for _ in range(6)]

    def cols(self, array, x_at, core_at):
        width = self.shards[array].shape[1]
        return pl.ds(pl.multiple_of((2 * x_at + core_at) * width, 128), width)

    def copies(self, array, stage):
        place, full = self.place, self.fulls[array]
        high, z, y, x, core = place.high, place.z, place.y, place.x, place.core
        half = high // 2
        mine = self.cols(array, x, core)
        lower, upper = pl.ds(0, half), pl.ds(half, high - half)
        local, send, recv = self.sems
        if stage == 0:
            target = full.at[z, y, :, mine]
            own = pltpu.make_async_copy(self.shards[array], target, local.at[array])
            return [own] + [
                remote(
                    self.shards[array],
                    target,
                    send.at[array, k - 1],
                    recv.at[array, k - 1],
                    place.z_peer(k),
                )
                for k in range(1, high)
            ]
        if stage == 1:
            pairs = [
                (full.at[lower, y, :, mine], place.x_peer()),
                (full.at[upper, y, :, mine], place.y_peer()),
            ]
        elif stage == 2:
            pairs = [
                (full.at[lower, y, :, self.cols(array, 0, core)], place.y_peer()),
                (full.at[lower, y, :, self.cols(array, 1, core)], place.y_peer()),
                (full.at[upper, :, :, mine], place.x_peer()),
            ]
        else:
            pairs = [
                (full.at[:, :, :, self.cols(array, 0, core)], place.core_peer()),
                (full.at[:, :, :, self.cols(array, 1, core)], place.core_peer()),
            ]
        base = high - 1 + [0, 0, 2, 5][stage]
        return [
            remote(ref, ref, send.at[array, base + i], recv.at[array, base + i], peer)
            for i, (ref, peer) in enumerate(pairs)
        ]

    def advance(self, *arrays):
        for array in arrays if self.shards else ():
            for copy in self.running[array]:
                copy.wait()
            self.running[array] = []
            if self.stage[array] < 4:
                self.running[array] = self.copies(array, self.stage[array])
                for copy in self.running[array]:
                    copy.start()
            self.stage[array] += 1


class Scatter:
    def __init__(self, place, r, kind, use, result):
        self.place, self.use, self.result = place, use, result
        self.keep, self.from_core = r.keep[kind], r.from_core[kind]
        self.low, self.upper = r.from_low[kind], r.from_upper[kind]
        self.two, self.from_high = r.from_two[kind], r.from_high[kind]
        self.send, self.recv, self.free = r.scatter_send[kind], r.scatter_recv[kind], r.scatter_free[kind]
        self.staging, self.staging_sem = r.staging, r.staging_sem
        self.result_sem = r.result_sem.at[kind]
        self.rows, self.width = self.keep.shape[1], self.keep.shape[2]
        self.block = self.rows // place.dp_size
        self.tiles = self.rows // lane_block
        self.stage = 0
        self.running = []

    def cols(self, x_at, core_at):
        return pl.ds(pl.multiple_of((2 * x_at + core_at) * self.width, 128), self.width)

    def at(self, high, y):
        return pl.ds(pl.multiple_of((2 * high + y) * self.block, self.block), self.block)

    def to_core(self, t, i, src):
        rows = pl.ds(pl.multiple_of(t * lane_block, lane_block), lane_block)
        return remote(
            src,
            self.from_core.at[i, rows],
            self.send.at[2 * t + i],
            self.recv.at[2 * t + i],
            self.place.core_peer(),
        )

    def tile_copies(self, t):
        slot = lax.rem(t, 2)
        rows = pl.ds(pl.multiple_of(t * lane_block, lane_block), lane_block)
        core = self.place.core
        away = [self.to_core(t, i, self.staging.at[slot, :, self.cols(i, 1 - core)]) for i in (0, 1)]
        home = [
            pltpu.make_async_copy(
                self.staging.at[slot, :, self.cols(i, core)],
                self.keep.at[i, rows],
                self.staging_sem.at[slot, i],
            )
            for i in (0, 1)
        ]
        return away, home

    def settle_tile(self, t):
        away, home = self.tile_copies(t)
        for copy in away:
            copy.wait_send()
        for copy in home:
            copy.wait()

    def result_copy(self):
        place = self.place
        return pltpu.make_async_copy(
            self.keep.at[place.x, self.at(place.z, place.y)], self.result, self.result_sem
        )

    def begin(self):
        if self.use == 1:
            self.result_copy().wait()
            pl.semaphore_wait(self.free.at[0], 1)

    def fill(self, first, last, compute):
        def body(i):
            t = first + i

            @pl.when(i >= 2)
            def _():
                self.settle_tile(t - 2)

            compute(t, self.staging.at[lax.rem(t, 2)])
            away, home = self.tile_copies(t)
            for copy in away + home:
                copy.start()

        loop(last - first, body)
        for t in range(max(first, last - 2), last):
            self.settle_tile(t)

    def fill_by_columns(self, compute):
        core = self.place.core

        def away(i):
            self.staging[i] = compute(self.cols(i, 1 - core)).astype(bf16)
            self.to_core(0, i, self.staging.at[i]).start()

        def home(i):
            self.keep[i] = compute(self.cols(i, core)).astype(bf16)

        loop(2, away)
        loop(2, home)
        for i in (0, 1):
            self.to_core(0, i, self.staging.at[i]).wait_send()

    def copies(self, stage):
        place = self.place
        x, y, z, half = place.x, place.y, place.z, place.high // 2
        items = []
        if stage == 1:
            for i in (0, 1):
                for b in range(half):
                    items.append((self.keep.at[i, self.at(b, 1 - y)], self.low.at[i, b], place.y_peer()))
            upper = pl.ds(self.rows // 2, self.rows // 2)
            items.append((self.keep.at[1 - x, upper], self.upper, place.x_peer()))
        elif stage == 2:
            for b in range(half):
                items.append((self.keep.at[1 - x, self.at(b, y)], self.two.at[0, b], place.x_peer()))
                items.append(
                    (self.keep.at[x, self.at(half + b, 1 - y)], self.two.at[1, b], place.y_peer())
                )
        else:
            for k in range(1, place.high):
                there = self.at(lax.rem(z + k, place.high), y)
                items.append((self.keep.at[x, there], self.from_high.at[k - 1], place.z_peer(k)))
        base = 2 * self.tiles + [0, 0, 2 * half + 1, 4 * half + 1][stage]
        return [
            remote(src, dst, self.send.at[base + i], self.recv.at[base + i], peer)
            for i, (src, dst, peer) in enumerate(items)
        ]

    def add(self, target, extra):
        target[...] = target[...] + extra[...]

    def finish(self, stage):
        place = self.place
        x, y, z, half = place.x, place.y, place.z, place.high // 2
        if stage == 0:
            piece = 64
            for i in (0, 1):

                def body(k, i=i):
                    rows = slab(k, piece)
                    self.add(self.keep.at[i, rows], self.from_core.at[i, rows])

                loop(self.rows // piece, body)
            peers = [place.core_peer()]
        elif stage == 1:
            for b in range(half):
                for i in (0, 1):
                    self.add(self.keep.at[i, self.at(b, y)], self.low.at[i, b])
            piece = 64

            def body(k):
                rows = pl.ds(pl.multiple_of(self.rows // 2 + k * piece, piece), piece)
                self.add(self.keep.at[x, rows], self.upper.at[slab(k, piece)])

            loop(self.rows // 2 // piece, body)
            peers = [place.x_peer(), place.y_peer()]
        elif stage == 2:
            for b in range(half):
                self.add(self.keep.at[x, self.at(b, y)], self.two.at[0, b])
                self.add(self.keep.at[x, self.at(half + b, y)], self.two.at[1, b])
            peers = [place.x_peer(), place.y_peer()]
        else:
            total = self.keep[x, self.at(z, y)].astype(f32)
            for k in range(1, place.high):
                total = total + self.from_high[k - 1].astype(f32)
            self.keep[x, self.at(z, y)] = total.astype(bf16)
            self.result_copy().start()
            peers = [place.z_peer(k) for k in range(1, place.high)]
        if self.use == 0:
            for peer in peers:
                pl.semaphore_signal(self.free.at[stage], inc=1, device_id=peer, device_id_type=MESH)

    def advance(self):
        if self.stage > 3:
            return
        if self.stage == 0:
            for t in range(self.tiles):
                for i in (0, 1):
                    self.to_core(t, i, self.staging.at[0, :, self.cols(i, 0)] if self.tiles > 1 else self.staging.at[i]).wait_recv()
        for copy in self.running:
            copy.wait()
        self.finish(self.stage)
        self.stage += 1
        if self.stage <= 3:
            if self.use == 1:
                waits = [0, 2, 2, self.place.high - 1][self.stage]
                pl.semaphore_wait(self.free.at[self.stage], waits)
            self.running = self.copies(self.stage)
            for copy in self.running:
                copy.start()

    def drain(self):
        while self.stage <= 3:
            self.advance()

    def end(self):
        self.result_copy().wait()


class Whole:
    def __init__(self, r, result):
        self.staging, self.staging_sem, self.result = r.staging, r.staging_sem, result

    def begin(self):
        pass

    def fill(self, first, last, compute):
        def body(i):
            t = first + i
            compute(t, self.staging.at[0])
            rows = pl.ds(pl.multiple_of(t * lane_block, lane_block), lane_block)
            pltpu.sync_copy(self.staging.at[0], self.result.at[rows])

        loop(last - first, body)

    def fill_by_columns(self, compute):
        def body(i):
            lanes = pl.ds(pl.multiple_of(i * lane_block, lane_block), lane_block)
            self.staging[0] = compute(lanes).astype(bf16)
            pltpu.sync_copy(self.staging.at[0], self.result.at[:, lanes])

        loop(self.result.shape[1] // lane_block, body)

    def advance(self):
        pass

    drain = advance
    end = advance


class TableSum:
    def __init__(self, place, r):
        self.place, self.r = place, r
        self.each = r.table16.shape[0] // place.count
        self.stage, self.running = 0, []

    def part(self, mp, dp=None):
        quarter = self.each * self.place.dp_size
        if dp is None:
            return pl.ds(pl.multiple_of(mp * quarter, self.each), quarter)
        return pl.ds(pl.multiple_of(mp * quarter + dp * self.each, self.each), self.each)

    def copies(self, stage):
        place, r = self.place, self.r
        dp, mp, table, result = place.dp, place.mp, r.table16, r.offset_grad
        items = []
        over_mp = [lax.rem(mp + k, place.mp_size) for k in range(1, place.mp_size)]
        over_dp = [lax.rem(dp + k, place.dp_size) for k in range(1, place.dp_size)]
        if stage == 0:
            for k, to in enumerate(over_mp):
                items.append((table.at[self.part(to)], r.table_one.at[k], (dp, to)))
        elif stage == 1:
            for k, to in enumerate(over_dp):
                items.append((table.at[self.part(mp, to)], r.table_two.at[k], (to, mp)))
        elif stage == 2:
            mine = self.part(mp, dp)
            items = [(result.at[mine], result.at[mine], (to, mp)) for to in over_dp]
        else:
            mine = self.part(mp)
            items = [(result.at[mine], result.at[mine], (dp, to)) for to in over_mp]
        send, recv = r.table_send.at[stage], r.table_recv.at[stage]
        return [remote(a, b, send.at[i], recv.at[i], to) for i, (a, b, to) in enumerate(items)]

    def advance(self):
        place, r = self.place, self.r
        for copy in self.running:
            copy.wait()
        mine = self.part(place.mp), self.part(place.mp, place.dp)
        if self.stage == 0:
            r.table16[...] = r.table[...].astype(bf16)
        elif self.stage == 1:
            total = r.table16[mine[0], :].astype(f32)
            for k in range(place.mp_size - 1):
                total = total + r.table_one[k].astype(f32)
            r.table16[mine[0], :] = total.astype(bf16)
        elif self.stage == 2:
            total = r.table16[mine[1], :].astype(f32)
            for k in range(place.dp_size - 1):
                total = total + r.table_two[k].astype(f32)
            r.offset_grad[mine[1], :] = total.astype(bf16)
        self.running = self.copies(self.stage) if self.stage < 4 else []
        for copy in self.running:
            copy.start()
        self.stage += 1


def geometry(place, r):
    heights, widths, identity, row_width = r.heights, r.widths, r.identity, r.row_width
    images = heights.shape[1]
    rows = r.valid.shape[0] // breadth
    all_rows = rows * place.count
    group_rows = all_rows // 2 + rows // 2
    one, none = jnp.int32(1), jnp.int32(0)

    def row_facts(k):
        row = place.me * rows - halo_rows + k
        group = jnp.where(row >= group_rows, one, none)
        local = row - group * group_rows

        def image(j, carry):
            begin, number, found = carry
            end = begin + heights[group, j]
            number = number + jnp.where(local >= end, one, none)
            here = (local >= begin) & (local < end)
            return end, number, jnp.where(here, widths[group, j], found)

        _, number, found = lax.fori_loop(0, images, image, (none, none, none))
        inside = (row >= 0) & (row < all_rows)
        identity[k] = jnp.where(inside, group * images + number, -one)
        row_width[k] = jnp.where(inside, found, none)

    loop(rows + 2 * halo_rows, row_facts)

    def row_masks(k):
        centre = identity[k + halo_rows]
        for s in range(6):
            r.masks[k, s] = jnp.where(identity[k + s + 1] == centre, 1.0, 0.0).astype(f32)
        column = lax.broadcasted_iota(jnp.int32, (breadth, 128), 0)
        r.valid[slab(k, breadth), :] = jnp.where(column < row_width[k + halo_rows], 1.0, 0.0)

    loop(rows, row_masks)

    def pixels_of(first, last):
        def add(k, total):
            return total + row_width[k + halo_rows]

        return lax.fori_loop(first, last, add, none).astype(f32)

    def add_image(j, total):
        return total + heights[0, j] * widths[0, j] + heights[1, j] * widths[1, j]

    local = pixels_of(0, rows)
    r.counts[0] = local
    r.counts[1] = 1.0 / local
    r.counts[2] = 1.0 / lax.fori_loop(0, images, add_image, none).astype(f32)
    r.counts[3] = 1.0 / pixels_of(0, chunk // breadth)

    count = r.offset_bias.shape[0]
    width = r.offset_weight.shape[1]
    lane = lax.broadcasted_iota(jnp.int32, (1, 128), 1)
    bias = jnp.zeros((1, 128), f32)
    for j in range(count):
        bias = jnp.where(lane == j, r.offset_bias[j], bias)
    r.bias_row[...] = bias
    down = lax.broadcasted_iota(jnp.int32, (count, 128), 0)
    across = lax.broadcasted_iota(jnp.int32, (count, 128), 1)
    for tap_row in range(3):
        total = jnp.zeros((width, 128), f32)
        for tap_col in range(3):
            place_at = jnp.where(across == down + 32 * tap_col, 1.0, 0.0).astype(bf16)
            columns = pl.ds((3 * tap_row + tap_col) * width, width)
            total = total + tn_dot(r.weight_offset[:, columns], place_at)
        r.offset_weight[tap_row] = total.astype(bf16)


def forward_part(place, syncs, box, r):
    gather = Gather(place, r)
    valid, masks, counts = r.valid, r.masks, r.counts
    third, field, hidden, pool = r.grad, r.field, r.hidden, r.pool
    pixels, wide = third.shape
    width = hidden.shape[1]
    halo = halo_rows * breadth
    chunks = pixels // chunk
    first = r.small.at[pl.ds(halo, pixels)]
    samp_rows = 9 * chunk

    def load(array, dst, sem):
        return load_weight(r.fulls[array], dst, r.load_sem.at[sem])

    def gather_sums(i, got, first_chunk):
        block_width = got.shape[1]
        sums, centre = r.sums.at[:, :, 0:block_width], r.centre.at[:, 0:block_width]
        mask = wide_valid(valid, slab(i, chunk), block_width)
        if first_chunk:
            centre[...] = jnp.sum(fold8(got * mask), axis=0, keepdims=True) * counts[3]
            sums[...] = jnp.zeros((2, 8, block_width), f32)
        apart = (got - centre[...]) * mask
        sums[0] = sums[0] + fold8(apart)
        sums[1] = sums[1] + fold8(apart * apart)

    def over_chunks(target, compute):
        def body(i, first_chunk=False):
            got = compute(i)
            target[slab(i, chunk), :] = got
            gather_sums(i, got, first_chunk)

        body(0, True)
        loop(chunks - 1, lambda i: body(i + 1))

    def moments(block_width, rstd, mean, meanwhile=None):
        stages = syncs.take(block_width + 128)
        src = stages[0][3][0]
        first_sum = jnp.sum(r.sums[0, :, 0:block_width], axis=0, keepdims=True)
        second_sum = jnp.sum(r.sums[1, :, 0:block_width], axis=0, keepdims=True)
        src[0:1, 0:block_width] = first_sum + r.centre[:, 0:block_width] * counts[0]
        src[1:2, 0:block_width] = second_sum - first_sum * first_sum * counts[1]
        src[:, block_width:] = jnp.full((2, 128), counts[0], f32)
        syncs.start(stages[0])
        merged = syncs.rest(stages, True, meanwhile)
        mean[...] = merged[0:1, 0:block_width] * counts[2]
        spread = jnp.maximum(merged[1:2, 0:block_width], 0.0) * counts[2]
        rstd[...] = lax.rsqrt(spread + norm_eps)

    def activate(norm, hat, target, target_row):
        mean, rstd = r.mean_narrow, r.rstd_narrow.at[norm : norm + 1, :]
        gain, bias = mid_row(r.mid_gain, norm), mid_row(r.mid_bias, norm)

        def body(i):
            at = slab(i, strip)
            normed = (first[at, :] - mean[...]) * rstd[...]
            hat[at, :] = normed.astype(bf16)
            act = gelu_of(normed * gain[...] + bias[...]) * wide_valid(valid, at, width)
            rows = pl.ds(pl.multiple_of(target_row + i * strip, strip), strip)
            target[rows, :] = act.astype(bf16)

        loop(pixels // strip, body)

    def narrow_moments(norm):
        moments(width, r.rstd_narrow.at[norm : norm + 1, :], r.mean_narrow)

    def project(lhs, weight, target):
        over_chunks(target, lambda i: nn_dot(lhs[slab(i, chunk), :], weight[...]))

    def halo_copies(block):
        send, recv = r.halo_send.at[block], r.halo_recv.at[block]
        last_rows, below = field.at[pl.ds(pixels, halo)], field.at[pl.ds(pixels + halo, halo)]
        first_rows, above = field.at[pl.ds(halo, halo)], field.at[pl.ds(0, halo)]
        return [
            remote(last_rows, above, send.at[0], recv.at[0], place.next(1)),
            remote(first_rows, below, send.at[1], recv.at[1], place.next(-1)),
        ]

    def mid_deformable(i, slot):
        base = halo + i * chunk
        first_row = i * (chunk // breadth)
        total = jnp.zeros((chunk, 128), f32)
        for tap_row in range(3):
            start = pl.multiple_of(base + (2 * tap_row - 2) * breadth, breadth)
            part = nn_dot(field[pl.ds(start, chunk), :], r.offset_weight[tap_row])
            total = total + part * row_scales(masks, first_row, 2 * tap_row, 128)
        left = shifted(total, -2)
        middle = pltpu.roll(total, 128 - 32, 1)
        right = pltpu.roll(shifted(total, 2), 128 - 64, 1)
        lane = lax.broadcasted_iota(jnp.int32, total.shape, 1)
        raw = jnp.where(lane < 32, left + middle + right, 0.0) + r.bias_row[...]
        tanh_raw = jnp.tanh(raw)
        r.tanh_raw[slab(i, chunk), :] = tanh_raw
        r.off[...] = 0.5 + 0.45 * tanh_raw

        def one_row(k):
            off = r.off[slab(k, breadth), :]
            for tap_row in range(3):
                weights = []
                for tap_col in range(3):
                    down, across, _, _ = tap_terms(off, masks, first_row + k, tap_row, tap_col)
                    weights.append((down * across).astype(bf16))
                start = pl.multiple_of(base + (k + 2 * tap_row - 2) * breadth, breadth)
                got = nn_dot(jnp.concatenate(weights, axis=0), field[pl.ds(start, 2 * breadth), :])
                for tap_col in range(3):
                    to = slot * samp_rows + (3 * tap_row + tap_col) * chunk + k * breadth
                    piece = got[breadth * tap_col : breadth * (tap_col + 1)]
                    pool[pl.ds(pl.multiple_of(to, breadth), breadth), :] = piece.astype(bf16)

        loop(chunk // breadth // 2, lambda k: [one_row(2 * k), one_row(2 * k + 1)])
        taps = [pool[pl.ds(slot * samp_rows + t * chunk, chunk), :] for t in range(9)]
        got = nn_dot(jnp.concatenate(taps, axis=1), r.w_mid[...])
        first[slab(i, chunk), :] = got
        gather_sums(i, got, i == 0)

    def mid_plain(i):
        lhs = []
        for tap_row in range(3):
            start = pl.multiple_of(halo + i * chunk + (2 * tap_row - 2) * breadth, breadth)
            part = field[pl.ds(start, chunk), :]
            if tap_row != 1:
                part = masked_rows(part, masks, i * (chunk // breadth), 2 * tap_row)
            lhs.append(part)
        total = None
        for tap_col in range(3):
            partial_sum = None
            for tap_row in range(3):
                weight = r.w_mid[pl.ds((3 * tap_row + tap_col) * width, width), :]
                part = nn_dot(lhs[tap_row], weight)
                partial_sum = part if partial_sum is None else partial_sum + part
            partial_sum = shifted(partial_sum, 2 * tap_col - 2)
            total = partial_sum if total is None else total + partial_sum
        return total

    def finish_block(block, inputs, result):
        gain, bias = r.out_gain.at[block : block + 1, :], r.out_bias.at[block : block + 1, :]
        mean, rstd = r.mean_wide, r.rstd_wide.at[block : block + 1, :]

        def body(i):
            at = slab(i, strip)
            mask = wide_valid(valid, at, lane_block)
            for j in range(wide // lane_block):
                lanes = pl.ds(j * lane_block, lane_block)
                normed = (third[at, lanes] - mean[:, lanes]) * rstd[:, lanes]
                r.hat3[at, lanes] = normed.astype(bf16)
                pre = inputs[at, lanes].astype(f32) + (normed * gain[:, lanes] + bias[:, lanes])
                result[at, lanes] = (mask * gelu_of(pre)).astype(bf16)

        loop(pixels // strip, body)

    def wide_moments(block, meanwhile=None):
        moments(wide, r.rstd_wide.at[block : block + 1, :], r.mean_wide, meanwhile)

    def samp_copy(i):
        rows = pl.ds(i % 2 * samp_rows, samp_rows)
        return pltpu.make_async_copy(
            pool.at[rows], r.samp_out.at[slab(i, samp_rows)], r.samp_sem.at[i % 2]
        )

    place.greet_all()
    gather.advance(0)
    gather.advance(1)
    box.put(0, r.image, r.wide_act)
    geometry(place, r)
    gather.advance(0)
    gather.advance(0)
    gather.advance(2)
    gather.advance(0)
    gather.advance(1)
    gather.advance(0)
    loaded = load(0, r.w_in, 0)
    gather.advance(1)
    loaded.wait()
    box.settle(0)
    project(r.wide_act, r.w_in, first)
    narrow_moments(0)
    activate(0, r.da, field, halo)
    box.put(1, r.da, r.hat1_out)
    edges = halo_copies(0)
    for copy in edges:
        copy.start()
    gather.advance(1, 2)
    for copy in edges:
        copy.wait()
    box.put(2, field, r.field_out)
    gather.advance(1, 3)
    load(1, r.w_mid, 1).wait()
    for i in range(chunks):
        if i >= 2:
            samp_copy(i - 2).wait()
        mid_deformable(i, i % 2)
        samp_copy(i).start()
        gather.advance(*{0: (2,), 1: (3, 4), 2: (2,), 3: (2, 3)}.get(i, ()))
    loaded = load(2, r.w_out, 2)
    narrow_moments(1)
    gather.advance(3, 4)
    activate(1, r.hat2, hidden, 0)
    box.put(3, r.hat2, r.hat2_out)
    box.put(4, hidden, r.hidden_out)
    loaded.wait()
    project(hidden, r.w_out, third)
    gather.advance(3)
    loaded_in = load(3, r.w_in, 0)
    gather.advance(5)
    wide_moments(0, lambda: gather.advance(4))
    finish_block(0, r.wide_act, r.inputs)
    box.put(0, r.cotangent, r.wide_act)
    box.put(5, r.hat3, r.hat3_out)
    gather.advance(5)
    loaded_in.wait()
    box.settle(1, 2)
    project(r.inputs, r.w_in, first)
    gather.advance(4)
    narrow_moments(2)
    gather.advance(4, 5)
    loaded = load(4, r.w_mid, 1)
    activate(2, r.da, field, halo)
    edges = halo_copies(1)
    for copy in edges:
        copy.start()
    for copy in edges:
        copy.wait()
    loaded.wait()
    over_chunks(first, mid_plain)
    gather.advance(5)
    narrow_moments(3)
    gather.advance(5)
    loaded_out = load(5, r.w_out, 2)
    box.settle(3, 4)
    activate(3, r.hat2, hidden, 0)
    loaded_out.wait()
    project(hidden, r.w_out, third)
    wide_moments(1)
    for i in range(max(0, chunks - 2), chunks):
        samp_copy(i).wait()
    box.settle(0, 5)


def backward_part(place, syncs, box, in_kernel, r):
    valid, masks, counts = r.valid, r.masks, r.counts
    grad, small, inputs, hat3, wide_act = r.grad, r.small, r.inputs, r.hat3, r.wide_act
    pixels, wide, width = grad.shape[0], grad.shape[1], small.shape[1]
    halo = halo_rows * breadth
    chunks, chunk_rows = pixels // chunk, chunk // breadth
    per_pixel = counts[2]
    own = pl.ds(halo, pixels)
    kinds = [0, 1, 2]

    def scatter(kind, use):
        result = r.grads[3 * use + kind]
        if in_kernel:
            return Scatter(place, r, kind, use, result)
        return Whole(r, result)

    def weight(array, dst, sem):
        box.running[sem] = load_weight(r.fulls[array], dst, r.box_sem.at[sem])

    def open_sync(terms, block_width, last_row=None):
        stages = syncs.take(block_width)
        src = stages[0][3][0]
        strip_sums(pixels, block_width, terms, src, [0, 1])
        if last_row is not None:
            src[2:3, :] = jnp.zeros((1, block_width), f32)
            src[2:3, 0:128] = last_row
        syncs.start(stages[0])
        return stages

    def pre_back(block, upstream, image):
        gain, bias = r.out_gain.at[block : block + 1, :], r.out_bias.at[block : block + 1, :]

        def terms(at, lanes):
            hat = hat3[at, lanes].astype(f32)
            pre = image[at, lanes].astype(f32) + (hat * gain[:, lanes] + bias[:, lanes])
            slope = gelu_slope(pre) * wide_valid(valid, at, lane_block)
            d = upstream[at, lanes].astype(f32) * slope
            grad[at, lanes] = d
            return d, d * hat

        return open_sync(terms, wide)

    def finish_and_back():
        gain, bias = r.out_gain.at[1:2, :], r.out_bias.at[1:2, :]
        mean, rstd = r.mean_wide, r.rstd_wide.at[1:2, :]

        def terms(at, lanes):
            normed = (grad[at, lanes] - mean[:, lanes]) * rstd[:, lanes]
            hat3[at, lanes] = normed.astype(bf16)
            pre = inputs[at, lanes].astype(f32) + (normed * gain[:, lanes] + bias[:, lanes])
            half, slope = gelu_pair(pre)
            mask = wide_valid(valid, at, lane_block)
            d = wide_act[at, lanes].astype(f32) * (slope * mask)
            wide_act[at, lanes] = (pre * (half * mask)).astype(bf16)
            grad[at, lanes] = d
            return d, d * normed

        return open_sync(terms, wide)

    def last_norm_back(block):
        sums, rstd = r.wide_sums.at[block], r.rstd_wide.at[block : block + 1, :]
        gain = r.out_gain.at[block : block + 1, :]

        def body(i):
            at = slab(i, strip)
            mask = wide_valid(valid, at, lane_block)
            for j in range(wide // lane_block):
                lanes = pl.ds(j * lane_block, lane_block)
                hat = hat3[at, lanes].astype(f32)
                inner = grad[at, lanes] - sums[0:1, lanes] * per_pixel
                inner = inner - hat * (sums[1:2, lanes] * per_pixel)
                scaled = mask * (gain[:, lanes] * rstd[:, lanes]) * inner
                wide_act[at, lanes] = scaled.astype(bf16)

        loop(pixels // strip, body)

    def act_back(norm, hat):
        gain, bias = mid_row(r.mid_gain, norm), mid_row(r.mid_bias, norm)

        def terms(at, lanes):
            normed = hat[at, lanes].astype(f32)
            slope = gelu_slope(normed * gain[:, lanes] + bias[:, lanes])
            rows = pl.ds(pl.multiple_of(halo + at.start, strip), strip)
            d = small[rows, lanes] * slope * wide_valid(valid, at, lane_block)
            small[rows, lanes] = d
            return d, d * normed

        return terms

    def inner_norm_back(norm, hat, target, target_row):
        sums, rstd = r.narrow_sums.at[norm], r.rstd_narrow.at[norm : norm + 1, :]
        gain = mid_row(r.mid_gain, norm)

        def body(i):
            at = slab(i, strip)
            rows = pl.ds(pl.multiple_of(halo + i * strip, strip), strip)
            inner = small[rows, :] - sums[0:1, :] * per_pixel
            inner = inner - hat[at, :].astype(f32) * (sums[1:2, :] * per_pixel)
            scaled = wide_valid(valid, at, width) * (gain[...] * rstd[...]) * inner
            target[pl.ds(pl.multiple_of(target_row + i * strip, strip), strip), :] = scaled.astype(bf16)

        loop(pixels // strip, body)

    def out_back(block):
        def body(i):
            rows = pl.ds(pl.multiple_of(halo + i * chunk, breadth), chunk)
            small[rows, :] = nt_dot(wide_act[slab(i, chunk), :], r.w_out[...])

        loop(chunks, body)
        return open_sync(act_back(2 * block + 1, r.hat2), width)

    def out_grad(target):
        target.begin()
        target.fill_by_columns(lambda lanes: tn_dot(r.hidden[...], wide_act[:, lanes]))

    def in_grad(target):
        target.begin()

        def compute(t, ref):
            lanes = pl.ds(pl.multiple_of(t * lane_block, lane_block), lane_block)
            ref[...] = tn_dot(inputs[:, lanes], r.da[...]).astype(bf16)

        target.fill(0, wide // lane_block, compute)

    def in_back(i):
        at = slab(i, chunk)
        grad[at, :] = grad[at, :] + nt_dot(r.da[at, :], r.w_in[...])

    def neighbours(before_src, before_dst, after_src, after_dst, which):
        send, recv = r.edge_send.at[which], r.edge_recv.at[which]
        return [
            remote(after_src, after_dst, send.at[0], recv.at[0], place.next(1)),
            remote(before_src, before_dst, send.at[1], recv.at[1], place.next(-1)),
        ]

    out_b, mid_b, in_b = [scatter(kind, 0) for kind in kinds]
    stages = finish_and_back()
    box.put(6, wide_act, r.image_out)
    r.wide_sums[1] = syncs.rest(stages, False)
    box.settle(6)
    last_norm_back(1)
    box.put(1, r.hat3_out, hat3)
    stages = out_back(1)
    weight(2, r.w_out, 3)
    out_grad(out_b)
    box.put(2, r.image, wide_act)
    box.put(5, r.hidden_out, r.hidden)
    r.narrow_sums[3] = syncs.rest(stages, False)

    pool, side = r.pool, 2 * breadth
    span = pixels + 2 * side
    centre = 2 * span
    inner_norm_back(3, r.hat2, pool, centre + side)
    box.put(4, r.hat2_out, r.hat2)
    edges = neighbours(
        pool.at[pl.ds(centre + side, side)],
        pool.at[pl.ds(centre + side + pixels, side)],
        pool.at[pl.ds(centre + pixels, side)],
        pool.at[pl.ds(centre, side)],
        0,
    )
    for copy in edges:
        copy.start()

    def shift_row(row):
        at = pl.ds(pl.multiple_of(centre + row * breadth, breadth), breadth)
        value = pool[at, :].astype(f32)
        for slot, amount in ((0, 2), (1, -2)):
            rows = pl.ds(pl.multiple_of(slot * span + row * breadth, breadth), breadth)
            pool[rows, :] = shifted(value, amount).astype(bf16)

    loop(pixels // breadth, lambda row: shift_row(row + 2))
    out_b.advance()
    for copy in edges:
        copy.wait()
    loop(2, shift_row)
    loop(2, lambda row: shift_row(row + 2 + pixels // breadth))
    slot_of = (0, 2, 1)

    def mid_back_plain(i):
        first_row = i * chunk_rows
        total = None
        for tap_row in range(3):
            for tap_col in range(3):
                start = slot_of[tap_col] * span + (4 - 2 * tap_row) * breadth + i * chunk
                part = pool[pl.ds(pl.multiple_of(start, breadth), chunk), :]
                if tap_row != 1:
                    part = masked_rows(part, masks, first_row, 4 - 2 * tap_row)
                tap = pl.ds((3 * tap_row + tap_col) * width, width)
                term = nt_dot(part, r.w_mid[tap, :])
                total = term if total is None else total + term
        rows = pl.ds(pl.multiple_of(halo + i * chunk, breadth), chunk)
        small[rows, :] = total

    loop(chunks, mid_back_plain)
    weight(1, r.w_mid, 7)
    out_b.advance()
    stages = open_sync(act_back(2, r.da), width)
    mid_b.begin()
    shifted_rows = 3 * span

    def mid_grad_plain(t, ref):
        tap_row, tap_col = t // 3, lax.rem(t, 3)
        slot = jnp.where(tap_col == 0, 0, jnp.where(tap_col == 1, 2, 1))

        def copy_row(row):
            start = slot * span + (4 - 2 * tap_row + row) * breadth
            part = pool[pl.ds(pl.multiple_of(start, breadth), breadth), :]
            rows = pl.ds(pl.multiple_of(shifted_rows + row * breadth, breadth), breadth)
            pool[rows, :] = masked_rows(part, masks, row, 4 - 2 * tap_row)

        loop(pixels // breadth, copy_row)
        ref[...] = tn_dot(r.field[own, :], pool[pl.ds(shifted_rows, pixels), :]).astype(bf16)

    mid_b.fill(0, 9, mid_grad_plain)
    out_b.advance()
    r.narrow_sums[2] = syncs.rest(stages, False)
    inner_norm_back(2, r.da, r.da, 0)
    box.put(6, r.field_out, r.field)
    loop(chunks, in_back)
    mid_b.advance()
    out_b.advance()
    weight(0, r.w_in, 8)

    out_a, mid_a, in_a = [scatter(kind, 1) for kind in kinds]
    box.settle(1, 2)
    stages = pre_back(0, grad, wide_act)
    out_b.drain()
    in_grad(in_b)
    r.wide_sums[0] = syncs.rest(stages, False)
    box.put(0, r.image, inputs)
    mid_b.advance()
    in_b.advance()
    last_norm_back(0)
    box.settle(3, 4)
    stages = out_back(0)
    box.settle(5)
    out_grad(out_a)
    r.narrow_sums[1] = syncs.rest(stages, False)
    inner_norm_back(1, r.hat2, r.da, 0)
    mid_b.advance()
    in_b.advance()
    out_a.advance()
    box.put(5, r.hat1_out, r.hidden)
    slots = 9 * chunk

    def samp_load(t):
        slot, sem = slots + lax.rem(t, 2) * pixels, r.samp_sem.at[lax.rem(t, 2)]
        for c in range(chunks):
            src = pl.ds(pl.multiple_of(c * 9 * chunk + t * chunk, chunk), chunk)
            dst = pl.ds(pl.multiple_of(slot + c * chunk, breadth), chunk)
            pltpu.make_async_copy(r.samp_out.at[src], pool.at[dst], sem).start()

    def samp_settle(t):
        rows = pool.at[pl.ds(pl.multiple_of(slots + lax.rem(t, 2) * pixels, breadth), pixels)]
        pltpu.make_async_copy(rows, rows, r.samp_sem.at[lax.rem(t, 2)]).wait()

    def mid_grad_deformable(t, ref):
        @pl.when(t < 8)
        def _():
            samp_load(t + 1)

        samp_settle(t)
        slot = pl.ds(pl.multiple_of(slots + lax.rem(t, 2) * pixels, breadth), pixels)
        ref[...] = tn_dot(pool[slot, :], r.da[...]).astype(bf16)

    box.settle(6, 7)

    def clear(i):
        small[slab(i, breadth), :] = jnp.zeros((breadth, width), f32)

    loop((pixels + 2 * halo) // breadth, clear)
    table = r.table
    table[...] = jnp.zeros_like(table)
    r.draw_sum[...] = jnp.zeros_like(r.draw_sum)

    def mid_back_deformable(i):
        first_row = i * chunk_rows
        part = r.da[slab(i, chunk), :]
        for tap_row in range(3):
            for tap_col in range(3):
                tap = pl.ds((3 * tap_row + tap_col) * width, width)
                dsamp = nt_dot(part, r.w_mid[tap, :]).astype(bf16)
                for k in range(chunk_rows):
                    start = ((tap_row * chunk_rows + k) * 3 + tap_col) * breadth
                    pool[pl.ds(start, breadth), :] = dsamp[breadth * k : breadth * (k + 1)]
        th = r.tanh_raw[slab(i, chunk), :]
        r.off[...] = 0.5 + 0.45 * th
        lane = lax.broadcasted_iota(jnp.int32, (breadth, 128), 1)

        def one_row(k):
            off = r.off[slab(k, breadth), :]
            doff = jnp.zeros((breadth, 128), f32)
            for tap_row in range(3):
                start = (tap_row * chunk_rows + k) * 3 * breadth
                dsamp = pool[pl.ds(pl.multiple_of(start, breadth), 3 * breadth), :]
                start = halo + i * chunk + (k + 2 * tap_row - 2) * breadth
                rows = pl.ds(pl.multiple_of(start, breadth), 2 * breadth)
                dots = nt_dot(dsamp, r.field[rows, :])
                weights = []
                for tap_col in range(3):
                    terms = tap_terms(off, masks, first_row + k, tap_row, tap_col)
                    down, across, down_slope, across_slope = terms
                    weights.append((down * across).astype(bf16))
                    part = dots[breadth * tap_col : breadth * (tap_col + 1)]
                    doy = jnp.sum(part * (across * down_slope), axis=1, keepdims=True)
                    dox = jnp.sum(part * (across_slope * down), axis=1, keepdims=True)
                    tap = 3 * tap_row + tap_col
                    doff = jnp.where(lane == 2 * tap, doy, jnp.where(lane == 2 * tap + 1, dox, doff))
                small[rows, :] = small[rows, :] + tn_dot(jnp.concatenate(weights, axis=0), dsamp)
            th_row = r.tanh_raw[pl.ds(pl.multiple_of(i * chunk + k * breadth, breadth), breadth), :]
            draw = (0.45 * (1.0 - th_row * th_row) * doff).astype(bf16).astype(f32)
            r.off[slab(k, breadth), :] = draw
            r.draw_sum[...] = r.draw_sum[...] + fold8(draw)

        loop(chunk_rows // 2, lambda k: [one_row(2 * k), one_row(2 * k + 1)])
        draw = r.off[...]
        spread = shifted(draw, 2) + pltpu.roll(draw, 32, 1) + pltpu.roll(shifted(draw, -2), 64, 1)
        for tap_row in range(3):
            part = (spread * row_scales(masks, first_row, 2 * tap_row, 128)).astype(bf16)
            start = halo + i * chunk + (2 * tap_row - 2) * breadth
            rows = pl.ds(pl.multiple_of(start, breadth), chunk)
            small[rows, :] = small[rows, :] + nt_dot(part, r.offset_weight[tap_row])
            to = pl.ds(tap_row * width, width)
            table[to, :] = table[to, :] + tn_dot(r.field[rows, :], part)

    mid_back_deformable(0)
    mid_b.drain()
    in_b.advance()
    out_a.advance()
    mid_a.begin()
    samp_load(0)
    mid_a.fill(0, 9, mid_grad_deformable)
    in_b.drain()
    out_a.advance()
    mid_back_deformable(chunks - 1)
    mid_a.advance()
    rims = [r.staging.at[i, pl.ds(0, halo)] for i in (0, 1)]
    rims[0][...] = small[pl.ds(0, halo), :].astype(bf16)
    rims[1][...] = small[pl.ds(halo + pixels, halo), :].astype(bf16)
    edges = neighbours(rims[0], r.got_rims.at[0], rims[1], r.got_rims.at[1], 1)
    for copy in edges:
        copy.start()
    loop(chunks - 2, lambda i: mid_back_deformable(i + 1))
    out_a.drain()

    offset_sum = TableSum(place, r)
    offset_sum.advance()
    for copy in edges:
        copy.wait()
    first_rows, last_rows = pl.ds(halo, halo), pl.ds(pixels, halo)
    small[first_rows, :] = small[first_rows, :] + r.got_rims[1].astype(f32)
    small[last_rows, :] = small[last_rows, :] + r.got_rims[0].astype(f32)
    box.settle(5)
    draw_sum = jnp.sum(r.draw_sum[...], axis=0, keepdims=True)
    stages = open_sync(act_back(0, r.hidden), width, draw_sum)
    mid_a.advance()

    merged = syncs.rest(stages, False)
    r.narrow_sums[0] = merged[0:2]
    r.bias_sum[...] = merged[2:3, 0:128]
    inner_norm_back(0, r.hidden, r.da, 0)
    box.settle(0)
    mid_a.advance()
    offset_sum.advance()
    in_grad(in_a)
    box.settle(8)
    for i in range(chunks):
        in_back(i)
        at = slab(i, chunk)
        box.put(9 + i, grad.at[at], r.image_grad.at[at])
        if i == 0:
            in_a.advance()
    offset_sum.advance()
    mid_a.drain()
    in_a.advance()
    offset_sum.advance()
    in_a.drain()
    offset_sum.advance()
    box.settle()
    for one in (out_a, mid_a, in_a):
        one.end()


def whole_pass(sizes, in_kernel, r):
    place = Place(*sizes)
    syncs = Syncs(place, r.syncs)
    box = Outbox(r.box_sem)
    forward_part(place, syncs, box, r)
    backward_part(place, syncs, box, in_kernel, r)


def run_kernel(image, cotangent, heights, widths, shards, offset_weight, offset_bias, norms, sizes):
    pixels, wide = image.shape
    width = shards[0].shape[1] * sizes[1]
    taps = 9 * width
    count, high = sizes[0] * sizes[1], sizes[0] // 2
    half = high // 2
    rows = pixels // breadth
    ext_pixels = pixels + 2 * halo_rows * breadth
    each = 16 * (-(-3 * width // (16 * count)))
    in_kernel = all(s.shape[0] % 16 == 0 for s in shards)
    kinds = [(width, wide), (taps, width), (wide, width)]
    owned = [(down // sizes[0], across // sizes[1]) for down, across in kinds]
    ins = dict(
        image=image,
        cotangent=cotangent,
        heights=heights,
        widths=widths,
        weight_offset=offset_weight,
        offset_bias=offset_bias,
        mid_gain=norms[0],
        mid_bias=norms[1],
        out_gain=norms[2],
        out_bias=norms[3],
        shards=list(shards) if in_kernel else [],
    )
    narrow, broad = shape((pixels, width), bf16), shape((pixels, wide), bf16)
    outs = dict(
        hat1_out=narrow,
        hat2_out=narrow,
        hidden_out=narrow,
        field_out=shape((ext_pixels, width), bf16),
        hat3_out=broad,
        image_out=broad,
        samp_out=shape((9 * pixels, width), bf16),
        image_grad=shape((pixels, wide), f32),
        narrow_sums=shape((4, 2, width), f32),
        wide_sums=shape((2, 2, wide), f32),
        offset_grad=shape((count * each, 128), bf16),
        bias_sum=shape((1, 128), f32),
    )
    in_specs = dict(
        image=anywhere,
        cotangent=anywhere,
        heights=smem,
        widths=smem,
        offset_bias=smem,
        shards=anywhere,
        fulls=anywhere,
    )
    out_specs = dict(narrow_sums=vmem, wide_sums=vmem, offset_grad=vmem, bias_sum=vmem)
    scatter = dict()
    if in_kernel:
        outs.update(
            fulls=[shape((high, 2, s.shape[0], s.shape[1] * sizes[1]), bf16) for s in shards],
            grads=[shape(o, bf16) for o in owned] * 2,
        )
        halves = [(2, down, o[1]) for (down, _), o in zip(kinds, owned)]
        sems = [dma((2 * (down // lane_block) + 4 * half + high,)) for down, _ in kinds]
        scatter.update(
            keep=[pltpu.VMEM(h, bf16) for h in halves],
            from_core=[pltpu.VMEM(h, bf16) for h in halves],
            from_low=[pltpu.VMEM((2, half) + o, bf16) for o in owned],
            from_upper=[pltpu.VMEM((h[1] // 2, h[2]), bf16) for h in halves],
            from_two=[pltpu.VMEM((2, half) + o, bf16) for o in owned],
            from_high=[pltpu.VMEM((high - 1,) + o, bf16) for o in owned],
            result_sem=dma((3,)),
            scatter_free=[pltpu.SemaphoreType.REGULAR((4,))] * 3,
            scatter_send=sems,
            scatter_recv=sems,
        )
    else:
        fulls = [lax.all_gather(s, "mp", axis=1, tiled=True) for s in shards]
        ins.update(fulls=[lax.all_gather(s, "dp", axis=0, tiled=True) for s in fulls])
        outs.update(grads=[shape(k, bf16) for k in kinds] * 2)
    plan = [(2, width + 128), (2, width + 128), (2, wide + 128)] * 2
    plan += [(2, wide), (2, width), (2, width), (2, wide), (2, width), (3, width)]
    span = pixels + 4 * breadth
    pool_rows = max(3 * span + pixels, 9 * chunk + 2 * pixels, 18 * chunk)
    scratch = dict(
        grad=pltpu.VMEM((pixels, wide), f32),
        inputs=pltpu.VMEM((pixels, wide), bf16),
        hat3=pltpu.VMEM((pixels, wide), bf16),
        wide_act=pltpu.VMEM((pixels, wide), bf16),
        w_in=pltpu.VMEM((wide, width), bf16),
        w_mid=pltpu.VMEM((taps, width), bf16),
        w_out=pltpu.VMEM((width, wide), bf16),
        small=pltpu.VMEM((ext_pixels, width), f32),
        hat2=pltpu.VMEM((pixels, width), bf16),
        hidden=pltpu.VMEM((pixels, width), bf16),
        da=pltpu.VMEM((pixels, width), bf16),
        field=pltpu.VMEM((ext_pixels, width), bf16),
        pool=pltpu.VMEM((pool_rows, width), bf16),
        off=pltpu.VMEM((chunk, 128), f32),
        tanh_raw=pltpu.VMEM((pixels, 128), f32),
        draw_sum=pltpu.VMEM((8, 128), f32),
        table=pltpu.VMEM((count * each, 128), f32),
        table16=pltpu.VMEM((count * each, 128), bf16),
        table_one=pltpu.VMEM((sizes[1] - 1, sizes[0] * each, 128), bf16),
        table_two=pltpu.VMEM((sizes[0] - 1, each, 128), bf16),
        got_rims=pltpu.VMEM((2, halo_rows * breadth, width), bf16),
        staging=pltpu.VMEM((2, lane_block, lane_block), bf16),
        valid=pltpu.VMEM((pixels, 128), f32),
        offset_weight=pltpu.VMEM((3, width, 128), bf16),
        bias_row=pltpu.VMEM((1, 128), f32),
        sums=pltpu.VMEM((2, 8, wide), f32),
        centre=pltpu.VMEM((1, wide), f32),
        mean_narrow=pltpu.VMEM((1, width), f32),
        mean_wide=pltpu.VMEM((1, wide), f32),
        rstd_narrow=pltpu.VMEM((4, width), f32),
        rstd_wide=pltpu.VMEM((2, wide), f32),
        identity=pltpu.SMEM((rows + 2 * halo_rows,), jnp.int32),
        row_width=pltpu.SMEM((rows + 2 * halo_rows,), jnp.int32),
        masks=pltpu.SMEM((rows, 6), f32),
        counts=pltpu.SMEM((4,), f32),
        gather_local=dma((6,)),
        gather_send=dma((6, high - 1 + 7)),
        gather_recv=dma((6, high - 1 + 7)),
        halo_send=dma((2, 2)),
        halo_recv=dma((2, 2)),
        edge_send=dma((2, 2)),
        edge_recv=dma((2, 2)),
        samp_sem=dma((2,)),
        load_sem=dma((3,)),
        box_sem=dma((9 + pixels // chunk,)),
        staging_sem=dma((2, 2)),
        table_send=dma((4, max(sizes))),
        table_recv=dma((4, max(sizes))),
        syncs=sync_scratch(plan, sizes),
        **scatter,
    )
    result = launch(
        partial(whole_pass, sizes, in_kernel), ins, in_specs, outs, out_specs, scratch, 0, 63
    )
    if not in_kernel:
        result.grads = [
            lax.psum_scatter(
                lax.psum_scatter(g.astype(f32), "dp", scatter_dimension=0, tiled=True),
                "mp",
                scatter_dimension=1,
                tiled=True,
            )
            for g in result.grads
        ]
    return result


def hand_over(r):
    pieces = r.big_sem.shape[2]
    moves = []
    for i in range(pieces):
        for n, (src, through, dst) in enumerate(
            ((r.image_out, r.through_out, r.to_out), (r.image_grad, r.through_grad, r.to_grad))
        ):
            rows = src.shape[0] // pieces
            at = pl.ds(i * rows, rows)
            moves.append(
                (
                    pltpu.make_async_copy(src.at[at], through.at[at], r.big_sem.at[n, 0, i]),
                    pltpu.make_async_copy(through.at[at], dst.at[at], r.big_sem.at[n, 1, i]),
                )
            )
    for arrive, leave in moves:
        arrive.start()
    for src, dst in zip(r.grads, r.to_grads):
        dst[...] = src[...].astype(f32)
    for block in range(2):
        for j in range(2):
            norm = 2 * block + j
            r.to_mid_bias[block, j : j + 1, :] = r.narrow_sums[norm, 0:1, :]
            r.to_mid_gain[block, j : j + 1, :] = r.narrow_sums[norm, 1:2, :]
        r.to_out_bias[block : block + 1, :] = r.wide_sums[block, 0:1, :]
        r.to_out_gain[block : block + 1, :] = r.wide_sums[block, 1:2, :]
    width = r.to_mid_bias.shape[2]
    for tap_row in range(3):
        part = r.offset_grad[tap_row * width : (tap_row + 1) * width, :].astype(f32).T
        for tap_col in range(3):
            at = pl.ds((3 * tap_row + tap_col) * width, width)
            r.to_offset[:, at] = part[32 * tap_col : 32 * tap_col + offsets_count, :]
    r.to_bias[...] = r.bias_sum[:, 0 : r.to_bias.shape[1]]
    for arrive, leave in moves:
        arrive.wait()
        leave.start()
    for arrive, leave in moves:
        leave.wait()


def results_of(back, image, norms, width):
    ins = dict(
        image_out=back.image_out,
        image_grad=back.image_grad,
        grads=back.grads,
        narrow_sums=back.narrow_sums,
        wide_sums=back.wide_sums,
        offset_grad=back.offset_grad,
        bias_sum=back.bias_sum,
    )
    like = [shape(g.shape, f32) for g in norms]
    outs = dict(
        to_out=shape(image.shape, bf16),
        to_grad=shape(image.shape, f32),
        to_grads=[shape(g.shape, f32) for g in back.grads],
        to_mid_gain=like[0],
        to_mid_bias=like[1],
        to_out_gain=like[2],
        to_out_bias=like[3],
        to_offset=shape((offsets_count, 9 * width), f32),
        to_bias=shape((1, offsets_count), f32),
    )
    specs = dict(image_out=anywhere, image_grad=anywhere)
    out_specs = dict((name, vmem) for name in outs)
    out_specs.update(to_out=anywhere, to_grad=anywhere)
    scratch = dict(
        big_sem=dma((2, 2, 8)),
        through_out=pltpu.VMEM(image.shape, bf16),
        through_grad=pltpu.VMEM(image.shape, f32),
    )
    return launch(partial(hand_over), ins, specs, outs, out_specs, scratch, None, 60)


def per_device(
    image_in,
    cotangent,
    heights,
    widths,
    weight_in_a,
    weight_offset,
    bias_offset,
    weight_mid_a,
    weight_out_a,
    weight_in_b,
    weight_mid_b,
    weight_out_b,
    mid_gain,
    mid_bias,
    out_gain,
    out_bias,
):
    height, wide = image_in.shape[0], image_in.shape[2]
    sizes = (lax.axis_size("dp"), lax.axis_size("mp"))
    shards = (weight_in_a, weight_mid_a, weight_out_a, weight_in_b, weight_mid_b, weight_out_b)
    norms = (mid_gain, mid_bias, out_gain, out_bias)
    image = image_in.reshape(height * breadth, wide)
    back = run_kernel(
        image,
        cotangent.reshape(height * breadth, wide),
        heights,
        widths,
        shards,
        weight_offset.T,
        bias_offset,
        norms,
        sizes,
    )
    final = results_of(back, image, norms, weight_offset.shape[0] // 9)
    grads = final.to_grads
    return (
        final.to_out.reshape(image_in.shape),
        final.to_grad.reshape(image_in.shape),
        grads[5],
        final.to_offset.T,
        final.to_bias.reshape(bias_offset.shape),
        grads[4],
        grads[3],
        grads[2],
        grads[1],
        grads[0],
        final.to_mid_gain,
        final.to_mid_bias,
        final.to_out_gain,
        final.to_out_bias,
    )


def solution(mesh):
    rows, split, both = P(("dp", "mp"), None, None), P("dp", "mp"), P()
    in_specs = (rows, rows, both, both, split, both, both, split, split, split, split, split)
    in_specs += (both,) * 4
    out_specs = (rows, rows, split, both, both, split, split, split, split, split) + (both,) * 4
    return jax.shard_map(
        per_device, mesh=mesh, in_specs=in_specs, out_specs=out_specs, check_vma=False
    )
```

```python
from functools import partial
from types import SimpleNamespace

import jax
import jax.numpy as jnp
from jax import lax
from jax.experimental import pallas as pl
from jax.experimental.pallas import tpu as pltpu
from jax.sharding import PartitionSpec as P

norm_eps = 1e-05
halo_rows = 3
breadth = 64
chunk = 256
strip = 32
lane_block = 512
offsets_count = 18
gelu_a = 0.7978845608028654
gelu_b = gelu_a * 0.044715
MESH = pl.DeviceIdType.MESH
f32 = jnp.float32
bf16 = jnp.bfloat16
shape = jax.ShapeDtypeStruct
dma = pltpu.SemaphoreType.DMA
vmem = pl.BlockSpec(memory_space=pltpu.VMEM)
smem = pl.BlockSpec(memory_space=pltpu.SMEM)
anywhere = pl.BlockSpec(memory_space=pl.ANY)


class Place:
    def __init__(self, dp_size, mp_size):
        self.dp_size, self.mp_size = dp_size, mp_size
        self.count = dp_size * mp_size
        self.high = dp_size // 2
        self.dp = lax.axis_index("dp")
        self.mp = lax.axis_index("mp")
        self.me = self.dp * mp_size + self.mp
        self.z = self.dp // 2
        self.y = lax.rem(self.dp, 2)
        self.x = self.mp // 2
        self.core = lax.rem(self.mp, 2)

    def at(self, linear):
        return (linear // self.mp_size, lax.rem(linear, self.mp_size))

    def next(self, step):
        return self.at(lax.rem(self.me + self.count + step, self.count))

    def core_peer(self):
        return (self.dp, self.mp + 1 - 2 * self.core)

    def x_peer(self):
        return (self.dp, self.mp + 2 - 4 * self.x)

    def y_peer(self):
        return (self.dp + 1 - 2 * self.y, self.mp)

    def z_peer(self, step):
        return (lax.rem(self.z + step, self.high) * 2 + self.y, self.mp)

    def greet_all(self):
        barrier = pltpu.get_barrier_semaphore()

        def greet_one(k):
            pl.semaphore_signal(barrier, inc=1, device_id=self.next(k + 1), device_id_type=MESH)

        loop(self.count - 1, greet_one)
        pl.semaphore_wait(barrier, self.count - 1)


def remote(src, dst, send, recv, peer):
    return pltpu.make_async_remote_copy(
        src_ref=src,
        dst_ref=dst,
        send_sem=send,
        recv_sem=recv,
        device_id=peer,
        device_id_type=MESH,
    )


def slab(index, size):
    return pl.ds(pl.multiple_of(index * size, size), size)


def loop(count, body):
    def step(i, carry):
        body(i)
        return carry

    lax.fori_loop(0, count, step, 0)


def launch(kernel, ins, specs, outs, out_specs, scratch, collective_id, vmem_mib):
    flat_in, tree_in = jax.tree.flatten(ins)
    flat_out, tree_out = jax.tree.flatten(outs)
    is_leaf = lambda s: not isinstance(s, (dict, list))
    flat_scratch, tree_scratch = jax.tree.flatten(scratch, is_leaf=is_leaf)
    spec_in = [s for n in sorted(ins) for s in [specs.get(n, vmem)] * len(jax.tree.leaves(ins[n]))]
    spec_out = [
        s for n in sorted(outs) for s in [out_specs.get(n, anywhere)] * len(jax.tree.leaves(outs[n]))
    ]

    def body(*refs):
        a, b = len(flat_in), len(flat_in) + len(flat_out)
        everything = dict(jax.tree.unflatten(tree_in, refs[:a]))
        everything.update(jax.tree.unflatten(tree_out, refs[a:b]))
        everything.update(jax.tree.unflatten(tree_scratch, refs[b:]))
        kernel(SimpleNamespace(**everything))

    results = pl.pallas_call(
        body,
        out_shape=flat_out,
        in_specs=spec_in,
        out_specs=spec_out,
        scratch_shapes=flat_scratch,
        compiler_params=pltpu.CompilerParams(
            collective_id=collective_id,
            has_side_effects=collective_id is not None,
            vmem_limit_bytes=vmem_mib * 1024 * 1024,
        ),
        name=kernel.func.__name__,
    )(*flat_in)
    return SimpleNamespace(**jax.tree.unflatten(tree_out, results))


def gelu_of(v):
    return 0.5 * v * (1.0 + jnp.tanh(v * (gelu_a + gelu_b * v * v)))


def gelu_pair(v):
    square = v * v
    half = 0.5 + 0.5 * jnp.tanh(v * (gelu_a + gelu_b * square))
    return half, half * (1.0 + (1.0 - half) * (v * (2.0 * gelu_a + 6.0 * gelu_b * square)))


def gelu_slope(v):
    return gelu_pair(v)[1]


def mid_row(table, norm):
    return table.at[norm // 2, norm % 2 : norm % 2 + 1, :]


def wide_valid(valid, rows, width):
    mask = valid[rows, :]
    return jnp.concatenate([mask] * (width // 128), axis=1)


def fold8(x):
    return jnp.sum(x.reshape(x.shape[0] // 8, 8, x.shape[1]), axis=0)


def strip_sums(pixel_count, width, terms, out, row_at):
    for block in range(width // lane_block):
        lanes = pl.ds(block * lane_block, lane_block)

        def step(i, carry, lanes=lanes):
            parts = terms(slab(i, strip), lanes)
            return tuple(c + fold8(p) for c, p in zip(carry, parts))

        zeros = tuple(jnp.zeros((8, lane_block), f32) for _ in row_at)
        sums = lax.fori_loop(0, pixel_count // strip, step, zeros)
        for row, total in zip(row_at, sums):
            out[row : row + 1, lanes] = jnp.sum(total, axis=0, keepdims=True)


def merge(parts, moments_mode):
    if not moments_mode:
        return jnp.sum(parts, axis=0)
    width = parts.shape[2] - 128
    pixels = jnp.concatenate([parts[:, 0:1, width:]] * (width // 128), axis=2)
    sums, squares = parts[:, 0:1, 0:width], parts[:, 1:2, 0:width]
    all_pixels, all_sums = jnp.sum(pixels, axis=0), jnp.sum(sums, axis=0)
    apart = sums / pixels - (all_sums / all_pixels)[None]
    all_squares = jnp.sum(squares + pixels * apart * apart, axis=0)
    behind = jnp.sum(parts[:, :, width:], axis=0)
    return jnp.concatenate([jnp.concatenate([all_sums, all_squares], axis=0), behind], axis=1)


def sync_groups(width, sizes):
    count = sizes[0] * sizes[1]
    if count > 64:
        return (16, count // 16)
    return sizes[::-1] if width > 1024 else (count,)


def sync_scratch(plan, sizes):
    out = []
    for rows, width in plan:
        for size in sync_groups(width, sizes):
            out += [pltpu.VMEM((rows, width), f32), pltpu.VMEM((size, rows, width), f32), dma, dma]
    return out


class Syncs:
    def __init__(self, place, buffers):
        self.place, self.buffers = place, buffers
        self.at = 0

    def take(self, width):
        stages = []
        stride = 1
        for size in sync_groups(width, (self.place.dp_size, self.place.mp_size)):
            digit = lax.rem(self.place.me // stride, size)
            stages.append((stride, size, digit, self.buffers[self.at : self.at + 4]))
            self.at += 4
            stride *= size
        return stages

    def start(self, stage, value=None):
        stride, size, digit, (src, slots, send, recv) = stage
        me = self.place.me
        if value is not None:
            src[...] = value

        def push(k):
            peer = me + (lax.rem(digit + k + 1, size) - digit) * stride
            remote(src, slots.at[digit], send, recv, self.place.at(peer)).start()

        loop(size - 1, push)
        pltpu.make_async_copy(src, slots.at[digit], recv).start()

    def finish(self, stage, moments_mode):
        stride, size, digit, (src, slots, send, recv) = stage
        pltpu.make_async_copy(slots, slots, recv).wait()
        rest = slots.at[pl.ds(0, size - 1)]
        pltpu.make_async_copy(rest, rest, send).wait()
        return merge(slots[...], moments_mode)

    def rest(self, stages, moments_mode, meanwhile=None):
        value = self.finish(stages[0], moments_mode)
        for stage in stages[1:]:
            self.start(stage, value)
            if meanwhile is not None:
                meanwhile()
            value = self.finish(stage, moments_mode)
        return value


def shifted(x, shift):
    if shift == 0:
        return x
    pixels = x.shape[0]
    column = lax.broadcasted_iota(jnp.int32, x.shape, 0) % breadth + shift
    inside = (column >= 0) & (column < breadth)
    return jnp.where(inside, pltpu.roll(x, (-shift) % pixels, 0), 0.0)


def row_scales(masks, first_row, which, width):
    row_of = lax.broadcasted_iota(jnp.int32, (chunk, width), 0) // breadth
    scale = jnp.zeros((chunk, width), f32)
    for k in range(chunk // breadth):
        scale = jnp.where(row_of == k, masks[first_row + k, which], scale)
    return scale


def masked_rows(part, masks, first_row, which):
    scaled = []
    for k in range(part.shape[0] // breadth):
        piece = part[breadth * k : breadth * (k + 1)].astype(f32)
        scaled.append((piece * masks[first_row + k, which]).astype(bf16))
    return jnp.concatenate(scaled, axis=0)


def tap_terms(off, masks, row, tap_row, tap_col):
    lane = lax.broadcasted_iota(jnp.int32, (breadth, 2 * breadth), 1)
    sub = lax.broadcasted_iota(jnp.int32, (breadth, 2 * breadth), 0)
    upper = lane >= breadth
    apart = jnp.where(upper, lane - breadth, lane) - sub
    tap, shift = 3 * tap_row + tap_col, 2 * tap_col - 2
    oy, ox = off[:, 2 * tap : 2 * tap + 1], off[:, 2 * tap + 1 : 2 * tap + 2]
    low, high = masks[row, 2 * tap_row], masks[row, 2 * tap_row + 1]
    down = jnp.where(upper, oy * high, (1.0 - oy) * low)
    across = jnp.where(apart == shift, 1.0 - ox, jnp.where(apart == shift + 1, ox, 0.0))
    down_slope = jnp.where(upper, high, -low)
    across_slope = jnp.where(apart == shift, -1.0, jnp.where(apart == shift + 1, 1.0, 0.0))
    return down, across, down_slope, across_slope


def nt_dot(a, b):
    return lax.dot_general(a, b, (((1,), (1,)), ((), ())), preferred_element_type=f32)


def tn_dot(a, b):
    return lax.dot_general(a, b, (((0,), (0,)), ((), ())), preferred_element_type=f32)


def nn_dot(a, b):
    return jnp.dot(a, b, preferred_element_type=f32)


class Outbox:
    def __init__(self, sems):
        self.sems, self.running = sems, {}

    def put(self, at, src, dst):
        copy = pltpu.make_async_copy(src, dst, self.sems.at[at])
        copy.start()
        self.running[at] = copy

    def settle(self, *which):
        for at in which or list(self.running):
            self.running.pop(at).wait()


def load_weight(full, dst, sem):
    if len(full.shape) == 2:
        copy = pltpu.make_async_copy(full, dst, sem)
        copy.start()
        return copy
    block = full.shape[2]
    for z in range(full.shape[0]):
        for y in range(2):
            rows = pl.ds((2 * z + y) * block, block)
            pltpu.make_async_copy(full.at[z, y], dst.at[rows], sem).start()
    return pltpu.make_async_copy(dst, dst, sem)


class Gather:
    def __init__(self, place, r):
        self.place, self.fulls, self.sems = place, r.fulls, (r.gather_local, r.gather_send, r.gather_recv)
        self.shards = r.shards
        self.stage = [0] * 6
        self.running = [[] for _ in range(6)]

    def cols(self, array, x_at, core_at):
        width = self.shards[array].shape[1]
        return pl.ds(pl.multiple_of((2 * x_at + core_at) * width, 128), width)

    def copies(self, array, stage):
        place, full = self.place, self.fulls[array]
        high, z, y, x, core = place.high, place.z, place.y, place.x, place.core
        half = high // 2
        mine = self.cols(array, x, core)
        lower, upper = pl.ds(0, half), pl.ds(half, high - half)
        local, send, recv = self.sems
        if stage == 0:
            target = full.at[z, y, :, mine]
            own = pltpu.make_async_copy(self.shards[array], target, local.at[array])
            return [own] + [
                remote(
                    self.shards[array],
                    target,
                    send.at[array, k - 1],
                    recv.at[array, k - 1],
                    place.z_peer(k),
                )
                for k in range(1, high)
            ]
        if stage == 1:
            pairs = [
                (full.at[lower, y, :, mine], place.x_peer()),
                (full.at[upper, y, :, mine], place.y_peer()),
            ]
        elif stage == 2:
            pairs = [
                (full.at[lower, y, :, self.cols(array, 0, core)], place.y_peer()),
                (full.at[lower, y, :, self.cols(array, 1, core)], place.y_peer()),
                (full.at[upper, :, :, mine], place.x_peer()),
            ]
        else:
            pairs = [
                (full.at[:, :, :, self.cols(array, 0, core)], place.core_peer()),
                (full.at[:, :, :, self.cols(array, 1, core)], place.core_peer()),
            ]
        base = high - 1 + [0, 0, 2, 5][stage]
        return [
            remote(ref, ref, send.at[array, base + i], recv.at[array, base + i], peer)
            for i, (ref, peer) in enumerate(pairs)
        ]

    def advance(self, *arrays):
        for array in arrays if self.shards else ():
            for copy in self.running[array]:
                copy.wait()
            self.running[array] = []
            if self.stage[array] < 4:
                self.running[array] = self.copies(array, self.stage[array])
                for copy in self.running[array]:
                    copy.start()
            self.stage[array] += 1


class Scatter:
    def __init__(self, place, r, kind, use, result):
        self.place, self.use, self.result = place, use, result
        self.keep, self.from_core = r.keep[kind], r.from_core[kind]
        self.low, self.upper = r.from_low[kind], r.from_upper[kind]
        self.two, self.from_high = r.from_two[kind], r.from_high[kind]
        self.send, self.recv, self.free = r.scatter_send[kind], r.scatter_recv[kind], r.scatter_free[kind]
        self.staging, self.staging_sem = r.staging, r.staging_sem
        self.result_sem = r.result_sem.at[kind]
        self.rows, self.width = self.keep.shape[1], self.keep.shape[2]
        self.block = self.rows // place.dp_size
        self.tiles = self.rows // lane_block
        self.stage = 0
        self.running = []

    def cols(self, x_at, core_at):
        return pl.ds(pl.multiple_of((2 * x_at + core_at) * self.width, 128), self.width)

    def at(self, high, y):
        return pl.ds(pl.multiple_of((2 * high + y) * self.block, self.block), self.block)

    def to_core(self, t, i, src):
        rows = pl.ds(pl.multiple_of(t * lane_block, lane_block), lane_block)
        return remote(
            src,
            self.from_core.at[i, rows],
            self.send.at[2 * t + i],
            self.recv.at[2 * t + i],
            self.place.core_peer(),
        )

    def tile_copies(self, t):
        slot = lax.rem(t, 2)
        rows = pl.ds(pl.multiple_of(t * lane_block, lane_block), lane_block)
        core = self.place.core
        away = [self.to_core(t, i, self.staging.at[slot, :, self.cols(i, 1 - core)]) for i in (0, 1)]
        home = [
            pltpu.make_async_copy(
                self.staging.at[slot, :, self.cols(i, core)],
                self.keep.at[i, rows],
                self.staging_sem.at[slot, i],
            )
            for i in (0, 1)
        ]
        return away, home

    def settle_tile(self, t):
        away, home = self.tile_copies(t)
        for copy in away:
            copy.wait_send()
        for copy in home:
            copy.wait()

    def result_copy(self):
        place = self.place
        return pltpu.make_async_copy(
            self.keep.at[place.x, self.at(place.z, place.y)], self.result, self.result_sem
        )

    def begin(self):
        if self.use == 1:
            self.result_copy().wait()
            pl.semaphore_wait(self.free.at[0], 1)

    def fill(self, first, last, compute):
        def body(i):
            t = first + i

            @pl.when(i >= 2)
            def _():
                self.settle_tile(t - 2)

            compute(t, self.staging.at[lax.rem(t, 2)])
            away, home = self.tile_copies(t)
            for copy in away + home:
                copy.start()

        loop(last - first, body)
        for t in range(max(first, last - 2), last):
            self.settle_tile(t)

    def fill_by_columns(self, compute):
        core = self.place.core

        def away(i):
            self.staging[i] = compute(self.cols(i, 1 - core)).astype(bf16)
            self.to_core(0, i, self.staging.at[i]).start()

        def home(i):
            self.keep[i] = compute(self.cols(i, core)).astype(bf16)

        loop(2, away)
        loop(2, home)
        for i in (0, 1):
            self.to_core(0, i, self.staging.at[i]).wait_send()

    def copies(self, stage):
        place = self.place
        x, y, z, half = place.x, place.y, place.z, place.high // 2
        items = []
        if stage == 1:
            for i in (0, 1):
                for b in range(half):
                    items.append((self.keep.at[i, self.at(b, 1 - y)], self.low.at[i, b], place.y_peer()))
            upper = pl.ds(self.rows // 2, self.rows // 2)
            items.append((self.keep.at[1 - x, upper], self.upper, place.x_peer()))
        elif stage == 2:
            for b in range(half):
                items.append((self.keep.at[1 - x, self.at(b, y)], self.two.at[0, b], place.x_peer()))
                items.append(
                    (self.keep.at[x, self.at(half + b, 1 - y)], self.two.at[1, b], place.y_peer())
                )
        else:
            for k in range(1, place.high):
                there = self.at(lax.rem(z + k, place.high), y)
                items.append((self.keep.at[x, there], self.from_high.at[k - 1], place.z_peer(k)))
        base = 2 * self.tiles + [0, 0, 2 * half + 1, 4 * half + 1][stage]
        return [
            remote(src, dst, self.send.at[base + i], self.recv.at[base + i], peer)
            for i, (src, dst, peer) in enumerate(items)
        ]

    def add(self, target, extra):
        target[...] = target[...] + extra[...]

    def finish(self, stage):
        place = self.place
        x, y, z, half = place.x, place.y, place.z, place.high // 2
        if stage == 0:
            piece = 64
            for i in (0, 1):

                def body(k, i=i):
                    rows = slab(k, piece)
                    self.add(self.keep.at[i, rows], self.from_core.at[i, rows])

                loop(self.rows // piece, body)
            peers = [place.core_peer()]
        elif stage == 1:
            for b in range(half):
                for i in (0, 1):
                    self.add(self.keep.at[i, self.at(b, y)], self.low.at[i, b])
            piece = 64

            def body(k):
                rows = pl.ds(pl.multiple_of(self.rows // 2 + k * piece, piece), piece)
                self.add(self.keep.at[x, rows], self.upper.at[slab(k, piece)])

            loop(self.rows // 2 // piece, body)
            peers = [place.x_peer(), place.y_peer()]
        elif stage == 2:
            for b in range(half):
                self.add(self.keep.at[x, self.at(b, y)], self.two.at[0, b])
                self.add(self.keep.at[x, self.at(half + b, y)], self.two.at[1, b])
            peers = [place.x_peer(), place.y_peer()]
        else:
            total = self.keep[x, self.at(z, y)].astype(f32)
            for k in range(1, place.high):
                total = total + self.from_high[k - 1].astype(f32)
            self.keep[x, self.at(z, y)] = total.astype(bf16)
            self.result_copy().start()
            peers = [place.z_peer(k) for k in range(1, place.high)]
        if self.use == 0:
            for peer in peers:
                pl.semaphore_signal(self.free.at[stage], inc=1, device_id=peer, device_id_type=MESH)

    def advance(self):
        if self.stage > 3:
            return
        if self.stage == 0:
            for t in range(self.tiles):
                for i in (0, 1):
                    self.to_core(t, i, self.staging.at[0, :, self.cols(i, 0)] if self.tiles > 1 else self.staging.at[i]).wait_recv()
        for copy in self.running:
            copy.wait()
        self.finish(self.stage)
        self.stage += 1
        if self.stage <= 3:
            if self.use == 1:
                waits = [0, 2, 2, self.place.high - 1][self.stage]
                pl.semaphore_wait(self.free.at[self.stage], waits)
            self.running = self.copies(self.stage)
            for copy in self.running:
                copy.start()

    def drain(self):
        while self.stage <= 3:
            self.advance()

    def end(self):
        self.result_copy().wait()


class Whole:
    def __init__(self, r, result):
        self.staging, self.staging_sem, self.result = r.staging, r.staging_sem, result

    def begin(self):
        pass

    def fill(self, first, last, compute):
        def body(i):
            t = first + i
            compute(t, self.staging.at[0])
            rows = pl.ds(pl.multiple_of(t * lane_block, lane_block), lane_block)
            pltpu.sync_copy(self.staging.at[0], self.result.at[rows])

        loop(last - first, body)

    def fill_by_columns(self, compute):
        def body(i):
            lanes = pl.ds(pl.multiple_of(i * lane_block, lane_block), lane_block)
            self.staging[0] = compute(lanes).astype(bf16)
            pltpu.sync_copy(self.staging.at[0], self.result.at[:, lanes])

        loop(self.result.shape[1] // lane_block, body)

    def advance(self):
        pass

    drain = advance
    end = advance


class TableSum:
    def __init__(self, place, r):
        self.place, self.r = place, r
        self.each = r.table16.shape[0] // place.count
        self.stage, self.running = 0, []

    def part(self, mp, dp=None):
        quarter = self.each * self.place.dp_size
        if dp is None:
            return pl.ds(pl.multiple_of(mp * quarter, self.each), quarter)
        return pl.ds(pl.multiple_of(mp * quarter + dp * self.each, self.each), self.each)

    def copies(self, stage):
        place, r = self.place, self.r
        dp, mp, table, result = place.dp, place.mp, r.table16, r.offset_grad
        items = []
        over_mp = [lax.rem(mp + k, place.mp_size) for k in range(1, place.mp_size)]
        over_dp = [lax.rem(dp + k, place.dp_size) for k in range(1, place.dp_size)]
        if stage == 0:
            for k, to in enumerate(over_mp):
                items.append((table.at[self.part(to)], r.table_one.at[k], (dp, to)))
        elif stage == 1:
            for k, to in enumerate(over_dp):
                items.append((table.at[self.part(mp, to)], r.table_two.at[k], (to, mp)))
        elif stage == 2:
            mine = self.part(mp, dp)
            items = [(result.at[mine], result.at[mine], (to, mp)) for to in over_dp]
        else:
            mine = self.part(mp)
            items = [(result.at[mine], result.at[mine], (dp, to)) for to in over_mp]
        send, recv = r.table_send.at[stage], r.table_recv.at[stage]
        return [remote(a, b, send.at[i], recv.at[i], to) for i, (a, b, to) in enumerate(items)]

    def advance(self):
        place, r = self.place, self.r
        for copy in self.running:
            copy.wait()
        mine = self.part(place.mp), self.part(place.mp, place.dp)
        if self.stage == 0:
            r.table16[...] = r.table[...].astype(bf16)
        elif self.stage == 1:
            total = r.table16[mine[0], :].astype(f32)
            for k in range(place.mp_size - 1):
                total = total + r.table_one[k].astype(f32)
            r.table16[mine[0], :] = total.astype(bf16)
        elif self.stage == 2:
            total = r.table16[mine[1], :].astype(f32)
            for k in range(place.dp_size - 1):
                total = total + r.table_two[k].astype(f32)
            r.offset_grad[mine[1], :] = total.astype(bf16)
        self.running = self.copies(self.stage) if self.stage < 4 else []
        for copy in self.running:
            copy.start()
        self.stage += 1


def geometry(place, r):
    heights, widths, identity, row_width = r.heights, r.widths, r.identity, r.row_width
    images = heights.shape[1]
    rows = r.valid.shape[0] // breadth
    all_rows = rows * place.count
    group_rows = all_rows // 2 + rows // 2
    one, none = jnp.int32(1), jnp.int32(0)

    def row_facts(k):
        row = place.me * rows - halo_rows + k
        group = jnp.where(row >= group_rows, one, none)
        local = row - group * group_rows

        def image(j, carry):
            begin, number, found = carry
            end = begin + heights[group, j]
            number = number + jnp.where(local >= end, one, none)
            here = (local >= begin) & (local < end)
            return end, number, jnp.where(here, widths[group, j], found)

        _, number, found = lax.fori_loop(0, images, image, (none, none, none))
        inside = (row >= 0) & (row < all_rows)
        identity[k] = jnp.where(inside, group * images + number, -one)
        row_width[k] = jnp.where(inside, found, none)

    loop(rows + 2 * halo_rows, row_facts)

    def row_masks(k):
        centre = identity[k + halo_rows]
        for s in range(6):
            r.masks[k, s] = jnp.where(identity[k + s + 1] == centre, 1.0, 0.0).astype(f32)
        column = lax.broadcasted_iota(jnp.int32, (breadth, 128), 0)
        r.valid[slab(k, breadth), :] = jnp.where(column < row_width[k + halo_rows], 1.0, 0.0)

    loop(rows, row_masks)

    def pixels_of(first, last):
        def add(k, total):
            return total + row_width[k + halo_rows]

        return lax.fori_loop(first, last, add, none).astype(f32)

    def add_image(j, total):
        return total + heights[0, j] * widths[0, j] + heights[1, j] * widths[1, j]

    local = pixels_of(0, rows)
    r.counts[0] = local
    r.counts[1] = 1.0 / local
    r.counts[2] = 1.0 / lax.fori_loop(0, images, add_image, none).astype(f32)
    r.counts[3] = 1.0 / pixels_of(0, chunk // breadth)
    r.counts[4] = 1.0 / pixels_of(chunk // breadth, 2 * chunk // breadth)

    count = r.offset_bias.shape[0]
    width = r.offset_weight.shape[1]
    lane = lax.broadcasted_iota(jnp.int32, (1, 128), 1)
    bias = jnp.zeros((1, 128), f32)
    for j in range(count):
        bias = jnp.where(lane == j, r.offset_bias[j], bias)
    r.bias_row[...] = bias
    down = lax.broadcasted_iota(jnp.int32, (count, 128), 0)
    across = lax.broadcasted_iota(jnp.int32, (count, 128), 1)
    for tap_row in range(3):
        total = jnp.zeros((width, 128), f32)
        for tap_col in range(3):
            place_at = jnp.where(across == down + 32 * tap_col, 1.0, 0.0).astype(bf16)
            columns = pl.ds((3 * tap_row + tap_col) * width, width)
            total = total + tn_dot(r.weight_offset[:, columns], place_at)
        r.offset_weight[tap_row] = total.astype(bf16)


def forward_part(place, syncs, box, r):
    gather = Gather(place, r)
    valid, masks, counts = r.valid, r.masks, r.counts
    third, field, hidden, pool = r.grad, r.field, r.hidden, r.pool
    pixels, wide = third.shape
    width = hidden.shape[1]
    halo = halo_rows * breadth
    chunks = pixels // chunk
    first = r.small.at[pl.ds(halo, pixels)]

    def load(array, dst, sem):
        return load_weight(r.fulls[array], dst, r.load_sem.at[sem])

    def gather_sums(i, got, scale):
        block_width = got.shape[1]
        sums, centre = r.sums.at[:, :, 0:block_width], r.centre.at[:, 0:block_width]
        mask = wide_valid(valid, slab(i, chunk), block_width)
        if scale is not None:
            centre[...] = jnp.sum(fold8(got * mask), axis=0, keepdims=True) * scale
            sums[...] = jnp.zeros((2, 8, block_width), f32)
        apart = (got - centre[...]) * mask
        sums[0] = sums[0] + fold8(apart)
        sums[1] = sums[1] + fold8(apart * apart)

    def over_chunks(target, compute, between=None):
        def body(i, scale=None):
            got = compute(i)
            target[slab(i, chunk), :] = got
            gather_sums(i, got, scale)

        if between is None:
            body(0, counts[3])
            loop(chunks - 1, lambda i: body(i + 1))
        else:
            body(1, counts[4])
            loop(chunks - 3, lambda i: body(i + 2))
            between()
            loop(2, lambda i: body(i * (chunks - 1)))

    def moments(block_width, rstd, mean, meanwhile=None, early=None):
        stages = syncs.take(block_width + 128)
        src = stages[0][3][0]
        first_sum = jnp.sum(r.sums[0, :, 0:block_width], axis=0, keepdims=True)
        second_sum = jnp.sum(r.sums[1, :, 0:block_width], axis=0, keepdims=True)
        src[0:1, 0:block_width] = first_sum + r.centre[:, 0:block_width] * counts[0]
        src[1:2, 0:block_width] = second_sum - first_sum * first_sum * counts[1]
        src[:, block_width:] = jnp.full((2, 128), counts[0], f32)
        syncs.start(stages[0])
        if early is not None:
            early()
        merged = syncs.rest(stages, True, meanwhile)
        mean[...] = merged[0:1, 0:block_width] * counts[2]
        spread = jnp.maximum(merged[1:2, 0:block_width], 0.0) * counts[2]
        rstd[...] = lax.rsqrt(spread + norm_eps)

    def activate(norm, hat, target, target_row):
        mean, rstd = r.mean_narrow, r.rstd_narrow.at[norm : norm + 1, :]
        gain, bias = mid_row(r.mid_gain, norm), mid_row(r.mid_bias, norm)

        def body(i):
            at = slab(i, strip)
            normed = (first[at, :] - mean[...]) * rstd[...]
            hat[at, :] = normed.astype(bf16)
            act = gelu_of(normed * gain[...] + bias[...]) * wide_valid(valid, at, width)
            rows = pl.ds(pl.multiple_of(target_row + i * strip, strip), strip)
            target[rows, :] = act.astype(bf16)

        loop(pixels // strip, body)

    def narrow_moments(norm, early=None):
        moments(width, r.rstd_narrow.at[norm : norm + 1, :], r.mean_narrow, None, early)

    def project(lhs, weight, target):
        over_chunks(target, lambda i: nn_dot(lhs[slab(i, chunk), :], weight[...]))

    def halo_copies(block):
        send, recv = r.halo_send.at[block], r.halo_recv.at[block]
        last_rows, below = field.at[pl.ds(pixels, halo)], field.at[pl.ds(pixels + halo, halo)]
        first_rows, above = field.at[pl.ds(halo, halo)], field.at[pl.ds(0, halo)]
        return [
            remote(last_rows, above, send.at[0], recv.at[0], place.next(1)),
            remote(first_rows, below, send.at[1], recv.at[1], place.next(-1)),
        ]

    samples = [r.inputs, r.hat3, pool]

    def sample_at(tap, i):
        return samples[tap // 4], slab(i, chunk), pl.ds(tap % 4 * width, width)

    def sample_chunk(i):
        base = halo + i * chunk
        first_row = i * (chunk // breadth)
        total = jnp.zeros((chunk, 128), f32)
        for tap_row in range(3):
            start = pl.multiple_of(base + (2 * tap_row - 2) * breadth, breadth)
            part = nn_dot(field[pl.ds(start, chunk), :], r.offset_weight[tap_row])
            total = total + part * row_scales(masks, first_row, 2 * tap_row, 128)
        left = shifted(total, -2)
        middle = pltpu.roll(total, 128 - 32, 1)
        right = pltpu.roll(shifted(total, 2), 128 - 64, 1)
        lane = lax.broadcasted_iota(jnp.int32, total.shape, 1)
        raw = jnp.where(lane < 32, left + middle + right, 0.0) + r.bias_row[...]
        tanh_raw = jnp.tanh(raw)
        r.tanh_raw[slab(i, chunk), :] = tanh_raw
        r.off[...] = 0.5 + 0.45 * tanh_raw

        def one_row(k):
            off = r.off[slab(k, breadth), :]
            for tap_row in range(3):
                weights = []
                for tap_col in range(3):
                    down, across, _, _ = tap_terms(off, masks, first_row + k, tap_row, tap_col)
                    weights.append((down * across).astype(bf16))
                start = pl.multiple_of(base + (k + 2 * tap_row - 2) * breadth, breadth)
                got = nn_dot(jnp.concatenate(weights, axis=0), field[pl.ds(start, 2 * breadth), :])
                for tap_col in range(3):
                    ref, _, lanes = sample_at(3 * tap_row + tap_col, i)
                    rows = pl.ds(pl.multiple_of(i * chunk + k * breadth, breadth), breadth)
                    piece = got[breadth * tap_col : breadth * (tap_col + 1)]
                    ref[rows, lanes] = piece.astype(bf16)

        loop(chunk // breadth // 2, lambda k: [one_row(2 * k), one_row(2 * k + 1)])

    def mid_deformable(i):
        rows = slab(i, chunk)
        samp = jnp.concatenate([r.inputs[rows, :], r.hat3[rows, :], pool[rows, :]], axis=1)
        return nn_dot(samp, r.w_mid[...])

    def samp_copies():
        copies = []
        for tap in range(9):
            ref, _, lanes = sample_at(tap, 0)
            src = ref.at[pl.ds(0, pixels), lanes]
            copies.append(
                pltpu.make_async_copy(src, r.samp_out.at[pl.ds(tap * pixels, pixels)], r.samp_sem.at[0])
            )
        return copies

    def mid_plain(i):
        lhs = []
        for tap_row in range(3):
            start = pl.multiple_of(halo + i * chunk + (2 * tap_row - 2) * breadth, breadth)
            part = field[pl.ds(start, chunk), :]
            if tap_row != 1:
                part = masked_rows(part, masks, i * (chunk // breadth), 2 * tap_row)
            lhs.append(part)
        total = None
        for tap_col in range(3):
            partial_sum = None
            for tap_row in range(3):
                weight = r.w_mid[pl.ds((3 * tap_row + tap_col) * width, width), :]
                part = nn_dot(lhs[tap_row], weight)
                partial_sum = part if partial_sum is None else partial_sum + part
            partial_sum = shifted(partial_sum, 2 * tap_col - 2)
            total = partial_sum if total is None else total + partial_sum
        return total

    def finish_block(block, inputs, result):
        gain, bias = r.out_gain.at[block : block + 1, :], r.out_bias.at[block : block + 1, :]
        mean, rstd = r.mean_wide, r.rstd_wide.at[block : block + 1, :]

        def body(i):
            at = slab(i, strip)
            mask = wide_valid(valid, at, lane_block)
            for j in range(wide // lane_block):
                lanes = pl.ds(j * lane_block, lane_block)
                normed = (third[at, lanes] - mean[:, lanes]) * rstd[:, lanes]
                r.hat3[at, lanes] = normed.astype(bf16)
                pre = inputs[at, lanes].astype(f32) + (normed * gain[:, lanes] + bias[:, lanes])
                result[at, lanes] = (mask * gelu_of(pre)).astype(bf16)

        loop(pixels // strip, body)

    def wide_moments(block, meanwhile=None):
        moments(wide, r.rstd_wide.at[block : block + 1, :], r.mean_wide, meanwhile)

    place.greet_all()
    gather.advance(0)
    gather.advance(1)
    box.put(0, r.image, r.wide_act)
    geometry(place, r)
    gather.advance(0)
    gather.advance(0)
    gather.advance(0)
    gather.advance(1)
    gather.advance(2)
    gather.advance(0)
    loaded = load(0, r.w_in, 0)
    loaded.wait()
    box.settle(0)
    project(r.wide_act, r.w_in, first)
    narrow_moments(0, lambda: gather.advance(1))
    activate(0, r.da, field, halo)
    edges = halo_copies(0)
    for copy in edges:
        copy.start()
    gather.advance(4, 3)
    box.put(1, r.da, r.hat1_out)
    loop(chunks - 2, lambda i: sample_chunk(i + 1))
    gather.advance(1)
    for copy in edges:
        copy.wait()
    gather.advance(2)
    box.put(2, field, r.field_out)
    loop(2, lambda i: sample_chunk(i * (chunks - 1)))
    gather.advance(1)
    loaded = load(1, r.w_mid, 1)
    gather.advance(2)
    samp_out = samp_copies()
    for copy in samp_out:
        copy.start()
    loaded.wait()
    over_chunks(first, mid_deformable)
    narrow_moments(1, lambda: gather.advance(2, 4, 3, 5))
    gather.advance(2)
    loaded = load(2, r.w_out, 2)
    activate(1, r.hat2, hidden, 0)
    box.put(3, r.hat2, r.hat2_out)
    box.put(4, hidden, r.hidden_out)
    for copy in samp_out:
        copy.wait()
    loaded.wait()
    project(hidden, r.w_out, third)
    wide_moments(0, lambda: gather.advance(3, 4))
    finish_block(0, r.wide_act, r.inputs)
    box.put(0, r.cotangent, r.wide_act)
    box.put(5, r.hat3, r.hat3_out)
    gather.advance(3)
    gather.advance(3)
    load(3, r.w_in, 0).wait()
    box.settle(1, 2)
    project(r.inputs, r.w_in, first)
    narrow_moments(2, lambda: gather.advance(4))
    gather.advance(4)
    loaded = load(4, r.w_mid, 1)
    activate(2, r.da, field, halo)
    edges = halo_copies(1)
    for copy in edges:
        copy.start()
    gather.advance(5)

    def edges_here():
        for copy in edges:
            copy.wait()

    loaded.wait()
    over_chunks(first, mid_plain, edges_here)
    narrow_moments(3, lambda: gather.advance(5))
    gather.advance(5)
    gather.advance(5)
    loaded_out = load(5, r.w_out, 2)
    box.settle(3, 4)
    activate(3, r.hat2, hidden, 0)
    loaded_out.wait()
    project(hidden, r.w_out, third)
    wide_moments(1)
    box.settle(0, 5)


def backward_part(place, syncs, box, in_kernel, r):
    valid, masks, counts = r.valid, r.masks, r.counts
    grad, small, inputs, hat3, wide_act = r.grad, r.small, r.inputs, r.hat3, r.wide_act
    pixels, wide, width = grad.shape[0], grad.shape[1], small.shape[1]
    halo = halo_rows * breadth
    chunks, chunk_rows = pixels // chunk, chunk // breadth
    per_pixel = counts[2]
    own = pl.ds(halo, pixels)
    kinds = [0, 1, 2]

    def scatter(kind, use):
        result = r.grads[3 * use + kind]
        if in_kernel:
            return Scatter(place, r, kind, use, result)
        return Whole(r, result)

    def weight(array, dst, sem):
        box.running[sem] = load_weight(r.fulls[array], dst, r.box_sem.at[sem])

    def open_sync(terms, block_width, last_row=None):
        stages = syncs.take(block_width)
        src = stages[0][3][0]
        strip_sums(pixels, block_width, terms, src, [0, 1])
        if last_row is not None:
            src[2:3, :] = jnp.zeros((1, block_width), f32)
            src[2:3, 0:128] = last_row
        syncs.start(stages[0])
        return stages

    def pre_back(block, upstream, image):
        gain, bias = r.out_gain.at[block : block + 1, :], r.out_bias.at[block : block + 1, :]

        def terms(at, lanes):
            hat = hat3[at, lanes].astype(f32)
            pre = image[at, lanes].astype(f32) + (hat * gain[:, lanes] + bias[:, lanes])
            slope = gelu_slope(pre) * wide_valid(valid, at, lane_block)
            d = upstream[at, lanes].astype(f32) * slope
            grad[at, lanes] = d
            return d, d * hat

        return open_sync(terms, wide)

    def finish_and_back():
        gain, bias = r.out_gain.at[1:2, :], r.out_bias.at[1:2, :]
        mean, rstd = r.mean_wide, r.rstd_wide.at[1:2, :]

        def terms(at, lanes):
            normed = (grad[at, lanes] - mean[:, lanes]) * rstd[:, lanes]
            hat3[at, lanes] = normed.astype(bf16)
            pre = inputs[at, lanes].astype(f32) + (normed * gain[:, lanes] + bias[:, lanes])
            half, slope = gelu_pair(pre)
            mask = wide_valid(valid, at, lane_block)
            d = wide_act[at, lanes].astype(f32) * (slope * mask)
            wide_act[at, lanes] = (pre * (half * mask)).astype(bf16)
            grad[at, lanes] = d
            return d, d * normed

        return open_sync(terms, wide)

    def last_norm_back(block):
        sums, rstd = r.wide_sums.at[block], r.rstd_wide.at[block : block + 1, :]
        gain = r.out_gain.at[block : block + 1, :]

        def body(i):
            at = slab(i, strip)
            mask = wide_valid(valid, at, lane_block)
            for j in range(wide // lane_block):
                lanes = pl.ds(j * lane_block, lane_block)
                hat = hat3[at, lanes].astype(f32)
                inner = grad[at, lanes] - sums[0:1, lanes] * per_pixel
                inner = inner - hat * (sums[1:2, lanes] * per_pixel)
                scaled = mask * (gain[:, lanes] * rstd[:, lanes]) * inner
                wide_act[at, lanes] = scaled.astype(bf16)

        loop(pixels // strip, body)

    def act_back(norm, hat):
        gain, bias = mid_row(r.mid_gain, norm), mid_row(r.mid_bias, norm)

        def terms(at, lanes):
            normed = hat[at, lanes].astype(f32)
            slope = gelu_slope(normed * gain[:, lanes] + bias[:, lanes])
            rows = pl.ds(pl.multiple_of(halo + at.start, strip), strip)
            d = small[rows, lanes] * slope * wide_valid(valid, at, lane_block)
            small[rows, lanes] = d
            return d, d * normed

        return terms

    def inner_norm_back(norm, hat, target, target_row):
        sums, rstd = r.narrow_sums.at[norm], r.rstd_narrow.at[norm : norm + 1, :]
        gain = mid_row(r.mid_gain, norm)

        def body(i):
            at = slab(i, strip)
            rows = pl.ds(pl.multiple_of(halo + i * strip, strip), strip)
            inner = small[rows, :] - sums[0:1, :] * per_pixel
            inner = inner - hat[at, :].astype(f32) * (sums[1:2, :] * per_pixel)
            scaled = wide_valid(valid, at, width) * (gain[...] * rstd[...]) * inner
            target[pl.ds(pl.multiple_of(target_row + i * strip, strip), strip), :] = scaled.astype(bf16)

        loop(pixels // strip, body)

    def out_back(block):
        def body(i):
            rows = pl.ds(pl.multiple_of(halo + i * chunk, breadth), chunk)
            small[rows, :] = nt_dot(wide_act[slab(i, chunk), :], r.w_out[...])

        loop(chunks, body)
        return open_sync(act_back(2 * block + 1, r.hat2), width)

    def out_grad(target):
        target.begin()
        target.fill_by_columns(lambda lanes: tn_dot(r.hidden[...], wide_act[:, lanes]))

    def in_grad(target):
        target.begin()

        def compute(t, ref):
            lanes = pl.ds(pl.multiple_of(t * lane_block, lane_block), lane_block)
            ref[...] = tn_dot(inputs[:, lanes], r.da[...]).astype(bf16)

        target.fill(0, wide // lane_block, compute)

    def in_back(i):
        at = slab(i, chunk)
        grad[at, :] = grad[at, :] + nt_dot(r.da[at, :], r.w_in[...])

    def neighbours(before_src, before_dst, after_src, after_dst, which):
        send, recv = r.edge_send.at[which], r.edge_recv.at[which]
        return [
            remote(after_src, after_dst, send.at[0], recv.at[0], place.next(1)),
            remote(before_src, before_dst, send.at[1], recv.at[1], place.next(-1)),
        ]

    out_b, mid_b, in_b = [scatter(kind, 0) for kind in kinds]
    stages = finish_and_back()
    box.put(6, wide_act, r.image_out)
    r.wide_sums[1] = syncs.rest(stages, False)
    box.settle(6)
    last_norm_back(1)
    box.put(1, r.hat3_out, hat3)
    stages = out_back(1)
    weight(2, r.w_out, 3)
    out_grad(out_b)
    box.put(2, r.image, wide_act)
    box.put(5, r.hidden_out, r.hidden)
    r.narrow_sums[3] = syncs.rest(stages, False)

    pool, side = r.pool, 2 * breadth
    span = pixels + 2 * side
    centre = 2 * span
    inner_norm_back(3, r.hat2, pool, centre + side)
    box.put(4, r.hat2_out, r.hat2)
    edges = neighbours(
        pool.at[pl.ds(centre + side, side)],
        pool.at[pl.ds(centre + side + pixels, side)],
        pool.at[pl.ds(centre + pixels, side)],
        pool.at[pl.ds(centre, side)],
        0,
    )
    for copy in edges:
        copy.start()

    def shift_row(row):
        at = pl.ds(pl.multiple_of(centre + row * breadth, breadth), breadth)
        value = pool[at, :].astype(f32)
        for slot, amount in ((0, 2), (1, -2)):
            rows = pl.ds(pl.multiple_of(slot * span + row * breadth, breadth), breadth)
            pool[rows, :] = shifted(value, amount).astype(bf16)

    loop(pixels // breadth, lambda row: shift_row(row + 2))
    out_b.advance()
    for copy in edges:
        copy.wait()
    loop(2, shift_row)
    loop(2, lambda row: shift_row(row + 2 + pixels // breadth))
    slot_of = (0, 2, 1)

    def mid_back_plain(i):
        first_row = i * chunk_rows
        total = None
        for tap_row in range(3):
            for tap_col in range(3):
                start = slot_of[tap_col] * span + (4 - 2 * tap_row) * breadth + i * chunk
                part = pool[pl.ds(pl.multiple_of(start, breadth), chunk), :]
                if tap_row != 1:
                    part = masked_rows(part, masks, first_row, 4 - 2 * tap_row)
                tap = pl.ds((3 * tap_row + tap_col) * width, width)
                term = nt_dot(part, r.w_mid[tap, :])
                total = term if total is None else total + term
        rows = pl.ds(pl.multiple_of(halo + i * chunk, breadth), chunk)
        small[rows, :] = total

    loop(chunks, mid_back_plain)
    weight(1, r.w_mid, 7)
    stages = open_sync(act_back(2, r.da), width)
    out_b.advance()
    mid_b.begin()
    shifted_rows = 3 * span

    def mid_grad_plain(t, ref):
        tap_row, tap_col = t // 3, lax.rem(t, 3)
        slot = jnp.where(tap_col == 0, 0, jnp.where(tap_col == 1, 2, 1))

        def copy_row(row):
            start = slot * span + (4 - 2 * tap_row + row) * breadth
            part = pool[pl.ds(pl.multiple_of(start, breadth), breadth), :]
            rows = pl.ds(pl.multiple_of(shifted_rows + row * breadth, breadth), breadth)
            pool[rows, :] = masked_rows(part, masks, row, 4 - 2 * tap_row)

        loop(pixels // breadth, copy_row)
        ref[...] = tn_dot(r.field[own, :], pool[pl.ds(shifted_rows, pixels), :]).astype(bf16)

    mid_b.fill(0, 9, mid_grad_plain)
    out_b.advance()
    r.narrow_sums[2] = syncs.rest(stages, False)
    mid_b.advance()
    inner_norm_back(2, r.da, r.da, 0)
    box.put(6, r.field_out, r.field)
    loop(chunks, in_back)
    out_b.advance()
    weight(0, r.w_in, 8)

    out_a, mid_a, in_a = [scatter(kind, 1) for kind in kinds]
    box.settle(1, 2)
    stages = pre_back(0, grad, wide_act)
    out_b.drain()
    in_grad(in_b)
    box.put(0, r.image, inputs)
    r.wide_sums[0] = syncs.rest(stages, False, lambda: [mid_b.advance(), in_b.advance()])
    last_norm_back(0)
    box.settle(3, 4)
    stages = out_back(0)
    box.settle(5)
    out_grad(out_a)
    mid_b.advance()
    in_b.advance()
    r.narrow_sums[1] = syncs.rest(stages, False)
    inner_norm_back(1, r.hat2, r.da, 0)
    out_a.advance()
    box.put(5, r.hat1_out, r.hidden)
    slots = 9 * chunk

    def samp_load(t):
        slot = pl.ds(pl.multiple_of(slots + lax.rem(t, 2) * pixels, breadth), pixels)
        src = r.samp_out.at[pl.ds(pl.multiple_of(t * pixels, breadth), pixels)]
        pltpu.make_async_copy(src, pool.at[slot], r.samp_sem.at[lax.rem(t, 2)]).start()

    def samp_settle(t):
        rows = pool.at[pl.ds(pl.multiple_of(slots + lax.rem(t, 2) * pixels, breadth), pixels)]
        pltpu.make_async_copy(rows, rows, r.samp_sem.at[lax.rem(t, 2)]).wait()

    def mid_grad_deformable(t, ref):
        @pl.when(t < 8)
        def _():
            samp_load(t + 1)

        samp_settle(t)
        slot = pl.ds(pl.multiple_of(slots + lax.rem(t, 2) * pixels, breadth), pixels)
        ref[...] = tn_dot(pool[slot, :], r.da[...]).astype(bf16)

    box.settle(6, 7)

    def clear(i):
        small[slab(i, breadth), :] = jnp.zeros((breadth, width), f32)

    loop((pixels + 2 * halo) // breadth, clear)
    table = r.table
    table[...] = jnp.zeros_like(table)
    r.draw_sum[...] = jnp.zeros_like(r.draw_sum)

    def mid_back_deformable(i):
        first_row = i * chunk_rows
        part = r.da[slab(i, chunk), :]
        for tap_row in range(3):
            for tap_col in range(3):
                tap = pl.ds((3 * tap_row + tap_col) * width, width)
                dsamp = nt_dot(part, r.w_mid[tap, :]).astype(bf16)
                for k in range(chunk_rows):
                    start = ((tap_row * chunk_rows + k) * 3 + tap_col) * breadth
                    pool[pl.ds(start, breadth), :] = dsamp[breadth * k : breadth * (k + 1)]
        th = r.tanh_raw[slab(i, chunk), :]
        r.off[...] = 0.5 + 0.45 * th
        lane = lax.broadcasted_iota(jnp.int32, (breadth, 128), 1)

        def one_row(k):
            off = r.off[slab(k, breadth), :]
            doff = jnp.zeros((breadth, 128), f32)
            for tap_row in range(3):
                start = (tap_row * chunk_rows + k) * 3 * breadth
                dsamp = pool[pl.ds(pl.multiple_of(start, breadth), 3 * breadth), :]
                start = halo + i * chunk + (k + 2 * tap_row - 2) * breadth
                rows = pl.ds(pl.multiple_of(start, breadth), 2 * breadth)
                dots = nt_dot(dsamp, r.field[rows, :])
                weights = []
                for tap_col in range(3):
                    terms = tap_terms(off, masks, first_row + k, tap_row, tap_col)
                    down, across, down_slope, across_slope = terms
                    weights.append((down * across).astype(bf16))
                    part = dots[breadth * tap_col : breadth * (tap_col + 1)]
                    doy = jnp.sum(part * (across * down_slope), axis=1, keepdims=True)
                    dox = jnp.sum(part * (across_slope * down), axis=1, keepdims=True)
                    tap = 3 * tap_row + tap_col
                    doff = jnp.where(lane == 2 * tap, doy, jnp.where(lane == 2 * tap + 1, dox, doff))
                small[rows, :] = small[rows, :] + tn_dot(jnp.concatenate(weights, axis=0), dsamp)
            th_row = r.tanh_raw[pl.ds(pl.multiple_of(i * chunk + k * breadth, breadth), breadth), :]
            draw = (0.45 * (1.0 - th_row * th_row) * doff).astype(bf16).astype(f32)
            r.off[slab(k, breadth), :] = draw
            r.draw_sum[...] = r.draw_sum[...] + fold8(draw)

        loop(chunk_rows // 2, lambda k: [one_row(2 * k), one_row(2 * k + 1)])
        draw = r.off[...]
        spread = shifted(draw, 2) + pltpu.roll(draw, 32, 1) + pltpu.roll(shifted(draw, -2), 64, 1)
        for tap_row in range(3):
            part = (spread * row_scales(masks, first_row, 2 * tap_row, 128)).astype(bf16)
            start = halo + i * chunk + (2 * tap_row - 2) * breadth
            rows = pl.ds(pl.multiple_of(start, breadth), chunk)
            small[rows, :] = small[rows, :] + nt_dot(part, r.offset_weight[tap_row])
            to = pl.ds(tap_row * width, width)
            table[to, :] = table[to, :] + tn_dot(r.field[rows, :], part)

    mid_back_deformable(0)
    mid_b.drain()
    in_b.advance()
    out_a.advance()
    mid_a.begin()
    samp_load(0)
    mid_a.fill(0, 9, mid_grad_deformable)
    in_b.drain()
    out_a.advance()
    mid_back_deformable(chunks - 1)
    mid_a.advance()
    rims = [r.staging.at[i, pl.ds(0, halo)] for i in (0, 1)]
    rims[0][...] = small[pl.ds(0, halo), :].astype(bf16)
    rims[1][...] = small[pl.ds(halo + pixels, halo), :].astype(bf16)
    edges = neighbours(rims[0], r.got_rims.at[0], rims[1], r.got_rims.at[1], 1)
    for copy in edges:
        copy.start()
    loop(chunks - 2, lambda i: mid_back_deformable(i + 1))
    out_a.drain()

    offset_sum = TableSum(place, r)
    for copy in edges:
        copy.wait()
    first_rows, last_rows = pl.ds(halo, halo), pl.ds(pixels, halo)
    small[first_rows, :] = small[first_rows, :] + r.got_rims[1].astype(f32)
    small[last_rows, :] = small[last_rows, :] + r.got_rims[0].astype(f32)
    box.settle(5)
    draw_sum = jnp.sum(r.draw_sum[...], axis=0, keepdims=True)
    stages = open_sync(act_back(0, r.hidden), width, draw_sum)
    offset_sum.advance()
    mid_a.advance()

    merged = syncs.rest(stages, False)
    r.narrow_sums[0] = merged[0:2]
    r.bias_sum[...] = merged[2:3, 0:128]
    inner_norm_back(0, r.hidden, r.da, 0)
    box.settle(0)
    mid_a.advance()
    offset_sum.advance()
    in_grad(in_a)
    box.settle(8)
    for i in range(chunks):
        in_back(i)
        at = slab(i, chunk)
        box.put(9 + i, grad.at[at], r.image_grad.at[at])
        if i == 0:
            in_a.advance()
    offset_sum.advance()
    mid_a.drain()
    in_a.advance()
    offset_sum.advance()
    in_a.drain()
    offset_sum.advance()
    box.settle()
    for one in (out_a, mid_a, in_a):
        one.end()


def whole_pass(sizes, in_kernel, r):
    place = Place(*sizes)
    syncs = Syncs(place, r.syncs)
    box = Outbox(r.box_sem)
    forward_part(place, syncs, box, r)
    backward_part(place, syncs, box, in_kernel, r)


def run_kernel(image, cotangent, heights, widths, shards, offset_weight, offset_bias, norms, sizes):
    pixels, wide = image.shape
    width = shards[0].shape[1] * sizes[1]
    taps = 9 * width
    count, high = sizes[0] * sizes[1], sizes[0] // 2
    half = high // 2
    rows = pixels // breadth
    ext_pixels = pixels + 2 * halo_rows * breadth
    each = 16 * (-(-3 * width // (16 * count)))
    in_kernel = all(s.shape[0] % 16 == 0 for s in shards)
    kinds = [(width, wide), (taps, width), (wide, width)]
    owned = [(down // sizes[0], across // sizes[1]) for down, across in kinds]
    ins = dict(
        image=image,
        cotangent=cotangent,
        heights=heights,
        widths=widths,
        weight_offset=offset_weight,
        offset_bias=offset_bias,
        mid_gain=norms[0],
        mid_bias=norms[1],
        out_gain=norms[2],
        out_bias=norms[3],
        shards=list(shards) if in_kernel else [],
    )
    narrow, broad = shape((pixels, width), bf16), shape((pixels, wide), bf16)
    outs = dict(
        hat1_out=narrow,
        hat2_out=narrow,
        hidden_out=narrow,
        field_out=shape((ext_pixels, width), bf16),
        hat3_out=broad,
        image_out=broad,
        samp_out=shape((9 * pixels, width), bf16),
        image_grad=shape((pixels, wide), f32),
        narrow_sums=shape((4, 2, width), f32),
        wide_sums=shape((2, 2, wide), f32),
        offset_grad=shape((count * each, 128), bf16),
        bias_sum=shape((1, 128), f32),
    )
    in_specs = dict(
        image=anywhere,
        cotangent=anywhere,
        heights=smem,
        widths=smem,
        offset_bias=smem,
        shards=anywhere,
        fulls=anywhere,
    )
    out_specs = dict(narrow_sums=vmem, wide_sums=vmem, offset_grad=vmem, bias_sum=vmem)
    scatter = dict()
    if in_kernel:
        outs.update(
            fulls=[shape((high, 2, s.shape[0], s.shape[1] * sizes[1]), bf16) for s in shards],
            grads=[shape(o, bf16) for o in owned] * 2,
        )
        halves = [(2, down, o[1]) for (down, _), o in zip(kinds, owned)]
        sems = [dma((2 * (down // lane_block) + 4 * half + high,)) for down, _ in kinds]
        scatter.update(
            keep=[pltpu.VMEM(h, bf16) for h in halves],
            from_core=[pltpu.VMEM(h, bf16) for h in halves],
            from_low=[pltpu.VMEM((2, half) + o, bf16) for o in owned],
            from_upper=[pltpu.VMEM((h[1] // 2, h[2]), bf16) for h in halves],
            from_two=[pltpu.VMEM((2, half) + o, bf16) for o in owned],
            from_high=[pltpu.VMEM((high - 1,) + o, bf16) for o in owned],
            result_sem=dma((3,)),
            scatter_free=[pltpu.SemaphoreType.REGULAR((4,))] * 3,
            scatter_send=sems,
            scatter_recv=sems,
        )
    else:
        fulls = [lax.all_gather(s, "mp", axis=1, tiled=True) for s in shards]
        ins.update(fulls=[lax.all_gather(s, "dp", axis=0, tiled=True) for s in fulls])
        outs.update(grads=[shape(k, bf16) for k in kinds] * 2)
    plan = [(2, width + 128), (2, width + 128), (2, wide + 128)] * 2
    plan += [(2, wide), (2, width), (2, width), (2, wide), (2, width), (3, width)]
    span = pixels + 4 * breadth
    pool_rows = max(3 * span + pixels, 9 * chunk + 2 * pixels)
    scratch = dict(
        grad=pltpu.VMEM((pixels, wide), f32),
        inputs=pltpu.VMEM((pixels, wide), bf16),
        hat3=pltpu.VMEM((pixels, wide), bf16),
        wide_act=pltpu.VMEM((pixels, wide), bf16),
        w_in=pltpu.VMEM((wide, width), bf16),
        w_mid=pltpu.VMEM((taps, width), bf16),
        w_out=pltpu.VMEM((width, wide), bf16),
        small=pltpu.VMEM((ext_pixels, width), f32),
        hat2=pltpu.VMEM((pixels, width), bf16),
        hidden=pltpu.VMEM((pixels, width), bf16),
        da=pltpu.VMEM((pixels, width), bf16),
        field=pltpu.VMEM((ext_pixels, width), bf16),
        pool=pltpu.VMEM((pool_rows, width), bf16),
        off=pltpu.VMEM((chunk, 128), f32),
        tanh_raw=pltpu.VMEM((pixels, 128), f32),
        draw_sum=pltpu.VMEM((8, 128), f32),
        table=pltpu.VMEM((count * each, 128), f32),
        table16=pltpu.VMEM((count * each, 128), bf16),
        table_one=pltpu.VMEM((sizes[1] - 1, sizes[0] * each, 128), bf16),
        table_two=pltpu.VMEM((sizes[0] - 1, each, 128), bf16),
        got_rims=pltpu.VMEM((2, halo_rows * breadth, width), bf16),
        staging=pltpu.VMEM((2, lane_block, lane_block), bf16),
        valid=pltpu.VMEM((pixels, 128), f32),
        offset_weight=pltpu.VMEM((3, width, 128), bf16),
        bias_row=pltpu.VMEM((1, 128), f32),
        sums=pltpu.VMEM((2, 8, wide), f32),
        centre=pltpu.VMEM((1, wide), f32),
        mean_narrow=pltpu.VMEM((1, width), f32),
        mean_wide=pltpu.VMEM((1, wide), f32),
        rstd_narrow=pltpu.VMEM((4, width), f32),
        rstd_wide=pltpu.VMEM((2, wide), f32),
        identity=pltpu.SMEM((rows + 2 * halo_rows,), jnp.int32),
        row_width=pltpu.SMEM((rows + 2 * halo_rows,), jnp.int32),
        masks=pltpu.SMEM((rows, 6), f32),
        counts=pltpu.SMEM((5,), f32),
        gather_local=dma((6,)),
        gather_send=dma((6, high - 1 + 7)),
        gather_recv=dma((6, high - 1 + 7)),
        halo_send=dma((2, 2)),
        halo_recv=dma((2, 2)),
        edge_send=dma((2, 2)),
        edge_recv=dma((2, 2)),
        samp_sem=dma((2,)),
        load_sem=dma((3,)),
        box_sem=dma((9 + pixels // chunk,)),
        staging_sem=dma((2, 2)),
        table_send=dma((4, max(sizes))),
        table_recv=dma((4, max(sizes))),
        syncs=sync_scratch(plan, sizes),
        **scatter,
    )
    result = launch(
        partial(whole_pass, sizes, in_kernel), ins, in_specs, outs, out_specs, scratch, 0, 63
    )
    if not in_kernel:
        result.grads = [
            lax.psum_scatter(
                lax.psum_scatter(g.astype(f32), "dp", scatter_dimension=0, tiled=True),
                "mp",
                scatter_dimension=1,
                tiled=True,
            )
            for g in result.grads
        ]
    return result


def hand_over(r):
    pieces = r.big_sem.shape[2]
    moves = []
    for i in range(pieces):
        for n, (src, through, dst) in enumerate(
            ((r.image_out, r.through_out, r.to_out), (r.image_grad, r.through_grad, r.to_grad))
        ):
            rows = src.shape[0] // pieces
            at = pl.ds(i * rows, rows)
            moves.append(
                (
                    pltpu.make_async_copy(src.at[at], through.at[at], r.big_sem.at[n, 0, i]),
                    pltpu.make_async_copy(through.at[at], dst.at[at], r.big_sem.at[n, 1, i]),
                )
            )
    for arrive, leave in moves:
        arrive.start()
    for src, dst in zip(r.grads, r.to_grads):
        dst[...] = src[...].astype(f32)
    for block in range(2):
        for j in range(2):
            norm = 2 * block + j
            r.to_mid_bias[block, j : j + 1, :] = r.narrow_sums[norm, 0:1, :]
            r.to_mid_gain[block, j : j + 1, :] = r.narrow_sums[norm, 1:2, :]
        r.to_out_bias[block : block + 1, :] = r.wide_sums[block, 0:1, :]
        r.to_out_gain[block : block + 1, :] = r.wide_sums[block, 1:2, :]
    width = r.to_mid_bias.shape[2]
    for tap_row in range(3):
        part = r.offset_grad[tap_row * width : (tap_row + 1) * width, :].astype(f32).T
        for tap_col in range(3):
            at = pl.ds((3 * tap_row + tap_col) * width, width)
            r.to_offset[:, at] = part[32 * tap_col : 32 * tap_col + offsets_count, :]
    r.to_bias[...] = r.bias_sum[:, 0 : r.to_bias.shape[1]]
    for arrive, leave in moves:
        arrive.wait()
        leave.start()
    for arrive, leave in moves:
        leave.wait()


def results_of(back, image, norms, width):
    ins = dict(
        image_out=back.image_out,
        image_grad=back.image_grad,
        grads=back.grads,
        narrow_sums=back.narrow_sums,
        wide_sums=back.wide_sums,
        offset_grad=back.offset_grad,
        bias_sum=back.bias_sum,
    )
    like = [shape(g.shape, f32) for g in norms]
    outs = dict(
        to_out=shape(image.shape, bf16),
        to_grad=shape(image.shape, f32),
        to_grads=[shape(g.shape, f32) for g in back.grads],
        to_mid_gain=like[0],
        to_mid_bias=like[1],
        to_out_gain=like[2],
        to_out_bias=like[3],
        to_offset=shape((offsets_count, 9 * width), f32),
        to_bias=shape((1, offsets_count), f32),
    )
    specs = dict(image_out=anywhere, image_grad=anywhere)
    out_specs = dict((name, vmem) for name in outs)
    out_specs.update(to_out=anywhere, to_grad=anywhere)
    scratch = dict(
        big_sem=dma((2, 2, 8)),
        through_out=pltpu.VMEM(image.shape, bf16),
        through_grad=pltpu.VMEM(image.shape, f32),
    )
    return launch(partial(hand_over), ins, specs, outs, out_specs, scratch, None, 60)


def per_device(
    image_in,
    cotangent,
    heights,
    widths,
    weight_in_a,
    weight_offset,
    bias_offset,
    weight_mid_a,
    weight_out_a,
    weight_in_b,
    weight_mid_b,
    weight_out_b,
    mid_gain,
    mid_bias,
    out_gain,
    out_bias,
):
    height, wide = image_in.shape[0], image_in.shape[2]
    sizes = (lax.axis_size("dp"), lax.axis_size("mp"))
    shards = (weight_in_a, weight_mid_a, weight_out_a, weight_in_b, weight_mid_b, weight_out_b)
    norms = (mid_gain, mid_bias, out_gain, out_bias)
    image = image_in.reshape(height * breadth, wide)
    back = run_kernel(
        image,
        cotangent.reshape(height * breadth, wide),
        heights,
        widths,
        shards,
        weight_offset.T,
        bias_offset,
        norms,
        sizes,
    )
    final = results_of(back, image, norms, weight_offset.shape[0] // 9)
    grads = final.to_grads
    return (
        final.to_out.reshape(image_in.shape),
        final.to_grad.reshape(image_in.shape),
        grads[5],
        final.to_offset.T,
        final.to_bias.reshape(bias_offset.shape),
        grads[4],
        grads[3],
        grads[2],
        grads[1],
        grads[0],
        final.to_mid_gain,
        final.to_mid_bias,
        final.to_out_gain,
        final.to_out_bias,
    )


def solution(mesh):
    rows, split, both = P(("dp", "mp"), None, None), P("dp", "mp"), P()
    in_specs = (rows, rows, both, both, split, both, both, split, split, split, split, split)
    in_specs += (both,) * 4
    out_specs = (rows, rows, split, both, both, split, split, split, split, split) + (both,) * 4
    return jax.shard_map(
        per_device, mesh=mesh, in_specs=in_specs, out_specs=out_specs, check_vma=False
    )
```

```python
from functools import partial
from types import SimpleNamespace

import jax
import jax.numpy as jnp
from jax import lax
from jax.experimental import pallas as pl
from jax.experimental.pallas import tpu as pltpu
from jax.sharding import PartitionSpec as P

norm_eps = 1e-05
halo_rows = 3
breadth = 64
chunk = 256
strip = 32
lane_block = 512
offsets_count = 18
gelu_a = 0.7978845608028654
gelu_b = gelu_a * 0.044715
MESH = pl.DeviceIdType.MESH
f32 = jnp.float32
bf16 = jnp.bfloat16
shape = jax.ShapeDtypeStruct
dma = pltpu.SemaphoreType.DMA
vmem = pl.BlockSpec(memory_space=pltpu.VMEM)
smem = pl.BlockSpec(memory_space=pltpu.SMEM)
anywhere = pl.BlockSpec(memory_space=pl.ANY)


class Place:
    def __init__(self, dp_size, mp_size):
        self.dp_size, self.mp_size = dp_size, mp_size
        self.count = dp_size * mp_size
        self.high = dp_size // 2
        self.dp = lax.axis_index("dp")
        self.mp = lax.axis_index("mp")
        self.me = self.dp * mp_size + self.mp
        self.z = self.dp // 2
        self.y = lax.rem(self.dp, 2)
        self.x = self.mp // 2
        self.core = lax.rem(self.mp, 2)

    def at(self, linear):
        return (linear // self.mp_size, lax.rem(linear, self.mp_size))

    def next(self, step):
        return self.at(lax.rem(self.me + self.count + step, self.count))

    def core_peer(self):
        return (self.dp, self.mp + 1 - 2 * self.core)

    def x_peer(self):
        return (self.dp, self.mp + 2 - 4 * self.x)

    def y_peer(self):
        return (self.dp + 1 - 2 * self.y, self.mp)

    def z_peer(self, step):
        return (lax.rem(self.z + step, self.high) * 2 + self.y, self.mp)

    def greet_all(self):
        barrier = pltpu.get_barrier_semaphore()

        def greet_one(k):
            pl.semaphore_signal(barrier, inc=1, device_id=self.next(k + 1), device_id_type=MESH)

        loop(self.count - 1, greet_one)
        pl.semaphore_wait(barrier, self.count - 1)


def remote(src, dst, send, recv, peer):
    return pltpu.make_async_remote_copy(
        src_ref=src,
        dst_ref=dst,
        send_sem=send,
        recv_sem=recv,
        device_id=peer,
        device_id_type=MESH,
    )


def slab(index, size):
    return pl.ds(pl.multiple_of(index * size, size), size)


def loop(count, body):
    def step(i, carry):
        body(i)
        return carry

    lax.fori_loop(0, count, step, 0)


def launch(kernel, ins, specs, outs, out_specs, scratch, collective_id, vmem_mib):
    flat_in, tree_in = jax.tree.flatten(ins)
    flat_out, tree_out = jax.tree.flatten(outs)
    is_leaf = lambda s: not isinstance(s, (dict, list))
    flat_scratch, tree_scratch = jax.tree.flatten(scratch, is_leaf=is_leaf)
    spec_in = [s for n in sorted(ins) for s in [specs.get(n, vmem)] * len(jax.tree.leaves(ins[n]))]
    spec_out = [
        s for n in sorted(outs) for s in [out_specs.get(n, anywhere)] * len(jax.tree.leaves(outs[n]))
    ]

    def body(*refs):
        a, b = len(flat_in), len(flat_in) + len(flat_out)
        everything = dict(jax.tree.unflatten(tree_in, refs[:a]))
        everything.update(jax.tree.unflatten(tree_out, refs[a:b]))
        everything.update(jax.tree.unflatten(tree_scratch, refs[b:]))
        kernel(SimpleNamespace(**everything))

    results = pl.pallas_call(
        body,
        out_shape=flat_out,
        in_specs=spec_in,
        out_specs=spec_out,
        scratch_shapes=flat_scratch,
        compiler_params=pltpu.CompilerParams(
            collective_id=collective_id,
            has_side_effects=collective_id is not None,
            vmem_limit_bytes=vmem_mib * 1024 * 1024,
        ),
        name=kernel.func.__name__,
    )(*flat_in)
    return SimpleNamespace(**jax.tree.unflatten(tree_out, results))


def gelu_of(v):
    return 0.5 * v * (1.0 + jnp.tanh(v * (gelu_a + gelu_b * v * v)))


def gelu_pair(v):
    square = v * v
    half = 0.5 + 0.5 * jnp.tanh(v * (gelu_a + gelu_b * square))
    return half, half * (1.0 + (1.0 - half) * (v * (2.0 * gelu_a + 6.0 * gelu_b * square)))


def gelu_slope(v):
    return gelu_pair(v)[1]


def mid_row(table, norm):
    return table.at[norm // 2, norm % 2 : norm % 2 + 1, :]


def wide_valid(valid, rows, width):
    mask = valid[rows, :]
    return jnp.concatenate([mask] * (width // 128), axis=1)


def fold8(x):
    return jnp.sum(x.reshape(x.shape[0] // 8, 8, x.shape[1]), axis=0)


def strip_sums(pixel_count, width, terms, out, row_at):
    for block in range(width // lane_block):
        lanes = pl.ds(block * lane_block, lane_block)

        def step(i, carry, lanes=lanes):
            parts = terms(slab(i, strip), lanes)
            return tuple(c + fold8(p) for c, p in zip(carry, parts))

        zeros = tuple(jnp.zeros((8, lane_block), f32) for _ in row_at)
        sums = lax.fori_loop(0, pixel_count // strip, step, zeros)
        for row, total in zip(row_at, sums):
            out[row : row + 1, lanes] = jnp.sum(total, axis=0, keepdims=True)


def merge(parts, moments_mode):
    if not moments_mode:
        return jnp.sum(parts, axis=0)
    width = parts.shape[2] - 128
    pixels = jnp.concatenate([parts[:, 0:1, width:]] * (width // 128), axis=2)
    sums, squares = parts[:, 0:1, 0:width], parts[:, 1:2, 0:width]
    all_pixels, all_sums = jnp.sum(pixels, axis=0), jnp.sum(sums, axis=0)
    apart = sums / pixels - (all_sums / all_pixels)[None]
    all_squares = jnp.sum(squares + pixels * apart * apart, axis=0)
    behind = jnp.sum(parts[:, :, width:], axis=0)
    return jnp.concatenate([jnp.concatenate([all_sums, all_squares], axis=0), behind], axis=1)


def sync_groups(width, sizes):
    count = sizes[0] * sizes[1]
    if count > 64:
        return (16, count // 16)
    return sizes[::-1] if width > 1024 else (count,)


def sync_scratch(plan, sizes):
    out = []
    for rows, width in plan:
        for size in sync_groups(width, sizes):
            out += [pltpu.VMEM((rows, width), f32), pltpu.VMEM((size, rows, width), f32), dma, dma]
    return out


class Syncs:
    def __init__(self, place, buffers):
        self.place, self.buffers = place, buffers
        self.at = 0

    def take(self, width):
        stages = []
        stride = 1
        for size in sync_groups(width, (self.place.dp_size, self.place.mp_size)):
            digit = lax.rem(self.place.me // stride, size)
            stages.append((stride, size, digit, self.buffers[self.at : self.at + 4]))
            self.at += 4
            stride *= size
        return stages

    def start(self, stage, value=None):
        stride, size, digit, (src, slots, send, recv) = stage
        me = self.place.me
        if value is not None:
            src[...] = value

        def push(k):
            peer = me + (lax.rem(digit + k + 1, size) - digit) * stride
            remote(src, slots.at[digit], send, recv, self.place.at(peer)).start()

        loop(size - 1, push)
        pltpu.make_async_copy(src, slots.at[digit], recv).start()

    def finish(self, stage, moments_mode):
        stride, size, digit, (src, slots, send, recv) = stage
        pltpu.make_async_copy(slots, slots, recv).wait()
        rest = slots.at[pl.ds(0, size - 1)]
        pltpu.make_async_copy(rest, rest, send).wait()
        return merge(slots[...], moments_mode)

    def rest(self, stages, moments_mode, meanwhile=None):
        value = self.finish(stages[0], moments_mode)
        for stage in stages[1:]:
            self.start(stage, value)
            if meanwhile is not None:
                meanwhile()
            value = self.finish(stage, moments_mode)
        return value


def shifted(x, shift):
    if shift == 0:
        return x
    pixels = x.shape[0]
    column = lax.broadcasted_iota(jnp.int32, x.shape, 0) % breadth + shift
    inside = (column >= 0) & (column < breadth)
    return jnp.where(inside, pltpu.roll(x, (-shift) % pixels, 0), 0.0)


def row_scales(masks, first_row, which, width):
    row_of = lax.broadcasted_iota(jnp.int32, (chunk, width), 0) // breadth
    scale = jnp.zeros((chunk, width), f32)
    for k in range(chunk // breadth):
        scale = jnp.where(row_of == k, masks[first_row + k, which], scale)
    return scale


def masked_rows(part, masks, first_row, which):
    scaled = []
    for k in range(part.shape[0] // breadth):
        piece = part[breadth * k : breadth * (k + 1)].astype(f32)
        scaled.append((piece * masks[first_row + k, which]).astype(bf16))
    return jnp.concatenate(scaled, axis=0)


def tap_terms(off, masks, row, tap_row, tap_col):
    lane = lax.broadcasted_iota(jnp.int32, (breadth, 2 * breadth), 1)
    sub = lax.broadcasted_iota(jnp.int32, (breadth, 2 * breadth), 0)
    upper = lane >= breadth
    apart = jnp.where(upper, lane - breadth, lane) - sub
    tap, shift = 3 * tap_row + tap_col, 2 * tap_col - 2
    oy, ox = off[:, 2 * tap : 2 * tap + 1], off[:, 2 * tap + 1 : 2 * tap + 2]
    low, high = masks[row, 2 * tap_row], masks[row, 2 * tap_row + 1]
    down = jnp.where(upper, oy * high, (1.0 - oy) * low)
    across = jnp.where(apart == shift, 1.0 - ox, jnp.where(apart == shift + 1, ox, 0.0))
    down_slope = jnp.where(upper, high, -low)
    across_slope = jnp.where(apart == shift, -1.0, jnp.where(apart == shift + 1, 1.0, 0.0))
    return down, across, down_slope, across_slope


def nt_dot(a, b):
    return lax.dot_general(a, b, (((1,), (1,)), ((), ())), preferred_element_type=f32)


def tn_dot(a, b):
    return lax.dot_general(a, b, (((0,), (0,)), ((), ())), preferred_element_type=f32)


def nn_dot(a, b):
    return jnp.dot(a, b, preferred_element_type=f32)


class Outbox:
    def __init__(self, sems):
        self.sems, self.running = sems, {}

    def put(self, at, src, dst):
        copy = pltpu.make_async_copy(src, dst, self.sems.at[at])
        copy.start()
        self.running[at] = copy

    def settle(self, *which):
        for at in which or list(self.running):
            self.running.pop(at).wait()


def load_weight(full, dst, sem, part=0, parts=1):
    everything = pltpu.make_async_copy(dst, dst, sem)
    if len(full.shape) == 2:
        if part == 0:
            pltpu.make_async_copy(full, dst, sem).start()
        return everything
    block = full.shape[2]
    rows = block // parts
    for z in range(full.shape[0]):
        for y in range(2):
            src = full.at[z, y, pl.ds(part * rows, rows)]
            to = pl.ds((2 * z + y) * block + part * rows, rows)
            pltpu.make_async_copy(src, dst.at[to], sem).start()
    return everything


class Gather:
    units = ((0, 0, 1), (1, 0, 3), (1, 1, 3), (1, 2, 3), (2, 0, 1)) + (
        (3, 0, 1),
        (4, 0, 3),
        (4, 1, 3),
        (4, 2, 3),
        (5, 0, 1),
    )

    def __init__(self, place, r):
        self.place, self.fulls, self.sems = place, r.fulls, (r.gather_local, r.gather_send, r.gather_recv)
        self.shards = r.shards
        self.stage = [0] * len(self.units)
        self.running = [[] for _ in self.units]

    def cols(self, array, x_at, core_at):
        width = self.shards[array].shape[1]
        return pl.ds(pl.multiple_of((2 * x_at + core_at) * width, 128), width)

    def copies(self, unit, stage):
        array, part, parts = self.units[unit]
        place, full, shard = self.place, self.fulls[array], self.shards[array]
        high, z, y, x, core = place.high, place.z, place.y, place.x, place.core
        half = high // 2
        mine = self.cols(array, x, core)
        lower, upper = pl.ds(0, half), pl.ds(half, high - half)
        count = shard.shape[0] // parts
        rows = pl.ds(part * count, count)
        local, send, recv = self.sems
        if stage == 0:
            source, target = shard.at[rows], full.at[z, y, rows, mine]
            own = pltpu.make_async_copy(source, target, local.at[unit])
            return [own] + [
                remote(source, target, send.at[unit, k - 1], recv.at[unit, k - 1], place.z_peer(k))
                for k in range(1, high)
            ]
        if stage == 1:
            pairs = [
                (full.at[lower, y, rows, mine], place.x_peer()),
                (full.at[upper, y, rows, mine], place.y_peer()),
            ]
        elif stage == 2:
            pairs = [
                (full.at[lower, y, rows, self.cols(array, 0, core)], place.y_peer()),
                (full.at[lower, y, rows, self.cols(array, 1, core)], place.y_peer()),
                (full.at[upper, :, rows, mine], place.x_peer()),
            ]
        else:
            pairs = [
                (full.at[:, :, rows, self.cols(array, 0, core)], place.core_peer()),
                (full.at[:, :, rows, self.cols(array, 1, core)], place.core_peer()),
            ]
        base = high - 1 + [0, 0, 2, 5][stage]
        return [
            remote(ref, ref, send.at[unit, base + i], recv.at[unit, base + i], peer)
            for i, (ref, peer) in enumerate(pairs)
        ]

    def advance(self, *units):
        for unit in units if self.shards else ():
            for copy in self.running[unit]:
                copy.wait()
            self.running[unit] = []
            if self.stage[unit] < 4:
                self.running[unit] = self.copies(unit, self.stage[unit])
                for copy in self.running[unit]:
                    copy.start()
            self.stage[unit] += 1


class Scatter:
    def __init__(self, place, r, kind, use, result):
        self.place, self.use, self.result = place, use, result
        self.keep, self.from_core = r.keep[kind], r.from_core[kind]
        self.low, self.upper = r.from_low[kind], r.from_upper[kind]
        self.two, self.from_high = r.from_two[kind], r.from_high[kind]
        self.send, self.recv, self.free = r.scatter_send[kind], r.scatter_recv[kind], r.scatter_free[kind]
        self.staging, self.staging_sem = r.staging, r.staging_sem
        self.result_sem = r.result_sem.at[kind]
        self.rows, self.width = self.keep.shape[1], self.keep.shape[2]
        self.block = self.rows // place.dp_size
        self.tiles = self.rows // lane_block
        self.stage = 0
        self.running = []

    def cols(self, x_at, core_at):
        return pl.ds(pl.multiple_of((2 * x_at + core_at) * self.width, 128), self.width)

    def at(self, high, y):
        return pl.ds(pl.multiple_of((2 * high + y) * self.block, self.block), self.block)

    def to_core(self, t, i, src):
        rows = pl.ds(pl.multiple_of(t * lane_block, lane_block), lane_block)
        return remote(
            src,
            self.from_core.at[i, rows],
            self.send.at[2 * t + i],
            self.recv.at[2 * t + i],
            self.place.core_peer(),
        )

    def tile_copies(self, t):
        slot = lax.rem(t, 2)
        rows = pl.ds(pl.multiple_of(t * lane_block, lane_block), lane_block)
        core = self.place.core
        away = [self.to_core(t, i, self.staging.at[slot, :, self.cols(i, 1 - core)]) for i in (0, 1)]
        home = [
            pltpu.make_async_copy(
                self.staging.at[slot, :, self.cols(i, core)],
                self.keep.at[i, rows],
                self.staging_sem.at[slot, i],
            )
            for i in (0, 1)
        ]
        return away, home

    def settle_tile(self, t):
        away, home = self.tile_copies(t)
        for copy in away:
            copy.wait_send()
        for copy in home:
            copy.wait()

    def result_copy(self):
        place = self.place
        return pltpu.make_async_copy(
            self.keep.at[place.x, self.at(place.z, place.y)], self.result, self.result_sem
        )

    def begin(self):
        if self.use == 1:
            self.result_copy().wait()
            pl.semaphore_wait(self.free.at[0], 1)

    def fill(self, first, last, compute):
        def body(i):
            t = first + i

            @pl.when(i >= 2)
            def _():
                self.settle_tile(t - 2)

            compute(t, self.staging.at[lax.rem(t, 2)])
            away, home = self.tile_copies(t)
            for copy in away + home:
                copy.start()

        loop(last - first, body)
        for t in range(max(first, last - 2), last):
            self.settle_tile(t)

    def fill_by_columns(self, compute):
        core = self.place.core

        def away(i):
            self.staging[i] = compute(self.cols(i, 1 - core)).astype(bf16)
            self.to_core(0, i, self.staging.at[i]).start()

        def home(i):
            self.keep[i] = compute(self.cols(i, core)).astype(bf16)

        loop(2, away)
        loop(2, home)
        for i in (0, 1):
            self.to_core(0, i, self.staging.at[i]).wait_send()

    def copies(self, stage):
        place = self.place
        x, y, z, half = place.x, place.y, place.z, place.high // 2
        items = []
        if stage == 1:
            for i in (0, 1):
                for b in range(half):
                    items.append((self.keep.at[i, self.at(b, 1 - y)], self.low.at[i, b], place.y_peer()))
            upper = pl.ds(self.rows // 2, self.rows // 2)
            items.append((self.keep.at[1 - x, upper], self.upper, place.x_peer()))
        elif stage == 2:
            for b in range(half):
                items.append((self.keep.at[1 - x, self.at(b, y)], self.two.at[0, b], place.x_peer()))
                items.append(
                    (self.keep.at[x, self.at(half + b, 1 - y)], self.two.at[1, b], place.y_peer())
                )
        else:
            for k in range(1, place.high):
                there = self.at(lax.rem(z + k, place.high), y)
                items.append((self.keep.at[x, there], self.from_high.at[k - 1], place.z_peer(k)))
        base = 2 * self.tiles + [0, 0, 2 * half + 1, 4 * half + 1][stage]
        return [
            remote(src, dst, self.send.at[base + i], self.recv.at[base + i], peer)
            for i, (src, dst, peer) in enumerate(items)
        ]

    def add(self, target, extra):
        target[...] = target[...] + extra[...]

    def finish(self, stage):
        place = self.place
        x, y, z, half = place.x, place.y, place.z, place.high // 2
        if stage == 0:
            piece = 256
            for i in (0, 1):

                def body(k, i=i):
                    rows = slab(k, piece)
                    self.add(self.keep.at[i, rows], self.from_core.at[i, rows])

                loop(self.rows // piece, body)
            peers = [place.core_peer()]
        elif stage == 1:
            for b in range(half):
                for i in (0, 1):
                    self.add(self.keep.at[i, self.at(b, y)], self.low.at[i, b])
            piece = 256

            def body(k):
                rows = pl.ds(pl.multiple_of(self.rows // 2 + k * piece, piece), piece)
                self.add(self.keep.at[x, rows], self.upper.at[slab(k, piece)])

            loop(self.rows // 2 // piece, body)
            peers = [place.x_peer(), place.y_peer()]
        elif stage == 2:
            for b in range(half):
                self.add(self.keep.at[x, self.at(b, y)], self.two.at[0, b])
                self.add(self.keep.at[x, self.at(half + b, y)], self.two.at[1, b])
            peers = [place.x_peer(), place.y_peer()]
        else:
            total = self.keep[x, self.at(z, y)].astype(f32)
            for k in range(1, place.high):
                total = total + self.from_high[k - 1].astype(f32)
            self.keep[x, self.at(z, y)] = total.astype(bf16)
            self.result_copy().start()
            peers = [place.z_peer(k) for k in range(1, place.high)]
        if self.use == 0:
            for peer in peers:
                pl.semaphore_signal(self.free.at[stage], inc=1, device_id=peer, device_id_type=MESH)

    def advance(self):
        if self.stage > 3:
            return
        if self.stage == 0:
            for t in range(self.tiles):
                for i in (0, 1):
                    self.to_core(t, i, self.staging.at[0, :, self.cols(i, 0)] if self.tiles > 1 else self.staging.at[i]).wait_recv()
        for copy in self.running:
            copy.wait()
        self.finish(self.stage)
        self.stage += 1
        if self.stage <= 3:
            if self.use == 1:
                waits = [0, 2, 2, self.place.high - 1][self.stage]
                pl.semaphore_wait(self.free.at[self.stage], waits)
            self.running = self.copies(self.stage)
            for copy in self.running:
                copy.start()

    def drain(self):
        while self.stage <= 3:
            self.advance()

    def end(self):
        self.result_copy().wait()


class Whole:
    def __init__(self, r, result):
        self.staging, self.staging_sem, self.result = r.staging, r.staging_sem, result

    def begin(self):
        pass

    def fill(self, first, last, compute):
        def body(i):
            t = first + i
            compute(t, self.staging.at[0])
            rows = pl.ds(pl.multiple_of(t * lane_block, lane_block), lane_block)
            pltpu.sync_copy(self.staging.at[0], self.result.at[rows])

        loop(last - first, body)

    def fill_by_columns(self, compute):
        def body(i):
            lanes = pl.ds(pl.multiple_of(i * lane_block, lane_block), lane_block)
            self.staging[0] = compute(lanes).astype(bf16)
            pltpu.sync_copy(self.staging.at[0], self.result.at[:, lanes])

        loop(self.result.shape[1] // lane_block, body)

    def advance(self):
        pass

    drain = advance
    end = advance


class TableSum:
    def __init__(self, place, r):
        self.place, self.r = place, r
        self.each = r.table16.shape[0] // place.count
        self.stage, self.running = 0, []

    def part(self, mp, dp=None):
        quarter = self.each * self.place.dp_size
        if dp is None:
            return pl.ds(pl.multiple_of(mp * quarter, self.each), quarter)
        return pl.ds(pl.multiple_of(mp * quarter + dp * self.each, self.each), self.each)

    def copies(self, stage):
        place, r = self.place, self.r
        dp, mp, table, result = place.dp, place.mp, r.table16, r.offset_grad
        items = []
        over_mp = [lax.rem(mp + k, place.mp_size) for k in range(1, place.mp_size)]
        over_dp = [lax.rem(dp + k, place.dp_size) for k in range(1, place.dp_size)]
        if stage == 0:
            for k, to in enumerate(over_mp):
                items.append((table.at[self.part(to)], r.table_one.at[k], (dp, to)))
        elif stage == 1:
            for k, to in enumerate(over_dp):
                items.append((table.at[self.part(mp, to)], r.table_two.at[k], (to, mp)))
        elif stage == 2:
            mine = self.part(mp, dp)
            items = [(result.at[mine], result.at[mine], (to, mp)) for to in over_dp]
        else:
            mine = self.part(mp)
            items = [(result.at[mine], result.at[mine], (dp, to)) for to in over_mp]
        send, recv = r.table_send.at[stage], r.table_recv.at[stage]
        return [remote(a, b, send.at[i], recv.at[i], to) for i, (a, b, to) in enumerate(items)]

    def advance(self):
        place, r = self.place, self.r
        for copy in self.running:
            copy.wait()
        mine = self.part(place.mp), self.part(place.mp, place.dp)
        if self.stage == 0:
            r.table16[...] = r.table[...].astype(bf16)
        elif self.stage == 1:
            total = r.table16[mine[0], :].astype(f32)
            for k in range(place.mp_size - 1):
                total = total + r.table_one[k].astype(f32)
            r.table16[mine[0], :] = total.astype(bf16)
        elif self.stage == 2:
            total = r.table16[mine[1], :].astype(f32)
            for k in range(place.dp_size - 1):
                total = total + r.table_two[k].astype(f32)
            r.offset_grad[mine[1], :] = total.astype(bf16)
        self.running = self.copies(self.stage) if self.stage < 4 else []
        for copy in self.running:
            copy.start()
        self.stage += 1


def geometry(place, r):
    heights, widths, identity, row_width = r.heights, r.widths, r.identity, r.row_width
    images = heights.shape[1]
    rows = r.valid.shape[0] // breadth
    all_rows = rows * place.count
    group_rows = all_rows // 2 + rows // 2
    one, none = jnp.int32(1), jnp.int32(0)

    def row_facts(k):
        row = place.me * rows - halo_rows + k
        group = jnp.where(row >= group_rows, one, none)
        local = row - group * group_rows

        def image(j, carry):
            begin, number, found = carry
            end = begin + heights[group, j]
            number = number + jnp.where(local >= end, one, none)
            here = (local >= begin) & (local < end)
            return end, number, jnp.where(here, widths[group, j], found)

        _, number, found = lax.fori_loop(0, images, image, (none, none, none))
        inside = (row >= 0) & (row < all_rows)
        identity[k] = jnp.where(inside, group * images + number, -one)
        row_width[k] = jnp.where(inside, found, none)

    loop(rows + 2 * halo_rows, row_facts)

    def row_masks(k):
        centre = identity[k + halo_rows]
        for s in range(6):
            r.masks[k, s] = jnp.where(identity[k + s + 1] == centre, 1.0, 0.0).astype(f32)
        column = lax.broadcasted_iota(jnp.int32, (breadth, 128), 0)
        r.valid[slab(k, breadth), :] = jnp.where(column < row_width[k + halo_rows], 1.0, 0.0)

    loop(rows, row_masks)

    def pixels_of(first, last):
        def add(k, total):
            return total + row_width[k + halo_rows]

        return lax.fori_loop(first, last, add, none).astype(f32)

    def add_image(j, total):
        return total + heights[0, j] * widths[0, j] + heights[1, j] * widths[1, j]

    local = pixels_of(0, rows)
    r.counts[0] = local
    r.counts[1] = 1.0 / local
    r.counts[2] = 1.0 / lax.fori_loop(0, images, add_image, none).astype(f32)
    r.counts[3] = 1.0 / pixels_of(0, chunk // breadth)
    r.counts[4] = 1.0 / pixels_of(chunk // breadth, 2 * chunk // breadth)

    count = r.offset_bias.shape[0]
    width = r.offset_weight.shape[1]
    lane = lax.broadcasted_iota(jnp.int32, (1, 128), 1)
    bias = jnp.zeros((1, 128), f32)
    for j in range(count):
        bias = jnp.where(lane == j, r.offset_bias[j], bias)
    r.bias_row[...] = bias
    down = lax.broadcasted_iota(jnp.int32, (count, 128), 0)
    across = lax.broadcasted_iota(jnp.int32, (count, 128), 1)
    for tap_row in range(3):
        total = jnp.zeros((width, 128), f32)
        for tap_col in range(3):
            place_at = jnp.where(across == down + 32 * tap_col, 1.0, 0.0).astype(bf16)
            columns = pl.ds((3 * tap_row + tap_col) * width, width)
            total = total + tn_dot(r.weight_offset[:, columns], place_at)
        r.offset_weight[tap_row] = total.astype(bf16)


def forward_part(place, syncs, box, r):
    gather = Gather(place, r)
    valid, masks, counts = r.valid, r.masks, r.counts
    third, field, hidden, pool = r.grad, r.field, r.hidden, r.pool
    pixels, wide = third.shape
    width = hidden.shape[1]
    halo = halo_rows * breadth
    chunks = pixels // chunk
    first = r.small.at[pl.ds(halo, pixels)]

    def load(array, dst, sem, part=0, parts=1):
        return load_weight(r.fulls[array], dst, r.load_sem.at[sem], part, parts)

    def gather_sums(i, got, scale):
        block_width = got.shape[1]
        sums, centre = r.sums.at[:, :, 0:block_width], r.centre.at[:, 0:block_width]
        mask = wide_valid(valid, slab(i, chunk), block_width)
        if scale is not None:
            centre[...] = jnp.sum(fold8(got * mask), axis=0, keepdims=True) * scale
            sums[...] = jnp.zeros((2, 8, block_width), f32)
        apart = (got - centre[...]) * mask
        sums[0] = sums[0] + fold8(apart)
        sums[1] = sums[1] + fold8(apart * apart)

    def over_chunks(target, compute, between=None):
        def body(i, scale=None):
            got = compute(i)
            target[slab(i, chunk), :] = got
            gather_sums(i, got, scale)

        if between is None:
            body(0, counts[3])
            loop(chunks - 1, lambda i: body(i + 1))
        else:
            body(1, counts[4])
            loop(chunks - 3, lambda i: body(i + 2))
            between()
            loop(2, lambda i: body(i * (chunks - 1)))

    def moments(block_width, rstd, mean, meanwhile=None, early=None):
        stages = syncs.take(block_width + 128)
        src = stages[0][3][0]
        first_sum = jnp.sum(r.sums[0, :, 0:block_width], axis=0, keepdims=True)
        second_sum = jnp.sum(r.sums[1, :, 0:block_width], axis=0, keepdims=True)
        src[0:1, 0:block_width] = first_sum + r.centre[:, 0:block_width] * counts[0]
        src[1:2, 0:block_width] = second_sum - first_sum * first_sum * counts[1]
        src[:, block_width:] = jnp.full((2, 128), counts[0], f32)
        syncs.start(stages[0])
        if early is not None:
            early()
        merged = syncs.rest(stages, True, meanwhile)
        mean[...] = merged[0:1, 0:block_width] * counts[2]
        spread = jnp.maximum(merged[1:2, 0:block_width], 0.0) * counts[2]
        rstd[...] = lax.rsqrt(spread + norm_eps)

    def activate(norm, hat, target, target_row):
        mean, rstd = r.mean_narrow, r.rstd_narrow.at[norm : norm + 1, :]
        gain, bias = mid_row(r.mid_gain, norm), mid_row(r.mid_bias, norm)

        def body(i):
            at = slab(i, strip)
            normed = (first[at, :] - mean[...]) * rstd[...]
            hat[at, :] = normed.astype(bf16)
            act = gelu_of(normed * gain[...] + bias[...]) * wide_valid(valid, at, width)
            rows = pl.ds(pl.multiple_of(target_row + i * strip, strip), strip)
            target[rows, :] = act.astype(bf16)

        loop(pixels // strip, body)

    def narrow_moments(norm, early=None):
        moments(width, r.rstd_narrow.at[norm : norm + 1, :], r.mean_narrow, None, early)

    def project(lhs, weight, target):
        over_chunks(target, lambda i: nn_dot(lhs[slab(i, chunk), :], weight[...]))

    def halo_copies(block):
        send, recv = r.halo_send.at[block], r.halo_recv.at[block]
        last_rows, below = field.at[pl.ds(pixels, halo)], field.at[pl.ds(pixels + halo, halo)]
        first_rows, above = field.at[pl.ds(halo, halo)], field.at[pl.ds(0, halo)]
        return [
            remote(last_rows, above, send.at[0], recv.at[0], place.next(1)),
            remote(first_rows, below, send.at[1], recv.at[1], place.next(-1)),
        ]

    samples = [r.inputs, r.hat3, pool]

    def sample_at(tap, i):
        return samples[tap // 4], slab(i, chunk), pl.ds(tap % 4 * width, width)

    def sample_chunk(i):
        base = halo + i * chunk
        first_row = i * (chunk // breadth)
        total = jnp.zeros((chunk, 128), f32)
        for tap_row in range(3):
            start = pl.multiple_of(base + (2 * tap_row - 2) * breadth, breadth)
            part = nn_dot(field[pl.ds(start, chunk), :], r.offset_weight[tap_row])
            total = total + part * row_scales(masks, first_row, 2 * tap_row, 128)
        left = shifted(total, -2)
        middle = pltpu.roll(total, 128 - 32, 1)
        right = pltpu.roll(shifted(total, 2), 128 - 64, 1)
        lane = lax.broadcasted_iota(jnp.int32, total.shape, 1)
        raw = jnp.where(lane < 32, left + middle + right, 0.0) + r.bias_row[...]
        tanh_raw = jnp.tanh(raw)
        r.tanh_raw[slab(i, chunk), :] = tanh_raw
        r.off[...] = 0.5 + 0.45 * tanh_raw

        def one_row(k):
            off = r.off[slab(k, breadth), :]
            for tap_row in range(3):
                weights = []
                for tap_col in range(3):
                    down, across, _, _ = tap_terms(off, masks, first_row + k, tap_row, tap_col)
                    weights.append((down * across).astype(bf16))
                start = pl.multiple_of(base + (k + 2 * tap_row - 2) * breadth, breadth)
                got = nn_dot(jnp.concatenate(weights, axis=0), field[pl.ds(start, 2 * breadth), :])
                for tap_col in range(3):
                    ref, _, lanes = sample_at(3 * tap_row + tap_col, i)
                    rows = pl.ds(pl.multiple_of(i * chunk + k * breadth, breadth), breadth)
                    piece = got[breadth * tap_col : breadth * (tap_col + 1)]
                    ref[rows, lanes] = piece.astype(bf16)

        loop(chunk // breadth // 2, lambda k: [one_row(2 * k), one_row(2 * k + 1)])

    def mid_deformable(i):
        rows = slab(i, chunk)
        samp = jnp.concatenate([r.inputs[rows, :], r.hat3[rows, :], pool[rows, :]], axis=1)
        return nn_dot(samp, r.w_mid[...])

    def samp_copies():
        copies = []
        for tap in range(9):
            ref, _, lanes = sample_at(tap, 0)
            src = ref.at[pl.ds(0, pixels), lanes]
            copies.append(
                pltpu.make_async_copy(src, r.samp_out.at[pl.ds(tap * pixels, pixels)], r.samp_sem.at[0])
            )
        return copies

    def mid_plain(i):
        lhs = []
        for tap_row in range(3):
            start = pl.multiple_of(halo + i * chunk + (2 * tap_row - 2) * breadth, breadth)
            part = field[pl.ds(start, chunk), :]
            if tap_row != 1:
                part = masked_rows(part, masks, i * (chunk // breadth), 2 * tap_row)
            lhs.append(part)
        total = None
        for tap_col in range(3):
            partial_sum = None
            for tap_row in range(3):
                weight = r.w_mid[pl.ds((3 * tap_row + tap_col) * width, width), :]
                part = nn_dot(lhs[tap_row], weight)
                partial_sum = part if partial_sum is None else partial_sum + part
            partial_sum = shifted(partial_sum, 2 * tap_col - 2)
            total = partial_sum if total is None else total + partial_sum
        return total

    def finish_block(block, inputs, result):
        gain, bias = r.out_gain.at[block : block + 1, :], r.out_bias.at[block : block + 1, :]
        mean, rstd = r.mean_wide, r.rstd_wide.at[block : block + 1, :]

        def body(i):
            at = slab(i, strip)
            mask = wide_valid(valid, at, lane_block)
            for j in range(wide // lane_block):
                lanes = pl.ds(j * lane_block, lane_block)
                normed = (third[at, lanes] - mean[:, lanes]) * rstd[:, lanes]
                r.hat3[at, lanes] = normed.astype(bf16)
                pre = inputs[at, lanes].astype(f32) + (normed * gain[:, lanes] + bias[:, lanes])
                result[at, lanes] = (mask * gelu_of(pre)).astype(bf16)

        loop(pixels // strip, body)

    def wide_moments(block, meanwhile=None):
        moments(wide, r.rstd_wide.at[block : block + 1, :], r.mean_wide, meanwhile)

    place.greet_all()
    gather.advance(0, 1, 2, 3)
    box.put(0, r.image, r.wide_act)
    geometry(place, r)
    gather.advance(0)
    gather.advance(0, 1, 2)
    gather.advance(0, 3, 4)
    gather.advance(0)
    load(0, r.w_in, 0).wait()
    box.settle(0)
    project(r.wide_act, r.w_in, first)
    narrow_moments(0, lambda: gather.advance(1, 2))
    activate(0, r.da, field, halo)
    edges = halo_copies(0)
    for copy in edges:
        copy.start()
    gather.advance(3, 6, 7, 8, 5)
    gather.advance(1)
    box.put(1, r.da, r.hat1_out)
    loop(chunks - 2, lambda i: sample_chunk(i + 1))
    gather.advance(2, 1)
    load(1, r.w_mid, 1, 0, 3)
    for copy in edges:
        copy.wait()
    gather.advance(4, 3)
    box.put(2, field, r.field_out)
    loop(2, lambda i: sample_chunk(i * (chunks - 1)))
    gather.advance(2, 3, 4)
    load(1, r.w_mid, 1, 1, 3)
    loaded = load(1, r.w_mid, 1, 2, 3)
    samp_out = samp_copies()
    for copy in samp_out:
        copy.start()
    loaded.wait()
    over_chunks(first, mid_deformable)
    narrow_moments(1, lambda: gather.advance(4, 6, 7, 8, 5, 9))
    gather.advance(4)
    loaded = load(2, r.w_out, 2)
    activate(1, r.hat2, hidden, 0)
    box.put(3, r.hat2, r.hat2_out)
    box.put(4, hidden, r.hidden_out)
    for copy in samp_out:
        copy.wait()
    loaded.wait()
    project(hidden, r.w_out, third)
    wide_moments(0, lambda: gather.advance(5, 6, 7, 8))
    finish_block(0, r.wide_act, r.inputs)
    box.put(0, r.cotangent, r.wide_act)
    box.put(5, r.hat3, r.hat3_out)
    gather.advance(5)
    gather.advance(5)
    load(3, r.w_in, 0).wait()
    box.settle(1, 2)
    project(r.inputs, r.w_in, first)
    narrow_moments(2, lambda: gather.advance(6, 7, 8))
    gather.advance(6, 7, 8)
    load(4, r.w_mid, 1, 0, 3)
    load(4, r.w_mid, 1, 1, 3)
    loaded = load(4, r.w_mid, 1, 2, 3)
    activate(2, r.da, field, halo)
    edges = halo_copies(1)
    for copy in edges:
        copy.start()
    gather.advance(9)

    def edges_here():
        for copy in edges:
            copy.wait()

    loaded.wait()
    over_chunks(first, mid_plain, edges_here)
    narrow_moments(3, lambda: gather.advance(9))
    gather.advance(9)
    gather.advance(9)
    loaded_out = load(5, r.w_out, 2)
    box.settle(3, 4)
    activate(3, r.hat2, hidden, 0)
    loaded_out.wait()
    project(hidden, r.w_out, third)
    wide_moments(1)
    box.settle(0, 5)


def backward_part(place, syncs, box, in_kernel, r):
    valid, masks, counts = r.valid, r.masks, r.counts
    grad, small, inputs, hat3, wide_act = r.grad, r.small, r.inputs, r.hat3, r.wide_act
    pixels, wide, width = grad.shape[0], grad.shape[1], small.shape[1]
    halo = halo_rows * breadth
    chunks, chunk_rows = pixels // chunk, chunk // breadth
    per_pixel = counts[2]
    own = pl.ds(halo, pixels)
    kinds = [0, 1, 2]

    def scatter(kind, use):
        result = r.grads[3 * use + kind]
        if in_kernel:
            return Scatter(place, r, kind, use, result)
        return Whole(r, result)

    def weight(array, dst, sem):
        box.running[sem] = load_weight(r.fulls[array], dst, r.box_sem.at[sem])

    def open_sync(terms, block_width, last_row=None):
        stages = syncs.take(block_width)
        src = stages[0][3][0]
        strip_sums(pixels, block_width, terms, src, [0, 1])
        if last_row is not None:
            src[2:3, :] = jnp.zeros((1, block_width), f32)
            src[2:3, 0:128] = last_row
        syncs.start(stages[0])
        return stages

    def pre_back(block, upstream, image):
        gain, bias = r.out_gain.at[block : block + 1, :], r.out_bias.at[block : block + 1, :]

        def terms(at, lanes):
            hat = hat3[at, lanes].astype(f32)
            pre = image[at, lanes].astype(f32) + (hat * gain[:, lanes] + bias[:, lanes])
            slope = gelu_slope(pre) * wide_valid(valid, at, lane_block)
            d = upstream[at, lanes].astype(f32) * slope
            grad[at, lanes] = d
            return d, d * hat

        return open_sync(terms, wide)

    def finish_and_back():
        gain, bias = r.out_gain.at[1:2, :], r.out_bias.at[1:2, :]
        mean, rstd = r.mean_wide, r.rstd_wide.at[1:2, :]

        def terms(at, lanes):
            normed = (grad[at, lanes] - mean[:, lanes]) * rstd[:, lanes]
            hat3[at, lanes] = normed.astype(bf16)
            pre = inputs[at, lanes].astype(f32) + (normed * gain[:, lanes] + bias[:, lanes])
            half, slope = gelu_pair(pre)
            mask = wide_valid(valid, at, lane_block)
            d = wide_act[at, lanes].astype(f32) * (slope * mask)
            wide_act[at, lanes] = (pre * (half * mask)).astype(bf16)
            grad[at, lanes] = d
            return d, d * normed

        return open_sync(terms, wide)

    def last_norm_back(block):
        sums, rstd = r.wide_sums.at[block], r.rstd_wide.at[block : block + 1, :]
        gain = r.out_gain.at[block : block + 1, :]

        def body(i):
            at = slab(i, strip)
            mask = wide_valid(valid, at, lane_block)
            for j in range(wide // lane_block):
                lanes = pl.ds(j * lane_block, lane_block)
                hat = hat3[at, lanes].astype(f32)
                inner = grad[at, lanes] - sums[0:1, lanes] * per_pixel
                inner = inner - hat * (sums[1:2, lanes] * per_pixel)
                scaled = mask * (gain[:, lanes] * rstd[:, lanes]) * inner
                wide_act[at, lanes] = scaled.astype(bf16)

        loop(pixels // strip, body)

    def act_back(norm, hat):
        gain, bias = mid_row(r.mid_gain, norm), mid_row(r.mid_bias, norm)

        def terms(at, lanes):
            normed = hat[at, lanes].astype(f32)
            slope = gelu_slope(normed * gain[:, lanes] + bias[:, lanes])
            rows = pl.ds(pl.multiple_of(halo + at.start, strip), strip)
            d = small[rows, lanes] * slope * wide_valid(valid, at, lane_block)
            small[rows, lanes] = d
            return d, d * normed

        return terms

    def inner_norm_back(norm, hat, target, target_row):
        sums, rstd = r.narrow_sums.at[norm], r.rstd_narrow.at[norm : norm + 1, :]
        gain = mid_row(r.mid_gain, norm)

        def body(i):
            at = slab(i, strip)
            rows = pl.ds(pl.multiple_of(halo + i * strip, strip), strip)
            inner = small[rows, :] - sums[0:1, :] * per_pixel
            inner = inner - hat[at, :].astype(f32) * (sums[1:2, :] * per_pixel)
            scaled = wide_valid(valid, at, width) * (gain[...] * rstd[...]) * inner
            target[pl.ds(pl.multiple_of(target_row + i * strip, strip), strip), :] = scaled.astype(bf16)

        loop(pixels // strip, body)

    def out_back(block):
        def body(i):
            rows = pl.ds(pl.multiple_of(halo + i * chunk, breadth), chunk)
            small[rows, :] = nt_dot(wide_act[slab(i, chunk), :], r.w_out[...])

        loop(chunks, body)
        return open_sync(act_back(2 * block + 1, r.hat2), width)

    def out_grad(target):
        target.begin()
        target.fill_by_columns(lambda lanes: tn_dot(r.hidden[...], wide_act[:, lanes]))

    def in_grad(target):
        target.begin()

        def compute(t, ref):
            lanes = pl.ds(pl.multiple_of(t * lane_block, lane_block), lane_block)
            ref[...] = tn_dot(inputs[:, lanes], r.da[...]).astype(bf16)

        target.fill(0, wide // lane_block, compute)

    def in_back(i):
        at = slab(i, chunk)
        grad[at, :] = grad[at, :] + nt_dot(r.da[at, :], r.w_in[...])

    def neighbours(before_src, before_dst, after_src, after_dst, which):
        send, recv = r.edge_send.at[which], r.edge_recv.at[which]
        return [
            remote(after_src, after_dst, send.at[0], recv.at[0], place.next(1)),
            remote(before_src, before_dst, send.at[1], recv.at[1], place.next(-1)),
        ]

    out_b, mid_b, in_b = [scatter(kind, 0) for kind in kinds]
    stages = finish_and_back()
    box.put(6, wide_act, r.image_out)
    r.wide_sums[1] = syncs.rest(stages, False)
    box.settle(6)
    last_norm_back(1)
    box.put(1, r.hat3_out, hat3)
    stages = out_back(1)
    weight(2, r.w_out, 3)
    out_grad(out_b)
    box.put(2, r.image, wide_act)
    box.put(5, r.hidden_out, r.hidden)
    r.narrow_sums[3] = syncs.rest(stages, False)

    pool, side = r.pool, 2 * breadth
    span = pixels + 2 * side
    centre = 2 * span
    inner_norm_back(3, r.hat2, pool, centre + side)
    box.put(4, r.hat2_out, r.hat2)
    edges = neighbours(
        pool.at[pl.ds(centre + side, side)],
        pool.at[pl.ds(centre + side + pixels, side)],
        pool.at[pl.ds(centre + pixels, side)],
        pool.at[pl.ds(centre, side)],
        0,
    )
    for copy in edges:
        copy.start()

    def shift_row(row):
        at = pl.ds(pl.multiple_of(centre + row * breadth, breadth), breadth)
        value = pool[at, :].astype(f32)
        for slot, amount in ((0, 2), (1, -2)):
            rows = pl.ds(pl.multiple_of(slot * span + row * breadth, breadth), breadth)
            pool[rows, :] = shifted(value, amount).astype(bf16)

    loop(pixels // breadth, lambda row: shift_row(row + 2))
    out_b.advance()
    for copy in edges:
        copy.wait()
    loop(2, shift_row)
    loop(2, lambda row: shift_row(row + 2 + pixels // breadth))
    slot_of = (0, 2, 1)

    def mid_back_plain(i):
        first_row = i * chunk_rows
        total = None
        for tap_row in range(3):
            for tap_col in range(3):
                start = slot_of[tap_col] * span + (4 - 2 * tap_row) * breadth + i * chunk
                part = pool[pl.ds(pl.multiple_of(start, breadth), chunk), :]
                if tap_row != 1:
                    part = masked_rows(part, masks, first_row, 4 - 2 * tap_row)
                tap = pl.ds((3 * tap_row + tap_col) * width, width)
                term = nt_dot(part, r.w_mid[tap, :])
                total = term if total is None else total + term
        rows = pl.ds(pl.multiple_of(halo + i * chunk, breadth), chunk)
        small[rows, :] = total

    loop(chunks, mid_back_plain)
    weight(1, r.w_mid, 7)
    stages = open_sync(act_back(2, r.da), width)
    out_b.advance()
    mid_b.begin()
    shifted_rows = 3 * span

    def mid_grad_plain(t, ref):
        tap_row, tap_col = t // 3, lax.rem(t, 3)
        slot = jnp.where(tap_col == 0, 0, jnp.where(tap_col == 1, 2, 1))

        def copy_rows(i):
            start = slot * span + (4 - 2 * tap_row) * breadth + i * chunk
            part = pool[pl.ds(pl.multiple_of(start, breadth), chunk), :]
            rows = pl.ds(pl.multiple_of(shifted_rows + i * chunk, breadth), chunk)
            pool[rows, :] = masked_rows(part, masks, i * chunk_rows, 4 - 2 * tap_row)

        loop(chunks, copy_rows)
        ref[...] = tn_dot(r.field[own, :], pool[pl.ds(shifted_rows, pixels), :]).astype(bf16)

    mid_b.fill(0, 9, mid_grad_plain)
    out_b.advance()
    r.narrow_sums[2] = syncs.rest(stages, False)
    mid_b.advance()
    inner_norm_back(2, r.da, r.da, 0)
    box.put(6, r.field_out, r.field)
    loop(chunks, in_back)
    weight(0, r.w_in, 8)

    out_a, mid_a, in_a = [scatter(kind, 1) for kind in kinds]
    box.settle(1, 2)
    stages = pre_back(0, grad, wide_act)
    out_b.drain()
    in_grad(in_b)
    box.put(0, r.image, inputs)
    r.wide_sums[0] = syncs.rest(stages, False, mid_b.advance)
    last_norm_back(0)
    box.settle(3, 4)
    stages = out_back(0)
    box.settle(5)
    out_grad(out_a)
    mid_b.advance()
    in_b.advance()
    r.narrow_sums[1] = syncs.rest(stages, False)
    inner_norm_back(1, r.hat2, r.da, 0)
    out_a.advance()
    box.put(5, r.hat1_out, r.hidden)
    slots = 9 * chunk

    def samp_load(t):
        slot = pl.ds(pl.multiple_of(slots + lax.rem(t, 2) * pixels, breadth), pixels)
        src = r.samp_out.at[pl.ds(pl.multiple_of(t * pixels, breadth), pixels)]
        pltpu.make_async_copy(src, pool.at[slot], r.samp_sem.at[lax.rem(t, 2)]).start()

    def samp_settle(t):
        rows = pool.at[pl.ds(pl.multiple_of(slots + lax.rem(t, 2) * pixels, breadth), pixels)]
        pltpu.make_async_copy(rows, rows, r.samp_sem.at[lax.rem(t, 2)]).wait()

    def mid_grad_deformable(t, ref):
        @pl.when(t < 8)
        def _():
            samp_load(t + 1)

        samp_settle(t)
        slot = pl.ds(pl.multiple_of(slots + lax.rem(t, 2) * pixels, breadth), pixels)
        ref[...] = tn_dot(pool[slot, :], r.da[...]).astype(bf16)

    box.settle(6, 7)

    def clear(i):
        small[slab(i, breadth), :] = jnp.zeros((breadth, width), f32)

    loop((pixels + 2 * halo) // breadth, clear)
    table = r.table
    table[...] = jnp.zeros_like(table)
    r.draw_sum[...] = jnp.zeros_like(r.draw_sum)

    def mid_back_deformable(i):
        first_row = i * chunk_rows
        part = r.da[slab(i, chunk), :]
        for tap_row in range(3):
            for tap_col in range(3):
                tap = pl.ds((3 * tap_row + tap_col) * width, width)
                dsamp = nt_dot(part, r.w_mid[tap, :]).astype(bf16)
                for k in range(chunk_rows):
                    start = ((tap_row * chunk_rows + k) * 3 + tap_col) * breadth
                    pool[pl.ds(start, breadth), :] = dsamp[breadth * k : breadth * (k + 1)]
        th = r.tanh_raw[slab(i, chunk), :]
        r.off[...] = 0.5 + 0.45 * th
        lane = lax.broadcasted_iota(jnp.int32, (breadth, 128), 1)

        def one_row(k):
            off = r.off[slab(k, breadth), :]
            doff = jnp.zeros((breadth, 128), f32)
            for tap_row in range(3):
                start = (tap_row * chunk_rows + k) * 3 * breadth
                dsamp = pool[pl.ds(pl.multiple_of(start, breadth), 3 * breadth), :]
                start = halo + i * chunk + (k + 2 * tap_row - 2) * breadth
                rows = pl.ds(pl.multiple_of(start, breadth), 2 * breadth)
                dots = nt_dot(dsamp, r.field[rows, :])
                weights = []
                for tap_col in range(3):
                    terms = tap_terms(off, masks, first_row + k, tap_row, tap_col)
                    down, across, down_slope, across_slope = terms
                    weights.append((down * across).astype(bf16))
                    part = dots[breadth * tap_col : breadth * (tap_col + 1)]
                    doy = jnp.sum(part * (across * down_slope), axis=1, keepdims=True)
                    dox = jnp.sum(part * (across_slope * down), axis=1, keepdims=True)
                    tap = 3 * tap_row + tap_col
                    doff = jnp.where(lane == 2 * tap, doy, jnp.where(lane == 2 * tap + 1, dox, doff))
                small[rows, :] = small[rows, :] + tn_dot(jnp.concatenate(weights, axis=0), dsamp)
            th_row = r.tanh_raw[pl.ds(pl.multiple_of(i * chunk + k * breadth, breadth), breadth), :]
            draw = (0.45 * (1.0 - th_row * th_row) * doff).astype(bf16).astype(f32)
            r.off[slab(k, breadth), :] = draw
            r.draw_sum[...] = r.draw_sum[...] + fold8(draw)

        loop(chunk_rows // 2, lambda k: [one_row(2 * k), one_row(2 * k + 1)])
        draw = r.off[...]
        spread = shifted(draw, 2) + pltpu.roll(draw, 32, 1) + pltpu.roll(shifted(draw, -2), 64, 1)
        for tap_row in range(3):
            part = (spread * row_scales(masks, first_row, 2 * tap_row, 128)).astype(bf16)
            start = halo + i * chunk + (2 * tap_row - 2) * breadth
            rows = pl.ds(pl.multiple_of(start, breadth), chunk)
            small[rows, :] = small[rows, :] + nt_dot(part, r.offset_weight[tap_row])
            to = pl.ds(tap_row * width, width)
            table[to, :] = table[to, :] + tn_dot(r.field[rows, :], part)

    mid_back_deformable(0)
    mid_b.drain()
    in_b.advance()
    out_a.advance()
    mid_a.begin()
    samp_load(0)
    mid_a.fill(0, 9, mid_grad_deformable)
    in_b.advance()
    out_a.advance()
    mid_back_deformable(chunks - 1)
    rims = [r.staging.at[i, pl.ds(0, halo)] for i in (0, 1)]
    rims[0][...] = small[pl.ds(0, halo), :].astype(bf16)
    rims[1][...] = small[pl.ds(halo + pixels, halo), :].astype(bf16)
    edges = neighbours(rims[0], r.got_rims.at[0], rims[1], r.got_rims.at[1], 1)
    for copy in edges:
        copy.start()
    mid_a.advance()
    loop(chunks - 2, lambda i: mid_back_deformable(i + 1))
    in_b.drain()
    out_a.drain()

    offset_sum = TableSum(place, r)
    for copy in edges:
        copy.wait()
    first_rows, last_rows = pl.ds(halo, halo), pl.ds(pixels, halo)
    small[first_rows, :] = small[first_rows, :] + r.got_rims[1].astype(f32)
    small[last_rows, :] = small[last_rows, :] + r.got_rims[0].astype(f32)
    box.settle(5)
    draw_sum = jnp.sum(r.draw_sum[...], axis=0, keepdims=True)
    stages = open_sync(act_back(0, r.hidden), width, draw_sum)
    offset_sum.advance()
    mid_a.advance()

    merged = syncs.rest(stages, False)
    r.narrow_sums[0] = merged[0:2]
    r.bias_sum[...] = merged[2:3, 0:128]
    inner_norm_back(0, r.hidden, r.da, 0)
    box.settle(0)
    mid_a.advance()
    offset_sum.advance()
    in_grad(in_a)
    box.settle(8)
    for i in range(chunks):
        at = slab(i, chunk)
        wide_act[at, :] = (grad[at, :] + nt_dot(r.da[at, :], r.w_in[...])).astype(bf16)
        box.put(9 + i, wide_act.at[at], r.image_grad.at[at])
        if i == 0:
            in_a.advance()
    offset_sum.advance()
    mid_a.drain()
    in_a.advance()
    offset_sum.advance()
    in_a.drain()
    offset_sum.advance()
    box.settle()
    for one in (out_a, mid_a, in_a):
        one.end()


def whole_pass(sizes, in_kernel, r):
    place = Place(*sizes)
    syncs = Syncs(place, r.syncs)
    box = Outbox(r.box_sem)
    forward_part(place, syncs, box, r)
    backward_part(place, syncs, box, in_kernel, r)


def run_kernel(image, cotangent, heights, widths, shards, offset_weight, offset_bias, norms, sizes):
    pixels, wide = image.shape
    width = shards[0].shape[1] * sizes[1]
    taps = 9 * width
    count, high = sizes[0] * sizes[1], sizes[0] // 2
    half = high // 2
    rows = pixels // breadth
    ext_pixels = pixels + 2 * halo_rows * breadth
    each = 16 * (-(-3 * width // (16 * count)))
    in_kernel = all(s.shape[0] % 16 == 0 for s in shards) and shards[1].shape[0] % 48 == 0
    kinds = [(width, wide), (taps, width), (wide, width)]
    owned = [(down // sizes[0], across // sizes[1]) for down, across in kinds]
    ins = dict(
        image=image,
        cotangent=cotangent,
        heights=heights,
        widths=widths,
        weight_offset=offset_weight,
        offset_bias=offset_bias,
        mid_gain=norms[0],
        mid_bias=norms[1],
        out_gain=norms[2],
        out_bias=norms[3],
        shards=list(shards) if in_kernel else [],
    )
    narrow, broad = shape((pixels, width), bf16), shape((pixels, wide), bf16)
    outs = dict(
        hat1_out=narrow,
        hat2_out=narrow,
        hidden_out=narrow,
        field_out=shape((ext_pixels, width), bf16),
        hat3_out=broad,
        image_out=broad,
        samp_out=shape((9 * pixels, width), bf16),
        image_grad=broad,
        narrow_sums=shape((4, 2, width), f32),
        wide_sums=shape((2, 2, wide), f32),
        offset_grad=shape((count * each, 128), bf16),
        bias_sum=shape((1, 128), f32),
    )
    in_specs = dict(
        image=anywhere,
        cotangent=anywhere,
        heights=smem,
        widths=smem,
        offset_bias=smem,
        shards=anywhere,
        fulls=anywhere,
    )
    out_specs = dict(narrow_sums=vmem, wide_sums=vmem, offset_grad=vmem, bias_sum=vmem)
    scatter = dict()
    if in_kernel:
        outs.update(
            fulls=[shape((high, 2, s.shape[0], s.shape[1] * sizes[1]), bf16) for s in shards],
            grads=[shape(o, bf16) for o in owned] * 2,
        )
        halves = [(2, down, o[1]) for (down, _), o in zip(kinds, owned)]
        sems = [dma((2 * (down // lane_block) + 4 * half + high,)) for down, _ in kinds]
        scatter.update(
            keep=[pltpu.VMEM(h, bf16) for h in halves],
            from_core=[pltpu.VMEM(h, bf16) for h in halves],
            from_low=[pltpu.VMEM((2, half) + o, bf16) for o in owned],
            from_upper=[pltpu.VMEM((h[1] // 2, h[2]), bf16) for h in halves],
            from_two=[pltpu.VMEM((2, half) + o, bf16) for o in owned],
            from_high=[pltpu.VMEM((high - 1,) + o, bf16) for o in owned],
            result_sem=dma((3,)),
            scatter_free=[pltpu.SemaphoreType.REGULAR((4,))] * 3,
            scatter_send=sems,
            scatter_recv=sems,
        )
    else:
        fulls = [lax.all_gather(s, "mp", axis=1, tiled=True) for s in shards]
        ins.update(fulls=[lax.all_gather(s, "dp", axis=0, tiled=True) for s in fulls])
        outs.update(grads=[shape(k, bf16) for k in kinds] * 2)
    plan = [(2, width + 128), (2, width + 128), (2, wide + 128)] * 2
    plan += [(2, wide), (2, width), (2, width), (2, wide), (2, width), (3, width)]
    span = pixels + 4 * breadth
    pool_rows = max(3 * span + pixels, 9 * chunk + 2 * pixels)
    scratch = dict(
        grad=pltpu.VMEM((pixels, wide), f32),
        inputs=pltpu.VMEM((pixels, wide), bf16),
        hat3=pltpu.VMEM((pixels, wide), bf16),
        wide_act=pltpu.VMEM((pixels, wide), bf16),
        w_in=pltpu.VMEM((wide, width), bf16),
        w_mid=pltpu.VMEM((taps, width), bf16),
        w_out=pltpu.VMEM((width, wide), bf16),
        small=pltpu.VMEM((ext_pixels, width), f32),
        hat2=pltpu.VMEM((pixels, width), bf16),
        hidden=pltpu.VMEM((pixels, width), bf16),
        da=pltpu.VMEM((pixels, width), bf16),
        field=pltpu.VMEM((ext_pixels, width), bf16),
        pool=pltpu.VMEM((pool_rows, width), bf16),
        off=pltpu.VMEM((chunk, 128), f32),
        tanh_raw=pltpu.VMEM((pixels, 128), f32),
        draw_sum=pltpu.VMEM((8, 128), f32),
        table=pltpu.VMEM((count * each, 128), f32),
        table16=pltpu.VMEM((count * each, 128), bf16),
        table_one=pltpu.VMEM((sizes[1] - 1, sizes[0] * each, 128), bf16),
        table_two=pltpu.VMEM((sizes[0] - 1, each, 128), bf16),
        got_rims=pltpu.VMEM((2, halo_rows * breadth, width), bf16),
        staging=pltpu.VMEM((2, lane_block, lane_block), bf16),
        valid=pltpu.VMEM((pixels, 128), f32),
        offset_weight=pltpu.VMEM((3, width, 128), bf16),
        bias_row=pltpu.VMEM((1, 128), f32),
        sums=pltpu.VMEM((2, 8, wide), f32),
        centre=pltpu.VMEM((1, wide), f32),
        mean_narrow=pltpu.VMEM((1, width), f32),
        mean_wide=pltpu.VMEM((1, wide), f32),
        rstd_narrow=pltpu.VMEM((4, width), f32),
        rstd_wide=pltpu.VMEM((2, wide), f32),
        identity=pltpu.SMEM((rows + 2 * halo_rows,), jnp.int32),
        row_width=pltpu.SMEM((rows + 2 * halo_rows,), jnp.int32),
        masks=pltpu.SMEM((rows, 6), f32),
        counts=pltpu.SMEM((5,), f32),
        gather_local=dma((10,)),
        gather_send=dma((10, high - 1 + 7)),
        gather_recv=dma((10, high - 1 + 7)),
        halo_send=dma((2, 2)),
        halo_recv=dma((2, 2)),
        edge_send=dma((2, 2)),
        edge_recv=dma((2, 2)),
        samp_sem=dma((2,)),
        load_sem=dma((3,)),
        box_sem=dma((9 + pixels // chunk,)),
        staging_sem=dma((2, 2)),
        table_send=dma((4, max(sizes))),
        table_recv=dma((4, max(sizes))),
        syncs=sync_scratch(plan, sizes),
        **scatter,
    )
    result = launch(
        partial(whole_pass, sizes, in_kernel), ins, in_specs, outs, out_specs, scratch, 0, 63
    )
    if not in_kernel:
        result.grads = [
            lax.psum_scatter(
                lax.psum_scatter(g.astype(f32), "dp", scatter_dimension=0, tiled=True),
                "mp",
                scatter_dimension=1,
                tiled=True,
            )
            for g in result.grads
        ]
    return result


def hand_over(r):
    pieces = r.big_sem.shape[2]
    moves = []
    for i in range(pieces):
        for n, (src, through, dst) in enumerate(
            ((r.image_out, r.through_out, r.to_out), (r.image_grad, r.through_grad, r.to_grad))
        ):
            rows = src.shape[0] // pieces
            at = pl.ds(i * rows, rows)
            last = through if n == 0 else r.wide_grad
            moves.append(
                (
                    pltpu.make_async_copy(src.at[at], through.at[at], r.big_sem.at[n, 0, i]),
                    pltpu.make_async_copy(last.at[at], dst.at[at], r.big_sem.at[n, 1, i]),
                    None if n == 0 else at,
                )
            )
    for arrive, _, _ in moves:
        arrive.start()
    for src, dst in zip(r.grads, r.to_grads):
        dst[...] = src[...].astype(f32)
    for block in range(2):
        for j in range(2):
            norm = 2 * block + j
            r.to_mid_bias[block, j : j + 1, :] = r.narrow_sums[norm, 0:1, :]
            r.to_mid_gain[block, j : j + 1, :] = r.narrow_sums[norm, 1:2, :]
        r.to_out_bias[block : block + 1, :] = r.wide_sums[block, 0:1, :]
        r.to_out_gain[block : block + 1, :] = r.wide_sums[block, 1:2, :]
    width = r.to_mid_bias.shape[2]
    for tap_row in range(3):
        part = r.offset_grad[tap_row * width : (tap_row + 1) * width, :].astype(f32).T
        for tap_col in range(3):
            at = pl.ds((3 * tap_row + tap_col) * width, width)
            r.to_offset[:, at] = part[32 * tap_col : 32 * tap_col + offsets_count, :]
    r.to_bias[...] = r.bias_sum[:, 0 : r.to_bias.shape[1]]
    for arrive, leave, at in moves:
        arrive.wait()
        if at is not None:
            r.wide_grad[at, :] = r.through_grad[at, :].astype(f32)
        leave.start()
    for _, leave, _ in moves:
        leave.wait()


def results_of(back, image, norms, width):
    ins = dict(
        image_out=back.image_out,
        image_grad=back.image_grad,
        grads=back.grads,
        narrow_sums=back.narrow_sums,
        wide_sums=back.wide_sums,
        offset_grad=back.offset_grad,
        bias_sum=back.bias_sum,
    )
    like = [shape(g.shape, f32) for g in norms]
    outs = dict(
        to_out=shape(image.shape, bf16),
        to_grad=shape(image.shape, f32),
        to_grads=[shape(g.shape, f32) for g in back.grads],
        to_mid_gain=like[0],
        to_mid_bias=like[1],
        to_out_gain=like[2],
        to_out_bias=like[3],
        to_offset=shape((offsets_count, 9 * width), f32),
        to_bias=shape((1, offsets_count), f32),
    )
    specs = dict(image_out=anywhere, image_grad=anywhere)
    out_specs = dict((name, vmem) for name in outs)
    out_specs.update(to_out=anywhere, to_grad=anywhere)
    scratch = dict(
        big_sem=dma((2, 2, 8)),
        through_out=pltpu.VMEM(image.shape, bf16),
        through_grad=pltpu.VMEM(image.shape, bf16),
        wide_grad=pltpu.VMEM(image.shape, f32),
    )
    return launch(partial(hand_over), ins, specs, outs, out_specs, scratch, None, 60)


def per_device(
    image_in,
    cotangent,
    heights,
    widths,
    weight_in_a,
    weight_offset,
    bias_offset,
    weight_mid_a,
    weight_out_a,
    weight_in_b,
    weight_mid_b,
    weight_out_b,
    mid_gain,
    mid_bias,
    out_gain,
    out_bias,
):
    height, wide = image_in.shape[0], image_in.shape[2]
    sizes = (lax.axis_size("dp"), lax.axis_size("mp"))
    shards = (weight_in_a, weight_mid_a, weight_out_a, weight_in_b, weight_mid_b, weight_out_b)
    norms = (mid_gain, mid_bias, out_gain, out_bias)
    image = image_in.reshape(height * breadth, wide)
    back = run_kernel(
        image,
        cotangent.reshape(height * breadth, wide),
        heights,
        widths,
        shards,
        weight_offset.T,
        bias_offset,
        norms,
        sizes,
    )
    final = results_of(back, image, norms, weight_offset.shape[0] // 9)
    grads = final.to_grads
    return (
        final.to_out.reshape(image_in.shape),
        final.to_grad.reshape(image_in.shape),
        grads[5],
        final.to_offset.T,
        final.to_bias.reshape(bias_offset.shape),
        grads[4],
        grads[3],
        grads[2],
        grads[1],
        grads[0],
        final.to_mid_gain,
        final.to_mid_bias,
        final.to_out_gain,
        final.to_out_bias,
    )


def solution(mesh):
    rows, split, both = P(("dp", "mp"), None, None), P("dp", "mp"), P()
    in_specs = (rows, rows, both, both, split, both, both, split, split, split, split, split)
    in_specs += (both,) * 4
    out_specs = (rows, rows, split, both, both, split, split, split, split, split) + (both,) * 4
    return jax.shard_map(
        per_device, mesh=mesh, in_specs=in_specs, out_specs=out_specs, check_vma=False
    )
```

```python
from functools import partial
from types import SimpleNamespace

import jax
import jax.numpy as jnp
from jax import lax
from jax.experimental import pallas as pl
from jax.experimental.pallas import tpu as pltpu
from jax.sharding import PartitionSpec as P

norm_eps = 1e-05
halo_rows = 3
breadth = 64
chunk = 256
strip = 32
lane_block = 512
offsets_count = 18
gelu_a = 0.7978845608028654
gelu_b = gelu_a * 0.044715
MESH = pl.DeviceIdType.MESH
f32 = jnp.float32
bf16 = jnp.bfloat16
shape = jax.ShapeDtypeStruct
dma = pltpu.SemaphoreType.DMA
vmem = pl.BlockSpec(memory_space=pltpu.VMEM)
smem = pl.BlockSpec(memory_space=pltpu.SMEM)
anywhere = pl.BlockSpec(memory_space=pl.ANY)


class Place:
    def __init__(self, dp_size, mp_size):
        self.dp_size, self.mp_size = dp_size, mp_size
        self.count = dp_size * mp_size
        self.high = dp_size // 2
        self.dp = lax.axis_index("dp")
        self.mp = lax.axis_index("mp")
        self.me = self.dp * mp_size + self.mp
        self.z = self.dp // 2
        self.y = lax.rem(self.dp, 2)
        self.x = self.mp // 2
        self.core = lax.rem(self.mp, 2)

    def at(self, linear):
        return (linear // self.mp_size, lax.rem(linear, self.mp_size))

    def next(self, step):
        return self.at(lax.rem(self.me + self.count + step, self.count))

    def core_peer(self):
        return (self.dp, self.mp + 1 - 2 * self.core)

    def x_peer(self):
        return (self.dp, self.mp + 2 - 4 * self.x)

    def y_peer(self):
        return (self.dp + 1 - 2 * self.y, self.mp)

    def z_peer(self, step):
        return (lax.rem(self.z + step, self.high) * 2 + self.y, self.mp)

    def greet_all(self):
        barrier = pltpu.get_barrier_semaphore()

        def greet_one(k):
            pl.semaphore_signal(barrier, inc=1, device_id=self.next(k + 1), device_id_type=MESH)

        loop(self.count - 1, greet_one)
        pl.semaphore_wait(barrier, self.count - 1)


def remote(src, dst, send, recv, peer):
    return pltpu.make_async_remote_copy(
        src_ref=src,
        dst_ref=dst,
        send_sem=send,
        recv_sem=recv,
        device_id=peer,
        device_id_type=MESH,
    )


def slab(index, size):
    return pl.ds(pl.multiple_of(index * size, size), size)


def loop(count, body):
    def step(i, carry):
        body(i)
        return carry

    lax.fori_loop(0, count, step, 0)


def launch(kernel, ins, specs, outs, out_specs, scratch, collective_id, vmem_mib):
    flat_in, tree_in = jax.tree.flatten(ins)
    flat_out, tree_out = jax.tree.flatten(outs)
    is_leaf = lambda s: not isinstance(s, (dict, list))
    flat_scratch, tree_scratch = jax.tree.flatten(scratch, is_leaf=is_leaf)
    spec_in = [s for n in sorted(ins) for s in [specs.get(n, vmem)] * len(jax.tree.leaves(ins[n]))]
    spec_out = [
        s for n in sorted(outs) for s in [out_specs.get(n, anywhere)] * len(jax.tree.leaves(outs[n]))
    ]

    def body(*refs):
        a, b = len(flat_in), len(flat_in) + len(flat_out)
        everything = dict(jax.tree.unflatten(tree_in, refs[:a]))
        everything.update(jax.tree.unflatten(tree_out, refs[a:b]))
        everything.update(jax.tree.unflatten(tree_scratch, refs[b:]))
        kernel(SimpleNamespace(**everything))

    results = pl.pallas_call(
        body,
        out_shape=flat_out,
        in_specs=spec_in,
        out_specs=spec_out,
        scratch_shapes=flat_scratch,
        compiler_params=pltpu.CompilerParams(
            collective_id=collective_id,
            has_side_effects=collective_id is not None,
            vmem_limit_bytes=vmem_mib * 1024 * 1024,
        ),
        name=kernel.func.__name__,
    )(*flat_in)
    return SimpleNamespace(**jax.tree.unflatten(tree_out, results))


def gelu_of(v):
    return 0.5 * v * (1.0 + jnp.tanh(v * (gelu_a + gelu_b * v * v)))


def gelu_pair(v):
    square = v * v
    half = 0.5 + 0.5 * jnp.tanh(v * (gelu_a + gelu_b * square))
    return half, half * (1.0 + (1.0 - half) * (v * (2.0 * gelu_a + 6.0 * gelu_b * square)))


def gelu_slope(v):
    return gelu_pair(v)[1]


def mid_row(table, norm):
    return table.at[norm // 2, norm % 2 : norm % 2 + 1, :]


def wide_valid(valid, rows, width):
    mask = valid[rows, :]
    return jnp.concatenate([mask] * (width // 128), axis=1)


def fold8(x):
    return jnp.sum(x.reshape(x.shape[0] // 8, 8, x.shape[1]), axis=0)


def strip_sums(pixel_count, width, terms, out, row_at):
    for block in range(width // lane_block):
        lanes = pl.ds(block * lane_block, lane_block)

        def step(i, carry, lanes=lanes):
            parts = terms(slab(i, strip), lanes)
            return tuple(c + fold8(p) for c, p in zip(carry, parts))

        zeros = tuple(jnp.zeros((8, lane_block), f32) for _ in row_at)
        sums = lax.fori_loop(0, pixel_count // strip, step, zeros)
        for row, total in zip(row_at, sums):
            out[row : row + 1, lanes] = jnp.sum(total, axis=0, keepdims=True)


def merge(parts, moments_mode):
    if not moments_mode:
        return jnp.sum(parts, axis=0)
    width = parts.shape[2] - 128
    pixels = jnp.concatenate([parts[:, 0:1, width:]] * (width // 128), axis=2)
    sums, squares = parts[:, 0:1, 0:width], parts[:, 1:2, 0:width]
    all_pixels, all_sums = jnp.sum(pixels, axis=0), jnp.sum(sums, axis=0)
    apart = sums / pixels - (all_sums / all_pixels)[None]
    all_squares = jnp.sum(squares + pixels * apart * apart, axis=0)
    behind = jnp.sum(parts[:, :, width:], axis=0)
    return jnp.concatenate([jnp.concatenate([all_sums, all_squares], axis=0), behind], axis=1)


def sync_groups(width, sizes):
    count = sizes[0] * sizes[1]
    if count > 64:
        return (16, count // 16)
    return sizes[::-1] if width > 1024 else (count,)


def sync_scratch(plan, sizes):
    out = []
    for rows, width in plan:
        for size in sync_groups(width, sizes):
            out += [pltpu.VMEM((rows, width), f32), pltpu.VMEM((size, rows, width), f32), dma, dma]
    return out


class Syncs:
    def __init__(self, place, buffers):
        self.place, self.buffers = place, buffers
        self.at = 0

    def take(self, width):
        stages = []
        stride = 1
        for size in sync_groups(width, (self.place.dp_size, self.place.mp_size)):
            digit = lax.rem(self.place.me // stride, size)
            stages.append((stride, size, digit, self.buffers[self.at : self.at + 4]))
            self.at += 4
            stride *= size
        return stages

    def start(self, stage, value=None):
        stride, size, digit, (src, slots, send, recv) = stage
        me = self.place.me
        if value is not None:
            src[...] = value

        def push(k):
            peer = me + (lax.rem(digit + k + 1, size) - digit) * stride
            remote(src, slots.at[digit], send, recv, self.place.at(peer)).start()

        loop(size - 1, push)
        pltpu.make_async_copy(src, slots.at[digit], recv).start()

    def finish(self, stage, moments_mode):
        stride, size, digit, (src, slots, send, recv) = stage
        pltpu.make_async_copy(slots, slots, recv).wait()
        rest = slots.at[pl.ds(0, size - 1)]
        pltpu.make_async_copy(rest, rest, send).wait()
        return merge(slots[...], moments_mode)

    def rest(self, stages, moments_mode, meanwhile=None):
        value = self.finish(stages[0], moments_mode)
        for stage in stages[1:]:
            self.start(stage, value)
            if meanwhile is not None:
                meanwhile()
            value = self.finish(stage, moments_mode)
        return value


def shifted(x, shift):
    if shift == 0:
        return x
    pixels = x.shape[0]
    column = lax.broadcasted_iota(jnp.int32, x.shape, 0) % breadth + shift
    inside = (column >= 0) & (column < breadth)
    return jnp.where(inside, pltpu.roll(x, (-shift) % pixels, 0), 0.0)


def row_scales(masks, first_row, which, width):
    row_of = lax.broadcasted_iota(jnp.int32, (chunk, width), 0) // breadth
    scale = jnp.zeros((chunk, width), f32)
    for k in range(chunk // breadth):
        scale = jnp.where(row_of == k, masks[first_row + k, which], scale)
    return scale


def masked_rows(part, masks, first_row, which):
    scaled = []
    for k in range(part.shape[0] // breadth):
        piece = part[breadth * k : breadth * (k + 1)].astype(f32)
        scaled.append((piece * masks[first_row + k, which]).astype(bf16))
    return jnp.concatenate(scaled, axis=0)


def tap_terms(off, masks, row, tap_row, tap_col):
    lane = lax.broadcasted_iota(jnp.int32, (breadth, 2 * breadth), 1)
    sub = lax.broadcasted_iota(jnp.int32, (breadth, 2 * breadth), 0)
    upper = lane >= breadth
    apart = jnp.where(upper, lane - breadth, lane) - sub
    tap, shift = 3 * tap_row + tap_col, 2 * tap_col - 2
    oy, ox = off[:, 2 * tap : 2 * tap + 1], off[:, 2 * tap + 1 : 2 * tap + 2]
    low, high = masks[row, 2 * tap_row], masks[row, 2 * tap_row + 1]
    down = jnp.where(upper, oy * high, (1.0 - oy) * low)
    across = jnp.where(apart == shift, 1.0 - ox, jnp.where(apart == shift + 1, ox, 0.0))
    down_slope = jnp.where(upper, high, -low)
    across_slope = jnp.where(apart == shift, -1.0, jnp.where(apart == shift + 1, 1.0, 0.0))
    return down, across, down_slope, across_slope


def nt_dot(a, b):
    return lax.dot_general(a, b, (((1,), (1,)), ((), ())), preferred_element_type=f32)


def tn_dot(a, b):
    return lax.dot_general(a, b, (((0,), (0,)), ((), ())), preferred_element_type=f32)


def nn_dot(a, b):
    return jnp.dot(a, b, preferred_element_type=f32)


class Outbox:
    def __init__(self, sems):
        self.sems, self.running = sems, {}

    def put(self, at, src, dst):
        copy = pltpu.make_async_copy(src, dst, self.sems.at[at])
        copy.start()
        self.running[at] = copy

    def settle(self, *which):
        for at in which or list(self.running):
            self.running.pop(at).wait()


def load_weight(full, dst, sem, part=0, parts=1):
    everything = pltpu.make_async_copy(dst, dst, sem)
    if len(full.shape) == 2:
        if part == 0:
            pltpu.make_async_copy(full, dst, sem).start()
        return everything
    block = full.shape[2]
    rows = block // parts
    for z in range(full.shape[0]):
        for y in range(2):
            src = full.at[z, y, pl.ds(part * rows, rows)]
            to = pl.ds((2 * z + y) * block + part * rows, rows)
            pltpu.make_async_copy(src, dst.at[to], sem).start()
    return everything


class Gather:
    units = ((0, 0, 1), (1, 0, 3), (1, 1, 3), (1, 2, 3), (2, 0, 1)) + (
        (3, 0, 1),
        (4, 0, 3),
        (4, 1, 3),
        (4, 2, 3),
        (5, 0, 1),
    )

    def __init__(self, place, r):
        self.place, self.fulls, self.sems = place, r.fulls, (r.gather_local, r.gather_send, r.gather_recv)
        self.shards = r.shards
        self.stage = [0] * len(self.units)
        self.running = [[] for _ in self.units]

    def cols(self, array, x_at, core_at):
        width = self.shards[array].shape[1]
        return pl.ds(pl.multiple_of((2 * x_at + core_at) * width, 128), width)

    def copies(self, unit, stage):
        array, part, parts = self.units[unit]
        place, full, shard = self.place, self.fulls[array], self.shards[array]
        high, z, y, x, core = place.high, place.z, place.y, place.x, place.core
        half = high // 2
        mine = self.cols(array, x, core)
        lower, upper = pl.ds(0, half), pl.ds(half, high - half)
        count = shard.shape[0] // parts
        rows = pl.ds(part * count, count)
        local, send, recv = self.sems
        if stage == 0:
            source, target = shard.at[rows], full.at[z, y, rows, mine]
            own = pltpu.make_async_copy(source, target, local.at[unit])
            return [own] + [
                remote(source, target, send.at[unit, k - 1], recv.at[unit, k - 1], place.z_peer(k))
                for k in range(1, high)
            ]
        if stage == 1:
            pairs = [
                (full.at[lower, y, rows, mine], place.x_peer()),
                (full.at[upper, y, rows, mine], place.y_peer()),
            ]
        elif stage == 2:
            pairs = [
                (full.at[lower, y, rows, self.cols(array, 0, core)], place.y_peer()),
                (full.at[lower, y, rows, self.cols(array, 1, core)], place.y_peer()),
                (full.at[upper, :, rows, mine], place.x_peer()),
            ]
        else:
            pairs = [
                (full.at[:, :, rows, self.cols(array, 0, core)], place.core_peer()),
                (full.at[:, :, rows, self.cols(array, 1, core)], place.core_peer()),
            ]
        base = high - 1 + [0, 0, 2, 5][stage]
        return [
            remote(ref, ref, send.at[unit, base + i], recv.at[unit, base + i], peer)
            for i, (ref, peer) in enumerate(pairs)
        ]

    def advance(self, *units):
        for unit in units if self.shards else ():
            for copy in self.running[unit]:
                copy.wait()
            self.running[unit] = []
            if self.stage[unit] < 4:
                self.running[unit] = self.copies(unit, self.stage[unit])
                for copy in self.running[unit]:
                    copy.start()
            self.stage[unit] += 1


class Scatter:
    def __init__(self, place, r, kind, use, result):
        self.place, self.use, self.result = place, use, result
        self.keep, self.from_core = r.keep[kind], r.from_core[kind]
        self.low, self.upper = r.from_low[kind], r.from_upper[kind]
        self.two, self.from_high = r.from_two[kind], r.from_high[kind]
        self.send, self.recv, self.free = r.scatter_send[kind], r.scatter_recv[kind], r.scatter_free[kind]
        self.staging, self.staging_sem = r.staging, r.staging_sem
        self.result_sem = r.result_sem.at[kind]
        self.rows, self.width = self.keep.shape[1], self.keep.shape[2]
        self.block = self.rows // place.dp_size
        self.tiles = self.rows // lane_block
        self.stage = 0
        self.running = []

    def cols(self, x_at, core_at):
        return pl.ds(pl.multiple_of((2 * x_at + core_at) * self.width, 128), self.width)

    def at(self, high, y):
        return pl.ds(pl.multiple_of((2 * high + y) * self.block, self.block), self.block)

    def to_core(self, t, i, src):
        rows = pl.ds(pl.multiple_of(t * lane_block, lane_block), lane_block)
        return remote(
            src,
            self.from_core.at[i, rows],
            self.send.at[2 * t + i],
            self.recv.at[2 * t + i],
            self.place.core_peer(),
        )

    def tile_copies(self, t):
        slot = lax.rem(t, 2)
        rows = pl.ds(pl.multiple_of(t * lane_block, lane_block), lane_block)
        core = self.place.core
        away = [self.to_core(t, i, self.staging.at[slot, :, self.cols(i, 1 - core)]) for i in (0, 1)]
        home = [
            pltpu.make_async_copy(
                self.staging.at[slot, :, self.cols(i, core)],
                self.keep.at[i, rows],
                self.staging_sem.at[slot, i],
            )
            for i in (0, 1)
        ]
        return away, home

    def settle_tile(self, t):
        away, home = self.tile_copies(t)
        for copy in away:
            copy.wait_send()
        for copy in home:
            copy.wait()

    def result_copy(self):
        place = self.place
        return pltpu.make_async_copy(
            self.keep.at[place.x, self.at(place.z, place.y)], self.result, self.result_sem
        )

    def begin(self):
        if self.use == 1:
            self.result_copy().wait()
            pl.semaphore_wait(self.free.at[0], 1)

    def fill(self, first, last, compute):
        def body(i):
            t = first + i

            @pl.when(i >= 2)
            def _():
                self.settle_tile(t - 2)

            compute(t, self.staging.at[lax.rem(t, 2)])
            away, home = self.tile_copies(t)
            for copy in away + home:
                copy.start()

        loop(last - first, body)
        for t in range(max(first, last - 2), last):
            self.settle_tile(t)

    def fill_by_columns(self, compute):
        core = self.place.core

        def away(i):
            self.staging[i] = compute(self.cols(i, 1 - core)).astype(bf16)
            self.to_core(0, i, self.staging.at[i]).start()

        def home(i):
            self.keep[i] = compute(self.cols(i, core)).astype(bf16)

        loop(2, away)
        loop(2, home)
        for i in (0, 1):
            self.to_core(0, i, self.staging.at[i]).wait_send()

    def copies(self, stage):
        place = self.place
        x, y, z, half = place.x, place.y, place.z, place.high // 2
        items = []
        if stage == 1:
            for i in (0, 1):
                for b in range(half):
                    items.append((self.keep.at[i, self.at(b, 1 - y)], self.low.at[i, b], place.y_peer()))
            upper = pl.ds(self.rows // 2, self.rows // 2)
            items.append((self.keep.at[1 - x, upper], self.upper, place.x_peer()))
        elif stage == 2:
            for b in range(half):
                items.append((self.keep.at[1 - x, self.at(b, y)], self.two.at[0, b], place.x_peer()))
                items.append(
                    (self.keep.at[x, self.at(half + b, 1 - y)], self.two.at[1, b], place.y_peer())
                )
        else:
            for k in range(1, place.high):
                there = self.at(lax.rem(z + k, place.high), y)
                items.append((self.keep.at[x, there], self.from_high.at[k - 1], place.z_peer(k)))
        base = 2 * self.tiles + [0, 0, 2 * half + 1, 4 * half + 1][stage]
        return [
            remote(src, dst, self.send.at[base + i], self.recv.at[base + i], peer)
            for i, (src, dst, peer) in enumerate(items)
        ]

    def add(self, target, extra):
        target[...] = target[...] + extra[...]

    def finish(self, stage):
        place = self.place
        x, y, z, half = place.x, place.y, place.z, place.high // 2
        if stage == 0:
            piece = 256
            for i in (0, 1):

                def body(k, i=i):
                    rows = slab(k, piece)
                    self.add(self.keep.at[i, rows], self.from_core.at[i, rows])

                loop(self.rows // piece, body)
            peers = [place.core_peer()]
        elif stage == 1:
            for b in range(half):
                for i in (0, 1):
                    self.add(self.keep.at[i, self.at(b, y)], self.low.at[i, b])
            piece = 256

            def body(k):
                rows = pl.ds(pl.multiple_of(self.rows // 2 + k * piece, piece), piece)
                self.add(self.keep.at[x, rows], self.upper.at[slab(k, piece)])

            loop(self.rows // 2 // piece, body)
            peers = [place.x_peer(), place.y_peer()]
        elif stage == 2:
            for b in range(half):
                self.add(self.keep.at[x, self.at(b, y)], self.two.at[0, b])
                self.add(self.keep.at[x, self.at(half + b, y)], self.two.at[1, b])
            peers = [place.x_peer(), place.y_peer()]
        else:
            total = self.keep[x, self.at(z, y)].astype(f32)
            for k in range(1, place.high):
                total = total + self.from_high[k - 1].astype(f32)
            self.keep[x, self.at(z, y)] = total.astype(bf16)
            self.result_copy().start()
            peers = [place.z_peer(k) for k in range(1, place.high)]
        if self.use == 0:
            for peer in peers:
                pl.semaphore_signal(self.free.at[stage], inc=1, device_id=peer, device_id_type=MESH)

    def advance(self):
        if self.stage > 3:
            return
        if self.stage == 0:
            for t in range(self.tiles):
                for i in (0, 1):
                    self.to_core(t, i, self.staging.at[0, :, self.cols(i, 0)] if self.tiles > 1 else self.staging.at[i]).wait_recv()
        for copy in self.running:
            copy.wait()
        self.finish(self.stage)
        self.stage += 1
        if self.stage <= 3:
            if self.use == 1:
                waits = [0, 2, 2, self.place.high - 1][self.stage]
                pl.semaphore_wait(self.free.at[self.stage], waits)
            self.running = self.copies(self.stage)
            for copy in self.running:
                copy.start()

    def drain(self):
        while self.stage <= 3:
            self.advance()

    def end(self):
        self.result_copy().wait()


class Whole:
    def __init__(self, r, result):
        self.staging, self.staging_sem, self.result = r.staging, r.staging_sem, result

    def begin(self):
        pass

    def fill(self, first, last, compute):
        def body(i):
            t = first + i
            compute(t, self.staging.at[0])
            rows = pl.ds(pl.multiple_of(t * lane_block, lane_block), lane_block)
            pltpu.sync_copy(self.staging.at[0], self.result.at[rows])

        loop(last - first, body)

    def fill_by_columns(self, compute):
        def body(i):
            lanes = pl.ds(pl.multiple_of(i * lane_block, lane_block), lane_block)
            self.staging[0] = compute(lanes).astype(bf16)
            pltpu.sync_copy(self.staging.at[0], self.result.at[:, lanes])

        loop(self.result.shape[1] // lane_block, body)

    def advance(self):
        pass

    drain = advance
    end = advance


class TableSum:
    def __init__(self, place, r):
        self.place, self.r = place, r
        self.each = r.table16.shape[0] // place.count
        self.stage, self.running = 0, []

    def part(self, mp, dp=None):
        quarter = self.each * self.place.dp_size
        if dp is None:
            return pl.ds(pl.multiple_of(mp * quarter, self.each), quarter)
        return pl.ds(pl.multiple_of(mp * quarter + dp * self.each, self.each), self.each)

    def copies(self, stage):
        place, r = self.place, self.r
        dp, mp, table, result = place.dp, place.mp, r.table16, r.offset_grad
        items = []
        over_mp = [lax.rem(mp + k, place.mp_size) for k in range(1, place.mp_size)]
        over_dp = [lax.rem(dp + k, place.dp_size) for k in range(1, place.dp_size)]
        if stage == 0:
            for k, to in enumerate(over_mp):
                items.append((table.at[self.part(to)], r.table_one.at[k], (dp, to)))
        elif stage == 1:
            for k, to in enumerate(over_dp):
                items.append((table.at[self.part(mp, to)], r.table_two.at[k], (to, mp)))
        elif stage == 2:
            mine = self.part(mp, dp)
            items = [(result.at[mine], result.at[mine], (to, mp)) for to in over_dp]
        else:
            mine = self.part(mp)
            items = [(result.at[mine], result.at[mine], (dp, to)) for to in over_mp]
        send, recv = r.table_send.at[stage], r.table_recv.at[stage]
        return [remote(a, b, send.at[i], recv.at[i], to) for i, (a, b, to) in enumerate(items)]

    def advance(self):
        place, r = self.place, self.r
        for copy in self.running:
            copy.wait()
        mine = self.part(place.mp), self.part(place.mp, place.dp)
        if self.stage == 0:
            r.table16[...] = r.table[...].astype(bf16)
        elif self.stage == 1:
            total = r.table16[mine[0], :].astype(f32)
            for k in range(place.mp_size - 1):
                total = total + r.table_one[k].astype(f32)
            r.table16[mine[0], :] = total.astype(bf16)
        elif self.stage == 2:
            total = r.table16[mine[1], :].astype(f32)
            for k in range(place.dp_size - 1):
                total = total + r.table_two[k].astype(f32)
            r.offset_grad[mine[1], :] = total.astype(bf16)
        self.running = self.copies(self.stage) if self.stage < 4 else []
        for copy in self.running:
            copy.start()
        self.stage += 1


def geometry(place, r):
    heights, widths, identity, row_width = r.heights, r.widths, r.identity, r.row_width
    images = heights.shape[1]
    rows = r.valid.shape[0] // breadth
    all_rows = rows * place.count
    group_rows = all_rows // 2 + rows // 2
    one, none = jnp.int32(1), jnp.int32(0)

    def row_facts(k):
        row = place.me * rows - halo_rows + k
        group = jnp.where(row >= group_rows, one, none)
        local = row - group * group_rows

        def image(j, carry):
            begin, number, found = carry
            end = begin + heights[group, j]
            number = number + jnp.where(local >= end, one, none)
            here = (local >= begin) & (local < end)
            return end, number, jnp.where(here, widths[group, j], found)

        _, number, found = lax.fori_loop(0, images, image, (none, none, none))
        inside = (row >= 0) & (row < all_rows)
        identity[k] = jnp.where(inside, group * images + number, -one)
        row_width[k] = jnp.where(inside, found, none)

    loop(rows + 2 * halo_rows, row_facts)

    def row_masks(k):
        centre = identity[k + halo_rows]
        for s in range(6):
            r.masks[k, s] = jnp.where(identity[k + s + 1] == centre, 1.0, 0.0).astype(f32)
        column = lax.broadcasted_iota(jnp.int32, (breadth, 128), 0)
        r.valid[slab(k, breadth), :] = jnp.where(column < row_width[k + halo_rows], 1.0, 0.0)

    loop(rows, row_masks)

    def pixels_of(first, last):
        def add(k, total):
            return total + row_width[k + halo_rows]

        return lax.fori_loop(first, last, add, none).astype(f32)

    def add_image(j, total):
        return total + heights[0, j] * widths[0, j] + heights[1, j] * widths[1, j]

    local = pixels_of(0, rows)
    r.counts[0] = local
    r.counts[1] = 1.0 / local
    r.counts[2] = 1.0 / lax.fori_loop(0, images, add_image, none).astype(f32)
    r.counts[3] = 1.0 / pixels_of(0, chunk // breadth)
    r.counts[4] = 1.0 / pixels_of(chunk // breadth, 2 * chunk // breadth)

    count = r.offset_bias.shape[0]
    width = r.offset_weight.shape[1]
    lane = lax.broadcasted_iota(jnp.int32, (1, 128), 1)
    bias = jnp.zeros((1, 128), f32)
    for j in range(count):
        bias = jnp.where(lane == j, r.offset_bias[j], bias)
    r.bias_row[...] = bias
    down = lax.broadcasted_iota(jnp.int32, (count, 128), 0)
    across = lax.broadcasted_iota(jnp.int32, (count, 128), 1)
    for tap_row in range(3):
        total = jnp.zeros((width, 128), f32)
        for tap_col in range(3):
            place_at = jnp.where(across == down + 32 * tap_col, 1.0, 0.0).astype(bf16)
            columns = pl.ds((3 * tap_row + tap_col) * width, width)
            total = total + tn_dot(r.weight_offset[:, columns], place_at)
        r.offset_weight[tap_row] = total.astype(bf16)


def forward_part(place, syncs, box, r):
    gather = Gather(place, r)
    valid, masks, counts = r.valid, r.masks, r.counts
    third, field, hidden, pool = r.grad, r.field, r.hidden, r.pool
    pixels, wide = third.shape
    width = hidden.shape[1]
    halo = halo_rows * breadth
    chunks = pixels // chunk
    first = r.small.at[pl.ds(halo, pixels)]

    def load(array, dst, sem, part=0, parts=1):
        return load_weight(r.fulls[array], dst, r.load_sem.at[sem], part, parts)

    def gather_sums(i, got, scale):
        block_width = got.shape[1]
        sums, centre = r.sums.at[:, :, 0:block_width], r.centre.at[:, 0:block_width]
        mask = wide_valid(valid, slab(i, chunk), block_width)
        if scale is not None:
            centre[...] = jnp.sum(fold8(got * mask), axis=0, keepdims=True) * scale
            sums[...] = jnp.zeros((2, 8, block_width), f32)
        apart = (got - centre[...]) * mask
        sums[0] = sums[0] + fold8(apart)
        sums[1] = sums[1] + fold8(apart * apart)

    def over_chunks(target, compute, between=None):
        def body(i, scale=None):
            got = compute(i)
            target[slab(i, chunk), :] = got
            gather_sums(i, got, scale)

        if between is None:
            body(0, counts[3])
            loop(chunks - 1, lambda i: body(i + 1))
        else:
            body(1, counts[4])
            loop(chunks - 3, lambda i: body(i + 2))
            between()
            loop(2, lambda i: body(i * (chunks - 1)))

    def moments(block_width, rstd, mean, meanwhile=None, early=None):
        stages = syncs.take(block_width + 128)
        src = stages[0][3][0]
        first_sum = jnp.sum(r.sums[0, :, 0:block_width], axis=0, keepdims=True)
        second_sum = jnp.sum(r.sums[1, :, 0:block_width], axis=0, keepdims=True)
        src[0:1, 0:block_width] = first_sum + r.centre[:, 0:block_width] * counts[0]
        src[1:2, 0:block_width] = second_sum - first_sum * first_sum * counts[1]
        src[:, block_width:] = jnp.full((2, 128), counts[0], f32)
        syncs.start(stages[0])
        if early is not None:
            early()
        merged = syncs.rest(stages, True, meanwhile)
        mean[...] = merged[0:1, 0:block_width] * counts[2]
        spread = jnp.maximum(merged[1:2, 0:block_width], 0.0) * counts[2]
        rstd[...] = lax.rsqrt(spread + norm_eps)

    def activate(norm, hat, target, target_row):
        mean, rstd = r.mean_narrow, r.rstd_narrow.at[norm : norm + 1, :]
        gain, bias = mid_row(r.mid_gain, norm), mid_row(r.mid_bias, norm)

        def body(i):
            at = slab(i, strip)
            normed = (first[at, :] - mean[...]) * rstd[...]
            hat[at, :] = normed.astype(bf16)
            act = gelu_of(normed * gain[...] + bias[...]) * wide_valid(valid, at, width)
            rows = pl.ds(pl.multiple_of(target_row + i * strip, strip), strip)
            target[rows, :] = act.astype(bf16)

        loop(pixels // strip, body)

    def narrow_moments(norm, early=None):
        moments(width, r.rstd_narrow.at[norm : norm + 1, :], r.mean_narrow, None, early)

    def project(lhs, weight, target):
        over_chunks(target, lambda i: nn_dot(lhs[slab(i, chunk), :], weight[...]))

    def halo_copies(block):
        send, recv = r.halo_send.at[block], r.halo_recv.at[block]
        last_rows, below = field.at[pl.ds(pixels, halo)], field.at[pl.ds(pixels + halo, halo)]
        first_rows, above = field.at[pl.ds(halo, halo)], field.at[pl.ds(0, halo)]
        return [
            remote(last_rows, above, send.at[0], recv.at[0], place.next(1)),
            remote(first_rows, below, send.at[1], recv.at[1], place.next(-1)),
        ]

    samples = [r.inputs, r.hat3, pool]

    def sample_at(tap, i):
        return samples[tap // 4], slab(i, chunk), pl.ds(tap % 4 * width, width)

    def sample_chunk(i):
        base = halo + i * chunk
        first_row = i * (chunk // breadth)
        total = jnp.zeros((chunk, 128), f32)
        for tap_row in range(3):
            start = pl.multiple_of(base + (2 * tap_row - 2) * breadth, breadth)
            part = nn_dot(field[pl.ds(start, chunk), :], r.offset_weight[tap_row])
            total = total + part * row_scales(masks, first_row, 2 * tap_row, 128)
        left = shifted(total, -2)
        middle = pltpu.roll(total, 128 - 32, 1)
        right = pltpu.roll(shifted(total, 2), 128 - 64, 1)
        lane = lax.broadcasted_iota(jnp.int32, total.shape, 1)
        raw = jnp.where(lane < 32, left + middle + right, 0.0) + r.bias_row[...]
        tanh_raw = jnp.tanh(raw)
        r.tanh_raw[slab(i, chunk), :] = tanh_raw
        r.off[...] = 0.5 + 0.45 * tanh_raw

        def one_row(k):
            off = r.off[slab(k, breadth), :]
            for tap_row in range(3):
                weights = []
                for tap_col in range(3):
                    down, across, _, _ = tap_terms(off, masks, first_row + k, tap_row, tap_col)
                    weights.append((down * across).astype(bf16))
                start = pl.multiple_of(base + (k + 2 * tap_row - 2) * breadth, breadth)
                got = nn_dot(jnp.concatenate(weights, axis=0), field[pl.ds(start, 2 * breadth), :])
                for tap_col in range(3):
                    ref, _, lanes = sample_at(3 * tap_row + tap_col, i)
                    rows = pl.ds(pl.multiple_of(i * chunk + k * breadth, breadth), breadth)
                    piece = got[breadth * tap_col : breadth * (tap_col + 1)]
                    ref[rows, lanes] = piece.astype(bf16)

        loop(chunk // breadth // 2, lambda k: [one_row(2 * k), one_row(2 * k + 1)])

    def mid_deformable(i):
        rows = slab(i, chunk)
        samp = jnp.concatenate([r.inputs[rows, :], r.hat3[rows, :], pool[rows, :]], axis=1)
        return nn_dot(samp, r.w_mid[...])

    def samp_copies():
        copies = []
        for tap in range(9):
            ref, _, lanes = sample_at(tap, 0)
            src = ref.at[pl.ds(0, pixels), lanes]
            copies.append(
                pltpu.make_async_copy(src, r.samp_out.at[pl.ds(tap * pixels, pixels)], r.samp_sem.at[0])
            )
        return copies

    def mid_plain(i):
        lhs = []
        for tap_row in range(3):
            start = pl.multiple_of(halo + i * chunk + (2 * tap_row - 2) * breadth, breadth)
            part = field[pl.ds(start, chunk), :]
            if tap_row != 1:
                part = masked_rows(part, masks, i * (chunk // breadth), 2 * tap_row)
            lhs.append(part)
        total = None
        for tap_col in range(3):
            partial_sum = None
            for tap_row in range(3):
                weight = r.w_mid[pl.ds((3 * tap_row + tap_col) * width, width), :]
                part = nn_dot(lhs[tap_row], weight)
                partial_sum = part if partial_sum is None else partial_sum + part
            partial_sum = shifted(partial_sum, 2 * tap_col - 2)
            total = partial_sum if total is None else total + partial_sum
        return total

    def finish_block(block, inputs, result):
        gain, bias = r.out_gain.at[block : block + 1, :], r.out_bias.at[block : block + 1, :]
        mean, rstd = r.mean_wide, r.rstd_wide.at[block : block + 1, :]

        def body(i):
            at = slab(i, strip)
            mask = wide_valid(valid, at, lane_block)
            for j in range(wide // lane_block):
                lanes = pl.ds(j * lane_block, lane_block)
                normed = (third[at, lanes] - mean[:, lanes]) * rstd[:, lanes]
                r.hat3[at, lanes] = normed.astype(bf16)
                pre = inputs[at, lanes].astype(f32) + (normed * gain[:, lanes] + bias[:, lanes])
                result[at, lanes] = (mask * gelu_of(pre)).astype(bf16)

        loop(pixels // strip, body)

    def wide_moments(block, meanwhile=None):
        moments(wide, r.rstd_wide.at[block : block + 1, :], r.mean_wide, meanwhile)

    place.greet_all()
    gather.advance(0, 1, 2, 3)
    box.put(0, r.image, r.wide_act)
    geometry(place, r)
    gather.advance(0)
    gather.advance(0, 1, 2)
    gather.advance(0, 3, 4)
    gather.advance(0)
    load(0, r.w_in, 0).wait()
    box.settle(0)
    project(r.wide_act, r.w_in, first)
    narrow_moments(0, lambda: gather.advance(1, 2))
    activate(0, r.da, field, halo)
    edges = halo_copies(0)
    for copy in edges:
        copy.start()
    gather.advance(3, 6, 7, 8, 5)
    gather.advance(1)
    box.put(1, r.da, r.hat1_out)
    loop(chunks - 2, lambda i: sample_chunk(i + 1))
    gather.advance(2, 1)
    load(1, r.w_mid, 1, 0, 3)
    for copy in edges:
        copy.wait()
    gather.advance(4, 3)
    box.put(2, field, r.field_out)
    loop(2, lambda i: sample_chunk(i * (chunks - 1)))
    gather.advance(2, 3, 4)
    load(1, r.w_mid, 1, 1, 3)
    loaded = load(1, r.w_mid, 1, 2, 3)
    samp_out = samp_copies()
    for copy in samp_out:
        copy.start()
    loaded.wait()
    over_chunks(first, mid_deformable)
    narrow_moments(1, lambda: gather.advance(4, 6, 7, 8, 5, 9))
    gather.advance(4)
    loaded = load(2, r.w_out, 2)
    activate(1, r.hat2, hidden, 0)
    box.put(3, r.hat2, r.hat2_out)
    box.put(4, hidden, r.hidden_out)
    for copy in samp_out:
        copy.wait()
    loaded.wait()
    project(hidden, r.w_out, third)
    wide_moments(0, lambda: gather.advance(5, 6, 7, 8))
    finish_block(0, r.wide_act, r.inputs)
    box.put(0, r.cotangent, r.wide_act)
    box.put(5, r.hat3, r.hat3_out)
    gather.advance(5)
    gather.advance(5)
    load(3, r.w_in, 0).wait()
    box.settle(1, 2)
    project(r.inputs, r.w_in, first)
    narrow_moments(2, lambda: gather.advance(6, 7, 8))
    gather.advance(6, 7, 8)
    load(4, r.w_mid, 1, 0, 3)
    load(4, r.w_mid, 1, 1, 3)
    loaded = load(4, r.w_mid, 1, 2, 3)
    activate(2, r.da, field, halo)
    edges = halo_copies(1)
    for copy in edges:
        copy.start()
    gather.advance(9)

    def edges_here():
        for copy in edges:
            copy.wait()

    loaded.wait()
    over_chunks(first, mid_plain, edges_here)
    narrow_moments(3, lambda: gather.advance(9))
    gather.advance(9)
    gather.advance(9)
    loaded_out = load(5, r.w_out, 2)
    box.settle(3, 4)
    activate(3, r.hat2, hidden, 0)
    loaded_out.wait()
    project(hidden, r.w_out, third)
    wide_moments(1)
    box.settle(0, 5)


def backward_part(place, syncs, box, in_kernel, r):
    valid, masks, counts = r.valid, r.masks, r.counts
    grad, small, inputs, hat3, wide_act = r.grad, r.small, r.inputs, r.hat3, r.wide_act
    pixels, wide, width = grad.shape[0], grad.shape[1], small.shape[1]
    halo = halo_rows * breadth
    chunks, chunk_rows = pixels // chunk, chunk // breadth
    per_pixel = counts[2]
    own = pl.ds(halo, pixels)
    kinds = [0, 1, 2]

    def scatter(kind, use):
        result = r.grads[3 * use + kind]
        if in_kernel:
            return Scatter(place, r, kind, use, result)
        return Whole(r, result)

    def weight(array, dst, sem):
        box.running[sem] = load_weight(r.fulls[array], dst, r.box_sem.at[sem])

    def open_sync(terms, block_width, last_row=None):
        stages = syncs.take(block_width)
        src = stages[0][3][0]
        strip_sums(pixels, block_width, terms, src, [0, 1])
        if last_row is not None:
            src[2:3, :] = jnp.zeros((1, block_width), f32)
            src[2:3, 0:128] = last_row
        syncs.start(stages[0])
        return stages

    def pre_back(block, upstream, image):
        gain, bias = r.out_gain.at[block : block + 1, :], r.out_bias.at[block : block + 1, :]

        def terms(at, lanes):
            hat = hat3[at, lanes].astype(f32)
            pre = image[at, lanes].astype(f32) + (hat * gain[:, lanes] + bias[:, lanes])
            slope = gelu_slope(pre) * wide_valid(valid, at, lane_block)
            d = upstream[at, lanes].astype(f32) * slope
            grad[at, lanes] = d
            return d, d * hat

        return open_sync(terms, wide)

    def finish_and_back():
        gain, bias = r.out_gain.at[1:2, :], r.out_bias.at[1:2, :]
        mean, rstd = r.mean_wide, r.rstd_wide.at[1:2, :]

        def terms(at, lanes):
            normed = (grad[at, lanes] - mean[:, lanes]) * rstd[:, lanes]
            hat3[at, lanes] = normed.astype(bf16)
            pre = inputs[at, lanes].astype(f32) + (normed * gain[:, lanes] + bias[:, lanes])
            half, slope = gelu_pair(pre)
            mask = wide_valid(valid, at, lane_block)
            d = wide_act[at, lanes].astype(f32) * (slope * mask)
            wide_act[at, lanes] = (pre * (half * mask)).astype(bf16)
            grad[at, lanes] = d
            return d, d * normed

        return open_sync(terms, wide)

    def last_norm_back(block):
        sums, rstd = r.wide_sums.at[block], r.rstd_wide.at[block : block + 1, :]
        gain = r.out_gain.at[block : block + 1, :]

        def body(i):
            at = slab(i, strip)
            mask = wide_valid(valid, at, lane_block)
            for j in range(wide // lane_block):
                lanes = pl.ds(j * lane_block, lane_block)
                hat = hat3[at, lanes].astype(f32)
                inner = grad[at, lanes] - sums[0:1, lanes] * per_pixel
                inner = inner - hat * (sums[1:2, lanes] * per_pixel)
                scaled = mask * (gain[:, lanes] * rstd[:, lanes]) * inner
                wide_act[at, lanes] = scaled.astype(bf16)

        loop(pixels // strip, body)

    def act_back(norm, hat):
        gain, bias = mid_row(r.mid_gain, norm), mid_row(r.mid_bias, norm)

        def terms(at, lanes):
            normed = hat[at, lanes].astype(f32)
            slope = gelu_slope(normed * gain[:, lanes] + bias[:, lanes])
            rows = pl.ds(pl.multiple_of(halo + at.start, strip), strip)
            d = small[rows, lanes] * slope * wide_valid(valid, at, lane_block)
            small[rows, lanes] = d
            return d, d * normed

        return terms

    def inner_norm_back(norm, hat, target, target_row):
        sums, rstd = r.narrow_sums.at[norm], r.rstd_narrow.at[norm : norm + 1, :]
        gain = mid_row(r.mid_gain, norm)

        def body(i):
            at = slab(i, strip)
            rows = pl.ds(pl.multiple_of(halo + i * strip, strip), strip)
            inner = small[rows, :] - sums[0:1, :] * per_pixel
            inner = inner - hat[at, :].astype(f32) * (sums[1:2, :] * per_pixel)
            scaled = wide_valid(valid, at, width) * (gain[...] * rstd[...]) * inner
            target[pl.ds(pl.multiple_of(target_row + i * strip, strip), strip), :] = scaled.astype(bf16)

        loop(pixels // strip, body)

    def out_back(block):
        def body(i):
            rows = pl.ds(pl.multiple_of(halo + i * chunk, breadth), chunk)
            small[rows, :] = nt_dot(wide_act[slab(i, chunk), :], r.w_out[...])

        loop(chunks, body)
        return open_sync(act_back(2 * block + 1, r.hat2), width)

    def out_grad(target):
        target.begin()
        target.fill_by_columns(lambda lanes: tn_dot(r.hidden[...], wide_act[:, lanes]))

    def in_grad(target):
        target.begin()

        def compute(t, ref):
            lanes = pl.ds(pl.multiple_of(t * lane_block, lane_block), lane_block)
            ref[...] = tn_dot(inputs[:, lanes], r.da[...]).astype(bf16)

        target.fill(0, wide // lane_block, compute)

    def in_back(i):
        at = slab(i, chunk)
        grad[at, :] = grad[at, :] + nt_dot(r.da[at, :], r.w_in[...])

    def neighbours(before_src, before_dst, after_src, after_dst, which):
        send, recv = r.edge_send.at[which], r.edge_recv.at[which]
        return [
            remote(after_src, after_dst, send.at[0], recv.at[0], place.next(1)),
            remote(before_src, before_dst, send.at[1], recv.at[1], place.next(-1)),
        ]

    out_b, mid_b, in_b = [scatter(kind, 0) for kind in kinds]
    stages = finish_and_back()
    box.put(6, wide_act, r.image_out)
    r.wide_sums[1] = syncs.rest(stages, False)
    box.settle(6)
    last_norm_back(1)
    box.put(1, r.hat3_out, hat3)
    stages = out_back(1)
    weight(2, r.w_out, 3)
    out_grad(out_b)
    box.put(2, r.image, wide_act)
    box.put(5, r.hidden_out, r.hidden)
    r.narrow_sums[3] = syncs.rest(stages, False)

    pool, side = r.pool, 2 * breadth
    span = pixels + 2 * side
    centre = 2 * span
    inner_norm_back(3, r.hat2, pool, centre + side)
    box.put(4, r.hat2_out, r.hat2)
    edges = neighbours(
        pool.at[pl.ds(centre + side, side)],
        pool.at[pl.ds(centre + side + pixels, side)],
        pool.at[pl.ds(centre + pixels, side)],
        pool.at[pl.ds(centre, side)],
        0,
    )
    for copy in edges:
        copy.start()

    def shift_row(row):
        at = pl.ds(pl.multiple_of(centre + row * breadth, breadth), breadth)
        value = pool[at, :].astype(f32)
        for slot, amount in ((0, 2), (1, -2)):
            rows = pl.ds(pl.multiple_of(slot * span + row * breadth, breadth), breadth)
            pool[rows, :] = shifted(value, amount).astype(bf16)

    loop(pixels // breadth, lambda row: shift_row(row + 2))
    out_b.advance()
    for copy in edges:
        copy.wait()
    loop(2, shift_row)
    loop(2, lambda row: shift_row(row + 2 + pixels // breadth))
    slot_of = (0, 2, 1)

    def mid_back_plain(i):
        first_row = i * chunk_rows
        total = None
        for tap_row in range(3):
            for tap_col in range(3):
                start = slot_of[tap_col] * span + (4 - 2 * tap_row) * breadth + i * chunk
                part = pool[pl.ds(pl.multiple_of(start, breadth), chunk), :]
                if tap_row != 1:
                    part = masked_rows(part, masks, first_row, 4 - 2 * tap_row)
                tap = pl.ds((3 * tap_row + tap_col) * width, width)
                term = nt_dot(part, r.w_mid[tap, :])
                total = term if total is None else total + term
        rows = pl.ds(pl.multiple_of(halo + i * chunk, breadth), chunk)
        small[rows, :] = total

    loop(chunks, mid_back_plain)
    weight(1, r.w_mid, 7)
    stages = open_sync(act_back(2, r.da), width)
    out_b.advance()
    mid_b.begin()
    shifted_rows = 3 * span

    def mid_grad_plain(t, ref):
        tap_row, tap_col = t // 3, lax.rem(t, 3)
        slot = jnp.where(tap_col == 0, 0, jnp.where(tap_col == 1, 2, 1))

        def copy_rows(i):
            start = slot * span + (4 - 2 * tap_row) * breadth + i * chunk
            part = pool[pl.ds(pl.multiple_of(start, breadth), chunk), :]
            rows = pl.ds(pl.multiple_of(shifted_rows + i * chunk, breadth), chunk)
            pool[rows, :] = masked_rows(part, masks, i * chunk_rows, 4 - 2 * tap_row)

        loop(chunks, copy_rows)
        ref[...] = tn_dot(r.field[own, :], pool[pl.ds(shifted_rows, pixels), :]).astype(bf16)

    mid_b.fill(0, 9, mid_grad_plain)
    out_b.advance()
    r.narrow_sums[2] = syncs.rest(stages, False)
    mid_b.advance()
    inner_norm_back(2, r.da, r.da, 0)
    box.put(6, r.field_out, r.field)
    loop(chunks, in_back)
    weight(0, r.w_in, 8)

    out_a, mid_a, in_a = [scatter(kind, 1) for kind in kinds]
    box.settle(1, 2)
    stages = pre_back(0, grad, wide_act)
    out_b.drain()
    in_grad(in_b)
    box.put(0, r.image, inputs)
    r.wide_sums[0] = syncs.rest(stages, False, mid_b.advance)
    last_norm_back(0)
    box.settle(3, 4)
    stages = out_back(0)
    box.settle(5)
    out_grad(out_a)
    mid_b.advance()
    in_b.advance()
    r.narrow_sums[1] = syncs.rest(stages, False)
    inner_norm_back(1, r.hat2, r.da, 0)
    out_a.advance()
    box.put(5, r.hat1_out, r.hidden)
    slots = 9 * chunk

    def samp_load(t):
        slot = pl.ds(pl.multiple_of(slots + lax.rem(t, 2) * pixels, breadth), pixels)
        src = r.samp_out.at[pl.ds(pl.multiple_of(t * pixels, breadth), pixels)]
        pltpu.make_async_copy(src, pool.at[slot], r.samp_sem.at[lax.rem(t, 2)]).start()

    def samp_settle(t):
        rows = pool.at[pl.ds(pl.multiple_of(slots + lax.rem(t, 2) * pixels, breadth), pixels)]
        pltpu.make_async_copy(rows, rows, r.samp_sem.at[lax.rem(t, 2)]).wait()

    def mid_grad_deformable(t, ref):
        @pl.when(t < 8)
        def _():
            samp_load(t + 1)

        samp_settle(t)
        slot = pl.ds(pl.multiple_of(slots + lax.rem(t, 2) * pixels, breadth), pixels)
        ref[...] = tn_dot(pool[slot, :], r.da[...]).astype(bf16)

    box.settle(6, 7)

    def clear(i):
        small[slab(i, breadth), :] = jnp.zeros((breadth, width), f32)

    loop((pixels + 2 * halo) // breadth, clear)
    table = r.table
    table[...] = jnp.zeros_like(table)
    r.draw_sum[...] = jnp.zeros_like(r.draw_sum)

    def mid_back_deformable(i):
        first_row = i * chunk_rows
        part = r.da[slab(i, chunk), :]
        for tap_row in range(3):
            for tap_col in range(3):
                tap = pl.ds((3 * tap_row + tap_col) * width, width)
                dsamp = nt_dot(part, r.w_mid[tap, :]).astype(bf16)
                for k in range(chunk_rows):
                    start = ((tap_row * chunk_rows + k) * 3 + tap_col) * breadth
                    pool[pl.ds(start, breadth), :] = dsamp[breadth * k : breadth * (k + 1)]
        th = r.tanh_raw[slab(i, chunk), :]
        r.off[...] = 0.5 + 0.45 * th
        lane = lax.broadcasted_iota(jnp.int32, (breadth, 128), 1)

        def one_row(k):
            off = r.off[slab(k, breadth), :]
            doff = jnp.zeros((breadth, 128), f32)
            for tap_row in range(3):
                start = (tap_row * chunk_rows + k) * 3 * breadth
                dsamp = pool[pl.ds(pl.multiple_of(start, breadth), 3 * breadth), :]
                start = halo + i * chunk + (k + 2 * tap_row - 2) * breadth
                rows = pl.ds(pl.multiple_of(start, breadth), 2 * breadth)
                dots = nt_dot(dsamp, r.field[rows, :])
                weights = []
                for tap_col in range(3):
                    terms = tap_terms(off, masks, first_row + k, tap_row, tap_col)
                    down, across, down_slope, across_slope = terms
                    weights.append((down * across).astype(bf16))
                    part = dots[breadth * tap_col : breadth * (tap_col + 1)]
                    doy = jnp.sum(part * (across * down_slope), axis=1, keepdims=True)
                    dox = jnp.sum(part * (across_slope * down), axis=1, keepdims=True)
                    tap = 3 * tap_row + tap_col
                    doff = jnp.where(lane == 2 * tap, doy, jnp.where(lane == 2 * tap + 1, dox, doff))
                small[rows, :] = small[rows, :] + tn_dot(jnp.concatenate(weights, axis=0), dsamp)
            th_row = r.tanh_raw[pl.ds(pl.multiple_of(i * chunk + k * breadth, breadth), breadth), :]
            draw = (0.45 * (1.0 - th_row * th_row) * doff).astype(bf16).astype(f32)
            r.off[slab(k, breadth), :] = draw
            r.draw_sum[...] = r.draw_sum[...] + fold8(draw)

        loop(chunk_rows // 2, lambda k: [one_row(2 * k), one_row(2 * k + 1)])
        draw = r.off[...]
        spread = shifted(draw, 2) + pltpu.roll(draw, 32, 1) + pltpu.roll(shifted(draw, -2), 64, 1)
        for tap_row in range(3):
            part = (spread * row_scales(masks, first_row, 2 * tap_row, 128)).astype(bf16)
            start = halo + i * chunk + (2 * tap_row - 2) * breadth
            rows = pl.ds(pl.multiple_of(start, breadth), chunk)
            small[rows, :] = small[rows, :] + nt_dot(part, r.offset_weight[tap_row])
            to = pl.ds(tap_row * width, width)
            table[to, :] = table[to, :] + tn_dot(r.field[rows, :], part)

    mid_back_deformable(0)
    mid_b.drain()
    in_b.advance()
    out_a.advance()
    mid_a.begin()
    samp_load(0)
    mid_a.fill(0, 9, mid_grad_deformable)
    in_b.advance()
    out_a.advance()
    mid_back_deformable(chunks - 1)
    rims = [r.staging.at[i, pl.ds(0, halo)] for i in (0, 1)]
    rims[0][...] = small[pl.ds(0, halo), :].astype(bf16)
    rims[1][...] = small[pl.ds(halo + pixels, halo), :].astype(bf16)
    edges = neighbours(rims[0], r.got_rims.at[0], rims[1], r.got_rims.at[1], 1)
    for copy in edges:
        copy.start()
    mid_a.advance()
    loop(chunks - 2, lambda i: mid_back_deformable(i + 1))
    in_b.drain()
    out_a.drain()

    offset_sum = TableSum(place, r)
    for copy in edges:
        copy.wait()
    first_rows, last_rows = pl.ds(halo, halo), pl.ds(pixels, halo)
    small[first_rows, :] = small[first_rows, :] + r.got_rims[1].astype(f32)
    small[last_rows, :] = small[last_rows, :] + r.got_rims[0].astype(f32)
    box.settle(5)
    draw_sum = jnp.sum(r.draw_sum[...], axis=0, keepdims=True)
    stages = open_sync(act_back(0, r.hidden), width, draw_sum)
    offset_sum.advance()
    mid_a.advance()

    merged = syncs.rest(stages, False)
    r.narrow_sums[0] = merged[0:2]
    r.bias_sum[...] = merged[2:3, 0:128]
    inner_norm_back(0, r.hidden, r.da, 0)
    box.settle(0)
    in_grad(in_a)
    mid_a.advance()
    offset_sum.advance()
    box.settle(8)
    for i in range(chunks):
        at = slab(i, chunk)
        wide_act[at, :] = (grad[at, :] + nt_dot(r.da[at, :], r.w_in[...])).astype(bf16)
        box.put(9 + i, wide_act.at[at], r.image_grad.at[at])
        if i == 0:
            in_a.advance()
    offset_sum.advance()
    in_a.advance()
    offset_sum.advance()
    mid_a.drain()
    in_a.drain()
    offset_sum.advance()
    box.settle()
    for one in (out_a, mid_a, in_a):
        one.end()


def whole_pass(sizes, in_kernel, r):
    place = Place(*sizes)
    syncs = Syncs(place, r.syncs)
    box = Outbox(r.box_sem)
    forward_part(place, syncs, box, r)
    backward_part(place, syncs, box, in_kernel, r)


def run_kernel(image, cotangent, heights, widths, shards, offset_weight, offset_bias, norms, sizes):
    pixels, wide = image.shape
    width = shards[0].shape[1] * sizes[1]
    taps = 9 * width
    count, high = sizes[0] * sizes[1], sizes[0] // 2
    half = high // 2
    rows = pixels // breadth
    ext_pixels = pixels + 2 * halo_rows * breadth
    each = 16 * (-(-3 * width // (16 * count)))
    in_kernel = all(s.shape[0] % 16 == 0 for s in shards) and shards[1].shape[0] % 48 == 0
    kinds = [(width, wide), (taps, width), (wide, width)]
    owned = [(down // sizes[0], across // sizes[1]) for down, across in kinds]
    ins = dict(
        image=image,
        cotangent=cotangent,
        heights=heights,
        widths=widths,
        weight_offset=offset_weight,
        offset_bias=offset_bias,
        mid_gain=norms[0],
        mid_bias=norms[1],
        out_gain=norms[2],
        out_bias=norms[3],
        shards=list(shards) if in_kernel else [],
    )
    narrow, broad = shape((pixels, width), bf16), shape((pixels, wide), bf16)
    outs = dict(
        hat1_out=narrow,
        hat2_out=narrow,
        hidden_out=narrow,
        field_out=shape((ext_pixels, width), bf16),
        hat3_out=broad,
        image_out=broad,
        samp_out=shape((9 * pixels, width), bf16),
        image_grad=broad,
        narrow_sums=shape((4, 2, width), f32),
        wide_sums=shape((2, 2, wide), f32),
        offset_grad=shape((count * each, 128), bf16),
        bias_sum=shape((1, 128), f32),
    )
    in_specs = dict(
        image=anywhere,
        cotangent=anywhere,
        heights=smem,
        widths=smem,
        offset_bias=smem,
        shards=anywhere,
        fulls=anywhere,
    )
    out_specs = dict(narrow_sums=vmem, wide_sums=vmem, offset_grad=vmem, bias_sum=vmem)
    scatter = dict()
    if in_kernel:
        outs.update(
            fulls=[shape((high, 2, s.shape[0], s.shape[1] * sizes[1]), bf16) for s in shards],
            grads=[shape(o, bf16) for o in owned] * 2,
        )
        halves = [(2, down, o[1]) for (down, _), o in zip(kinds, owned)]
        sems = [dma((2 * (down // lane_block) + 4 * half + high,)) for down, _ in kinds]
        scatter.update(
            keep=[pltpu.VMEM(h, bf16) for h in halves],
            from_core=[pltpu.VMEM(h, bf16) for h in halves],
            from_low=[pltpu.VMEM((2, half) + o, bf16) for o in owned],
            from_upper=[pltpu.VMEM((h[1] // 2, h[2]), bf16) for h in halves],
            from_two=[pltpu.VMEM((2, half) + o, bf16) for o in owned],
            from_high=[pltpu.VMEM((high - 1,) + o, bf16) for o in owned],
            result_sem=dma((3,)),
            scatter_free=[pltpu.SemaphoreType.REGULAR((4,))] * 3,
            scatter_send=sems,
            scatter_recv=sems,
        )
    else:
        fulls = [lax.all_gather(s, "mp", axis=1, tiled=True) for s in shards]
        ins.update(fulls=[lax.all_gather(s, "dp", axis=0, tiled=True) for s in fulls])
        outs.update(grads=[shape(k, bf16) for k in kinds] * 2)
    plan = [(2, width + 128), (2, width + 128), (2, wide + 128)] * 2
    plan += [(2, wide), (2, width), (2, width), (2, wide), (2, width), (3, width)]
    span = pixels + 4 * breadth
    pool_rows = max(3 * span + pixels, 9 * chunk + 2 * pixels)
    scratch = dict(
        grad=pltpu.VMEM((pixels, wide), f32),
        inputs=pltpu.VMEM((pixels, wide), bf16),
        hat3=pltpu.VMEM((pixels, wide), bf16),
        wide_act=pltpu.VMEM((pixels, wide), bf16),
        w_in=pltpu.VMEM((wide, width), bf16),
        w_mid=pltpu.VMEM((taps, width), bf16),
        w_out=pltpu.VMEM((width, wide), bf16),
        small=pltpu.VMEM((ext_pixels, width), f32),
        hat2=pltpu.VMEM((pixels, width), bf16),
        hidden=pltpu.VMEM((pixels, width), bf16),
        da=pltpu.VMEM((pixels, width), bf16),
        field=pltpu.VMEM((ext_pixels, width), bf16),
        pool=pltpu.VMEM((pool_rows, width), bf16),
        off=pltpu.VMEM((chunk, 128), f32),
        tanh_raw=pltpu.VMEM((pixels, 128), f32),
        draw_sum=pltpu.VMEM((8, 128), f32),
        table=pltpu.VMEM((count * each, 128), f32),
        table16=pltpu.VMEM((count * each, 128), bf16),
        table_one=pltpu.VMEM((sizes[1] - 1, sizes[0] * each, 128), bf16),
        table_two=pltpu.VMEM((sizes[0] - 1, each, 128), bf16),
        got_rims=pltpu.VMEM((2, halo_rows * breadth, width), bf16),
        staging=pltpu.VMEM((2, lane_block, lane_block), bf16),
        valid=pltpu.VMEM((pixels, 128), f32),
        offset_weight=pltpu.VMEM((3, width, 128), bf16),
        bias_row=pltpu.VMEM((1, 128), f32),
        sums=pltpu.VMEM((2, 8, wide), f32),
        centre=pltpu.VMEM((1, wide), f32),
        mean_narrow=pltpu.VMEM((1, width), f32),
        mean_wide=pltpu.VMEM((1, wide), f32),
        rstd_narrow=pltpu.VMEM((4, width), f32),
        rstd_wide=pltpu.VMEM((2, wide), f32),
        identity=pltpu.SMEM((rows + 2 * halo_rows,), jnp.int32),
        row_width=pltpu.SMEM((rows + 2 * halo_rows,), jnp.int32),
        masks=pltpu.SMEM((rows, 6), f32),
        counts=pltpu.SMEM((5,), f32),
        gather_local=dma((10,)),
        gather_send=dma((10, high - 1 + 7)),
        gather_recv=dma((10, high - 1 + 7)),
        halo_send=dma((2, 2)),
        halo_recv=dma((2, 2)),
        edge_send=dma((2, 2)),
        edge_recv=dma((2, 2)),
        samp_sem=dma((2,)),
        load_sem=dma((3,)),
        box_sem=dma((9 + pixels // chunk,)),
        staging_sem=dma((2, 2)),
        table_send=dma((4, max(sizes))),
        table_recv=dma((4, max(sizes))),
        syncs=sync_scratch(plan, sizes),
        **scatter,
    )
    result = launch(
        partial(whole_pass, sizes, in_kernel), ins, in_specs, outs, out_specs, scratch, 0, 63
    )
    if not in_kernel:
        result.grads = [
            lax.psum_scatter(
                lax.psum_scatter(g.astype(f32), "dp", scatter_dimension=0, tiled=True),
                "mp",
                scatter_dimension=1,
                tiled=True,
            )
            for g in result.grads
        ]
    return result


def hand_over(r):
    pieces = r.big_sem.shape[2]
    moves = []
    for i in range(pieces):
        for n, (src, through, dst) in enumerate(
            ((r.image_out, r.through_out, r.to_out), (r.image_grad, r.through_grad, r.to_grad))
        ):
            rows = src.shape[0] // pieces
            at = pl.ds(i * rows, rows)
            last = through if n == 0 else r.wide_grad
            moves.append(
                (
                    pltpu.make_async_copy(src.at[at], through.at[at], r.big_sem.at[n, 0, i]),
                    pltpu.make_async_copy(last.at[at], dst.at[at], r.big_sem.at[n, 1, i]),
                    None if n == 0 else at,
                )
            )
    for arrive, _, _ in moves:
        arrive.start()
    for src, dst in zip(r.grads, r.to_grads):
        dst[...] = src[...].astype(f32)
    for block in range(2):
        for j in range(2):
            norm = 2 * block + j
            r.to_mid_bias[block, j : j + 1, :] = r.narrow_sums[norm, 0:1, :]
            r.to_mid_gain[block, j : j + 1, :] = r.narrow_sums[norm, 1:2, :]
        r.to_out_bias[block : block + 1, :] = r.wide_sums[block, 0:1, :]
        r.to_out_gain[block : block + 1, :] = r.wide_sums[block, 1:2, :]
    width = r.to_mid_bias.shape[2]
    for tap_row in range(3):
        part = r.offset_grad[tap_row * width : (tap_row + 1) * width, :].astype(f32).T
        for tap_col in range(3):
            at = pl.ds((3 * tap_row + tap_col) * width, width)
            r.to_offset[:, at] = part[32 * tap_col : 32 * tap_col + offsets_count, :]
    r.to_bias[...] = r.bias_sum[:, 0 : r.to_bias.shape[1]]
    for arrive, leave, at in moves:
        arrive.wait()
        if at is not None:
            r.wide_grad[at, :] = r.through_grad[at, :].astype(f32)
        leave.start()
    for _, leave, _ in moves:
        leave.wait()


def results_of(back, image, norms, width):
    ins = dict(
        image_out=back.image_out,
        image_grad=back.image_grad,
        grads=back.grads,
        narrow_sums=back.narrow_sums,
        wide_sums=back.wide_sums,
        offset_grad=back.offset_grad,
        bias_sum=back.bias_sum,
    )
    like = [shape(g.shape, f32) for g in norms]
    outs = dict(
        to_out=shape(image.shape, bf16),
        to_grad=shape(image.shape, f32),
        to_grads=[shape(g.shape, f32) for g in back.grads],
        to_mid_gain=like[0],
        to_mid_bias=like[1],
        to_out_gain=like[2],
        to_out_bias=like[3],
        to_offset=shape((offsets_count, 9 * width), f32),
        to_bias=shape((1, offsets_count), f32),
    )
    specs = dict(image_out=anywhere, image_grad=anywhere)
    out_specs = dict((name, vmem) for name in outs)
    out_specs.update(to_out=anywhere, to_grad=anywhere)
    scratch = dict(
        big_sem=dma((2, 2, 8)),
        through_out=pltpu.VMEM(image.shape, bf16),
        through_grad=pltpu.VMEM(image.shape, bf16),
        wide_grad=pltpu.VMEM(image.shape, f32),
    )
    return launch(partial(hand_over), ins, specs, outs, out_specs, scratch, None, 60)


def per_device(
    image_in,
    cotangent,
    heights,
    widths,
    weight_in_a,
    weight_offset,
    bias_offset,
    weight_mid_a,
    weight_out_a,
    weight_in_b,
    weight_mid_b,
    weight_out_b,
    mid_gain,
    mid_bias,
    out_gain,
    out_bias,
):
    height, wide = image_in.shape[0], image_in.shape[2]
    sizes = (lax.axis_size("dp"), lax.axis_size("mp"))
    shards = (weight_in_a, weight_mid_a, weight_out_a, weight_in_b, weight_mid_b, weight_out_b)
    norms = (mid_gain, mid_bias, out_gain, out_bias)
    image = image_in.reshape(height * breadth, wide)
    back = run_kernel(
        image,
        cotangent.reshape(height * breadth, wide),
        heights,
        widths,
        shards,
        weight_offset.T,
        bias_offset,
        norms,
        sizes,
    )
    final = results_of(back, image, norms, weight_offset.shape[0] // 9)
    grads = final.to_grads
    return (
        final.to_out.reshape(image_in.shape),
        final.to_grad.reshape(image_in.shape),
        grads[5],
        final.to_offset.T,
        final.to_bias.reshape(bias_offset.shape),
        grads[4],
        grads[3],
        grads[2],
        grads[1],
        grads[0],
        final.to_mid_gain,
        final.to_mid_bias,
        final.to_out_gain,
        final.to_out_bias,
    )


def solution(mesh):
    rows, split, both = P(("dp", "mp"), None, None), P("dp", "mp"), P()
    in_specs = (rows, rows, both, both, split, both, both, split, split, split, split, split)
    in_specs += (both,) * 4
    out_specs = (rows, rows, split, both, both, split, split, split, split, split) + (both,) * 4
    return jax.shard_map(
        per_device, mesh=mesh, in_specs=in_specs, out_specs=out_specs, check_vma=False
    )
```
